32 devices in a mesh: seq: 8 (over y, x, core), fsdp: 4 (over z).
Axes of the slice: x: 2, y: 2, z: 4, core: 2. Of those that a mesh axis runs over, the one named last changes fastest.
Arguments:
- tokens: bfloat16 [4, 2048, 2048], P('fsdp', 'seq'), may hold values from -6 to 6
- lengths: int32 [4], replicated, may hold values from 1793 to 2048, as said below
- norm_attn: bfloat16 [2048], replicated, may hold values from 0.099609375 to 1.8984375
- norm_ffn: bfloat16 [2048], replicated, may hold values from 0.099609375 to 1.8984375
- w_query: bfloat16 [2048, 2048], P(('seq', 'fsdp')), may hold values from -0.125 to 0.125
- key_projection: bfloat16 [2048, 512], P(('seq', 'fsdp')), may hold values from -0.125 to 0.125
- value_projection: bfloat16 [2048, 512], P(('seq', 'fsdp')), may hold values from -0.125 to 0.125
- w_output: bfloat16 [2048, 2048], P(('seq', 'fsdp')), may hold values from -0.75 to 0.75
- w_gate: bfloat16 [2048, 8192], P('seq', 'fsdp'), may hold values from -0.125 to 0.125
- w_up: bfloat16 [2048, 8192], P('seq', 'fsdp'), may hold values from -0.125 to 0.125
- w_down: bfloat16 [2048, 8192], P('seq', 'fsdp'), may hold values from -0.0625 to 0.0625
- down_query: bfloat16 [2048, 8], replicated, may hold values from -0.125 to 0.125
- up_query: bfloat16 [2048, 8], replicated, may hold values from -1 to 1
- key_down_matrix: bfloat16 [2048, 8], replicated, may hold values from -0.125 to 0.125
- key_up_matrix: bfloat16 [512, 8], replicated, may hold values from -1 to 1
- value_down_matrix: bfloat16 [2048, 8], replicated, may hold values from -0.125 to 0.125
- value_up_matrix: bfloat16 [512, 8], replicated, may hold values from -1 to 1
- down_output: bfloat16 [2048, 8], replicated, may hold values from -0.75 to 0.75
- up_output: bfloat16 [2048, 8], replicated, may hold values from -1 to 1
- feature_query: bfloat16 [2048, 64], replicated, may hold values from -0.75 to 0.75
- key_feature_weight: bfloat16 [512, 64], replicated, may hold values from -0.75 to 0.75
- cotangent: bfloat16 [4, 2048, 2048], P('fsdp', 'seq'), may hold values from -6 to 6
Outputs:
- output: bfloat16 [4, 2048, 2048], P('fsdp', 'seq')
- grad_tokens: bfloat16 [4, 2048, 2048], P('fsdp', 'seq')
- grad_down_query: float32 [2048, 8], P(('seq', 'fsdp'))
- grad_up_query: float32 [2048, 8], P(('seq', 'fsdp'))
- grad_down_key: float32 [2048, 8], P(('seq', 'fsdp'))
- grad_up_key: float32 [512, 8], P(('seq', 'fsdp'))
- grad_down_value: float32 [2048, 8], P(('seq', 'fsdp'))
- grad_up_value: float32 [512, 8], P(('seq', 'fsdp'))
- grad_down_output: float32 [2048, 8], P(('seq', 'fsdp'))
- grad_up_output: float32 [2048, 8], P(('seq', 'fsdp'))
- grad_feature_query: float32 [2048, 64], P(('seq', 'fsdp'))
- key_feature_gradient: float32 [512, 64], P(('seq', 'fsdp'))
- transfer_loss: float32 [32], P(('seq', 'fsdp'))
The draws below stay inside these ranges and needn't reach their ends.
Inputs may be any that keep to these rules, and one draw needn't show every extreme that they name: lengths holds the real tokens of each lane; every lane's sequence reaches into the last 256 positions of its lane.
All inputs are finite; a program needn't handle non-finite values.
Results may differ from the reference program's by a relative error of at most 0.015.
Values may be sent and summed in bfloat16 or wider, within the bound.
No kernel may reach another device: no remote copies, remote signals or barrier semaphores. Data moves between devices by JAX's collectives and lax.ppermute only.
A program may use at most 320 MiB of HBM per device.

```python
import math
import jax
import jax.numpy as jnp
from jax import lax

MODEL_WIDTH = 2048
QUERY_HEADS = 32
KEY_VALUE_HEADS = 8
HEAD_SIZE = 64
FF = 8192
ADAPTER_RANK = 8
WINDOW_KEYS = 64
DEVICE_TOKENS = 256
LANE_TOK = 2048
LANES = 4


def draw_lengths(key, part):
    key = jax.random.fold_in(key, 17)
    short_key, full_key = jax.random.split(key)
    shortfall = jax.random.randint(short_key, (LANES,), 0, DEVICE_TOKENS)
    full_lane = jax.random.randint(full_key, (), 0, LANES)
    shortfall = jnp.where(jnp.arange(LANES) == full_lane, 0, shortfall)
    return (LANE_TOK - shortfall).astype(jnp.int32)


def block_levels(key, dims, shards, smallest, largest):
    level, own = 1.0, jax.random.fold_in(key, 6)
    for dim, shards_of in shards:
        heights = jnp.exp(jax.random.uniform(jax.random.fold_in(own, dim), (shards_of,), jnp.float32, smallest / len(shards), largest / len(shards)))
        level = level * jnp.repeat(heights, dims[dim] // shards_of).reshape([-1 if axis == dim else 1 for axis in range(len(dims))])
    return level


def scatter_about(rng, extent, spread, reach, pieces=(), held_as=jnp.bfloat16):
    drawn = spread * jax.random.normal(rng, extent, jnp.float32)
    if pieces:
        drawn = drawn * block_levels(rng, extent, pieces, -0.22, 0.18)
    return jnp.clip(drawn, -reach, reach).astype(held_as)


def setup_inputs(seed: int = 0) -> dict:
    key_list = jax.random.split(jax.random.key(seed), 23)
    tokens = scatter_about(key_list[0], (LANES, LANE_TOK, MODEL_WIDTH), 1.0, 6.0, ((0, 4), (1, 8)))
    lengths = draw_lengths(jax.random.fold_in(key_list[22], 71), 0)
    norm_attn = jnp.clip(1.0 + 0.18 * jax.random.normal(key_list[2], (MODEL_WIDTH,), jnp.float32), 0.099609375, 1.8984375).astype(jnp.bfloat16)
    norm_ffn = jnp.clip(1.0 + 0.18 * jax.random.normal(key_list[3], (MODEL_WIDTH,), jnp.float32), 0.099609375, 1.8984375).astype(jnp.bfloat16)
    w_query = scatter_about(key_list[4], (MODEL_WIDTH, QUERY_HEADS * HEAD_SIZE), MODEL_WIDTH ** -0.5, 0.125, ((0, 32),))
    key_projection = scatter_about(key_list[5], (MODEL_WIDTH, KEY_VALUE_HEADS * HEAD_SIZE), MODEL_WIDTH ** -0.5, 0.125, ((0, 32),))
    value_projection = scatter_about(key_list[6], (MODEL_WIDTH, KEY_VALUE_HEADS * HEAD_SIZE), MODEL_WIDTH ** -0.5, 0.125, ((0, 32),))
    w_output = scatter_about(key_list[7], (QUERY_HEADS * HEAD_SIZE, MODEL_WIDTH), (QUERY_HEADS * HEAD_SIZE // 32) ** -0.5, 0.75, ((0, 32),))
    w_gate = scatter_about(key_list[8], (MODEL_WIDTH, FF), MODEL_WIDTH ** -0.5, 0.125, ((0, 8), (1, 4)))
    w_up = scatter_about(key_list[9], (MODEL_WIDTH, FF), MODEL_WIDTH ** -0.5, 0.125, ((0, 8), (1, 4)))
    w_down = scatter_about(key_list[10], (MODEL_WIDTH, FF), FF ** -0.5, 0.0625, ((0, 8), (1, 4)))
    down_query = scatter_about(key_list[11], (MODEL_WIDTH, ADAPTER_RANK), MODEL_WIDTH ** -0.5, 0.125)
    up_query = scatter_about(key_list[12], (QUERY_HEADS * HEAD_SIZE, ADAPTER_RANK), (4 * ADAPTER_RANK) ** -0.5, 1.0)
    key_down_matrix = scatter_about(key_list[13], (MODEL_WIDTH, ADAPTER_RANK), MODEL_WIDTH ** -0.5, 0.125)
    key_up_matrix = scatter_about(key_list[14], (KEY_VALUE_HEADS * HEAD_SIZE, ADAPTER_RANK), (4 * ADAPTER_RANK) ** -0.5, 1.0)
    value_down_matrix = scatter_about(key_list[15], (MODEL_WIDTH, ADAPTER_RANK), MODEL_WIDTH ** -0.5, 0.125)
    value_up_matrix = scatter_about(key_list[16], (KEY_VALUE_HEADS * HEAD_SIZE, ADAPTER_RANK), (4 * ADAPTER_RANK) ** -0.5, 1.0)
    down_output = scatter_about(key_list[17], (QUERY_HEADS * HEAD_SIZE, ADAPTER_RANK), (QUERY_HEADS * HEAD_SIZE // 32) ** -0.5, 0.75)
    up_output = scatter_about(key_list[18], (MODEL_WIDTH, ADAPTER_RANK), (4 * ADAPTER_RANK) ** -0.5, 1.0)
    feature_query = scatter_about(key_list[19], (QUERY_HEADS * HEAD_SIZE, HEAD_SIZE), HEAD_SIZE ** -0.5, 0.75)
    key_feature_weight = scatter_about(key_list[20], (KEY_VALUE_HEADS * HEAD_SIZE, HEAD_SIZE), HEAD_SIZE ** -0.5, 0.75)
    cotangent = scatter_about(key_list[21], (LANES, LANE_TOK, MODEL_WIDTH), 1.0, 6.0, ((0, 4), (1, 8)))
    return dict(tokens=tokens, lengths=lengths, norm_attn=norm_attn, norm_ffn=norm_ffn, w_query=w_query, key_projection=key_projection, value_projection=value_projection, w_output=w_output, w_gate=w_gate, w_up=w_up, w_down=w_down, down_query=down_query, up_query=up_query, key_down_matrix=key_down_matrix, key_up_matrix=key_up_matrix, value_down_matrix=value_down_matrix, value_up_matrix=value_up_matrix, down_output=down_output, up_output=up_output, feature_query=feature_query, key_feature_weight=key_feature_weight, cotangent=cotangent)


epsilon = 1e-05
rope_base = 500000.0
precise = lax.Precision.HIGHEST

@jax.custom_vjp
def low(v):
    return lax.optimization_barrier(v.astype(jnp.bfloat16)).astype(jnp.float32)

@jax.custom_vjp
def low_back(v):
    return v

def low_keep(v):
    return (low(v), None)

def low_pass(kept, grad):
    return (grad,)

def back_keep(v):
    return (v, None)

def back_low(kept, grad):
    return (low(grad),)
low.defvjp(low_keep, low_pass)
low_back.defvjp(back_keep, back_low)

def rms_norm(values, gain):
    return values * lax.rsqrt(lax.optimization_barrier(jnp.mean(values * values, axis=-1, keepdims=True)) + epsilon) * gain

def rotary(positions):
    half_dim = HEAD_SIZE // 2
    inverse = rope_base ** (-(jnp.arange(half_dim, dtype=jnp.float32) * 2.0) / HEAD_SIZE)
    phase = positions.astype(jnp.float32)[:, None] * inverse[None, :]
    return (jnp.cos(phase)[:, None, :], jnp.sin(phase)[:, None, :])

def apply_rotary(vectors, cosine_lookup, sine_lookup):
    half_dim = vectors.shape[-1] // 2
    first_half = vectors[..., :half_dim]
    second_half = vectors[..., half_dim:]
    return jnp.concatenate([first_half * cosine_lookup - second_half * sine_lookup, second_half * cosine_lookup + first_half * sine_lookup], axis=-1)

def apply_feature_map(vectors, weights):
    logits_map = jnp.einsum('thd,hde->the', vectors, weights, precision=precise)
    return jnp.concatenate([jax.nn.softmax(logits_map, axis=-1), jax.nn.softmax(-logits_map, axis=-1)], axis=-1)

def attend_group(query_rows, query_feature_maps, keys_ext, values_ext, key_maps, key_valid, carry_state, carry_total):
    row_count = query_rows.shape[0]
    key_count = keys_ext.shape[0]
    offset = jnp.arange(row_count)[:, None] + (key_count - row_count) - jnp.arange(key_count)[None, :]
    window = (offset >= 0) & (offset < WINDOW_KEYS) & key_valid[None, :]
    linear = (offset >= WINDOW_KEYS) & key_valid[None, :]
    scores = jnp.einsum('tjd,sd->jts', query_rows, keys_ext, precision=precise) / math.sqrt(HEAD_SIZE)
    near_terms = low(jnp.exp(scores))
    far_terms = jnp.einsum('tjf,sf->jts', query_feature_maps, key_maps, precision=precise)
    weights = jnp.where(window[None], near_terms, 0.0) + jnp.where(linear[None], far_terms, 0.0)
    numerator = jnp.einsum('jts,sd->tjd', weights, values_ext, precision=precise) + jnp.einsum('tjf,fd->tjd', query_feature_maps, carry_state, precision=precise)
    denominator = jnp.transpose(lax.optimization_barrier(jnp.sum(weights, axis=-1))) + jnp.einsum('tjf,f->tj', query_feature_maps, carry_total, precision=precise)
    return numerator / denominator[..., None]

def lane_inputs(tokens_lane, frozen, adapters):
    norm_attn, norm_ffn, w_query, key_projection, value_projection, w_output, w_gate, w_up, w_down = frozen
    down_query, up_query, key_down_matrix, key_up_matrix, value_down_matrix, value_up_matrix, down_output, up_output, feature_query, key_feature_weight = adapters
    lane_token_length = tokens_lane.shape[0]
    normed = low(rms_norm(tokens_lane, norm_attn))

    def apply_projection(weight, down_factor, up_factor):
        narrow = low(jnp.dot(normed, down_factor, precision=precise))
        return low_back(jnp.dot(normed, weight, precision=precise) + jnp.dot(narrow, up_factor.T, precision=precise))
    cosine_lookup, sine_lookup = rotary(jnp.arange(lane_token_length))
    query_rows = low(apply_rotary(apply_projection(w_query, down_query, up_query).reshape(lane_token_length, QUERY_HEADS, HEAD_SIZE), cosine_lookup, sine_lookup))
    gathered_keys = low(apply_rotary(apply_projection(key_projection, key_down_matrix, key_up_matrix).reshape(lane_token_length, KEY_VALUE_HEADS, HEAD_SIZE), cosine_lookup, sine_lookup))
    gathered_values = low(apply_projection(value_projection, value_down_matrix, value_up_matrix).reshape(lane_token_length, KEY_VALUE_HEADS, HEAD_SIZE))
    return (query_rows, gathered_keys, gathered_values)

def softmax_teacher(query_rows, gathered_keys, gathered_values):
    lane_token_length = query_rows.shape[0]
    count_of_blocks = lane_token_length // DEVICE_TOKENS
    heads_per_group = QUERY_HEADS // KEY_VALUE_HEADS
    blocked_queries = query_rows.reshape(count_of_blocks, DEVICE_TOKENS, KEY_VALUE_HEADS, heads_per_group, HEAD_SIZE)
    key_heads = jnp.moveaxis(gathered_keys, 1, 0)
    value_heads = jnp.moveaxis(gathered_values, 1, 0)

    def one_block(item):
        block_index, single_query_block = item
        query_pos = block_index * DEVICE_TOKENS + jnp.arange(DEVICE_TOKENS)
        allowed = query_pos[:, None] >= jnp.arange(lane_token_length)[None, :]

        def one_head(head_item):
            query_head, key_head, value_head = head_item
            scores = jnp.einsum('tjd,sd->jts', query_head, key_head, precision=precise) / math.sqrt(HEAD_SIZE)
            scores = jnp.where(allowed[None], scores, -1e+30)
            probs = jax.nn.softmax(scores, axis=-1)
            return jnp.einsum('jts,sd->tjd', probs, value_head, precision=precise)
        per_head = lax.map(one_head, (jnp.moveaxis(single_query_block, 1, 0), key_heads, value_heads))
        return jnp.moveaxis(per_head, 0, 1)
    blocks = lax.map(one_block, (jnp.arange(count_of_blocks), blocked_queries))
    return blocks.reshape(lane_token_length, QUERY_HEADS * HEAD_SIZE)

def lane_forward(tokens_lane, lane_length, teacher_lane, frozen, adapters):
    norm_attn, norm_ffn, w_query, key_projection, value_projection, w_output, w_gate, w_up, w_down = frozen
    down_query, up_query, key_down_matrix, key_up_matrix, value_down_matrix, value_up_matrix, down_output, up_output, feature_query, key_feature_weight = adapters
    lane_token_length = tokens_lane.shape[0]
    query_rows, gathered_keys, gathered_values = lane_inputs(tokens_lane, frozen, adapters)
    count_of_blocks = lane_token_length // DEVICE_TOKENS
    heads_per_group = QUERY_HEADS // KEY_VALUE_HEADS
    blocked_queries = query_rows.reshape(count_of_blocks, DEVICE_TOKENS, KEY_VALUE_HEADS, heads_per_group, HEAD_SIZE)
    blocked_keys = gathered_keys.reshape(count_of_blocks, DEVICE_TOKENS, KEY_VALUE_HEADS, HEAD_SIZE)
    blocked_values = gathered_values.reshape(count_of_blocks, DEVICE_TOKENS, KEY_VALUE_HEADS, HEAD_SIZE)
    empty_border = jnp.zeros((1, WINDOW_KEYS, KEY_VALUE_HEADS, HEAD_SIZE), jnp.float32)
    key_ext = jnp.concatenate([jnp.concatenate([empty_border, blocked_keys[:-1, DEVICE_TOKENS - WINDOW_KEYS:]], axis=0), blocked_keys], axis=1)
    value_ext = jnp.concatenate([jnp.concatenate([empty_border, blocked_values[:-1, DEVICE_TOKENS - WINDOW_KEYS:]], axis=0), blocked_values], axis=1)
    query_features = feature_query.reshape(QUERY_HEADS, HEAD_SIZE, HEAD_SIZE)
    key_features = key_feature_weight.reshape(KEY_VALUE_HEADS, HEAD_SIZE, HEAD_SIZE)

    def block_step(block_carry, inputs):
        carry_state, carry_total = block_carry
        block_index, single_query_block, key_block, value_block = inputs
        query_feature_maps = low(apply_feature_map(single_query_block.reshape(DEVICE_TOKENS, QUERY_HEADS, HEAD_SIZE), query_features)).reshape(DEVICE_TOKENS, KEY_VALUE_HEADS, heads_per_group, 2 * HEAD_SIZE)
        key_maps = low(apply_feature_map(key_block, key_features))
        positions = block_index * DEVICE_TOKENS - WINDOW_KEYS + jnp.arange(DEVICE_TOKENS + WINDOW_KEYS)
        key_valid = positions >= 0
        attn_out = jax.vmap(attend_group, in_axes=(1, 1, 1, 1, 1, None, 0, 0), out_axes=1)(single_query_block, query_feature_maps, key_block, value_block, key_maps, key_valid, carry_state, carry_total)
        used_maps = key_maps[:DEVICE_TOKENS] * key_valid[:DEVICE_TOKENS, None, None].astype(jnp.float32)
        carry_state = carry_state + jnp.einsum('sgf,sgd->gfd', used_maps, value_block[:DEVICE_TOKENS], precision=precise)
        carry_total = carry_total + lax.optimization_barrier(jnp.sum(used_maps, axis=0))
        return ((carry_state, carry_total), attn_out)
    initial_state = (jnp.zeros((KEY_VALUE_HEADS, 2 * HEAD_SIZE, HEAD_SIZE), jnp.float32), jnp.zeros((KEY_VALUE_HEADS, 2 * HEAD_SIZE), jnp.float32))
    final_carry, attn_blocks = lax.scan(jax.checkpoint(block_step), initial_state, (jnp.arange(count_of_blocks), blocked_queries, key_ext, value_ext))
    row_mask = (jnp.arange(lane_token_length) < lane_length).astype(jnp.float32)
    attended = low(low_back(attn_blocks.reshape(lane_token_length, QUERY_HEADS * HEAD_SIZE) * row_mask[:, None]))
    difference = attended - teacher_lane * row_mask[:, None]
    loss_blocks = lax.optimization_barrier(jnp.sum((difference * difference).reshape(count_of_blocks, DEVICE_TOKENS * QUERY_HEADS * HEAD_SIZE), axis=1))
    narrow_out = low(jnp.dot(attended, down_output, precision=precise))
    branch = low_back(jnp.dot(attended, w_output, precision=precise) + jnp.dot(narrow_out, up_output.T, precision=precise))
    residual = tokens_lane + branch
    normed_ffn = low(rms_norm(residual, norm_ffn))
    gate_pre = low_back(jnp.dot(normed_ffn, w_gate, precision=precise))
    up_pre = low_back(jnp.dot(normed_ffn, w_up, precision=precise))
    hidden = low(jax.nn.silu(gate_pre) * up_pre)
    return (residual + jnp.dot(hidden, w_down.T, precision=precise), loss_blocks)

def reference(tokens, lengths, norm_attn, norm_ffn, w_query, key_projection, value_projection, w_output, w_gate, w_up, w_down, down_query, up_query, key_down_matrix, key_up_matrix, value_down_matrix, value_up_matrix, down_output, up_output, feature_query, key_feature_weight, cotangent):
    frozen = tuple((member.astype(jnp.float32) for member in (norm_attn, norm_ffn, w_query, key_projection, value_projection, w_output, w_gate, w_up, w_down)))
    adapters = tuple((member.astype(jnp.float32) for member in (down_query, up_query, key_down_matrix, key_up_matrix, value_down_matrix, value_up_matrix, down_output, up_output, feature_query, key_feature_weight)))
    tokens_wide = tokens.astype(jnp.float32)

    def teach(lane_item):
        query_rows, gathered_keys, gathered_values = lane_inputs(lane_item, frozen, adapters)
        return softmax_teacher(query_rows, gathered_keys, gathered_values)
    teachers = lax.map(teach, tokens_wide)

    def forward(lanes_in, adapter_args):

        def one_lane(lane_item):
            return lane_forward(lane_item[0], lane_item[1], lane_item[2], frozen, adapter_args)
        return lax.map(jax.checkpoint(one_lane), (lanes_in, lengths, teachers))
    results, pullback = jax.vjp(forward, tokens_wide, adapters)
    outputs, losses = results
    grad_in, grad_adapters = pullback((cotangent.astype(jnp.float32), jnp.ones_like(losses)))
    flat_losses = jnp.transpose(losses).reshape(-1)
    transfer_loss = jnp.cumsum(flat_losses) / jnp.sum(lengths).astype(jnp.float32)
    return (outputs.astype(jnp.bfloat16), grad_in.astype(jnp.bfloat16), grad_adapters[0], grad_adapters[1], grad_adapters[2], grad_adapters[3], grad_adapters[4], grad_adapters[5], grad_adapters[6], grad_adapters[7], grad_adapters[8], grad_adapters[9], transfer_loss)
```

```python
import math

import jax
import jax.numpy as jnp
from jax import lax
from jax.experimental import pallas as pl
from jax.experimental.pallas import tpu as pltpu
from jax.sharding import PartitionSpec as P

QUERY_HEADS = 32
KEY_VALUE_HEADS = 8
HEAD_SIZE = 64
WINDOW_KEYS = 64


epsilon = 1e-05
rope_base = 500000.0
precise = lax.Precision.HIGHEST
lowest_precision = -1e30
ONES = 16
SUB = 128


def prefix(x, axis, join, neutral, backward):
    count = lax.axis_size(axis)
    place = lax.axis_index(axis)
    ahead = count - 1 - place if backward else place
    gathered = jax.tree.map(
        lambda a, kind: lax.all_gather(a.astype(kind), axis), x, (jnp.bfloat16, jnp.bfloat16)
    )
    state = jax.tree.map(lambda a, e: jnp.zeros_like(a) + jnp.asarray(e, a.dtype), x, neutral)

    def one(hop, state):
        source = count - 1 - hop if backward else hop
        return join(
            state,
            jax.tree.map(
                lambda a, own: lax.dynamic_index_in_dim(a, source, 0, False).astype(own.dtype),
                gathered,
                x,
            ),
        )

    return lax.fori_loop(0, ahead, one, state)


def as_sent(x):

    def short(part):
        return part.astype(jnp.bfloat16) if part.dtype == jnp.float32 else part

    return jax.tree.map(short, x)


def shifted(value, axis, steps):
    count = lax.axis_size(axis)
    first, last = (max(0, -steps), min(count, count - steps))
    return lax.ppermute(value, axis, [(source, source + steps) for source in range(first, last)])


def rotary(positions):
    half_dim = HEAD_SIZE // 2
    inverse = rope_base ** (-(jnp.arange(half_dim, dtype=jnp.float32) * 2.0) / HEAD_SIZE)
    phase = positions.astype(jnp.float32)[:, None] * inverse[None, :]
    return (jnp.cos(phase)[:, None, :], jnp.sin(phase)[:, None, :])


def apply_rotary(vectors, cosine_lookup, sine_lookup):
    half_dim = vectors.shape[-1] // 2
    first_half = vectors[..., :half_dim]
    second_half = vectors[..., half_dim:]
    return jnp.concatenate(
        [
            first_half * cosine_lookup - second_half * sine_lookup,
            second_half * cosine_lookup + first_half * sine_lookup,
        ],
        axis=-1,
    )


def inverse_rotary(gradient, cosine_lookup, sine_lookup):
    half_dim = gradient.shape[-1] // 2
    first_half = gradient[..., :half_dim]
    second_half = gradient[..., half_dim:]
    return jnp.concatenate(
        [
            first_half * cosine_lookup + second_half * sine_lookup,
            second_half * cosine_lookup - first_half * sine_lookup,
        ],
        axis=-1,
    )


def apply_feature_map(vectors, weights):
    logits_map = jnp.einsum("thd,hde->the", vectors, weights, preferred_element_type=jnp.float32)
    return jnp.concatenate(
        [jax.nn.softmax(logits_map, axis=-1), jax.nn.softmax(-logits_map, axis=-1)], axis=-1
    )


def feature_back(vectors, weights, gradient):
    logits_map = jnp.einsum("thd,hde->the", vectors, weights, preferred_element_type=jnp.float32)
    plus_soft = jax.nn.softmax(logits_map, axis=-1)
    minus_soft = jax.nn.softmax(-logits_map, axis=-1)
    grad_plus = gradient[..., :HEAD_SIZE]
    grad_minus = gradient[..., HEAD_SIZE:]
    grad_logits = plus_soft * (
        grad_plus - jnp.sum(grad_plus * plus_soft, axis=-1, keepdims=True)
    ) - minus_soft * (grad_minus - jnp.sum(grad_minus * minus_soft, axis=-1, keepdims=True))
    grad_vectors = jnp.einsum(
        "the,hde->thd", grad_logits, weights, preferred_element_type=jnp.float32
    )
    grad_weights = jnp.einsum(
        "thd,the->hde", vectors, grad_logits, preferred_element_type=jnp.float32
    )
    return (grad_vectors, grad_weights)


def norm_back(values, inverse, gain, gradient):
    scaled = gradient * gain
    return inverse * scaled - values * inverse * inverse * inverse * jnp.mean(
        scaled * values, axis=-1, keepdims=True
    )


def coefficients(query_rows, query_feature_maps, keys_ext, key_maps, key_valid):
    row_count = query_rows.shape[0]
    key_count = keys_ext.shape[0]
    offset = (
        jnp.arange(row_count)[:, None] + (key_count - row_count) - jnp.arange(key_count)[None, :]
    )
    window = ((offset >= 0) & (offset < WINDOW_KEYS) & key_valid[None, :])[None]
    linear = ((offset >= WINDOW_KEYS) & key_valid[None, :])[None]
    scores = jnp.einsum(
        "tjd,sd->jts", query_rows, keys_ext, preferred_element_type=jnp.float32
    ) / math.sqrt(HEAD_SIZE)
    exp_scores = jnp.exp(scores)
    near_terms = lax.optimization_barrier(exp_scores.astype(jnp.bfloat16)).astype(jnp.float32)
    far_terms = jnp.einsum(
        "tjf,sf->jts", query_feature_maps, key_maps, preferred_element_type=jnp.float32
    )
    weights = jnp.where(window, near_terms, 0.0) + jnp.where(linear, far_terms, 0.0)
    return (weights, exp_scores, window, linear)


def attend_group(operands, key_valid):
    query_rows, query_feature_maps, keys_ext, values_ext, key_maps, carry_state, carry_total = (
        operands
    )
    weights, exp_scores, window, linear = coefficients(
        query_rows, query_feature_maps, keys_ext, key_maps, key_valid
    )
    maps_wide = query_feature_maps.astype(jnp.float32)
    numerator = jnp.einsum(
        "jts,sd->tjd", weights, values_ext.astype(jnp.float32), precision=precise
    ) + jnp.einsum("tjf,fd->tjd", maps_wide, carry_state, precision=precise)
    denominator = jnp.transpose(jnp.sum(weights, axis=-1)) + jnp.einsum(
        "tjf,f->tj", maps_wide, carry_total, precision=precise
    )
    return (numerator, denominator)


def attend_back(operands, key_valid):
    (
        query_rows,
        query_feature_maps,
        keys_ext,
        values_ext,
        key_maps,
        carry_state,
        carry_total,
        numerator,
        denominator,
        grad_out,
    ) = operands
    weights, exp_scores, window, linear = coefficients(
        query_rows, query_feature_maps, keys_ext, key_maps, key_valid
    )
    grad_numer = grad_out / denominator[..., None]
    grad_denom = -jnp.sum(grad_out * numerator, axis=-1) / (denominator * denominator)
    grad_weights = (
        jnp.einsum("tjd,sd->jts", grad_numer, values_ext, preferred_element_type=jnp.float32)
        + jnp.transpose(grad_denom)[:, :, None]
    )
    grad_scores = jnp.where(window, grad_weights * exp_scores, 0.0) / math.sqrt(HEAD_SIZE)
    grad_far = jnp.where(linear, grad_weights, 0.0)
    grad_queries = jnp.einsum(
        "jts,sd->tjd", grad_scores, keys_ext, preferred_element_type=jnp.float32
    )
    grad_keys = jnp.einsum(
        "jts,tjd->sd", grad_scores, query_rows, preferred_element_type=jnp.float32
    )
    grad_qmaps = (
        jnp.einsum("jts,sf->tjf", grad_far, key_maps, preferred_element_type=jnp.float32)
        + jnp.einsum("tjd,fd->tjf", grad_numer, carry_state, preferred_element_type=jnp.float32)
        + grad_denom[..., None] * carry_total
    )
    grad_kmaps = jnp.einsum(
        "jts,tjf->sf", grad_far, query_feature_maps, preferred_element_type=jnp.float32
    )
    grad_values = jnp.einsum("jts,tjd->sd", weights, grad_numer, preferred_element_type=jnp.float32)
    grad_state = jnp.einsum(
        "tjf,tjd->fd", query_feature_maps, grad_numer, preferred_element_type=jnp.float32
    )
    grad_total = jnp.einsum(
        "tjf,tj->f", query_feature_maps, grad_denom, preferred_element_type=jnp.float32
    )
    return (grad_queries, grad_keys, grad_values, grad_qmaps, grad_kmaps, grad_state, grad_total)


def add_pair(earlier, later_part):
    return (earlier[0] + later_part[0], earlier[1] + later_part[1])


def local(
    tokens,
    lengths,
    norm_attn,
    norm_ffn,
    w_query,
    key_projection,
    value_projection,
    w_output,
    w_gate,
    w_up,
    w_down,
    down_query,
    up_query,
    key_down_matrix,
    key_up_matrix,
    value_down_matrix,
    value_up_matrix,
    down_output,
    up_output,
    feature_query,
    key_feature_weight,
    cotangent,
):
    rows_per_block = tokens.shape[1]
    ext_rows = rows_per_block + WINDOW_KEYS
    heads_per_group = QUERY_HEADS // KEY_VALUE_HEADS
    feature_width = 2 * HEAD_SIZE
    inputs_wide = tokens[0].astype(jnp.float32)
    cot_narrow = cotangent[0]
    cot_wide = cot_narrow.astype(jnp.float32)
    seq_index = lax.axis_index("seq")
    lane_length = lengths[lax.axis_index("fsdp")]
    positions = seq_index * rows_per_block + jnp.arange(rows_per_block)
    cosine_lookup, sine_lookup = rotary(positions)
    gain_attn = norm_attn.astype(jnp.float32)
    gain_ffn = norm_ffn.astype(jnp.float32)
    inverse_attn = lax.rsqrt(jnp.mean(inputs_wide * inputs_wide, axis=-1, keepdims=True) + epsilon)
    normed = (inputs_wide * inverse_attn * gain_attn).astype(jnp.bfloat16)
    pieces = (
        lax.all_gather(w_query, ("seq", "fsdp"), axis=0, tiled=True),
        lax.all_gather(key_projection, ("seq", "fsdp"), axis=0, tiled=True),
        lax.all_gather(value_projection, ("seq", "fsdp"), axis=0, tiled=True),
    )
    sliced = normed
    query_pre, key_before_rotation, value_before_adapter = tuple(
        (jnp.dot(sliced, block_piece, preferred_element_type=jnp.float32) for block_piece in pieces)
    )
    narrow_query = jnp.dot(normed, down_query, preferred_element_type=jnp.float32).astype(
        jnp.bfloat16
    )
    narrow_key = jnp.dot(normed, key_down_matrix, preferred_element_type=jnp.float32).astype(
        jnp.bfloat16
    )
    narrow_value = jnp.dot(normed, value_down_matrix, preferred_element_type=jnp.float32).astype(
        jnp.bfloat16
    )
    query_pre = query_pre + jnp.dot(narrow_query, up_query.T, preferred_element_type=jnp.float32)
    key_before_rotation = key_before_rotation + jnp.dot(
        narrow_key, key_up_matrix.T, preferred_element_type=jnp.float32
    )
    value_before_adapter = value_before_adapter + jnp.dot(
        narrow_value, value_up_matrix.T, preferred_element_type=jnp.float32
    )
    query_rows = apply_rotary(
        query_pre.reshape(rows_per_block, QUERY_HEADS, HEAD_SIZE), cosine_lookup, sine_lookup
    ).astype(jnp.bfloat16)
    device_keys = apply_rotary(
        key_before_rotation.reshape(rows_per_block, KEY_VALUE_HEADS, HEAD_SIZE),
        cosine_lookup,
        sine_lookup,
    ).astype(jnp.bfloat16)
    device_values = value_before_adapter.reshape(rows_per_block, KEY_VALUE_HEADS, HEAD_SIZE).astype(
        jnp.bfloat16
    )
    softmax_query_rows = query_rows.reshape(
        rows_per_block, KEY_VALUE_HEADS, heads_per_group, HEAD_SIZE
    )
    teacher_init = (
        jnp.full((KEY_VALUE_HEADS, heads_per_group, rows_per_block), lowest_precision, jnp.float32),
        jnp.zeros((KEY_VALUE_HEADS, heads_per_group, rows_per_block), jnp.float32),
        jnp.zeros((KEY_VALUE_HEADS, heads_per_group, rows_per_block, HEAD_SIZE), jnp.float32),
        jnp.zeros((WINDOW_KEYS, KEY_VALUE_HEADS, HEAD_SIZE), jnp.bfloat16),
        jnp.zeros((WINDOW_KEYS, KEY_VALUE_HEADS, HEAD_SIZE), jnp.bfloat16),
    )
    portion_keys = lax.all_gather(
        device_keys.reshape(rows_per_block, KEY_VALUE_HEADS * HEAD_SIZE), "seq", axis=0, tiled=True
    )
    portion_values = lax.all_gather(
        device_values.reshape(rows_per_block, KEY_VALUE_HEADS * HEAD_SIZE),
        "seq",
        axis=0,
        tiled=True,
    )
    count_of_shards = portion_keys.shape[0] // rows_per_block
    sharded_keys = portion_keys.reshape(count_of_shards, rows_per_block, KEY_VALUE_HEADS, HEAD_SIZE)
    sharded_values = portion_values.reshape(
        count_of_shards, rows_per_block, KEY_VALUE_HEADS, HEAD_SIZE
    )

    def one_shard(inner, item):
        best, total, accum, rim_keys, rim_values = inner
        shard_number, shard_keys, shard_values = item
        shard_start = shard_number * rows_per_block
        scores = jnp.einsum(
            "tgjd,sgd->gjts", softmax_query_rows, shard_keys, preferred_element_type=jnp.float32
        ) / math.sqrt(HEAD_SIZE)
        allowed = (positions[:, None] >= (shard_start + jnp.arange(rows_per_block))[None, :])[
            None, None
        ]
        masked = jnp.where(allowed, scores, lowest_precision)
        new_best = jnp.maximum(best, jnp.max(masked, axis=-1))
        probs = jnp.where(allowed, jnp.exp(masked - new_best[..., None]), 0.0)
        factor = jnp.exp(best - new_best)
        total = total * factor + jnp.sum(probs, axis=-1)
        accum = accum * factor[..., None] + jnp.einsum(
            "gjts,sgd->gjtd", probs, shard_values.astype(jnp.float32)
        )
        is_before = shard_start // rows_per_block == seq_index - 1
        rim_keys = jnp.where(is_before, shard_keys[rows_per_block - WINDOW_KEYS :], rim_keys)
        rim_values = jnp.where(is_before, shard_values[rows_per_block - WINDOW_KEYS :], rim_values)
        return ((new_best, total, accum, rim_keys, rim_values), None)

    result, unused = lax.scan(
        one_shard, teacher_init, (jnp.arange(count_of_shards), sharded_keys, sharded_values)
    )
    best_all, total_all, accum_all, rim_keys, rim_values = result
    teacher = jnp.transpose(accum_all / total_all[..., None], (2, 0, 1, 3)).reshape(
        rows_per_block, QUERY_HEADS * HEAD_SIZE
    )
    keys_ext = jnp.concatenate([rim_keys, device_keys], axis=0)
    values_ext = jnp.concatenate([rim_values, device_values], axis=0)
    query_features = feature_query.reshape(QUERY_HEADS, HEAD_SIZE, HEAD_SIZE)
    key_features = key_feature_weight.reshape(KEY_VALUE_HEADS, HEAD_SIZE, HEAD_SIZE)
    query_feature_maps = apply_feature_map(query_rows, query_features).astype(jnp.bfloat16)
    key_maps = apply_feature_map(keys_ext, key_features).astype(jnp.bfloat16)
    ext_positions = seq_index * rows_per_block - WINDOW_KEYS + jnp.arange(ext_rows)
    key_valid = ext_positions >= 0
    valid_rows = key_valid[:rows_per_block].astype(jnp.float32)
    used_maps = key_maps[:rows_per_block].astype(jnp.float32) * valid_rows[:, None, None]
    values_head = values_ext[:rows_per_block].astype(jnp.float32)
    local_state = jnp.einsum("sgf,sgd->gfd", used_maps, values_head, precision=precise)
    local_total = jnp.sum(used_maps, axis=0)
    zero_pair = (
        jnp.zeros((KEY_VALUE_HEADS, feature_width, HEAD_SIZE), jnp.float32),
        jnp.zeros((KEY_VALUE_HEADS, feature_width), jnp.float32),
    )
    state_in, total_in = prefix((local_state, local_total), "seq", add_pair, zero_pair, False)
    queries_by_group = jnp.moveaxis(
        query_rows.reshape(rows_per_block, KEY_VALUE_HEADS, heads_per_group, HEAD_SIZE), 1, 0
    )
    query_maps_by_group = jnp.moveaxis(
        query_feature_maps.reshape(rows_per_block, KEY_VALUE_HEADS, heads_per_group, feature_width),
        1,
        0,
    )
    grouped_keys = jnp.moveaxis(keys_ext, 1, 0)
    grouped_values = jnp.moveaxis(values_ext, 1, 0)
    grouped_kmaps = jnp.moveaxis(key_maps, 1, 0)

    def forward_group(operands):
        return attend_group(operands, key_valid)

    numerator, denominator = lax.map(
        forward_group,
        (
            queries_by_group,
            query_maps_by_group,
            grouped_keys,
            grouped_values,
            grouped_kmaps,
            state_in,
            total_in,
        ),
    )
    row_mask = (positions < lane_length).astype(jnp.float32)
    attn_mixed = jnp.moveaxis(numerator / denominator[..., None], 0, 1).reshape(
        rows_per_block, QUERY_HEADS * HEAD_SIZE
    )
    attended = (attn_mixed * row_mask[:, None]).astype(jnp.bfloat16)
    difference = attended.astype(jnp.float32) - teacher * row_mask[:, None]
    local_loss = jnp.sum(difference * difference)
    sliced = attended
    branch = jnp.dot(
        sliced,
        lax.all_gather(w_output, ("seq", "fsdp"), axis=0, tiled=True),
        preferred_element_type=jnp.float32,
    )
    narrow_out = jnp.dot(attended, down_output, preferred_element_type=jnp.float32).astype(
        jnp.bfloat16
    )
    branch = branch + jnp.dot(narrow_out, up_output.T, preferred_element_type=jnp.float32)
    residual = inputs_wide + branch
    inverse_ffn = lax.rsqrt(jnp.mean(residual * residual, axis=-1, keepdims=True) + epsilon)
    normed_ffn = (residual * inverse_ffn * gain_ffn).astype(jnp.bfloat16)
    ffn_weights = (
        lax.all_gather(w_gate, "fsdp", axis=1, tiled=True),
        lax.all_gather(w_up, "fsdp", axis=1, tiled=True),
        lax.all_gather(w_down, "fsdp", axis=1, tiled=True),
    )
    pieces = (
        lax.all_gather(ffn_weights[0], "seq", axis=0, tiled=True),
        lax.all_gather(ffn_weights[1], "seq", axis=0, tiled=True),
    )
    sliced = normed_ffn
    gate_pre = jnp.dot(sliced, pieces[0], preferred_element_type=jnp.float32)
    up_pre = jnp.dot(sliced, pieces[1], preferred_element_type=jnp.float32)
    sigmoid_gate = jax.nn.sigmoid(gate_pre)
    silu_gate = gate_pre * sigmoid_gate
    hidden = (silu_gate * up_pre).astype(jnp.bfloat16)
    ffn_part = jnp.dot(
        hidden,
        lax.all_gather(ffn_weights[2], "seq", axis=0, tiled=True).T,
        preferred_element_type=jnp.float32,
    )
    output = (residual + ffn_part).astype(jnp.bfloat16)
    sliced = cot_narrow
    grad_hidden = jnp.dot(
        sliced,
        lax.all_gather(ffn_weights[2], "seq", axis=0, tiled=True),
        preferred_element_type=jnp.float32,
    )
    grad_gate = (
        grad_hidden * up_pre * sigmoid_gate * (1.0 + gate_pre * (1.0 - sigmoid_gate))
    ).astype(jnp.bfloat16)
    grad_up = (grad_hidden * silu_gate).astype(jnp.bfloat16)
    pieces = lax.all_gather((ffn_weights[0], ffn_weights[1]), "seq", axis=0, tiled=True)
    grad_part = jnp.dot(grad_gate, pieces[0].T, preferred_element_type=jnp.float32) + jnp.dot(
        grad_up, pieces[1].T, preferred_element_type=jnp.float32
    )
    grad_residual = cot_wide + norm_back(residual, inverse_ffn, gain_ffn, grad_part)
    grad_branch = grad_residual.astype(jnp.bfloat16)
    grad_narrow_out = jnp.dot(grad_branch, up_output, preferred_element_type=jnp.float32)
    grad_up_output = jnp.dot(grad_branch.T, narrow_out, preferred_element_type=jnp.float32)
    grad_down_output = jnp.dot(attended.T, grad_narrow_out, preferred_element_type=jnp.float32)
    attended_gradient = (
        jnp.dot(
            grad_branch,
            lax.all_gather(w_output, ("seq", "fsdp"), axis=0, tiled=True).T,
            preferred_element_type=jnp.float32,
        )
        + jnp.dot(grad_narrow_out, down_output.T, preferred_element_type=jnp.float32)
        + 2.0 * difference
    )
    attended_gradient = (
        lax.optimization_barrier(attended_gradient.astype(jnp.bfloat16)).astype(jnp.float32)
        * row_mask[:, None]
    )
    gradient_by_group = jnp.moveaxis(
        attended_gradient.reshape(rows_per_block, KEY_VALUE_HEADS, heads_per_group, HEAD_SIZE), 1, 0
    )

    def backward_group(operands):
        return attend_back(operands, key_valid)

    grad_q, grad_k, grad_v, grad_qm, grad_km, grad_state, grad_total = lax.map(
        backward_group,
        (
            queries_by_group,
            query_maps_by_group,
            grouped_keys,
            grouped_values,
            grouped_kmaps,
            state_in,
            total_in,
            numerator,
            denominator,
            gradient_by_group,
        ),
    )
    later_state, later_total = prefix((grad_state, grad_total), "seq", add_pair, zero_pair, True)
    values_grouped_head = jnp.moveaxis(values_head, 1, 0)
    used_grouped = jnp.moveaxis(used_maps, 1, 0)
    kmaps_head = grad_km[:, :rows_per_block] + valid_rows[None, :, None] * (
        jnp.einsum("gfd,gsd->gsf", later_state, values_grouped_head, precision=precise)
        + later_total[:, None, :]
    )
    grad_km = jnp.concatenate([kmaps_head, grad_km[:, rows_per_block:]], axis=1)
    values_grad_head = grad_v[:, :rows_per_block] + jnp.einsum(
        "gsf,gfd->gsd", used_grouped, later_state, precision=precise
    )
    grad_v = jnp.concatenate([values_grad_head, grad_v[:, rows_per_block:]], axis=1)
    grad_k_feat, key_feature_gradient = feature_back(
        keys_ext, key_features, jnp.moveaxis(grad_km, 0, 1)
    )
    gathered_key_gradient = jnp.moveaxis(grad_k, 0, 1) + grad_k_feat
    gathered_value_gradient = jnp.moveaxis(grad_v, 0, 1)
    grad_q_feat, grad_feature_query = feature_back(
        query_rows,
        query_features,
        jnp.moveaxis(grad_qm, 0, 1).reshape(rows_per_block, QUERY_HEADS, feature_width),
    )
    grad_queries_rot = (
        jnp.moveaxis(grad_q, 0, 1).reshape(rows_per_block, QUERY_HEADS, HEAD_SIZE) + grad_q_feat
    )
    back_keys, back_values = (
        shifted(
            gathered_key_gradient[:WINDOW_KEYS]
            .reshape(WINDOW_KEYS, KEY_VALUE_HEADS * HEAD_SIZE)
            .astype(jnp.bfloat16),
            "seq",
            -1,
        ).astype(jnp.float32),
        shifted(
            as_sent(
                gathered_value_gradient[:WINDOW_KEYS].reshape(
                    WINDOW_KEYS, KEY_VALUE_HEADS * HEAD_SIZE
                )
            ),
            "seq",
            -1,
        ),
    )
    trailing_keys = gathered_key_gradient[WINDOW_KEYS:].reshape(
        rows_per_block, KEY_VALUE_HEADS * HEAD_SIZE
    )
    trailing_values = gathered_value_gradient[WINDOW_KEYS:].reshape(
        rows_per_block, KEY_VALUE_HEADS * HEAD_SIZE
    )
    trailing_keys = jnp.concatenate(
        [
            trailing_keys[: rows_per_block - WINDOW_KEYS],
            trailing_keys[rows_per_block - WINDOW_KEYS :] + back_keys,
        ],
        axis=0,
    )
    trailing_values = jnp.concatenate(
        [
            trailing_values[: rows_per_block - WINDOW_KEYS],
            trailing_values[rows_per_block - WINDOW_KEYS :] + back_values,
        ],
        axis=0,
    )
    grad_query_pre = (
        inverse_rotary(grad_queries_rot, cosine_lookup, sine_lookup)
        .reshape(rows_per_block, QUERY_HEADS * HEAD_SIZE)
        .astype(jnp.bfloat16)
    )
    grad_key_pre = (
        inverse_rotary(
            trailing_keys.reshape(rows_per_block, KEY_VALUE_HEADS, HEAD_SIZE),
            cosine_lookup,
            sine_lookup,
        )
        .reshape(rows_per_block, KEY_VALUE_HEADS * HEAD_SIZE)
        .astype(jnp.bfloat16)
    )
    grad_value_pre = trailing_values.astype(jnp.bfloat16)
    grad_narrow_query = jnp.dot(grad_query_pre, up_query, preferred_element_type=jnp.float32)
    grad_narrow_key = jnp.dot(grad_key_pre, key_up_matrix, preferred_element_type=jnp.float32)
    grad_narrow_value = jnp.dot(grad_value_pre, value_up_matrix, preferred_element_type=jnp.float32)
    grad_up_query = jnp.dot(grad_query_pre.T, narrow_query, preferred_element_type=jnp.float32)
    grad_up_key = jnp.dot(grad_key_pre.T, narrow_key, preferred_element_type=jnp.float32)
    grad_up_value = jnp.dot(grad_value_pre.T, narrow_value, preferred_element_type=jnp.float32)
    grad_down_query = jnp.dot(normed.T, grad_narrow_query, preferred_element_type=jnp.float32)
    grad_down_key = jnp.dot(normed.T, grad_narrow_key, preferred_element_type=jnp.float32)
    grad_down_value = jnp.dot(normed.T, grad_narrow_value, preferred_element_type=jnp.float32)
    pieces = lax.all_gather(
        (w_query, key_projection, value_projection), ("seq", "fsdp"), axis=0, tiled=True
    )
    grad_normed = (
        jnp.dot(grad_query_pre, pieces[0].T, preferred_element_type=jnp.float32)
        + jnp.dot(grad_key_pre, pieces[1].T, preferred_element_type=jnp.float32)
        + jnp.dot(grad_value_pre, pieces[2].T, preferred_element_type=jnp.float32)
    )
    grad_normed = grad_normed + jnp.dot(
        grad_narrow_query, down_query.T, preferred_element_type=jnp.float32
    )
    grad_normed = grad_normed + jnp.dot(
        grad_narrow_key, key_down_matrix.T, preferred_element_type=jnp.float32
    )
    grad_normed = grad_normed + jnp.dot(
        grad_narrow_value, value_down_matrix.T, preferred_element_type=jnp.float32
    )
    grad_tokens = (
        grad_residual + norm_back(inputs_wide, inverse_attn, gain_attn, grad_normed)
    ).astype(jnp.bfloat16)
    device_count = lax.axis_size(("seq", "fsdp"))
    device_number = lax.axis_index(("seq", "fsdp"))
    loss_terms = jnp.where(jnp.arange(device_count) >= device_number, local_loss, 0.0)
    summed = (
        lax.psum_scatter(grad_down_query, ("seq", "fsdp"), scatter_dimension=0, tiled=True),
        lax.psum_scatter(grad_up_query, ("seq", "fsdp"), scatter_dimension=0, tiled=True),
        lax.psum_scatter(grad_down_key, ("seq", "fsdp"), scatter_dimension=0, tiled=True),
        lax.psum_scatter(grad_up_key, ("seq", "fsdp"), scatter_dimension=0, tiled=True),
        lax.psum_scatter(grad_down_value, ("seq", "fsdp"), scatter_dimension=0, tiled=True),
        lax.psum_scatter(grad_up_value, ("seq", "fsdp"), scatter_dimension=0, tiled=True),
        lax.psum_scatter(grad_down_output, ("seq", "fsdp"), scatter_dimension=0, tiled=True),
        lax.psum_scatter(grad_up_output, ("seq", "fsdp"), scatter_dimension=0, tiled=True),
        lax.psum_scatter(
            grad_feature_query.reshape(QUERY_HEADS * HEAD_SIZE, HEAD_SIZE),
            ("seq", "fsdp"),
            scatter_dimension=0,
            tiled=True,
        ),
        lax.psum_scatter(
            key_feature_gradient.reshape(KEY_VALUE_HEADS * HEAD_SIZE, HEAD_SIZE),
            ("seq", "fsdp"),
            scatter_dimension=0,
            tiled=True,
        ),
        lax.psum_scatter(loss_terms, ("seq", "fsdp"), scatter_dimension=0, tiled=True),
    )
    transfer_loss = summed[10] / jnp.sum(lengths).astype(jnp.float32)
    return (
        output[None],
        grad_tokens[None],
        summed[0],
        summed[1],
        summed[2],
        summed[3],
        summed[4],
        summed[5],
        summed[6],
        summed[7],
        summed[8],
        summed[9],
        transfer_loss,
    )

def halves_rotated(first_half, second_half, cosine, sine):
    return (
        first_half * cosine - second_half * sine,
        second_half * cosine + first_half * sine,
    )


def soft_pair(logits):
    plus = jnp.exp(logits - jnp.max(logits, axis=0, keepdims=True))
    minus = jnp.exp(jnp.min(logits, axis=0, keepdims=True) - logits)
    plus = plus * (1.0 / jnp.sum(plus, axis=0, keepdims=True))
    minus = minus * (1.0 / jnp.sum(minus, axis=0, keepdims=True))
    return plus, minus


def mm(a, b):
    return jnp.dot(a, b, preferred_element_type=jnp.float32)


def mm_nt(a, b):
    return lax.dot_general(a, b, (((1,), (1,)), ((), ())), preferred_element_type=jnp.float32)


def split_wide(x):
    high = x.astype(jnp.bfloat16)
    low = (x - high.astype(jnp.float32)).astype(jnp.bfloat16)
    return high, low


def project_kernel(
    x_ref, w_ref, up_ref, map_ref, cos_ref, sin_ref,
    q_ref, kt_ref, vt_ref, k_ref, v_ref, pq_ref, pkt_ref, pk_ref, narrow_ref,
):
    group = q_ref.shape[0] // HEAD_SIZE
    half = HEAD_SIZE // 2
    width = (group + 2) * HEAD_SIZE
    full = mm_nt(w_ref[...], x_ref[...])
    narrow = full[width:].astype(jnp.bfloat16)
    narrow_ref[...] = narrow
    pre = full[:width] + mm(up_ref[...], narrow)
    cosine, sine = cos_ref[...], sin_ref[...]
    for head in range(group + 1):
        base = head * HEAD_SIZE
        low_half, high_half = halves_rotated(
            pre[base : base + half], pre[base + half : base + HEAD_SIZE], cosine, sine
        )
        wide = jnp.concatenate([low_half, high_half], axis=0)
        vector = wide.astype(jnp.bfloat16)
        logits = mm(map_ref[base : base + HEAD_SIZE], vector)
        plus, minus = soft_pair(logits)
        maps = jnp.concatenate([plus, minus], axis=0)
        if head < group:
            q_ref[base : base + HEAD_SIZE] = vector
            pq_ref[2 * base : 2 * base + 2 * HEAD_SIZE] = maps.astype(jnp.bfloat16)
        else:
            kt_ref[...] = vector
            k_ref[...] = jnp.transpose(wide).astype(jnp.bfloat16)
            pkt_ref[...] = maps.astype(jnp.bfloat16)
            pk_ref[...] = jnp.transpose(maps).astype(jnp.bfloat16)
    values = pre[width - HEAD_SIZE : width]
    vt_ref[:HEAD_SIZE] = values.astype(jnp.bfloat16)
    vt_ref[HEAD_SIZE:] = jnp.ones((ONES, values.shape[1]), jnp.bfloat16)
    v_ref[...] = jnp.transpose(values).astype(jnp.bfloat16)


def side_by_side(ref, size, group, columns):
    return jnp.concatenate(
        [ref[head * size : (head + 1) * size, columns] for head in range(group)], axis=1
    )


def band(group):
    shape = (2 * SUB, group * SUB)
    query_at = lax.rem(lax.broadcasted_iota(jnp.int32, shape, 1), SUB)
    key_at = lax.broadcasted_iota(jnp.int32, shape, 0) - SUB
    return query_at - key_at, key_at


def forward_kernel(
    length_ref, q_ref, pq_ref, k_ref, k_before, pk_ref, pk_before, vt_ref, vt_before,
    att_ref, out_ref, denom_ref, states_ref, state,
):
    step = pl.program_id(0)
    group = q_ref.shape[0] // HEAD_SIZE
    rows = q_ref.shape[1]

    @pl.when(step == 0)
    def _():
        state[...] = jnp.zeros_like(state)

    for sub in range(rows // SUB):
        columns = slice(sub * SUB, (sub + 1) * SUB)
        queries = side_by_side(q_ref, HEAD_SIZE, group, columns)
        query_maps = side_by_side(pq_ref, 2 * HEAD_SIZE, group, columns)
        if sub == 0:
            keys = jnp.concatenate([k_before[...], k_ref[:SUB]], axis=0)
            key_maps = jnp.concatenate([pk_before[...], pk_ref[:SUB]], axis=0)
            values = jnp.concatenate([vt_before[...], vt_ref[:, :SUB]], axis=1)
        else:
            around = slice((sub - 1) * SUB, (sub + 1) * SUB)
            keys, key_maps, values = k_ref[around], pk_ref[around], vt_ref[:, around]
        distance, key_at = band(group)
        window = (distance >= 0) & (distance < WINDOW_KEYS)
        linear = distance >= WINDOW_KEYS
        if sub == 0:
            inside = (key_at >= 0) | (step > 0)
            window, linear = window & inside, linear & inside
        near = jnp.exp(mm(keys, queries) * (1.0 / math.sqrt(HEAD_SIZE)))
        far = mm(key_maps, query_maps)
        weights = jnp.where(window, near, jnp.where(linear, far, 0.0)).astype(jnp.bfloat16)
        states_ref[sub] = state[...]
        high, low = split_wide(state[...])
        total = mm(values, weights) + mm(
            jnp.concatenate([high, low], axis=1),
            jnp.concatenate([query_maps, query_maps], axis=0),
        )
        denom = total[HEAD_SIZE : HEAD_SIZE + 1]
        out = total[:HEAD_SIZE] * (1.0 / denom)
        at = (
            step * rows
            + sub * SUB
            + lax.rem(lax.broadcasted_iota(jnp.int32, out.shape, 1), SUB)
        )
        attended = jnp.where(at < length_ref[0], out, 0.0).astype(jnp.bfloat16)
        for head in range(group):
            lanes = slice(head * SUB, (head + 1) * SUB)
            base = head * HEAD_SIZE
            out_ref[base : base + HEAD_SIZE, columns] = out[:, lanes]
            att_ref[base : base + HEAD_SIZE, columns] = attended[:, lanes]
            denom_ref[head : head + 1, columns] = denom[:, lanes]
        update = mm(values[:, :SUB], key_maps[:SUB])
        if sub == 0:
            update = jnp.where(step > 0, update, 0.0)
        state[...] = state[...] + update


def teacher_kernel(length_ref, q_ref, k_ref, vt_ref, att_ref, diff_ref, loss_ref):
    step = pl.program_id(0)
    group = q_ref.shape[0] // HEAD_SIZE
    rows = q_ref.shape[1]
    scale = 1.0 / math.sqrt(HEAD_SIZE)
    queries = [q_ref[head * HEAD_SIZE : (head + 1) * HEAD_SIZE] for head in range(group)]

    def one(block, carry, diagonal):
        start = pl.multiple_of(block * rows, rows)
        keys = k_ref[pl.ds(start, rows)]
        values = vt_ref[:, pl.ds(start, rows)]
        later = []
        for head in range(group):
            best, accum = carry[head]
            scores = mm(keys, queries[head])
            if diagonal:
                ahead = lax.broadcasted_iota(jnp.int32, scores.shape, 0) > (
                    lax.broadcasted_iota(jnp.int32, scores.shape, 1)
                )
                scores = jnp.where(ahead, lowest_precision, scores)
            new_best = jnp.maximum(best, jnp.max(scores, axis=0, keepdims=True))
            probs = jnp.exp((scores - new_best) * scale).astype(jnp.bfloat16)
            factor = jnp.exp((best - new_best) * scale)
            later.append((new_best, accum * factor + mm(values, probs)))
        return tuple(later)

    carry = tuple(
        (
            jnp.full((1, rows), lowest_precision, jnp.float32),
            jnp.zeros((HEAD_SIZE + ONES, rows), jnp.float32),
        )
        for _ in range(group)
    )
    carry = one(step, carry, True)
    carry = lax.fori_loop(0, step, lambda block, now: one(block, now, False), carry)
    loss = jnp.zeros((1, rows), jnp.float32)
    for head in range(group):
        accum = carry[head][1]
        taught = accum[:HEAD_SIZE] * (1.0 / accum[HEAD_SIZE : HEAD_SIZE + 1])
        at = step * rows + lax.broadcasted_iota(jnp.int32, taught.shape, 1)
        base = head * HEAD_SIZE
        difference = att_ref[base : base + HEAD_SIZE].astype(jnp.float32) - jnp.where(
            at < length_ref[0], taught, 0.0
        )
        diff_ref[base : base + HEAD_SIZE] = difference
        loss = loss + jnp.sum(difference * difference, axis=0, keepdims=True)
    loss_ref[...] = jnp.broadcast_to(loss, loss_ref.shape)


def backward_kernel(
    length_ref, grad_ref, diff_ref, out_ref, denom_ref, q_ref, pq_ref,
    k_ref, k_before, pk_ref, pk_before, v_ref, v_before,
    kt_ref, kt_before, pkt_ref, pkt_before, vt_ref, vt_before,
    states_ref, map_ref, back_ref, cos_ref, sin_ref,
    pre_ref, gain_ref, key_carry, value_carry, map_carry, later,
):
    blocks = pl.num_programs(0)
    step = blocks - 1 - pl.program_id(0)
    group = q_ref.shape[0] // HEAD_SIZE
    rows = q_ref.shape[1]
    half = HEAD_SIZE // 2
    scale = 1.0 / math.sqrt(HEAD_SIZE)

    @pl.when(pl.program_id(0) == 0)
    def _():
        gain_ref[...] = jnp.zeros_like(gain_ref)
        key_carry[...] = jnp.zeros_like(key_carry)
        value_carry[...] = jnp.zeros_like(value_carry)
        map_carry[...] = jnp.zeros_like(map_carry)
        later[...] = jnp.zeros_like(later)

    def through_map(head, vector, grad_maps):
        base = head * HEAD_SIZE
        plus, minus = soft_pair(mm(map_ref[base : base + HEAD_SIZE], vector))
        grad_plus, grad_minus = grad_maps[:HEAD_SIZE], grad_maps[HEAD_SIZE:]
        grad_logits = plus * (
            grad_plus - jnp.sum(grad_plus * plus, axis=0, keepdims=True)
        ) - minus * (grad_minus - jnp.sum(grad_minus * minus, axis=0, keepdims=True))
        grad_logits = grad_logits.astype(jnp.bfloat16)
        gain_ref[base : base + HEAD_SIZE] += mm_nt(vector, grad_logits)
        return mm(back_ref[base : base + HEAD_SIZE], grad_logits)

    for sub in reversed(range(rows // SUB)):
        columns = slice(sub * SUB, (sub + 1) * SUB)
        queries = side_by_side(q_ref, HEAD_SIZE, group, columns)
        query_maps = side_by_side(pq_ref, 2 * HEAD_SIZE, group, columns)
        if sub == 0:
            keys = jnp.concatenate([k_before[...], k_ref[:SUB]], axis=0)
            key_maps = jnp.concatenate([pk_before[...], pk_ref[:SUB]], axis=0)
            values = jnp.concatenate([v_before[...], v_ref[:SUB]], axis=0)
            keys_t = jnp.concatenate([kt_before[...], kt_ref[:, :SUB]], axis=1)
            key_maps_t = jnp.concatenate([pkt_before[...], pkt_ref[:, :SUB]], axis=1)
            values_before = vt_before[...]
        else:
            around = slice((sub - 1) * SUB, (sub + 1) * SUB)
            keys, key_maps, values = k_ref[around], pk_ref[around], v_ref[around]
            keys_t, key_maps_t = kt_ref[:, around], pkt_ref[:, around]
            values_before = vt_ref[:, (sub - 1) * SUB : sub * SUB]
        distance, key_at = band(group)
        window = (distance >= 0) & (distance < WINDOW_KEYS)
        linear = distance >= WINDOW_KEYS
        if sub == 0:
            inside = (key_at >= 0) | (step > 0)
            window, linear = window & inside, linear & inside
        incoming = side_by_side(grad_ref, HEAD_SIZE, group, columns).astype(jnp.float32)
        difference = side_by_side(diff_ref, HEAD_SIZE, group, columns)
        out = side_by_side(out_ref, HEAD_SIZE, group, columns)
        denom = side_by_side(denom_ref, 1, group, columns)
        at = (
            step * rows
            + sub * SUB
            + lax.rem(lax.broadcasted_iota(jnp.int32, out.shape, 1), SUB)
        )
        incoming = (incoming + 2.0 * difference).astype(jnp.bfloat16).astype(jnp.float32)
        incoming = jnp.where(at < length_ref[0], incoming, 0.0)
        inverse = 1.0 / denom
        grad_numer = (incoming * inverse).astype(jnp.bfloat16)
        grad_denom = -jnp.sum(incoming * out, axis=0, keepdims=True) * inverse
        rank = lax.broadcasted_iota(jnp.int32, (ONES, group * SUB), 0)
        denom_high = grad_denom.astype(jnp.bfloat16).astype(jnp.float32)
        extra = jnp.where(
            rank == 0, denom_high, jnp.where(rank == 1, grad_denom - denom_high, 0.0)
        ).astype(jnp.bfloat16)
        grad_both = jnp.concatenate([grad_numer, extra], axis=0)
        near = jnp.exp(mm(keys, queries) * scale)
        far = mm(key_maps, query_maps)
        weights = jnp.where(window, near, jnp.where(linear, far, 0.0)).astype(jnp.bfloat16)
        grad_weights = mm(values, grad_numer) + grad_denom
        grad_scores = jnp.where(window, grad_weights * near * scale, 0.0).astype(jnp.bfloat16)
        grad_far = jnp.where(linear, grad_weights, 0.0).astype(jnp.bfloat16)
        state_high, state_low = split_wide(jnp.transpose(states_ref[sub]))
        grad_queries = mm(keys_t, grad_scores)
        grad_query_maps = mm(key_maps_t, grad_far) + mm(
            jnp.concatenate([state_high, state_low], axis=1),
            jnp.concatenate([grad_both, grad_both], axis=0),
        )
        grad_keys = mm_nt(queries, grad_scores)
        grad_values = mm_nt(grad_numer, weights)
        grad_key_maps = mm_nt(query_maps, grad_far)
        own_keys = key_carry[...] + grad_keys[:, SUB:]
        own_values = value_carry[...] + grad_values[:, SUB:]
        own_maps = map_carry[...] + grad_key_maps[:, SUB:]
        later_now = later[...]
        later_high, later_low = split_wide(jnp.transpose(later_now))
        key_carry[...] = grad_keys[:, :SUB]
        value_carry[...] = grad_values[:, :SUB] + mm(
            later_now[:HEAD_SIZE].astype(jnp.bfloat16), key_maps_t[:, :SUB]
        )
        map_carry[...] = grad_key_maps[:, :SUB] + mm(
            jnp.concatenate([later_high, later_low], axis=1),
            jnp.concatenate([values_before, values_before], axis=0),
        )
        later[...] = later_now + mm_nt(grad_both, query_maps)
        cosine, sine = cos_ref[:, columns], sin_ref[:, columns]
        for head in range(group + 1):
            base = head * HEAD_SIZE
            lanes = slice(head * SUB, (head + 1) * SUB)
            if head < group:
                total = grad_queries[:, lanes] + through_map(
                    head, queries[:, lanes], grad_query_maps[:, lanes]
                )
            else:
                total = own_keys + through_map(head, keys_t[:, SUB:], own_maps)
            low_half, high_half = halves_rotated(total[:half], total[half:], cosine, -sine)
            pre_ref[base : base + HEAD_SIZE, columns] = jnp.concatenate(
                [low_half, high_half], axis=0
            ).astype(jnp.bfloat16)
        base = (group + 1) * HEAD_SIZE
        pre_ref[base : base + HEAD_SIZE, columns] = own_values.astype(jnp.bfloat16)


def exchanged(value, bits):
    count = lax.axis_size("seq")
    return lax.ppermute(value, "seq", [(place, place ^ bits) for place in range(count)])


def plane_gather(value):
    me = lax.axis_index("seq")
    middle = value.shape[0] // 2
    along_x, along_y = exchanged(value, 2), exchanged(value, 4)
    across = jnp.concatenate(
        [exchanged(along_x[:middle], 4), exchanged(along_y[middle:], 2)], axis=0
    )
    found = {0: value, 2: along_x, 4: along_y, 6: across}
    for bits in (0, 2, 4, 6):
        found[bits + 1] = exchanged(found[bits], 1)
    whole = jnp.zeros((lax.axis_size("seq"),) + value.shape, value.dtype)
    for bits in range(8):
        whole = lax.dynamic_update_slice_in_dim(whole, found[bits][None], me ^ bits, 0)
    return whole


def plane_scatter(parts):
    me = lax.axis_index("seq")
    core, chip = me % 2, me // 2
    shape = parts.shape[1:]
    by_core = parts.reshape((parts.shape[0] // 2, 2) + shape)
    keep = lax.dynamic_index_in_dim(by_core, core, 1, False)
    give = lax.dynamic_index_in_dim(by_core, 1 - core, 1, False)
    both = (keep.astype(jnp.float32) + exchanged(give, 1).astype(jnp.float32)).astype(jnp.bfloat16)
    pieces = [lax.dynamic_index_in_dim(both, chip ^ bits, 0, False) for bits in range(4)]
    total = pieces[0].astype(jnp.float32)
    for bits in (1, 2, 3):
        total = total + exchanged(pieces[bits], 2 * bits).astype(jnp.float32)
    return total


def ring(value):
    count = lax.axis_size("fsdp")
    found = [value]
    for _ in range(count - 1):
        found.append(
            lax.ppermute(found[-1], "fsdp", [(at, (at + 1) % count) for at in range(count)])
        )
    return found


def in_order(found):
    count = len(found)
    me = lax.axis_index("fsdp")
    whole = jnp.zeros((count,) + found[0].shape, found[0].dtype)
    for step in range(count):
        whole = lax.dynamic_update_slice_in_dim(
            whole, found[step][None], lax.rem(me - step + count, count), 0
        )
    return whole


def call(kernel, grid, in_specs, out_specs, out_shape, scratch, flops, moved, mib, scalars=1):
    spec = pltpu.PrefetchScalarGridSpec(
        num_scalar_prefetch=scalars,
        grid=grid,
        in_specs=in_specs,
        out_specs=out_specs,
        scratch_shapes=scratch,
    )
    return pl.pallas_call(
        kernel,
        grid_spec=spec,
        out_shape=out_shape,
        compiler_params=pltpu.CompilerParams(vmem_limit_bytes=mib * 2**20),
        cost_estimate=pl.CostEstimate(flops=flops, bytes_accessed=moved, transcendentals=0),
    )


def by_heads(
    tokens,
    lengths,
    norm_attn,
    norm_ffn,
    w_query,
    key_projection,
    value_projection,
    w_output,
    w_gate,
    w_up,
    w_down,
    down_query,
    up_query,
    key_down_matrix,
    key_up_matrix,
    value_down_matrix,
    value_up_matrix,
    down_output,
    up_output,
    feature_query,
    key_feature_weight,
    cotangent,
):
    places = lax.axis_size("seq")
    lanes = lax.axis_size("fsdp")
    rows = tokens.shape[1]
    model = tokens.shape[2]
    count = rows * places
    group = QUERY_HEADS // KEY_VALUE_HEADS
    query_width = group * HEAD_SIZE
    width = query_width + 2 * HEAD_SIZE
    rank = down_query.shape[1]
    place = lax.axis_index("seq")
    lane = lax.axis_index("fsdp")
    length = lax.dynamic_slice_in_dim(lengths, lane, 1)
    bf16, f32 = jnp.bfloat16, jnp.float32
    inputs_wide = tokens[0].astype(f32)
    cot_wide = cotangent[0].astype(f32)
    gain_attn = norm_attn.astype(f32)
    gain_ffn = norm_ffn.astype(f32)

    inverse_attn = lax.rsqrt(jnp.mean(inputs_wide * inputs_wide, axis=-1, keepdims=True) + epsilon)
    normed = (inputs_wide * inverse_attn * gain_attn).astype(bf16)
    normed_all = plane_gather(normed).reshape(count, model)

    shard = w_query.shape[0]
    by_place = jnp.concatenate(
        [
            w_query.reshape(shard, places, query_width),
            key_projection.reshape(shard, places, HEAD_SIZE),
            value_projection.reshape(shard, places, HEAD_SIZE),
        ],
        axis=2,
    )
    by_place = lax.all_to_all(jnp.moveaxis(by_place, 1, 0), "seq", 0, 0, tiled=True)
    own_weights = jnp.moveaxis(in_order(ring(by_place)), 0, 1).reshape(model, width)
    spare = 128
    own_weights_t = jnp.concatenate(
        [
            own_weights.T,
            down_query.T,
            key_down_matrix.T,
            value_down_matrix.T,
            jnp.zeros((spare - 3 * rank, model), bf16),
        ],
        axis=0,
    )
    output_rows = in_order(ring(w_output))
    output_weights = jnp.moveaxis(
        plane_gather(output_rows.reshape(lanes * shard, model)).reshape(
            places, lanes, shard, model
        ),
        0,
        0,
    ).reshape(model, model)

    def own_rows(matrix, size):
        return lax.dynamic_slice_in_dim(matrix, place * size, size, 0)

    up_own = (
        own_rows(up_query, query_width),
        own_rows(key_up_matrix, HEAD_SIZE),
        own_rows(value_up_matrix, HEAD_SIZE),
    )
    up_block = jnp.concatenate(
        [
            jnp.pad(part, ((0, 0), (at * rank, spare - (at + 1) * rank)))
            for at, part in enumerate(up_own)
        ],
        axis=0,
    )
    maps_back = jnp.concatenate(
        [own_rows(feature_query, query_width), own_rows(key_feature_weight, HEAD_SIZE)], axis=0
    )
    maps_ahead = jnp.swapaxes(
        maps_back.reshape(group + 1, HEAD_SIZE, HEAD_SIZE), 1, 2
    ).reshape((group + 1) * HEAD_SIZE, HEAD_SIZE)
    half = HEAD_SIZE // 2
    frequency = rope_base ** (-(jnp.arange(half, dtype=f32) * 2.0) / HEAD_SIZE)
    phase = jnp.arange(count, dtype=jnp.int32).astype(f32)[None, :] * frequency[:, None]
    cosine, sine = jnp.cos(phase), jnp.sin(phase)

    def whole(shape):
        return pl.BlockSpec(shape, lambda i, *_: (0,) * len(shape))

    def across(height):
        return pl.BlockSpec((height, rows), lambda i, *_: (0, i))

    def down(wide):
        return pl.BlockSpec((rows, wide), lambda i, *_: (i, 0))

    def shape(*dims, dtype=bf16):
        return jax.ShapeDtypeStruct(dims, dtype)

    value_rows = HEAD_SIZE + ONES
    maps_height = 2 * HEAD_SIZE
    q_t, k_t, v_t, keys, values, pq_t, pk_t, key_maps, narrow_t = call(
        project_kernel,
        (places,),
        [
            down(model),
            whole((width + spare, model)),
            whole((width, spare)),
            whole(((group + 1) * HEAD_SIZE, HEAD_SIZE)),
            across(half),
            across(half),
        ],
        [
            across(query_width),
            across(HEAD_SIZE),
            across(value_rows),
            down(HEAD_SIZE),
            down(HEAD_SIZE),
            across(group * maps_height),
            across(maps_height),
            down(maps_height),
            across(spare),
        ],
        [
            shape(query_width, count),
            shape(HEAD_SIZE, count),
            shape(value_rows, count),
            shape(count, HEAD_SIZE),
            shape(count, HEAD_SIZE),
            shape(group * maps_height, count),
            shape(maps_height, count),
            shape(count, maps_height),
            shape(spare, count),
        ],
        [],
        2 * count * model * (width + spare),
        2 * count * model * 2,
        32,
        scalars=0,
    )(normed_all, own_weights_t, up_block, maps_ahead, cosine, sine)

    per_step = rows // SUB

    def before_down(wide):
        return pl.BlockSpec((SUB, wide), lambda i, *_: (jnp.maximum(per_step * i - 1, 0), 0))

    def before_across(height):
        return pl.BlockSpec((height, SUB), lambda i, *_: (0, jnp.maximum(per_step * i - 1, 0)))

    states_shape = (count // SUB, value_rows, maps_height)
    att_t, out_t, denom, states = call(
        forward_kernel,
        (places,),
        [
            across(query_width),
            across(group * maps_height),
            down(HEAD_SIZE),
            before_down(HEAD_SIZE),
            down(maps_height),
            before_down(maps_height),
            across(value_rows),
            before_across(value_rows),
        ],
        [
            across(query_width),
            across(query_width),
            across(group),
            pl.BlockSpec((per_step,) + states_shape[1:], lambda i, *_: (i, 0, 0)),
        ],
        [
            shape(query_width, count),
            shape(query_width, count, dtype=f32),
            shape(group, count, dtype=f32),
            shape(*states_shape, dtype=f32),
        ],
        [pltpu.VMEM(states_shape[1:], f32)],
        8 * count * SUB * 2 * group * HEAD_SIZE,
        count * 4096,
        32,
    )(length, q_t, pq_t, keys, keys, key_maps, key_maps, v_t, v_t)

    sent = jnp.moveaxis(att_t.reshape(query_width, places, rows), 1, 0)
    att_all = lax.all_to_all(sent, "seq", 0, 0, tiled=True).reshape(places * query_width, rows)

    difference, loss_rows = call(
        teacher_kernel,
        (places,),
        [
            across(query_width),
            whole((count, HEAD_SIZE)),
            whole((value_rows, count)),
            across(query_width),
        ],
        [across(query_width), across(8)],
        [shape(query_width, count, dtype=f32), shape(8, count, dtype=f32)],
        [],
        4 * count * count * group * HEAD_SIZE,
        count * 4096,
        32,
    )(length, q_t, keys, v_t, att_t)
    losses = jnp.sum(loss_rows[0].reshape(places, rows), axis=1)

    def dot_tn(a, b):
        return lax.dot_general(a, b, (((0,), (0,)), ((), ())), preferred_element_type=f32)

    branch = dot_tn(att_all, output_weights)
    narrow_out = dot_tn(att_all, down_output).astype(bf16)
    branch = branch + mm_nt(narrow_out, up_output)
    residual = inputs_wide + branch
    inverse_ffn = lax.rsqrt(jnp.mean(residual * residual, axis=-1, keepdims=True) + epsilon)
    normed_ffn = (residual * inverse_ffn * gain_ffn).astype(bf16)
    ffn_all = plane_gather(normed_ffn).reshape(count, model)
    cot_all = plane_gather(cotangent[0]).reshape(count, model)

    def hidden_share(matrix):
        mine = lax.all_to_all(matrix, "seq", 1, 0, tiled=True)
        return jnp.concatenate(ring(mine), axis=1)

    gate_weights, up_weights, down_weights = (
        hidden_share(w_gate),
        hidden_share(w_up),
        hidden_share(w_down),
    )
    gate_pre = mm(ffn_all, gate_weights)
    up_pre = mm(ffn_all, up_weights)
    sigmoid_gate = jax.nn.sigmoid(gate_pre)
    silu_gate = gate_pre * sigmoid_gate
    hidden = (silu_gate * up_pre).astype(bf16)
    grad_hidden = mm(cot_all, down_weights)
    grad_gate = (
        grad_hidden * up_pre * sigmoid_gate * (1.0 + gate_pre * (1.0 - sigmoid_gate))
    ).astype(bf16)
    grad_up = (grad_hidden * silu_gate).astype(bf16)
    grad_ffn = (mm_nt(grad_gate, gate_weights) + mm_nt(grad_up, up_weights)).astype(bf16)
    grad_part = plane_scatter(grad_ffn.reshape(places, rows, model))
    ffn_out = mm_nt(hidden, down_weights).astype(bf16)
    output = (residual + plane_scatter(ffn_out.reshape(places, rows, model))).astype(bf16)

    grad_residual = cot_wide + norm_back(residual, inverse_ffn, gain_ffn, grad_part)
    grad_branch = grad_residual.astype(bf16)
    grad_narrow_out = mm(grad_branch, up_output)
    grad_up_output = dot_tn(narrow_out, grad_branch)
    grad_down_output = dot_tn(grad_narrow_out, att_all.T)
    grad_att = (
        mm_nt(output_weights, grad_branch) + mm_nt(down_output, grad_narrow_out)
    ).astype(bf16)
    grad_att = lax.all_to_all(
        grad_att.reshape(places, query_width, rows), "seq", 0, 0, tiled=True
    )

    def back(spec):
        return pl.BlockSpec(
            spec.block_shape, lambda i, *_: spec.index_map(places - 1 - i)
        )

    grad_pre_t, grad_maps = call(
        backward_kernel,
        (places,),
        [
            pl.BlockSpec((None, query_width, rows), lambda i, *_: (places - 1 - i, 0, 0)),
            back(across(query_width)),
            back(across(query_width)),
            back(across(group)),
            back(across(query_width)),
            back(across(group * maps_height)),
            back(down(HEAD_SIZE)),
            back(before_down(HEAD_SIZE)),
            back(down(maps_height)),
            back(before_down(maps_height)),
            back(down(HEAD_SIZE)),
            back(before_down(HEAD_SIZE)),
            back(across(HEAD_SIZE)),
            back(before_across(HEAD_SIZE)),
            back(across(maps_height)),
            back(before_across(maps_height)),
            back(across(value_rows)),
            back(before_across(value_rows)),
            pl.BlockSpec(
                (per_step,) + states_shape[1:], lambda i, *_: (places - 1 - i, 0, 0)
            ),
            whole(((group + 1) * HEAD_SIZE, HEAD_SIZE)),
            whole(((group + 1) * HEAD_SIZE, HEAD_SIZE)),
            back(across(half)),
            back(across(half)),
        ],
        [back(across(width)), whole(((group + 1) * HEAD_SIZE, HEAD_SIZE))],
        [shape(width, count), shape((group + 1) * HEAD_SIZE, HEAD_SIZE, dtype=f32)],
        [
            pltpu.VMEM((HEAD_SIZE, SUB), f32),
            pltpu.VMEM((HEAD_SIZE, SUB), f32),
            pltpu.VMEM((maps_height, SUB), f32),
            pltpu.VMEM((value_rows, maps_height), f32),
        ],
        20 * count * SUB * 2 * group * HEAD_SIZE,
        count * 8192,
        32,
    )(
        length, grad_att, difference, out_t, denom, q_t, pq_t,
        keys, keys, key_maps, key_maps, values, values,
        k_t, k_t, pk_t, pk_t, v_t, v_t,
        states, maps_ahead, maps_back, cosine, sine,
    )

    grad_narrow_t = dot_tn(up_block, grad_pre_t).astype(bf16)
    grad_up_block = mm_nt(grad_pre_t, narrow_t)
    grad_down_t = mm(grad_narrow_t[: 3 * rank], normed_all)
    grad_normed = dot_tn(
        jnp.concatenate([grad_pre_t, grad_narrow_t], axis=0), own_weights_t
    ).astype(bf16)
    grad_normed = plane_scatter(grad_normed.reshape(places, rows, model))
    grad_tokens = (
        grad_residual + norm_back(inputs_wide, inverse_attn, gain_attn, grad_normed)
    ).astype(bf16)

    devices = places * lanes
    ahead = jnp.arange(devices)[None, :] >= (jnp.arange(places) * lanes + lane)[:, None]
    running = jnp.sum(jnp.where(ahead, losses[:, None], 0.0), axis=0)
    loss_row = jnp.pad(running[:, None], ((0, 0), (0, model // devices - 1))).reshape(1, model)
    shared = jnp.concatenate([grad_down_t, grad_down_output, grad_up_output, loss_row], axis=0)
    shared = jnp.moveaxis(shared.reshape(-1, devices, model // devices), 1, 0)
    shared = jnp.sum(
        lax.all_to_all(shared, ("seq", "fsdp"), 0, 0, tiled=True).reshape(shared.shape), axis=0
    )

    def columns(at):
        return shared[at * rank : (at + 1) * rank].T

    transfer_loss = shared[5 * rank, :1] / jnp.sum(lengths).astype(f32)

    pieces = [
        grad_maps[:query_width].reshape(lanes, -1),
        grad_maps[query_width:].reshape(lanes, -1),
        grad_up_block[:query_width, :rank].reshape(lanes, -1),
        grad_up_block[query_width : query_width + HEAD_SIZE, rank : 2 * rank].reshape(lanes, -1),
        grad_up_block[query_width + HEAD_SIZE :, 2 * rank : 3 * rank].reshape(lanes, -1),
    ]
    packed = jnp.concatenate(pieces, axis=1)
    packed = jnp.sum(lax.all_to_all(packed, "fsdp", 0, 0, tiled=True).reshape(packed.shape), axis=0)
    ends = [0]
    for piece in pieces:
        ends.append(ends[-1] + piece.shape[1])
    map_query, map_key, up_q, up_k, up_v = (
        packed[ends[at] : ends[at + 1]].reshape(-1, wide)
        for at, wide in enumerate((HEAD_SIZE, HEAD_SIZE, rank, rank, rank))
    )
    return (
        output[None],
        grad_tokens[None],
        columns(0),
        up_q,
        columns(1),
        up_k,
        columns(2),
        up_v,
        columns(3),
        columns(4),
        map_query,
        map_key,
        transfer_loss,
    )


def solution(mesh):
    placed = (
        P("fsdp", "seq", None),
        P(),
        P(),
        P(),
        P(("seq", "fsdp"), None),
        P(("seq", "fsdp"), None),
        P(("seq", "fsdp"), None),
        P(("seq", "fsdp"), None),
        P("seq", "fsdp"),
        P("seq", "fsdp"),
        P("seq", "fsdp"),
        P(),
        P(),
        P(),
        P(),
        P(),
        P(),
        P(),
        P(),
        P(),
        P(),
        P("fsdp", "seq", None),
    )
    sizes = dict(mesh.shape)
    heads_match = sizes["seq"] == KEY_VALUE_HEADS == 8 and (
        QUERY_HEADS // KEY_VALUE_HEADS == sizes["fsdp"]
    )
    return jax.shard_map(
        by_heads if heads_match else local,
        mesh=mesh,
        in_specs=placed,
        out_specs=(
            P("fsdp", "seq", None),
            P("fsdp", "seq", None),
            P(("seq", "fsdp"), None),
            P(("seq", "fsdp"), None),
            P(("seq", "fsdp"), None),
            P(("seq", "fsdp"), None),
            P(("seq", "fsdp"), None),
            P(("seq", "fsdp"), None),
            P(("seq", "fsdp"), None),
            P(("seq", "fsdp"), None),
            P(("seq", "fsdp"), None),
            P(("seq", "fsdp"), None),
            P(("seq", "fsdp")),
        ),
        check_vma=False,
    )
```

```python
import functools
import math

import jax
import jax.numpy as jnp
from jax import lax
from jax.experimental import pallas as pl
from jax.experimental.pallas import tpu as pltpu
from jax.sharding import PartitionSpec as P

QUERY_HEADS = 32
KEY_VALUE_HEADS = 8
HEAD_SIZE = 64
WINDOW_KEYS = 64


epsilon = 1e-05
rope_base = 500000.0
precise = lax.Precision.HIGHEST
lowest_precision = -1e30
ONES = 16
SUB = 128
VMEM_MIB = 56
PARTS = 2
COST = 1.15e9


def prefix(x, axis, join, neutral, backward):
    count = lax.axis_size(axis)
    place = lax.axis_index(axis)
    ahead = count - 1 - place if backward else place
    gathered = jax.tree.map(
        lambda a, kind: lax.all_gather(a.astype(kind), axis), x, (jnp.bfloat16, jnp.bfloat16)
    )
    state = jax.tree.map(lambda a, e: jnp.zeros_like(a) + jnp.asarray(e, a.dtype), x, neutral)

    def one(hop, state):
        source = count - 1 - hop if backward else hop
        return join(
            state,
            jax.tree.map(
                lambda a, own: lax.dynamic_index_in_dim(a, source, 0, False).astype(own.dtype),
                gathered,
                x,
            ),
        )

    return lax.fori_loop(0, ahead, one, state)


def as_sent(x):

    def short(part):
        return part.astype(jnp.bfloat16) if part.dtype == jnp.float32 else part

    return jax.tree.map(short, x)


def shifted(value, axis, steps):
    count = lax.axis_size(axis)
    first, last = (max(0, -steps), min(count, count - steps))
    return lax.ppermute(value, axis, [(source, source + steps) for source in range(first, last)])


def rotary(positions):
    half_dim = HEAD_SIZE // 2
    inverse = rope_base ** (-(jnp.arange(half_dim, dtype=jnp.float32) * 2.0) / HEAD_SIZE)
    phase = positions.astype(jnp.float32)[:, None] * inverse[None, :]
    return (jnp.cos(phase)[:, None, :], jnp.sin(phase)[:, None, :])


def apply_rotary(vectors, cosine_lookup, sine_lookup):
    half_dim = vectors.shape[-1] // 2
    first_half = vectors[..., :half_dim]
    second_half = vectors[..., half_dim:]
    return jnp.concatenate(
        [
            first_half * cosine_lookup - second_half * sine_lookup,
            second_half * cosine_lookup + first_half * sine_lookup,
        ],
        axis=-1,
    )


def inverse_rotary(gradient, cosine_lookup, sine_lookup):
    half_dim = gradient.shape[-1] // 2
    first_half = gradient[..., :half_dim]
    second_half = gradient[..., half_dim:]
    return jnp.concatenate(
        [
            first_half * cosine_lookup + second_half * sine_lookup,
            second_half * cosine_lookup - first_half * sine_lookup,
        ],
        axis=-1,
    )


def apply_feature_map(vectors, weights):
    logits_map = jnp.einsum("thd,hde->the", vectors, weights, preferred_element_type=jnp.float32)
    return jnp.concatenate(
        [jax.nn.softmax(logits_map, axis=-1), jax.nn.softmax(-logits_map, axis=-1)], axis=-1
    )


def feature_back(vectors, weights, gradient):
    logits_map = jnp.einsum("thd,hde->the", vectors, weights, preferred_element_type=jnp.float32)
    plus_soft = jax.nn.softmax(logits_map, axis=-1)
    minus_soft = jax.nn.softmax(-logits_map, axis=-1)
    grad_plus = gradient[..., :HEAD_SIZE]
    grad_minus = gradient[..., HEAD_SIZE:]
    grad_logits = plus_soft * (
        grad_plus - jnp.sum(grad_plus * plus_soft, axis=-1, keepdims=True)
    ) - minus_soft * (grad_minus - jnp.sum(grad_minus * minus_soft, axis=-1, keepdims=True))
    grad_vectors = jnp.einsum(
        "the,hde->thd", grad_logits, weights, preferred_element_type=jnp.float32
    )
    grad_weights = jnp.einsum(
        "thd,the->hde", vectors, grad_logits, preferred_element_type=jnp.float32
    )
    return (grad_vectors, grad_weights)


def norm_back(values, inverse, gain, gradient):
    scaled = gradient * gain
    return inverse * scaled - values * inverse * inverse * inverse * jnp.mean(
        scaled * values, axis=-1, keepdims=True
    )


def coefficients(query_rows, query_feature_maps, keys_ext, key_maps, key_valid):
    row_count = query_rows.shape[0]
    key_count = keys_ext.shape[0]
    offset = (
        jnp.arange(row_count)[:, None] + (key_count - row_count) - jnp.arange(key_count)[None, :]
    )
    window = ((offset >= 0) & (offset < WINDOW_KEYS) & key_valid[None, :])[None]
    linear = ((offset >= WINDOW_KEYS) & key_valid[None, :])[None]
    scores = jnp.einsum(
        "tjd,sd->jts", query_rows, keys_ext, preferred_element_type=jnp.float32
    ) / math.sqrt(HEAD_SIZE)
    exp_scores = jnp.exp(scores)
    near_terms = lax.optimization_barrier(exp_scores.astype(jnp.bfloat16)).astype(jnp.float32)
    far_terms = jnp.einsum(
        "tjf,sf->jts", query_feature_maps, key_maps, preferred_element_type=jnp.float32
    )
    weights = jnp.where(window, near_terms, 0.0) + jnp.where(linear, far_terms, 0.0)
    return (weights, exp_scores, window, linear)


def attend_group(operands, key_valid):
    query_rows, query_feature_maps, keys_ext, values_ext, key_maps, carry_state, carry_total = (
        operands
    )
    weights, exp_scores, window, linear = coefficients(
        query_rows, query_feature_maps, keys_ext, key_maps, key_valid
    )
    maps_wide = query_feature_maps.astype(jnp.float32)
    numerator = jnp.einsum(
        "jts,sd->tjd", weights, values_ext.astype(jnp.float32), precision=precise
    ) + jnp.einsum("tjf,fd->tjd", maps_wide, carry_state, precision=precise)
    denominator = jnp.transpose(jnp.sum(weights, axis=-1)) + jnp.einsum(
        "tjf,f->tj", maps_wide, carry_total, precision=precise
    )
    return (numerator, denominator)


def attend_back(operands, key_valid):
    (
        query_rows,
        query_feature_maps,
        keys_ext,
        values_ext,
        key_maps,
        carry_state,
        carry_total,
        numerator,
        denominator,
        grad_out,
    ) = operands
    weights, exp_scores, window, linear = coefficients(
        query_rows, query_feature_maps, keys_ext, key_maps, key_valid
    )
    grad_numer = grad_out / denominator[..., None]
    grad_denom = -jnp.sum(grad_out * numerator, axis=-1) / (denominator * denominator)
    grad_weights = (
        jnp.einsum("tjd,sd->jts", grad_numer, values_ext, preferred_element_type=jnp.float32)
        + jnp.transpose(grad_denom)[:, :, None]
    )
    grad_scores = jnp.where(window, grad_weights * exp_scores, 0.0) / math.sqrt(HEAD_SIZE)
    grad_far = jnp.where(linear, grad_weights, 0.0)
    grad_queries = jnp.einsum(
        "jts,sd->tjd", grad_scores, keys_ext, preferred_element_type=jnp.float32
    )
    grad_keys = jnp.einsum(
        "jts,tjd->sd", grad_scores, query_rows, preferred_element_type=jnp.float32
    )
    grad_qmaps = (
        jnp.einsum("jts,sf->tjf", grad_far, key_maps, preferred_element_type=jnp.float32)
        + jnp.einsum("tjd,fd->tjf", grad_numer, carry_state, preferred_element_type=jnp.float32)
        + grad_denom[..., None] * carry_total
    )
    grad_kmaps = jnp.einsum(
        "jts,tjf->sf", grad_far, query_feature_maps, preferred_element_type=jnp.float32
    )
    grad_values = jnp.einsum("jts,tjd->sd", weights, grad_numer, preferred_element_type=jnp.float32)
    grad_state = jnp.einsum(
        "tjf,tjd->fd", query_feature_maps, grad_numer, preferred_element_type=jnp.float32
    )
    grad_total = jnp.einsum(
        "tjf,tj->f", query_feature_maps, grad_denom, preferred_element_type=jnp.float32
    )
    return (grad_queries, grad_keys, grad_values, grad_qmaps, grad_kmaps, grad_state, grad_total)


def add_pair(earlier, later_part):
    return (earlier[0] + later_part[0], earlier[1] + later_part[1])


def local(
    tokens,
    lengths,
    norm_attn,
    norm_ffn,
    w_query,
    key_projection,
    value_projection,
    w_output,
    w_gate,
    w_up,
    w_down,
    down_query,
    up_query,
    key_down_matrix,
    key_up_matrix,
    value_down_matrix,
    value_up_matrix,
    down_output,
    up_output,
    feature_query,
    key_feature_weight,
    cotangent,
):
    rows_per_block = tokens.shape[1]
    ext_rows = rows_per_block + WINDOW_KEYS
    heads_per_group = QUERY_HEADS // KEY_VALUE_HEADS
    feature_width = 2 * HEAD_SIZE
    inputs_wide = tokens[0].astype(jnp.float32)
    cot_narrow = cotangent[0]
    cot_wide = cot_narrow.astype(jnp.float32)
    seq_index = lax.axis_index("seq")
    lane_length = lengths[lax.axis_index("fsdp")]
    positions = seq_index * rows_per_block + jnp.arange(rows_per_block)
    cosine_lookup, sine_lookup = rotary(positions)
    gain_attn = norm_attn.astype(jnp.float32)
    gain_ffn = norm_ffn.astype(jnp.float32)
    inverse_attn = lax.rsqrt(jnp.mean(inputs_wide * inputs_wide, axis=-1, keepdims=True) + epsilon)
    normed = (inputs_wide * inverse_attn * gain_attn).astype(jnp.bfloat16)
    pieces = (
        lax.all_gather(w_query, ("seq", "fsdp"), axis=0, tiled=True),
        lax.all_gather(key_projection, ("seq", "fsdp"), axis=0, tiled=True),
        lax.all_gather(value_projection, ("seq", "fsdp"), axis=0, tiled=True),
    )
    sliced = normed
    query_pre, key_before_rotation, value_before_adapter = tuple(
        (jnp.dot(sliced, block_piece, preferred_element_type=jnp.float32) for block_piece in pieces)
    )
    narrow_query = jnp.dot(normed, down_query, preferred_element_type=jnp.float32).astype(
        jnp.bfloat16
    )
    narrow_key = jnp.dot(normed, key_down_matrix, preferred_element_type=jnp.float32).astype(
        jnp.bfloat16
    )
    narrow_value = jnp.dot(normed, value_down_matrix, preferred_element_type=jnp.float32).astype(
        jnp.bfloat16
    )
    query_pre = query_pre + jnp.dot(narrow_query, up_query.T, preferred_element_type=jnp.float32)
    key_before_rotation = key_before_rotation + jnp.dot(
        narrow_key, key_up_matrix.T, preferred_element_type=jnp.float32
    )
    value_before_adapter = value_before_adapter + jnp.dot(
        narrow_value, value_up_matrix.T, preferred_element_type=jnp.float32
    )
    query_rows = apply_rotary(
        query_pre.reshape(rows_per_block, QUERY_HEADS, HEAD_SIZE), cosine_lookup, sine_lookup
    ).astype(jnp.bfloat16)
    device_keys = apply_rotary(
        key_before_rotation.reshape(rows_per_block, KEY_VALUE_HEADS, HEAD_SIZE),
        cosine_lookup,
        sine_lookup,
    ).astype(jnp.bfloat16)
    device_values = value_before_adapter.reshape(rows_per_block, KEY_VALUE_HEADS, HEAD_SIZE).astype(
        jnp.bfloat16
    )
    softmax_query_rows = query_rows.reshape(
        rows_per_block, KEY_VALUE_HEADS, heads_per_group, HEAD_SIZE
    )
    teacher_init = (
        jnp.full((KEY_VALUE_HEADS, heads_per_group, rows_per_block), lowest_precision, jnp.float32),
        jnp.zeros((KEY_VALUE_HEADS, heads_per_group, rows_per_block), jnp.float32),
        jnp.zeros((KEY_VALUE_HEADS, heads_per_group, rows_per_block, HEAD_SIZE), jnp.float32),
        jnp.zeros((WINDOW_KEYS, KEY_VALUE_HEADS, HEAD_SIZE), jnp.bfloat16),
        jnp.zeros((WINDOW_KEYS, KEY_VALUE_HEADS, HEAD_SIZE), jnp.bfloat16),
    )
    portion_keys = lax.all_gather(
        device_keys.reshape(rows_per_block, KEY_VALUE_HEADS * HEAD_SIZE), "seq", axis=0, tiled=True
    )
    portion_values = lax.all_gather(
        device_values.reshape(rows_per_block, KEY_VALUE_HEADS * HEAD_SIZE),
        "seq",
        axis=0,
        tiled=True,
    )
    count_of_shards = portion_keys.shape[0] // rows_per_block
    sharded_keys = portion_keys.reshape(count_of_shards, rows_per_block, KEY_VALUE_HEADS, HEAD_SIZE)
    sharded_values = portion_values.reshape(
        count_of_shards, rows_per_block, KEY_VALUE_HEADS, HEAD_SIZE
    )

    def one_shard(inner, item):
        best, total, accum, rim_keys, rim_values = inner
        shard_number, shard_keys, shard_values = item
        shard_start = shard_number * rows_per_block
        scores = jnp.einsum(
            "tgjd,sgd->gjts", softmax_query_rows, shard_keys, preferred_element_type=jnp.float32
        ) / math.sqrt(HEAD_SIZE)
        allowed = (positions[:, None] >= (shard_start + jnp.arange(rows_per_block))[None, :])[
            None, None
        ]
        masked = jnp.where(allowed, scores, lowest_precision)
        new_best = jnp.maximum(best, jnp.max(masked, axis=-1))
        probs = jnp.where(allowed, jnp.exp(masked - new_best[..., None]), 0.0)
        factor = jnp.exp(best - new_best)
        total = total * factor + jnp.sum(probs, axis=-1)
        accum = accum * factor[..., None] + jnp.einsum(
            "gjts,sgd->gjtd", probs, shard_values.astype(jnp.float32)
        )
        is_before = shard_start // rows_per_block == seq_index - 1
        rim_keys = jnp.where(is_before, shard_keys[rows_per_block - WINDOW_KEYS :], rim_keys)
        rim_values = jnp.where(is_before, shard_values[rows_per_block - WINDOW_KEYS :], rim_values)
        return ((new_best, total, accum, rim_keys, rim_values), None)

    result, unused = lax.scan(
        one_shard, teacher_init, (jnp.arange(count_of_shards), sharded_keys, sharded_values)
    )
    best_all, total_all, accum_all, rim_keys, rim_values = result
    teacher = jnp.transpose(accum_all / total_all[..., None], (2, 0, 1, 3)).reshape(
        rows_per_block, QUERY_HEADS * HEAD_SIZE
    )
    keys_ext = jnp.concatenate([rim_keys, device_keys], axis=0)
    values_ext = jnp.concatenate([rim_values, device_values], axis=0)
    query_features = feature_query.reshape(QUERY_HEADS, HEAD_SIZE, HEAD_SIZE)
    key_features = key_feature_weight.reshape(KEY_VALUE_HEADS, HEAD_SIZE, HEAD_SIZE)
    query_feature_maps = apply_feature_map(query_rows, query_features).astype(jnp.bfloat16)
    key_maps = apply_feature_map(keys_ext, key_features).astype(jnp.bfloat16)
    ext_positions = seq_index * rows_per_block - WINDOW_KEYS + jnp.arange(ext_rows)
    key_valid = ext_positions >= 0
    valid_rows = key_valid[:rows_per_block].astype(jnp.float32)
    used_maps = key_maps[:rows_per_block].astype(jnp.float32) * valid_rows[:, None, None]
    values_head = values_ext[:rows_per_block].astype(jnp.float32)
    local_state = jnp.einsum("sgf,sgd->gfd", used_maps, values_head, precision=precise)
    local_total = jnp.sum(used_maps, axis=0)
    zero_pair = (
        jnp.zeros((KEY_VALUE_HEADS, feature_width, HEAD_SIZE), jnp.float32),
        jnp.zeros((KEY_VALUE_HEADS, feature_width), jnp.float32),
    )
    state_in, total_in = prefix((local_state, local_total), "seq", add_pair, zero_pair, False)
    queries_by_group = jnp.moveaxis(
        query_rows.reshape(rows_per_block, KEY_VALUE_HEADS, heads_per_group, HEAD_SIZE), 1, 0
    )
    query_maps_by_group = jnp.moveaxis(
        query_feature_maps.reshape(rows_per_block, KEY_VALUE_HEADS, heads_per_group, feature_width),
        1,
        0,
    )
    grouped_keys = jnp.moveaxis(keys_ext, 1, 0)
    grouped_values = jnp.moveaxis(values_ext, 1, 0)
    grouped_kmaps = jnp.moveaxis(key_maps, 1, 0)

    def forward_group(operands):
        return attend_group(operands, key_valid)

    numerator, denominator = lax.map(
        forward_group,
        (
            queries_by_group,
            query_maps_by_group,
            grouped_keys,
            grouped_values,
            grouped_kmaps,
            state_in,
            total_in,
        ),
    )
    row_mask = (positions < lane_length).astype(jnp.float32)
    attn_mixed = jnp.moveaxis(numerator / denominator[..., None], 0, 1).reshape(
        rows_per_block, QUERY_HEADS * HEAD_SIZE
    )
    attended = (attn_mixed * row_mask[:, None]).astype(jnp.bfloat16)
    difference = attended.astype(jnp.float32) - teacher * row_mask[:, None]
    local_loss = jnp.sum(difference * difference)
    sliced = attended
    branch = jnp.dot(
        sliced,
        lax.all_gather(w_output, ("seq", "fsdp"), axis=0, tiled=True),
        preferred_element_type=jnp.float32,
    )
    narrow_out = jnp.dot(attended, down_output, preferred_element_type=jnp.float32).astype(
        jnp.bfloat16
    )
    branch = branch + jnp.dot(narrow_out, up_output.T, preferred_element_type=jnp.float32)
    residual = inputs_wide + branch
    inverse_ffn = lax.rsqrt(jnp.mean(residual * residual, axis=-1, keepdims=True) + epsilon)
    normed_ffn = (residual * inverse_ffn * gain_ffn).astype(jnp.bfloat16)
    ffn_weights = (
        lax.all_gather(w_gate, "fsdp", axis=1, tiled=True),
        lax.all_gather(w_up, "fsdp", axis=1, tiled=True),
        lax.all_gather(w_down, "fsdp", axis=1, tiled=True),
    )
    pieces = (
        lax.all_gather(ffn_weights[0], "seq", axis=0, tiled=True),
        lax.all_gather(ffn_weights[1], "seq", axis=0, tiled=True),
    )
    sliced = normed_ffn
    gate_pre = jnp.dot(sliced, pieces[0], preferred_element_type=jnp.float32)
    up_pre = jnp.dot(sliced, pieces[1], preferred_element_type=jnp.float32)
    sigmoid_gate = jax.nn.sigmoid(gate_pre)
    silu_gate = gate_pre * sigmoid_gate
    hidden = (silu_gate * up_pre).astype(jnp.bfloat16)
    ffn_part = jnp.dot(
        hidden,
        lax.all_gather(ffn_weights[2], "seq", axis=0, tiled=True).T,
        preferred_element_type=jnp.float32,
    )
    output = (residual + ffn_part).astype(jnp.bfloat16)
    sliced = cot_narrow
    grad_hidden = jnp.dot(
        sliced,
        lax.all_gather(ffn_weights[2], "seq", axis=0, tiled=True),
        preferred_element_type=jnp.float32,
    )
    grad_gate = (
        grad_hidden * up_pre * sigmoid_gate * (1.0 + gate_pre * (1.0 - sigmoid_gate))
    ).astype(jnp.bfloat16)
    grad_up = (grad_hidden * silu_gate).astype(jnp.bfloat16)
    pieces = lax.all_gather((ffn_weights[0], ffn_weights[1]), "seq", axis=0, tiled=True)
    grad_part = jnp.dot(grad_gate, pieces[0].T, preferred_element_type=jnp.float32) + jnp.dot(
        grad_up, pieces[1].T, preferred_element_type=jnp.float32
    )
    grad_residual = cot_wide + norm_back(residual, inverse_ffn, gain_ffn, grad_part)
    grad_branch = grad_residual.astype(jnp.bfloat16)
    grad_narrow_out = jnp.dot(grad_branch, up_output, preferred_element_type=jnp.float32)
    grad_up_output = jnp.dot(grad_branch.T, narrow_out, preferred_element_type=jnp.float32)
    grad_down_output = jnp.dot(attended.T, grad_narrow_out, preferred_element_type=jnp.float32)
    attended_gradient = (
        jnp.dot(
            grad_branch,
            lax.all_gather(w_output, ("seq", "fsdp"), axis=0, tiled=True).T,
            preferred_element_type=jnp.float32,
        )
        + jnp.dot(grad_narrow_out, down_output.T, preferred_element_type=jnp.float32)
        + 2.0 * difference
    )
    attended_gradient = (
        lax.optimization_barrier(attended_gradient.astype(jnp.bfloat16)).astype(jnp.float32)
        * row_mask[:, None]
    )
    gradient_by_group = jnp.moveaxis(
        attended_gradient.reshape(rows_per_block, KEY_VALUE_HEADS, heads_per_group, HEAD_SIZE), 1, 0
    )

    def backward_group(operands):
        return attend_back(operands, key_valid)

    grad_q, grad_k, grad_v, grad_qm, grad_km, grad_state, grad_total = lax.map(
        backward_group,
        (
            queries_by_group,
            query_maps_by_group,
            grouped_keys,
            grouped_values,
            grouped_kmaps,
            state_in,
            total_in,
            numerator,
            denominator,
            gradient_by_group,
        ),
    )
    later_state, later_total = prefix((grad_state, grad_total), "seq", add_pair, zero_pair, True)
    values_grouped_head = jnp.moveaxis(values_head, 1, 0)
    used_grouped = jnp.moveaxis(used_maps, 1, 0)
    kmaps_head = grad_km[:, :rows_per_block] + valid_rows[None, :, None] * (
        jnp.einsum("gfd,gsd->gsf", later_state, values_grouped_head, precision=precise)
        + later_total[:, None, :]
    )
    grad_km = jnp.concatenate([kmaps_head, grad_km[:, rows_per_block:]], axis=1)
    values_grad_head = grad_v[:, :rows_per_block] + jnp.einsum(
        "gsf,gfd->gsd", used_grouped, later_state, precision=precise
    )
    grad_v = jnp.concatenate([values_grad_head, grad_v[:, rows_per_block:]], axis=1)
    grad_k_feat, key_feature_gradient = feature_back(
        keys_ext, key_features, jnp.moveaxis(grad_km, 0, 1)
    )
    gathered_key_gradient = jnp.moveaxis(grad_k, 0, 1) + grad_k_feat
    gathered_value_gradient = jnp.moveaxis(grad_v, 0, 1)
    grad_q_feat, grad_feature_query = feature_back(
        query_rows,
        query_features,
        jnp.moveaxis(grad_qm, 0, 1).reshape(rows_per_block, QUERY_HEADS, feature_width),
    )
    grad_queries_rot = (
        jnp.moveaxis(grad_q, 0, 1).reshape(rows_per_block, QUERY_HEADS, HEAD_SIZE) + grad_q_feat
    )
    back_keys, back_values = (
        shifted(
            gathered_key_gradient[:WINDOW_KEYS]
            .reshape(WINDOW_KEYS, KEY_VALUE_HEADS * HEAD_SIZE)
            .astype(jnp.bfloat16),
            "seq",
            -1,
        ).astype(jnp.float32),
        shifted(
            as_sent(
                gathered_value_gradient[:WINDOW_KEYS].reshape(
                    WINDOW_KEYS, KEY_VALUE_HEADS * HEAD_SIZE
                )
            ),
            "seq",
            -1,
        ),
    )
    trailing_keys = gathered_key_gradient[WINDOW_KEYS:].reshape(
        rows_per_block, KEY_VALUE_HEADS * HEAD_SIZE
    )
    trailing_values = gathered_value_gradient[WINDOW_KEYS:].reshape(
        rows_per_block, KEY_VALUE_HEADS * HEAD_SIZE
    )
    trailing_keys = jnp.concatenate(
        [
            trailing_keys[: rows_per_block - WINDOW_KEYS],
            trailing_keys[rows_per_block - WINDOW_KEYS :] + back_keys,
        ],
        axis=0,
    )
    trailing_values = jnp.concatenate(
        [
            trailing_values[: rows_per_block - WINDOW_KEYS],
            trailing_values[rows_per_block - WINDOW_KEYS :] + back_values,
        ],
        axis=0,
    )
    grad_query_pre = (
        inverse_rotary(grad_queries_rot, cosine_lookup, sine_lookup)
        .reshape(rows_per_block, QUERY_HEADS * HEAD_SIZE)
        .astype(jnp.bfloat16)
    )
    grad_key_pre = (
        inverse_rotary(
            trailing_keys.reshape(rows_per_block, KEY_VALUE_HEADS, HEAD_SIZE),
            cosine_lookup,
            sine_lookup,
        )
        .reshape(rows_per_block, KEY_VALUE_HEADS * HEAD_SIZE)
        .astype(jnp.bfloat16)
    )
    grad_value_pre = trailing_values.astype(jnp.bfloat16)
    grad_narrow_query = jnp.dot(grad_query_pre, up_query, preferred_element_type=jnp.float32)
    grad_narrow_key = jnp.dot(grad_key_pre, key_up_matrix, preferred_element_type=jnp.float32)
    grad_narrow_value = jnp.dot(grad_value_pre, value_up_matrix, preferred_element_type=jnp.float32)
    grad_up_query = jnp.dot(grad_query_pre.T, narrow_query, preferred_element_type=jnp.float32)
    grad_up_key = jnp.dot(grad_key_pre.T, narrow_key, preferred_element_type=jnp.float32)
    grad_up_value = jnp.dot(grad_value_pre.T, narrow_value, preferred_element_type=jnp.float32)
    grad_down_query = jnp.dot(normed.T, grad_narrow_query, preferred_element_type=jnp.float32)
    grad_down_key = jnp.dot(normed.T, grad_narrow_key, preferred_element_type=jnp.float32)
    grad_down_value = jnp.dot(normed.T, grad_narrow_value, preferred_element_type=jnp.float32)
    pieces = lax.all_gather(
        (w_query, key_projection, value_projection), ("seq", "fsdp"), axis=0, tiled=True
    )
    grad_normed = (
        jnp.dot(grad_query_pre, pieces[0].T, preferred_element_type=jnp.float32)
        + jnp.dot(grad_key_pre, pieces[1].T, preferred_element_type=jnp.float32)
        + jnp.dot(grad_value_pre, pieces[2].T, preferred_element_type=jnp.float32)
    )
    grad_normed = grad_normed + jnp.dot(
        grad_narrow_query, down_query.T, preferred_element_type=jnp.float32
    )
    grad_normed = grad_normed + jnp.dot(
        grad_narrow_key, key_down_matrix.T, preferred_element_type=jnp.float32
    )
    grad_normed = grad_normed + jnp.dot(
        grad_narrow_value, value_down_matrix.T, preferred_element_type=jnp.float32
    )
    grad_tokens = (
        grad_residual + norm_back(inputs_wide, inverse_attn, gain_attn, grad_normed)
    ).astype(jnp.bfloat16)
    device_count = lax.axis_size(("seq", "fsdp"))
    device_number = lax.axis_index(("seq", "fsdp"))
    loss_terms = jnp.where(jnp.arange(device_count) >= device_number, local_loss, 0.0)
    summed = (
        lax.psum_scatter(grad_down_query, ("seq", "fsdp"), scatter_dimension=0, tiled=True),
        lax.psum_scatter(grad_up_query, ("seq", "fsdp"), scatter_dimension=0, tiled=True),
        lax.psum_scatter(grad_down_key, ("seq", "fsdp"), scatter_dimension=0, tiled=True),
        lax.psum_scatter(grad_up_key, ("seq", "fsdp"), scatter_dimension=0, tiled=True),
        lax.psum_scatter(grad_down_value, ("seq", "fsdp"), scatter_dimension=0, tiled=True),
        lax.psum_scatter(grad_up_value, ("seq", "fsdp"), scatter_dimension=0, tiled=True),
        lax.psum_scatter(grad_down_output, ("seq", "fsdp"), scatter_dimension=0, tiled=True),
        lax.psum_scatter(grad_up_output, ("seq", "fsdp"), scatter_dimension=0, tiled=True),
        lax.psum_scatter(
            grad_feature_query.reshape(QUERY_HEADS * HEAD_SIZE, HEAD_SIZE),
            ("seq", "fsdp"),
            scatter_dimension=0,
            tiled=True,
        ),
        lax.psum_scatter(
            key_feature_gradient.reshape(KEY_VALUE_HEADS * HEAD_SIZE, HEAD_SIZE),
            ("seq", "fsdp"),
            scatter_dimension=0,
            tiled=True,
        ),
        lax.psum_scatter(loss_terms, ("seq", "fsdp"), scatter_dimension=0, tiled=True),
    )
    transfer_loss = summed[10] / jnp.sum(lengths).astype(jnp.float32)
    return (
        output[None],
        grad_tokens[None],
        summed[0],
        summed[1],
        summed[2],
        summed[3],
        summed[4],
        summed[5],
        summed[6],
        summed[7],
        summed[8],
        summed[9],
        transfer_loss,
    )

def halves_rotated(first_half, second_half, cosine, sine):
    return (
        first_half * cosine - second_half * sine,
        second_half * cosine + first_half * sine,
    )


def soft_pair(logits):
    plus = jnp.exp(logits - jnp.max(logits, axis=0, keepdims=True))
    minus = jnp.exp(jnp.min(logits, axis=0, keepdims=True) - logits)
    plus = plus * (1.0 / jnp.sum(plus, axis=0, keepdims=True))
    minus = minus * (1.0 / jnp.sum(minus, axis=0, keepdims=True))
    return plus, minus


def mm(a, b):
    return jnp.dot(a, b, preferred_element_type=jnp.float32)


def mm_nt(a, b):
    return lax.dot_general(a, b, (((1,), (1,)), ((), ())), preferred_element_type=jnp.float32)


def mm_tn(a, b):
    return lax.dot_general(a, b, (((0,), (0,)), ((), ())), preferred_element_type=jnp.float32)


def split_wide(x):
    high = x.astype(jnp.bfloat16)
    low = (x - high.astype(jnp.float32)).astype(jnp.bfloat16)
    return high, low


ANYWHERE = pl.BlockSpec(memory_space=pltpu.HBM)


def call(kernel, grid, in_specs, out_specs, out_shape, scratch, flops, moved, scalars=0):
    spec = pltpu.PrefetchScalarGridSpec(
        num_scalar_prefetch=scalars,
        grid=grid,
        in_specs=in_specs,
        out_specs=out_specs,
        scratch_shapes=scratch,
    )
    return pl.pallas_call(
        kernel,
        grid_spec=spec,
        out_shape=out_shape,
        compiler_params=pltpu.CompilerParams(vmem_limit_bytes=VMEM_MIB * 2**20),
        cost_estimate=pl.CostEstimate(
            flops=int(COST * moved), bytes_accessed=1, transcendentals=0
        ),
    )


def spec_whole(*dims):
    return pl.BlockSpec(dims, lambda i, *_: (0,) * len(dims))


def spec_across(height, columns):
    return pl.BlockSpec((height, columns), lambda i, *_: (0, i))


def spec_down(rows, wide):
    return pl.BlockSpec((rows, wide), lambda i, *_: (i, 0))


def spec_block(*dims):
    return pl.BlockSpec((None,) + dims, lambda i, *_: (i, 0, 0))


def spec_placed(spec):
    return pl.BlockSpec(
        spec.block_shape,
        lambda i, place_ref, *_: spec.index_map(lax.bitwise_xor(i, place_ref[0])),
    )


def array(*dims, dtype=jnp.bfloat16):
    return jax.ShapeDtypeStruct(dims, dtype)


def flat(found):
    return [part for parts in found for part in parts]


def grouped(refs, counts):
    found, start = [], 0
    for count in counts:
        found.append(tuple(refs[start : start + count]))
        start += count
    return found, refs[start:]


def fetch(refs, buffer, sems, at, order=lambda step: step):
    steps = len(refs)

    def start(step):
        slot = lax.rem(step, 2)
        wanted = order(step)
        for number, parts in enumerate(refs):

            @pl.when(wanted == number)
            def _():
                height = buffer.shape[1] // len(parts)
                for part, ref in enumerate(parts):
                    pltpu.make_async_copy(
                        ref, buffer.at[slot, part * height : (part + 1) * height], sems.at[slot]
                    ).start()

    @pl.when(at == 0)
    def _():
        start(at)

    @pl.when(at + 1 < steps)
    def _():
        start(at + 1)

    slot = lax.rem(at, 2)
    pltpu.make_async_copy(buffer.at[slot], buffer.at[slot], sems.at[slot]).wait()
    return slot


def start_columns(refs, span, buffer, sem):
    first, end = span
    wide = end - first
    for chunk, ref in enumerate(refs):
        pltpu.make_async_copy(
            ref.at[:, first:end], buffer.at[:, chunk * wide : (chunk + 1) * wide], sem
        ).start()


def chunks_of(ref, order_ref):
    return [ref.at[order_ref[chunk]] for chunk in range(ref.shape[0])]


def wait_whole(buffer, sem):
    pltpu.make_async_copy(buffer, buffer, sem).wait()


def block_shape(blocks):
    return sum(part.shape[0] for part in blocks[0]), blocks[0][0].shape[1]


def fetch_scratch(blocks):
    rows, wide = block_shape(blocks)
    return [pltpu.VMEM((2, rows, wide), jnp.bfloat16), pltpu.SemaphoreType.DMA((2,))]


def project_kernel(counts, place_ref, *refs):
    blocks, refs = grouped(refs, counts)
    (
        w_ref, down_ref, up_ref, map_ref, cos_ref, sin_ref,
        q_ref, kt_ref, vt_ref, k_ref, v_ref, pq_ref, pkt_ref, pk_ref, narrow_ref, wt_ref,
        buffer, sems,
    ) = refs
    group = q_ref.shape[0] // HEAD_SIZE
    half = HEAD_SIZE // 2
    width = (group + 2) * HEAD_SIZE
    slot = fetch(blocks, buffer, sems, pl.program_id(0))

    @pl.when(pl.program_id(0) == 0)
    def _():
        lanes, places, shard, _ = w_ref.shape
        for place in range(places):
            rows = jnp.concatenate([w_ref[lane, place] for lane in range(lanes)], axis=0)
            columns = slice(place * lanes * shard, (place + 1) * lanes * shard)
            wt_ref[:width, columns] = jnp.transpose(rows)
        wt_ref[width:] = down_ref[...]

    full = mm_nt(wt_ref[...], buffer[slot])
    narrow = full[width:].astype(jnp.bfloat16)
    narrow_ref[...] = narrow
    pre = full[:width] + mm(up_ref[...], narrow)
    cosine, sine = cos_ref[...], sin_ref[...]
    for head in range(group + 1):
        base = head * HEAD_SIZE
        low_half, high_half = halves_rotated(
            pre[base : base + half], pre[base + half : base + HEAD_SIZE], cosine, sine
        )
        wide = jnp.concatenate([low_half, high_half], axis=0)
        vector = wide.astype(jnp.bfloat16)
        logits = mm(map_ref[base : base + HEAD_SIZE], vector)
        plus, minus = soft_pair(logits)
        maps = jnp.concatenate([plus, minus], axis=0)
        if head < group:
            q_ref[base : base + HEAD_SIZE] = vector
            pq_ref[2 * base : 2 * base + 2 * HEAD_SIZE] = maps.astype(jnp.bfloat16)
        else:
            kt_ref[...] = vector
            k_ref[...] = jnp.transpose(wide).astype(jnp.bfloat16)
            pkt_ref[...] = maps.astype(jnp.bfloat16)
            pk_ref[...] = jnp.transpose(maps).astype(jnp.bfloat16)
    values = pre[width - HEAD_SIZE : width]
    vt_ref[:HEAD_SIZE] = values.astype(jnp.bfloat16)
    vt_ref[HEAD_SIZE:] = jnp.ones((ONES, values.shape[1]), jnp.bfloat16)
    v_ref[...] = jnp.transpose(values).astype(jnp.bfloat16)


def project(place_row, blocks, weights, down_block, up_block, maps_ahead, cosine, sine):
    places = len(blocks)
    rows, model = block_shape(blocks)
    count = places * rows
    width, spare = up_block.shape
    query_width = width - 2 * HEAD_SIZE
    group = query_width // HEAD_SIZE
    maps = 2 * HEAD_SIZE
    half = HEAD_SIZE // 2
    counts = [len(found) for found in blocks]
    outs = [
        (query_width, False),
        (HEAD_SIZE, False),
        (HEAD_SIZE + ONES, False),
        (HEAD_SIZE, True),
        (HEAD_SIZE, True),
        (group * maps, False),
        (maps, False),
        (maps, True),
        (spare, False),
    ]
    return call(
        functools.partial(project_kernel, counts),
        (places,),
        [ANYWHERE] * sum(counts)
        + [
            spec_whole(*weights.shape),
            spec_whole(spare, model),
            spec_whole(width, spare),
            spec_whole(*maps_ahead.shape),
            spec_placed(spec_across(half, rows)),
            spec_placed(spec_across(half, rows)),
        ],
        [
            spec_placed(spec_down(rows, size) if natural else spec_across(size, rows))
            for size, natural in outs
        ]
        + [spec_whole(width + spare, model)],
        [array(count, size) if natural else array(size, count) for size, natural in outs]
        + [array(width + spare, model)],
        fetch_scratch(blocks),
        0,
        17,
        scalars=1,
    )(place_row, *flat(blocks), weights, down_block, up_block, maps_ahead, cosine, sine)


def side_by_side(ref, size, group, columns):
    return jnp.concatenate(
        [ref[head * size : (head + 1) * size, columns] for head in range(group)], axis=1
    )


def bands():
    shape = (WINDOW_KEYS, SUB)
    query_at = lax.broadcasted_iota(jnp.int32, shape, 1)
    key_at = lax.broadcasted_iota(jnp.int32, shape, 0)
    distance = query_at - key_at
    return (
        distance < 0,
        (distance >= 0) & (distance < WINDOW_KEYS),
        distance >= WINDOW_KEYS,
        distance >= WINDOW_KEYS,
    )


def forward_kernel(
    length_ref, q_ref, pq_ref, k_ref, k_before, pk_ref, pk_before, vt_ref, vt_before,
    att_ref, out_ref, denom_ref, states_ref, weights_ref, state,
):
    step = pl.program_id(0)
    group = q_ref.shape[0] // HEAD_SIZE
    rows = q_ref.shape[1]
    quarter = WINDOW_KEYS
    second, third, third_far, fourth = bands()

    @pl.when(step == 0)
    def _():
        state[...] = jnp.zeros_like(state)

    now = state[...]
    for sub in range(rows // SUB):
        columns = slice(sub * SUB, (sub + 1) * SUB)
        queries = side_by_side(q_ref, HEAD_SIZE, group, columns)
        query_maps = side_by_side(pq_ref, 2 * HEAD_SIZE, group, columns)
        if sub == 0:
            keys = jnp.concatenate([k_before[...], k_ref[:SUB]], axis=0)
            key_maps = jnp.concatenate([pk_before[...], pk_ref[:SUB]], axis=0)
            values = jnp.concatenate([vt_before[...], vt_ref[:, :SUB]], axis=1)
        else:
            around = slice((sub - 1) * SUB, (sub + 1) * SUB)
            keys, key_maps, values = k_ref[around], pk_ref[around], vt_ref[:, around]
        scores = mm(keys[quarter:], queries)
        far = mm(key_maps[: 3 * quarter], query_maps)
        pieces = []
        for head in range(group):
            lanes = slice(head * SUB, (head + 1) * SUB)
            near = jnp.exp(scores[:, lanes] * (1.0 / math.sqrt(HEAD_SIZE)))
            away = far[:, lanes]
            before = jnp.concatenate(
                [
                    away[:quarter],
                    jnp.where(second, near[:quarter], away[quarter : 2 * quarter]),
                ],
                axis=0,
            )
            if sub == 0:
                before = jnp.where(step > 0, before, 0.0)
            pieces.append(
                jnp.concatenate(
                    [
                        before,
                        jnp.where(
                            third,
                            near[quarter : 2 * quarter],
                            jnp.where(third_far, away[2 * quarter :], 0.0),
                        ),
                        jnp.where(fourth, near[2 * quarter :], 0.0),
                    ],
                    axis=0,
                ).astype(jnp.bfloat16)
            )
        weights = jnp.concatenate(pieces, axis=1)
        weights_ref[sub] = weights
        states_ref[sub] = now
        high, low = split_wide(now)
        total = mm(values, weights) + mm(
            jnp.concatenate([high, low], axis=1),
            jnp.concatenate([query_maps, query_maps], axis=0),
        )
        denom = total[HEAD_SIZE : HEAD_SIZE + 1]
        out = total[:HEAD_SIZE] * (1.0 / denom)
        at = step * rows + sub * SUB + lax.broadcasted_iota(jnp.int32, (HEAD_SIZE, SUB), 1)
        inside = at < length_ref[0]
        for head in range(group):
            lanes = slice(head * SUB, (head + 1) * SUB)
            base = head * HEAD_SIZE
            out_ref[base : base + HEAD_SIZE, columns] = out[:, lanes]
            att_ref[base : base + HEAD_SIZE, columns] = jnp.where(
                inside, out[:, lanes], 0.0
            ).astype(jnp.bfloat16)
            denom_ref[head : head + 1, columns] = denom[:, lanes]
        update = mm(values[:, :SUB], key_maps[:SUB])
        if sub == 0:
            update = jnp.where(step > 0, update, 0.0)
        now = now + update
    state[...] = now


def before_down(rows, wide):
    per_step = rows // SUB
    return pl.BlockSpec((SUB, wide), lambda i, *_: (jnp.maximum(per_step * i - 1, 0), 0))


def before_across(rows, height):
    per_step = rows // SUB
    return pl.BlockSpec((height, SUB), lambda i, *_: (0, jnp.maximum(per_step * i - 1, 0)))


def attend(length, q_t, pq_t, keys, key_maps, v_t, rows):
    query_width, count = q_t.shape
    group = query_width // HEAD_SIZE
    places = count // rows
    per_step = rows // SUB
    maps = key_maps.shape[1]
    high = v_t.shape[0]
    wide = jnp.float32
    return call(
        forward_kernel,
        (places,),
        [
            spec_across(query_width, rows),
            spec_across(group * maps, rows),
            spec_down(rows, HEAD_SIZE),
            before_down(rows, HEAD_SIZE),
            spec_down(rows, maps),
            before_down(rows, maps),
            spec_across(high, rows),
            before_across(rows, high),
        ],
        [
            spec_block(query_width, rows),
            spec_across(query_width, rows),
            spec_across(group, rows),
            pl.BlockSpec((per_step, high, maps), lambda i, *_: (i, 0, 0)),
            pl.BlockSpec((per_step, 2 * SUB, group * SUB), lambda i, *_: (i, 0, 0)),
        ],
        [
            array(places, query_width, rows),
            array(query_width, count, dtype=wide),
            array(group, count, dtype=wide),
            array(count // SUB, high, maps, dtype=wide),
            array(count // SUB, 2 * SUB, group * SUB),
        ],
        [pltpu.VMEM((high, maps), wide)],
        0,
        10,
        scalars=1,
    )(length, q_t, pq_t, keys, keys, key_maps, key_maps, v_t, v_t)


def teacher_kernel(first, steps, length_ref, q_ref, k_ref, vt_ref, att_ref, *refs):
    diff_ref, loss_ref = refs[-2:]
    step = pl.program_id(0)
    group = q_ref.shape[0] // HEAD_SIZE
    rows = q_ref.shape[1]
    scale = 1.0 / math.sqrt(HEAD_SIZE)
    at = (first + step) * rows + lax.broadcasted_iota(jnp.int32, (HEAD_SIZE, rows), 1)
    inside = at < length_ref[0]
    shape = (rows, rows)
    ahead = lax.broadcasted_iota(jnp.int32, shape, 0) > lax.broadcasted_iota(jnp.int32, shape, 1)

    for blocks in range(first + 1, first + steps + 1):

        @pl.when(first + step == blocks - 1)
        def _():
            size = blocks * rows
            loss = jnp.zeros((1, rows), jnp.float32)
            for head in range(group):
                base = head * HEAD_SIZE
                query = q_ref[base : base + HEAD_SIZE]
                last = jnp.where(ahead, lowest_precision, mm(k_ref[size - rows : size], query))
                best = jnp.max(last, axis=0, keepdims=True)
                if blocks > 1:
                    early = mm(k_ref[: size - rows], query)
                    best = jnp.maximum(best, jnp.max(early, axis=0, keepdims=True))
                total = mm(
                    vt_ref[:, size - rows : size],
                    jnp.exp((last - best) * scale).astype(jnp.bfloat16),
                )
                if blocks > 1:
                    total = total + mm(
                        vt_ref[:, : size - rows],
                        jnp.exp((early - best) * scale).astype(jnp.bfloat16),
                    )
                taught = total[:HEAD_SIZE] * (1.0 / total[HEAD_SIZE : HEAD_SIZE + 1])
                difference = att_ref[base : base + HEAD_SIZE].astype(jnp.float32) - jnp.where(
                    inside, taught, 0.0
                )
                diff_ref[base : base + HEAD_SIZE] = difference
                loss = loss + jnp.sum(difference * difference, axis=0, keepdims=True)
            loss_ref[...] = jnp.broadcast_to(loss, loss_ref.shape)


def teach(length, q_t, keys, v_t, att, first, end, before=None):
    places, query_width, rows = att.shape
    count = places * rows
    wide = jnp.float32

    def ahead(spec):
        return pl.BlockSpec(spec.block_shape, lambda i, *_: spec.index_map(i + first))

    spec = pltpu.PrefetchScalarGridSpec(
        num_scalar_prefetch=1,
        grid=(end - first,),
        in_specs=[
            ahead(spec_across(query_width, rows)),
            spec_whole(*keys.shape),
            spec_whole(*v_t.shape),
            ahead(spec_block(query_width, rows)),
        ]
        + [ANYWHERE] * (2 if before else 0),
        out_specs=[ahead(spec_across(query_width, rows)), ahead(spec_across(8, rows))],
    )
    return pl.pallas_call(
        functools.partial(teacher_kernel, first, end - first),
        grid_spec=spec,
        out_shape=[array(query_width, count, dtype=wide), array(8, count, dtype=wide)],
        input_output_aliases={5: 0, 6: 1} if before else {},
        compiler_params=pltpu.CompilerParams(vmem_limit_bytes=VMEM_MIB * 2**20),
        cost_estimate=pl.CostEstimate(
            flops=int(COST * 16), bytes_accessed=1, transcendentals=0
        ),
    )(length, q_t, keys, v_t, att, *(before or ()))


def hidden_kernel(counts, order_ref, *refs):
    blocks, refs = grouped(refs, counts)
    *gates, ups, hidden_ref, by_gate_ref, by_up_ref, buffer, sems, both, both_sem = refs

    @pl.when(pl.program_id(0) == 0)
    def _():
        unit = ups.shape[2] // PARTS
        wide = ups.shape[0] * unit
        for part in range(PARTS):
            span = part * unit, (part + 1) * unit
            start_columns(gates, span, both.at[:, part * wide : (part + 1) * wide], both_sem)
            start = (PARTS + part) * wide
            start_columns(chunks_of(ups, order_ref), span, both.at[:, start : start + wide], both_sem)

    slot = fetch(blocks, buffer, sems, pl.program_id(0))

    @pl.when(pl.program_id(0) == 0)
    def _():
        wait_whole(both, both_sem)

    full = mm(buffer[slot], both[...])
    wide = full.shape[1] // 2
    gate, up = full[:, :wide], full[:, wide:]
    sigmoid = 1.0 / (1.0 + jnp.exp(-gate))
    silu = gate * sigmoid
    hidden_ref[...] = (silu * up).astype(jnp.bfloat16)
    by_gate_ref[...] = (up * (sigmoid + silu * (1.0 - sigmoid))).astype(jnp.bfloat16)
    by_up_ref[...] = silu.astype(jnp.bfloat16)


def hidden_units(order, blocks, gates, ups):
    rows, model = block_shape(blocks)
    count = rows * len(blocks)
    share = ups.shape[0] * ups.shape[2]
    counts = [len(found) for found in blocks]
    return call(
        functools.partial(hidden_kernel, counts),
        (len(blocks),),
        [ANYWHERE] * (sum(counts) + 1 + len(gates)),
        [spec_down(rows, share)] * 3,
        [array(count, share)] * 3,
        fetch_scratch(blocks)
        + [pltpu.VMEM((model, 2 * share), jnp.bfloat16), pltpu.SemaphoreType.DMA],
        0,
        25,
        scalars=1,
    )(order, *flat(blocks), *gates, ups)


def ffn_back_kernel(counts, chunks, part, more, order_ref, *refs):
    blocks, refs = grouped(refs, counts)
    *gates, ups, downs, by_gate_ref, by_up_ref = refs[: chunks + 4]
    before_ref = refs[chunks + 4] if more else None
    out_ref, buffer, sems, both, both_sem, down, down_sem = refs[-7:]

    @pl.when(pl.program_id(0) == 0)
    def _():
        wide = both.shape[1] // 2
        unit = downs.shape[2]
        span = part * unit, (part + 1) * unit
        start_columns(chunks_of(downs, order_ref), (0, unit), down, down_sem)
        start_columns(gates, span, both.at[:, :wide], both_sem)
        start_columns(chunks_of(ups, order_ref), span, both.at[:, wide:], both_sem)

    slot = fetch(blocks, buffer, sems, pl.program_id(0))

    @pl.when(pl.program_id(0) == 0)
    def _():
        wait_whole(down, down_sem)
        wait_whole(both, both_sem)

    grad_hidden = mm(buffer[slot], down[...])
    grad_gate = (grad_hidden * by_gate_ref[...].astype(jnp.float32)).astype(jnp.bfloat16)
    grad_up = (grad_hidden * by_up_ref[...].astype(jnp.float32)).astype(jnp.bfloat16)
    total = mm_nt(jnp.concatenate([grad_gate, grad_up], axis=1), both[...])
    if more:
        total = total + before_ref[...].astype(jnp.float32)
    out_ref[...] = total.astype(jnp.bfloat16)


def ffn_back(order, blocks, first, each, part, gates, ups, downs, by_gate, by_up, before):
    rows, model = block_shape(blocks)
    share = downs.shape[0] * downs.shape[2]
    counts = [len(found) for found in blocks]
    more = before is not None

    def rows_of(wide, at=0):
        return pl.BlockSpec((rows, wide), lambda i, *_: (first + each * i, at))

    return call(
        functools.partial(ffn_back_kernel, counts, len(gates), part, more),
        (len(blocks),),
        [ANYWHERE] * (sum(counts) + len(gates) + 2)
        + [rows_of(share, part)] * 2
        + [rows_of(model)] * more,
        spec_down(rows, model),
        array(len(blocks) * rows, model),
        fetch_scratch(blocks)
        + [pltpu.VMEM((model, 2 * share), jnp.bfloat16), pltpu.SemaphoreType.DMA]
        + [pltpu.VMEM((model, share), jnp.bfloat16), pltpu.SemaphoreType.DMA],
        0,
        3 * len(blocks),
        scalars=1,
    )(order, *flat(blocks), *gates, ups, downs, by_gate, by_up, *([before] if more else []))


def ffn_out_kernel(place_ref, order_ref, *refs):
    downs, (hidden_ref, out_ref, down, down_sem) = refs[:PARTS], refs[PARTS:]

    @pl.when(pl.program_id(0) == 0)
    def _():
        wide = down.shape[1] // PARTS
        for part, ref in enumerate(downs):
            start_columns(
                chunks_of(ref, order_ref), (0, ref.shape[2]), down.at[:, part * wide : (part + 1) * wide], down_sem
            )
        wait_whole(down, down_sem)

    out_ref[...] = mm_nt(hidden_ref[...], down[...]).astype(jnp.bfloat16)


def ffn_out(place_row, order, hidden, downs, places):
    count, share = hidden.shape
    rows = count // places
    model = downs[0].shape[1]
    return call(
        ffn_out_kernel,
        (places,),
        [ANYWHERE] * PARTS + [spec_down(rows, share)],
        spec_placed(spec_down(rows, model)),
        array(count, model),
        [pltpu.VMEM((model, share), jnp.bfloat16), pltpu.SemaphoreType.DMA],
        0,
        17,
        scalars=2,
    )(place_row, order, *downs, hidden)


def backward_kernel(
    counts, length_ref, place_ref, *refs
):
    blocks, refs = grouped(refs, counts)
    (
    grad_ref, diff_ref, out_ref, denom_ref, q_ref, pq_ref, weights_ref,
    v_ref, v_before, kt_ref, kt_before, pkt_ref, pkt_before, vt_ref, vt_before,
    states_ref, map_ref, back_ref, cos_ref, sin_ref, up_ref, wt_ref,
    pre_ref, gain_ref, fall_ref, give_ref, keep_ref, key_carry, value_carry, map_carry, later,
    buffer, sems,
    ) = refs
    step = pl.num_programs(0) - 1 - pl.program_id(0)
    group = q_ref.shape[0] // HEAD_SIZE
    rows = q_ref.shape[1]
    half = HEAD_SIZE // 2
    quarter = WINDOW_KEYS
    scale = 1.0 / math.sqrt(HEAD_SIZE)
    second, third, third_far, fourth = bands()
    short = jnp.bfloat16
    per_block = grad_ref.shape[2]
    inner = per_block // SUB

    @pl.when(pl.program_id(0) == 0)
    def _():
        gain_ref[...] = jnp.zeros_like(gain_ref)
        key_carry[...] = jnp.zeros_like(key_carry)
        value_carry[...] = jnp.zeros_like(value_carry)
        map_carry[...] = jnp.zeros_like(map_carry)
        later[...] = jnp.zeros_like(later)
        fall_ref[...] = jnp.zeros_like(fall_ref)

    carried_keys, carried_values, carried_maps = key_carry[...], value_carry[...], map_carry[...]
    later_now = later[...]
    query_parts, map_parts, key_parts, value_parts, key_map_parts = [], [], [], [], []
    for sub in reversed(range(rows // SUB)):
        columns = slice(sub * SUB, (sub + 1) * SUB)
        queries = side_by_side(q_ref, HEAD_SIZE, group, columns)
        query_maps = side_by_side(pq_ref, 2 * HEAD_SIZE, group, columns)
        if sub == 0:
            values = jnp.concatenate([v_before[...], v_ref[:SUB]], axis=0)
            keys_t = jnp.concatenate([kt_before[...], kt_ref[:, :SUB]], axis=1)
            key_maps_t = jnp.concatenate([pkt_before[...], pkt_ref[:, :SUB]], axis=1)
            values_before = vt_before[...]
        else:
            around = slice((sub - 1) * SUB, (sub + 1) * SUB)
            values = v_ref[around]
            keys_t, key_maps_t = kt_ref[:, around], pkt_ref[:, around]
            values_before = vt_ref[:, (sub - 1) * SUB : sub * SUB]
        at = step * rows + sub * SUB + lax.broadcasted_iota(jnp.int32, (HEAD_SIZE, SUB), 1)
        inside = at < length_ref[0]
        numers, denoms = [], []
        for head in range(group):
            base = head * HEAD_SIZE
            span = slice(base, base + HEAD_SIZE)
            place_in = slice(sub % inner * SUB, (sub % inner + 1) * SUB)
            incoming = grad_ref[sub // inner, span, place_in].astype(jnp.float32) + 2.0 * diff_ref[span, columns]
            incoming = jnp.where(inside, incoming.astype(short).astype(jnp.float32), 0.0)
            inverse = 1.0 / denom_ref[head : head + 1, columns]
            numers.append((incoming * inverse).astype(short))
            denoms.append(
                -jnp.sum(incoming * out_ref[span, columns], axis=0, keepdims=True) * inverse
            )
        grad_numer = jnp.concatenate(numers, axis=1)
        grad_denom = jnp.concatenate(denoms, axis=1)
        rank = lax.broadcasted_iota(jnp.int32, (ONES, group * SUB), 0)
        denom_high = grad_denom.astype(short).astype(jnp.float32)
        extra = jnp.where(
            rank == 0, denom_high, jnp.where(rank == 1, grad_denom - denom_high, 0.0)
        ).astype(short)
        grad_both = jnp.concatenate([grad_numer, extra], axis=0)
        weights = weights_ref[sub]
        raw = mm(values, grad_numer)
        scores, fars = [], []
        for head in range(group):
            lanes = slice(head * SUB, (head + 1) * SUB)
            grad_weights = raw[:, lanes] + denoms[head]
            if sub == 0:
                kept = jnp.where(step > 0, grad_weights[: 2 * quarter], 0.0)
                grad_weights = jnp.concatenate([kept, grad_weights[2 * quarter :]], axis=0)
            by_score = grad_weights[quarter:] * weights[quarter:, lanes].astype(jnp.float32)
            scores.append(
                jnp.concatenate(
                    [
                        jnp.where(second, by_score[:quarter], 0.0),
                        jnp.where(third, by_score[quarter : 2 * quarter], 0.0),
                        jnp.where(fourth, by_score[2 * quarter :], 0.0),
                    ],
                    axis=0,
                ).astype(short)
            )
            fars.append(
                jnp.concatenate(
                    [
                        grad_weights[:quarter],
                        jnp.where(second, 0.0, grad_weights[quarter : 2 * quarter]),
                        jnp.where(third_far, grad_weights[2 * quarter : 3 * quarter], 0.0),
                    ],
                    axis=0,
                ).astype(short)
            )
        grad_scores = jnp.concatenate(scores, axis=1)
        grad_far = jnp.concatenate(fars, axis=1)
        state_high, state_low = split_wide(jnp.transpose(states_ref[sub]))
        query_parts.append(mm(keys_t[:, quarter:], grad_scores) * scale)
        map_parts.append(
            mm(key_maps_t[:, : 3 * quarter], grad_far)
            + mm(
                jnp.concatenate([state_high, state_low], axis=1),
                jnp.concatenate([grad_both, grad_both], axis=0),
            )
        )
        grad_keys = mm_nt(queries, grad_scores) * scale
        grad_values = mm_nt(grad_numer, weights)
        grad_key_maps = mm_nt(query_maps, grad_far)
        key_parts.append(carried_keys + grad_keys[:, quarter:])
        value_parts.append(carried_values + grad_values[:, SUB:])
        key_map_parts.append(
            jnp.concatenate(
                [
                    carried_maps[:, :quarter] + grad_key_maps[:, 2 * quarter :],
                    carried_maps[:, quarter:],
                ],
                axis=1,
            )
        )
        later_high, later_low = split_wide(jnp.transpose(later_now))
        carried_keys = jnp.concatenate(
            [jnp.zeros((HEAD_SIZE, quarter), jnp.float32), grad_keys[:, :quarter]], axis=1
        )
        carried_values = grad_values[:, :SUB] + mm(
            later_now[:HEAD_SIZE].astype(short), key_maps_t[:, :SUB]
        )
        carried_maps = grad_key_maps[:, : 2 * quarter] + mm(
            jnp.concatenate([later_high, later_low], axis=1),
            jnp.concatenate([values_before, values_before], axis=0),
        )
        later_now = later_now + mm_nt(grad_both, query_maps)
    key_carry[...], value_carry[...], map_carry[...] = carried_keys, carried_values, carried_maps
    later[...] = later_now

    def joined(parts, lanes=slice(None)):
        return jnp.concatenate([part[:, lanes] for part in reversed(parts)], axis=1)

    cosine, sine = cos_ref[...], sin_ref[...]
    for head in range(group + 1):
        base = head * HEAD_SIZE
        span = slice(base, base + HEAD_SIZE)
        lanes = slice(head * SUB, (head + 1) * SUB)
        if head < group:
            vector, direct = q_ref[span], joined(query_parts, lanes)
            grad_maps = joined(map_parts, lanes)
        else:
            vector, direct, grad_maps = kt_ref[...], joined(key_parts), joined(key_map_parts)
        plus, minus = soft_pair(mm(map_ref[span], vector))
        grad_plus, grad_minus = grad_maps[:HEAD_SIZE], grad_maps[HEAD_SIZE:]
        grad_logits = plus * (
            grad_plus - jnp.sum(grad_plus * plus, axis=0, keepdims=True)
        ) - minus * (grad_minus - jnp.sum(grad_minus * minus, axis=0, keepdims=True))
        grad_logits = grad_logits.astype(short)
        gain_ref[span] += mm_nt(vector, grad_logits)
        total = direct + mm(back_ref[span], grad_logits)
        low_half, high_half = halves_rotated(total[:half], total[half:], cosine, -sine)
        pre_ref[base : base + half] = low_half.astype(short)
        pre_ref[base + half : base + HEAD_SIZE] = high_half.astype(short)
    width = (group + 2) * HEAD_SIZE
    pre_ref[width - HEAD_SIZE : width] = joined(value_parts).astype(short)
    pre_ref[width:] = mm_tn(up_ref[...], pre_ref[:width]).astype(short)
    per_step = rows // per_block

    def order(at):
        return (pl.num_programs(0) - 1 - at // per_step) * per_step + lax.rem(at, per_step)

    own_core = lax.rem(place_ref[0], 2)
    for block in range(rows // per_block):
        columns = slice(block * per_block, (block + 1) * per_block)
        here = pre_ref[:, columns]
        grad_normed = mm_tn(here, wt_ref[...]).astype(short)
        slot = fetch(
            blocks,
            buffer,
            sems,
            pl.program_id(0) * (rows // per_block) + block,
            lambda at: lax.bitwise_xor(order(at), place_ref[0]),
        )
        fall_ref[...] += mm(here[width:], buffer[slot])

        @pl.when(own_core == block % 2)
        def _():
            keep_ref[...] = grad_normed

        @pl.when(own_core != block % 2)
        def _():
            give_ref[...] = grad_normed


def heads_back(
    length, place_row, blocks, grad_att, difference, out_t, denom, q_t, pq_t, weights,
    values, k_t, pk_t, v_t, states, maps_ahead, maps_back, cosine, sine, up_block, weights_t,
):
    places, query_width, per_block = grad_att.shape
    count = places * per_block
    rows = 2 * per_block
    steps = count // rows
    group = query_width // HEAD_SIZE
    per_step = rows // SUB
    counts = [len(found) for found in blocks]
    width, spare = up_block.shape
    model = weights_t.shape[1]
    maps = pk_t.shape[0]
    high = v_t.shape[0]
    half = HEAD_SIZE // 2

    def back(spec):
        return pl.BlockSpec(spec.block_shape, lambda i, *_: spec.index_map(steps - 1 - i))

    def by_chip(i, length_ref, place_ref):
        return (lax.bitwise_xor(steps - 1 - i, place_ref[0] // 2), 0, 0)

    def leading(*dims):
        return pl.BlockSpec((per_step,) + dims, lambda i, *_: (i, 0, 0))

    return call(
        functools.partial(backward_kernel, counts),
        (steps,),
        [ANYWHERE] * sum(counts)
        + [
            back(pl.BlockSpec((2, query_width, per_block), lambda i, *_: (i, 0, 0))),
            back(spec_across(query_width, rows)),
            back(spec_across(query_width, rows)),
            back(spec_across(group, rows)),
            back(spec_across(query_width, rows)),
            back(spec_across(group * maps, rows)),
            back(leading(2 * SUB, group * SUB)),
            back(spec_down(rows, HEAD_SIZE)),
            back(before_down(rows, HEAD_SIZE)),
            back(spec_across(HEAD_SIZE, rows)),
            back(before_across(rows, HEAD_SIZE)),
            back(spec_across(maps, rows)),
            back(before_across(rows, maps)),
            back(spec_across(high, rows)),
            back(before_across(rows, high)),
            back(leading(high, maps)),
            spec_whole(*maps_ahead.shape),
            spec_whole(*maps_back.shape),
            back(spec_across(half, rows)),
            back(spec_across(half, rows)),
            spec_whole(width, spare),
            spec_whole(width + spare, model),
        ],
        [
            back(spec_across(width + spare, rows)),
            spec_whole(*maps_back.shape),
            spec_whole(spare, model),
            pl.BlockSpec((None, per_block, model), by_chip),
            pl.BlockSpec((None, per_block, model), by_chip),
        ],
        [
            array(width + spare, count),
            array(*maps_back.shape, dtype=jnp.float32),
            array(spare, model, dtype=jnp.float32),
            array(steps, per_block, model),
            array(steps, per_block, model),
        ],
        [
            pltpu.VMEM((HEAD_SIZE, SUB), jnp.float32),
            pltpu.VMEM((HEAD_SIZE, SUB), jnp.float32),
            pltpu.VMEM((maps, SUB), jnp.float32),
            pltpu.VMEM((high, maps), jnp.float32),
        ]
        + fetch_scratch(blocks),
        0,
        30,
        scalars=2,
    )(
        length, place_row, *flat(blocks), grad_att, difference, out_t, denom, q_t, pq_t, weights,
        values, values, k_t, k_t, pk_t, pk_t, v_t, v_t,
        states, maps_ahead, maps_back, cosine, sine, up_block, weights_t,
    )


def branch_kernel(
    counts, place_ref, *refs
):
    blocks, refs = grouped(refs, counts)
    (
        att_ref, down_ref, up_ref, tokens_ref, gain_ref,
        residual_ref, normed_ref, inverse_ref, narrow_ref, buffer, sems, total, slim,
    ) = refs
    step = pl.program_id(0)
    slot = fetch(blocks, buffer, sems, step)

    @pl.when(step == 0)
    def _():
        total[...] = tokens_ref[...].astype(jnp.float32)
        slim[...] = jnp.zeros_like(slim)

    total[...] += mm_tn(att_ref[...], buffer[slot])
    slim[...] += mm_tn(att_ref[...], down_ref[...])

    @pl.when(step == pl.num_programs(0) - 1)
    def _():
        narrow = slim[...].astype(jnp.bfloat16)
        narrow_ref[...] = narrow
        residual = total[...] + mm_nt(narrow, up_ref[...])
        residual_ref[...] = residual
        inverse = lax.rsqrt(jnp.mean(residual * residual, axis=-1, keepdims=True) + epsilon)
        inverse_ref[...] = jnp.broadcast_to(inverse, inverse_ref.shape)
        normed_ref[...] = (residual * inverse * gain_ref[...]).astype(jnp.bfloat16)


def branch_out(place_row, blocks, att, down_wide, up_wide, tokens, gain):
    places, query_width, rows = att.shape
    model = tokens.shape[1]
    spare = down_wide.shape[1]
    counts = [len(found) for found in blocks]
    wide = jnp.float32
    return call(
        functools.partial(branch_kernel, counts),
        (places,),
        [ANYWHERE] * sum(counts)
        + [
            spec_placed(spec_block(query_width, rows)),
            spec_placed(spec_down(query_width, spare)),
            spec_whole(model, spare),
            spec_whole(rows, model),
            spec_whole(1, model),
        ],
        [
            spec_whole(rows, model),
            spec_whole(rows, model),
            spec_whole(rows, 128),
            spec_whole(rows, spare),
        ],
        [
            array(rows, model, dtype=wide),
            array(rows, model),
            array(rows, 128, dtype=wide),
            array(rows, spare),
        ],
        fetch_scratch(blocks)
        + [pltpu.VMEM((rows, model), wide), pltpu.VMEM((rows, spare), wide)],
        0,
        13,
        scalars=1,
    )(place_row, *flat(blocks), att, down_wide, up_wide, tokens, gain)


def branch_back_kernel(counts, place_ref, *refs):
    blocks, refs = grouped(refs, counts)
    (
        own_ref, from_x, late_x, late_y, from_y, residual_ref, inverse_ref, gain_ref, cot_ref,
        down_ref, up_ref,
        grad_att_ref, grad_ref, branch_ref, slim_ref, buffer, sems,
    ) = refs
    step = pl.program_id(0)
    slot = fetch(blocks, buffer, sems, step)

    @pl.when(step == 0)
    def _():
        wide = jnp.float32
        middle = late_x.shape[0]
        for start, part in enumerate(sums_of(own_ref, from_x, late_x, late_y, from_y)):
            span = slice(start * middle, (start + 1) * middle)
            residual, inverse = residual_ref[span], inverse_ref[span, :1]
            scaled = part * gain_ref[...]
            mean = jnp.mean(scaled * residual, axis=-1, keepdims=True)
            grad = (
                cot_ref[span].astype(wide)
                + inverse * scaled
                - residual * (inverse * inverse * inverse * mean)
            )
            grad_ref[span] = grad
            branch_ref[span] = grad.astype(jnp.bfloat16)
        slim_ref[...] = mm(branch_ref[...], up_ref[...])

    slim = slim_ref[...].astype(jnp.bfloat16)
    grad_att_ref[...] = (
        mm_nt(buffer[slot], branch_ref[...]) + mm_nt(down_ref[...], slim)
    ).astype(jnp.bfloat16)


def branch_back(
    place_row, blocks, sums, residual, inverse, gain, cotangent, down_wide, up_wide
):
    places = len(blocks)
    rows, model = residual.shape
    query_width = model // places
    spare = down_wide.shape[1]
    counts = [len(found) for found in blocks]
    wide = jnp.float32
    return call(
        functools.partial(branch_back_kernel, counts),
        (places,),
        [ANYWHERE] * sum(counts)
        + [spec_whole(*part.shape) for part in sums]
        + [
            spec_whole(rows, model),
            spec_whole(rows, 128),
            spec_whole(1, model),
            spec_whole(rows, model),
            spec_placed(spec_down(query_width, spare)),
            spec_whole(model, spare),
        ],
        [
            spec_placed(spec_block(query_width, rows)),
            spec_whole(rows, model),
            spec_whole(rows, model),
            spec_whole(rows, spare),
        ],
        [
            array(places, query_width, rows),
            array(rows, model, dtype=wide),
            array(rows, model),
            array(rows, spare, dtype=wide),
        ],
        fetch_scratch(blocks),
        0,
        15,
        scalars=1,
    )(
        place_row, *flat(blocks), *sums, residual, inverse, gain, cotangent, down_wide, up_wide
    )


def exchanged(value, bits):
    count = lax.axis_size("seq")
    return lax.ppermute(value, "seq", [(place, place ^ bits) for place in range(count)])


def after(value, *others):
    return pl.pallas_call(
        lambda *refs: None,
        out_shape=jax.ShapeDtypeStruct(value.shape, value.dtype),
        in_specs=[pl.BlockSpec(memory_space=pl.ANY)] * (1 + len(others)),
        out_specs=pl.BlockSpec(memory_space=pl.ANY),
        input_output_aliases={0: 0},
    )(value, *others)


def halves(value):
    middle = value.shape[0] // 2
    return value[:middle], value[middle:]


def regroup_kernel(*refs):
    out_ref = refs[-1]
    for number, ref in enumerate(refs[:-1]):
        out_ref[number] = ref[...]


def regroup(places, *matrices):
    rows, wide = matrices[0].shape
    unit = wide // places
    return call(
        regroup_kernel,
        (places,),
        [spec_across(rows, unit)] * len(matrices),
        pl.BlockSpec((None, len(matrices), rows, unit), lambda i: (i, 0, 0, 0)),
        array(places, len(matrices), rows, unit),
        [],
        0,
        6,
    )(*matrices)


def ungroup_kernel(ref, *refs):
    for number, out_ref in enumerate(refs):
        out_ref[...] = ref[number]


def ungroup(blocks):
    places, count, rows, unit = blocks.shape
    return call(
        ungroup_kernel,
        (places,),
        [pl.BlockSpec((None, count, rows, unit), lambda i: (i, 0, 0, 0))],
        [spec_down(rows, unit)] * count,
        [array(places * rows, unit)] * count,
        [],
        0,
        6,
    )(blocks)


def gather_first(value):
    return exchanged(value, 1), exchanged(value, 2), exchanged(value, 4)


def gather_rest(value, beside, along_x, along_y, *others):
    upper, lower = halves(along_x)[0], halves(along_y)[1]
    if others:
        upper, lower = after(upper, *others), after(lower, *others)
    first, second = exchanged(upper, 4), exchanged(lower, 2)
    return [
        (value,),
        (beside,),
        (along_x,),
        (exchanged(along_x, 1),),
        (along_y,),
        (exchanged(along_y, 1),),
        (first, second),
        (exchanged(first, 1), exchanged(second, 1)),
    ]


def plane_gather(value):
    return gather_rest(value, *gather_first(value))


def core_sums_kernel(keep_ref, got_ref, own_ref, to_x, to_y, later_x, later_y):
    wide, short = jnp.float32, jnp.bfloat16
    middle = later_x.shape[0]

    def both(bits, span=slice(None)):
        return keep_ref[bits, span].astype(wide) + got_ref[bits, span].astype(wide)

    upper, lower = slice(0, middle), slice(middle, None)
    own_ref[...] = both(0)
    to_x[upper], to_x[lower] = both(3, upper).astype(short), both(1, upper).astype(short)
    to_y[upper], to_y[lower] = both(3, lower).astype(short), both(2, lower).astype(short)
    later_x[...] = both(1, lower).astype(short)
    later_y[...] = both(2, upper).astype(short)


def core_sums(keep, got):
    _, rows, model = keep.shape
    wide = model // 4
    block = pl.BlockSpec((4, rows, wide), lambda i: (0, 0, i))
    return call(
        core_sums_kernel,
        (4,),
        [block] * 2,
        [spec_across(rows, wide)] * 3 + [spec_across(rows // 2, wide)] * 2,
        [array(rows, model, dtype=jnp.float32)]
        + [array(rows, model)] * 2
        + [array(rows // 2, model)] * 2,
        [],
        0,
        5,
    )(keep, got)


def scatter_first(give, keep):
    own, to_x, to_y, later_x, later_y = core_sums(keep, exchanged(give, 1))
    return own, exchanged(to_x, 2), exchanged(to_y, 4), later_x, later_y


def scatter_rest(own, from_x, from_y, later_x, later_y, *others):
    middle = later_x.shape[0]
    wide, short = jnp.float32, jnp.bfloat16
    if others:
        later_x, later_y = after(later_x, *others), after(later_y, *others)
    late_y = exchanged((later_y.astype(wide) + from_x[:middle].astype(wide)).astype(short), 4)
    late_x = exchanged((later_x.astype(wide) + from_y[:middle].astype(wide)).astype(short), 2)
    return own, from_x, late_x, late_y, from_y


def sums_of(own_ref, from_x, late_x, late_y, from_y):
    wide = jnp.float32
    middle = late_x.shape[0]
    return (
        own_ref[:middle] + from_x[middle:].astype(wide) + late_y[...].astype(wide),
        own_ref[middle:] + late_x[...].astype(wide) + from_y[middle:].astype(wide),
    )


def tokens_back_kernel(
    own_ref, from_x, late_x, late_y, from_y, tokens_ref, inverse_ref, gain_ref, grad_ref, out_ref
):
    middle = late_x.shape[0]
    for start, part in enumerate(sums_of(own_ref, from_x, late_x, late_y, from_y)):
        span = slice(start * middle, (start + 1) * middle)
        values, inverse = tokens_ref[span].astype(jnp.float32), inverse_ref[span, :1]
        scaled = part * gain_ref[...]
        mean = jnp.mean(scaled * values, axis=-1, keepdims=True)
        out_ref[span] = (
            grad_ref[span] + inverse * scaled - values * (inverse * inverse * inverse * mean)
        ).astype(jnp.bfloat16)


def tokens_back(sums, tokens, inverse, gain, grad):
    rows, model = tokens.shape
    return call(
        tokens_back_kernel,
        (1,),
        [spec_whole(*part.shape) for part in (*sums, tokens, inverse, gain, grad)],
        spec_whole(rows, model),
        array(rows, model),
        [],
        0,
        6,
    )(*sums, tokens, inverse, gain, grad)


def ring(value):
    count = lax.axis_size("fsdp")
    found = [value]
    for _ in range(count - 1):
        found.append(ring_step(found[-1]))
    return found


def ring_step(value):
    count = lax.axis_size("fsdp")
    return lax.ppermute(value, "fsdp", [(at, (at + 1) % count) for at in range(count)])


def by_heads(
    tokens,
    lengths,
    norm_attn,
    norm_ffn,
    w_query,
    key_projection,
    value_projection,
    w_output,
    w_gate,
    w_up,
    w_down,
    down_query,
    up_query,
    key_down_matrix,
    key_up_matrix,
    value_down_matrix,
    value_up_matrix,
    down_output,
    up_output,
    feature_query,
    key_feature_weight,
    cotangent,
):
    places = lax.axis_size("seq")
    lanes = lax.axis_size("fsdp")
    rows = tokens.shape[1]
    model = tokens.shape[2]
    count = rows * places
    group = QUERY_HEADS // KEY_VALUE_HEADS
    query_width = group * HEAD_SIZE
    width = query_width + 2 * HEAD_SIZE
    rank = down_query.shape[1]
    spare = 128
    place = lax.axis_index("seq")
    lane = lax.axis_index("fsdp")
    place_row = place.astype(jnp.int32).reshape(1)
    length = lax.dynamic_slice_in_dim(lengths, lane, 1)
    bf16, f32 = jnp.bfloat16, jnp.float32
    inputs_wide = tokens[0].astype(f32)
    gain_attn = norm_attn.astype(f32)
    gain_ffn = norm_ffn.astype(f32).reshape(1, model)

    shard = w_query.shape[0]
    by_place = jnp.concatenate(
        [
            w_query.reshape(shard, places, query_width),
            key_projection.reshape(shard, places, HEAD_SIZE),
            value_projection.reshape(shard, places, HEAD_SIZE),
        ],
        axis=2,
    )
    by_place = lax.all_to_all(jnp.moveaxis(by_place, 1, 0), "seq", 0, 0, tiled=True)
    own_weights = lax.all_gather(by_place, "fsdp", axis=0)

    inverse_attn = lax.rsqrt(jnp.mean(inputs_wide * inputs_wide, axis=-1, keepdims=True) + epsilon)
    normed_all = plane_gather((inputs_wide * inverse_attn * gain_attn).astype(bf16))
    across = normed_all[6]
    down_block = jnp.concatenate(
        [
            down_query.T,
            key_down_matrix.T,
            value_down_matrix.T,
            jnp.zeros((spare - 3 * rank, model), bf16),
        ],
        axis=0,
    )

    output_rows = lax.all_gather(w_output, "fsdp", axis=0)
    swapped = after(regroup(places, w_gate, w_up, w_down), by_place)
    swapped = lax.all_to_all(swapped, "seq", 0, 0, tiled=True)

    def own_rows(matrix, size):
        return lax.dynamic_slice_in_dim(matrix, place * size, size, 0)

    up_own = (
        own_rows(up_query, query_width),
        own_rows(key_up_matrix, HEAD_SIZE),
        own_rows(value_up_matrix, HEAD_SIZE),
    )
    up_block = jnp.concatenate(
        [
            jnp.pad(part, ((0, 0), (at * rank, spare - (at + 1) * rank)))
            for at, part in enumerate(up_own)
        ],
        axis=0,
    )
    maps_back = jnp.concatenate(
        [own_rows(feature_query, query_width), own_rows(key_feature_weight, HEAD_SIZE)], axis=0
    )
    maps_ahead = jnp.swapaxes(
        maps_back.reshape(group + 1, HEAD_SIZE, HEAD_SIZE), 1, 2
    ).reshape((group + 1) * HEAD_SIZE, HEAD_SIZE)
    frequency = rope_base ** (-(jnp.arange(HEAD_SIZE // 2, dtype=f32) * 2.0) / HEAD_SIZE)
    phase = jnp.arange(count, dtype=jnp.int32).astype(f32)[None, :] * frequency[:, None]
    cosine, sine = jnp.cos(phase), jnp.sin(phase)
    down_wide = jnp.pad(down_output, ((0, 0), (0, spare - rank)))
    up_wide = jnp.pad(up_output, ((0, 0), (0, spare - rank)))

    q_t, k_t, v_t, keys, values, pq_t, pk_t, key_maps, narrow_t, own_weights_t = project(
        place_row, normed_all, own_weights, down_block, up_block, maps_ahead, cosine, sine
    )
    output_rows = after(output_rows.reshape(lanes * shard, model), q_t)
    output_first = gather_first(output_rows)
    att, out_t, denom, states, att_weights = attend(
        length, q_t, pq_t, keys, key_maps, v_t, rows
    )
    own_gate, own_up, own_down = ungroup(swapped)
    up_weights = lax.all_gather(own_up, "fsdp", axis=0)
    unit = own_down.shape[1] // PARTS
    down_weights = [
        lax.all_gather(own_down[:, part * unit : (part + 1) * unit], "fsdp", axis=0)
        for part in range(PARTS)
    ]
    gate_weights = ring(own_gate)
    chunk_order = lax.rem(lane - jnp.arange(lanes) + lanes, lanes).astype(jnp.int32)
    output_blocks = gather_rest(output_rows, *output_first, att)
    att_all = lax.all_to_all(att, "seq", 0, 0, tiled=True)
    middle = places // 2 + 1
    taught = teach(
        after(length, *output_first, gate_weights[1]), q_t, keys, v_t, att, 0, middle
    )
    residual, normed_ffn, inverse_ffn, narrow_out = branch_out(
        after(place_row, taught[1]), output_blocks, att_all, down_wide, up_wide, tokens[0], gain_ffn
    )
    ffn_first = gather_first(normed_ffn)
    difference, loss_rows = teach(
        after(length, normed_ffn), q_t, keys, v_t, att, middle, places, taught
    )
    ffn_all = gather_rest(normed_ffn, *ffn_first, loss_rows)
    cot_all = plane_gather(after(cotangent[0], *ffn_all[6], gate_weights[2]))
    losses = jnp.sum(loss_rows[0].reshape(places, rows), axis=1)
    hidden, by_gate, by_up = hidden_units(chunk_order, ffn_all, gate_weights, up_weights)
    early = None
    for part in range(PARTS - 1):
        early = ffn_back(
            chunk_order, cot_all, 0, 1, part, gate_weights, up_weights, down_weights[part], by_gate, by_up, early
        )
    by_chip = (places // 2, rows, model)
    last = (PARTS - 1, gate_weights, up_weights, down_weights[-1], by_gate, by_up, early)
    grad_give = ffn_back(chunk_order, cot_all[1::2], 1, 2, *last)
    grad_keep = ffn_back(chunk_order, cot_all[0::2], 0, 2, *last)
    grad_first = scatter_first(grad_give.reshape(by_chip), grad_keep.reshape(by_chip))
    out_part = ffn_out(after(place_row, grad_first[0]), chunk_order, hidden, down_weights, places)

    grad_sums = scatter_rest(*grad_first, out_part)
    grad_att, grad_residual, grad_branch, grad_narrow_out = branch_back(
        place_row,
        output_blocks, grad_sums, residual, inverse_ffn, gain_ffn, cotangent[0],
        down_wide, up_wide,
    )
    out_sum = lax.psum_scatter(out_part, "seq", scatter_dimension=0, tiled=True)
    output = (residual + out_sum.astype(f32)).astype(bf16)
    grad_att = lax.all_to_all(grad_att, "seq", 0, 0, tiled=True)
    grad_up_output = mm_tn(narrow_out, grad_branch)[:rank]
    grad_down_output = jnp.einsum(
        "sft,tr->rsf", att_all, grad_narrow_out[:, :rank].astype(bf16), preferred_element_type=f32
    ).reshape(rank, model)

    grad_pre_t, grad_maps, grad_down_t, normed_give, normed_keep = heads_back(
        length, place_row, normed_all, grad_att, difference, out_t, denom,
        q_t, pq_t, att_weights, values, k_t, pk_t, v_t, states, maps_ahead, maps_back,
        cosine, sine, up_block, own_weights_t,
    )
    normed_sums = scatter_rest(*scatter_first(normed_give, normed_keep))
    grad_up_block = mm_nt(grad_pre_t[:width], narrow_t)
    grad_down_t = grad_down_t[: 3 * rank]
    grad_tokens = tokens_back(
        normed_sums, tokens[0], jnp.broadcast_to(inverse_attn, (rows, spare)),
        gain_attn.reshape(1, model), grad_residual,
    )

    devices = places * lanes
    ahead = jnp.arange(devices)[None, :] >= (jnp.arange(places) * lanes + lane)[:, None]
    running = jnp.sum(jnp.where(ahead, losses[:, None], 0.0), axis=0)
    loss_row = jnp.pad(running[:, None], ((0, 0), (0, model // devices - 1))).reshape(1, model)
    shared = jnp.concatenate([grad_down_t, grad_down_output, grad_up_output, loss_row], axis=0)
    shared = after(jnp.moveaxis(shared.reshape(-1, devices, model // devices), 1, 0), normed_sums[0])
    shared = jnp.sum(
        lax.all_to_all(shared, ("seq", "fsdp"), 0, 0, tiled=True).reshape(shared.shape), axis=0
    )

    def columns(at):
        return shared[at * rank : (at + 1) * rank].T

    transfer_loss = shared[5 * rank, :1] / jnp.sum(lengths).astype(f32)

    pieces = [
        grad_maps[:query_width].reshape(lanes, -1),
        grad_maps[query_width:].reshape(lanes, -1),
        grad_up_block[:query_width, :rank].reshape(lanes, -1),
        grad_up_block[query_width : query_width + HEAD_SIZE, rank : 2 * rank].reshape(lanes, -1),
        grad_up_block[query_width + HEAD_SIZE :, 2 * rank : 3 * rank].reshape(lanes, -1),
    ]
    packed = after(jnp.concatenate(pieces, axis=1), normed_sums[0])
    packed = jnp.sum(lax.all_to_all(packed, "fsdp", 0, 0, tiled=True).reshape(packed.shape), axis=0)
    ends = [0]
    for piece in pieces:
        ends.append(ends[-1] + piece.shape[1])
    map_query, map_key, up_q, up_k, up_v = (
        packed[ends[at] : ends[at + 1]].reshape(-1, wide)
        for at, wide in enumerate((HEAD_SIZE, HEAD_SIZE, rank, rank, rank))
    )
    return (
        output[None],
        grad_tokens[None],
        columns(0),
        up_q,
        columns(1),
        up_k,
        columns(2),
        up_v,
        columns(3),
        columns(4),
        map_query,
        map_key,
        transfer_loss,
    )


def solution(mesh):
    placed = (
        P("fsdp", "seq", None),
        P(),
        P(),
        P(),
        P(("seq", "fsdp"), None),
        P(("seq", "fsdp"), None),
        P(("seq", "fsdp"), None),
        P(("seq", "fsdp"), None),
        P("seq", "fsdp"),
        P("seq", "fsdp"),
        P("seq", "fsdp"),
        P(),
        P(),
        P(),
        P(),
        P(),
        P(),
        P(),
        P(),
        P(),
        P(),
        P("fsdp", "seq", None),
    )
    sizes = dict(mesh.shape)
    heads_match = sizes["seq"] == KEY_VALUE_HEADS == 8 and (
        QUERY_HEADS // KEY_VALUE_HEADS == sizes["fsdp"]
    )
    return jax.shard_map(
        by_heads if heads_match else local,
        mesh=mesh,
        in_specs=placed,
        out_specs=(
            P("fsdp", "seq", None),
            P("fsdp", "seq", None),
            P(("seq", "fsdp"), None),
            P(("seq", "fsdp"), None),
            P(("seq", "fsdp"), None),
            P(("seq", "fsdp"), None),
            P(("seq", "fsdp"), None),
            P(("seq", "fsdp"), None),
            P(("seq", "fsdp"), None),
            P(("seq", "fsdp"), None),
            P(("seq", "fsdp"), None),
            P(("seq", "fsdp"), None),
            P(("seq", "fsdp")),
        ),
        check_vma=False,
    )
```

```python
import functools
import math

import jax
import jax.numpy as jnp
from jax import lax
from jax.experimental import pallas as pl
from jax.experimental.pallas import tpu as pltpu
from jax.sharding import PartitionSpec as P

QUERY_HEADS = 32
KEY_VALUE_HEADS = 8
HEAD_SIZE = 64
WINDOW_KEYS = 64


epsilon = 1e-05
rope_base = 500000.0
precise = lax.Precision.HIGHEST
lowest_precision = -1e30
ONES = 16
SUB = 128
VMEM_MIB = 56
PARTS = 2
COST = 1.15e9


def prefix(x, axis, join, neutral, backward):
    count = lax.axis_size(axis)
    place = lax.axis_index(axis)
    ahead = count - 1 - place if backward else place
    gathered = jax.tree.map(
        lambda a, kind: lax.all_gather(a.astype(kind), axis), x, (jnp.bfloat16, jnp.bfloat16)
    )
    state = jax.tree.map(lambda a, e: jnp.zeros_like(a) + jnp.asarray(e, a.dtype), x, neutral)

    def one(hop, state):
        source = count - 1 - hop if backward else hop
        return join(
            state,
            jax.tree.map(
                lambda a, own: lax.dynamic_index_in_dim(a, source, 0, False).astype(own.dtype),
                gathered,
                x,
            ),
        )

    return lax.fori_loop(0, ahead, one, state)


def as_sent(x):

    def short(part):
        return part.astype(jnp.bfloat16) if part.dtype == jnp.float32 else part

    return jax.tree.map(short, x)


def shifted(value, axis, steps):
    count = lax.axis_size(axis)
    first, last = (max(0, -steps), min(count, count - steps))
    return lax.ppermute(value, axis, [(source, source + steps) for source in range(first, last)])


def rotary(positions):
    half_dim = HEAD_SIZE // 2
    inverse = rope_base ** (-(jnp.arange(half_dim, dtype=jnp.float32) * 2.0) / HEAD_SIZE)
    phase = positions.astype(jnp.float32)[:, None] * inverse[None, :]
    return (jnp.cos(phase)[:, None, :], jnp.sin(phase)[:, None, :])


def apply_rotary(vectors, cosine_lookup, sine_lookup):
    half_dim = vectors.shape[-1] // 2
    first_half = vectors[..., :half_dim]
    second_half = vectors[..., half_dim:]
    return jnp.concatenate(
        [
            first_half * cosine_lookup - second_half * sine_lookup,
            second_half * cosine_lookup + first_half * sine_lookup,
        ],
        axis=-1,
    )


def inverse_rotary(gradient, cosine_lookup, sine_lookup):
    half_dim = gradient.shape[-1] // 2
    first_half = gradient[..., :half_dim]
    second_half = gradient[..., half_dim:]
    return jnp.concatenate(
        [
            first_half * cosine_lookup + second_half * sine_lookup,
            second_half * cosine_lookup - first_half * sine_lookup,
        ],
        axis=-1,
    )


def apply_feature_map(vectors, weights):
    logits_map = jnp.einsum("thd,hde->the", vectors, weights, preferred_element_type=jnp.float32)
    return jnp.concatenate(
        [jax.nn.softmax(logits_map, axis=-1), jax.nn.softmax(-logits_map, axis=-1)], axis=-1
    )


def feature_back(vectors, weights, gradient):
    logits_map = jnp.einsum("thd,hde->the", vectors, weights, preferred_element_type=jnp.float32)
    plus_soft = jax.nn.softmax(logits_map, axis=-1)
    minus_soft = jax.nn.softmax(-logits_map, axis=-1)
    grad_plus = gradient[..., :HEAD_SIZE]
    grad_minus = gradient[..., HEAD_SIZE:]
    grad_logits = plus_soft * (
        grad_plus - jnp.sum(grad_plus * plus_soft, axis=-1, keepdims=True)
    ) - minus_soft * (grad_minus - jnp.sum(grad_minus * minus_soft, axis=-1, keepdims=True))
    grad_vectors = jnp.einsum(
        "the,hde->thd", grad_logits, weights, preferred_element_type=jnp.float32
    )
    grad_weights = jnp.einsum(
        "thd,the->hde", vectors, grad_logits, preferred_element_type=jnp.float32
    )
    return (grad_vectors, grad_weights)


def norm_back(values, inverse, gain, gradient):
    scaled = gradient * gain
    return inverse * scaled - values * inverse * inverse * inverse * jnp.mean(
        scaled * values, axis=-1, keepdims=True
    )


def coefficients(query_rows, query_feature_maps, keys_ext, key_maps, key_valid):
    row_count = query_rows.shape[0]
    key_count = keys_ext.shape[0]
    offset = (
        jnp.arange(row_count)[:, None] + (key_count - row_count) - jnp.arange(key_count)[None, :]
    )
    window = ((offset >= 0) & (offset < WINDOW_KEYS) & key_valid[None, :])[None]
    linear = ((offset >= WINDOW_KEYS) & key_valid[None, :])[None]
    scores = jnp.einsum(
        "tjd,sd->jts", query_rows, keys_ext, preferred_element_type=jnp.float32
    ) / math.sqrt(HEAD_SIZE)
    exp_scores = jnp.exp(scores)
    near_terms = lax.optimization_barrier(exp_scores.astype(jnp.bfloat16)).astype(jnp.float32)
    far_terms = jnp.einsum(
        "tjf,sf->jts", query_feature_maps, key_maps, preferred_element_type=jnp.float32
    )
    weights = jnp.where(window, near_terms, 0.0) + jnp.where(linear, far_terms, 0.0)
    return (weights, exp_scores, window, linear)


def attend_group(operands, key_valid):
    query_rows, query_feature_maps, keys_ext, values_ext, key_maps, carry_state, carry_total = (
        operands
    )
    weights, exp_scores, window, linear = coefficients(
        query_rows, query_feature_maps, keys_ext, key_maps, key_valid
    )
    maps_wide = query_feature_maps.astype(jnp.float32)
    numerator = jnp.einsum(
        "jts,sd->tjd", weights, values_ext.astype(jnp.float32), precision=precise
    ) + jnp.einsum("tjf,fd->tjd", maps_wide, carry_state, precision=precise)
    denominator = jnp.transpose(jnp.sum(weights, axis=-1)) + jnp.einsum(
        "tjf,f->tj", maps_wide, carry_total, precision=precise
    )
    return (numerator, denominator)


def attend_back(operands, key_valid):
    (
        query_rows,
        query_feature_maps,
        keys_ext,
        values_ext,
        key_maps,
        carry_state,
        carry_total,
        numerator,
        denominator,
        grad_out,
    ) = operands
    weights, exp_scores, window, linear = coefficients(
        query_rows, query_feature_maps, keys_ext, key_maps, key_valid
    )
    grad_numer = grad_out / denominator[..., None]
    grad_denom = -jnp.sum(grad_out * numerator, axis=-1) / (denominator * denominator)
    grad_weights = (
        jnp.einsum("tjd,sd->jts", grad_numer, values_ext, preferred_element_type=jnp.float32)
        + jnp.transpose(grad_denom)[:, :, None]
    )
    grad_scores = jnp.where(window, grad_weights * exp_scores, 0.0) / math.sqrt(HEAD_SIZE)
    grad_far = jnp.where(linear, grad_weights, 0.0)
    grad_queries = jnp.einsum(
        "jts,sd->tjd", grad_scores, keys_ext, preferred_element_type=jnp.float32
    )
    grad_keys = jnp.einsum(
        "jts,tjd->sd", grad_scores, query_rows, preferred_element_type=jnp.float32
    )
    grad_qmaps = (
        jnp.einsum("jts,sf->tjf", grad_far, key_maps, preferred_element_type=jnp.float32)
        + jnp.einsum("tjd,fd->tjf", grad_numer, carry_state, preferred_element_type=jnp.float32)
        + grad_denom[..., None] * carry_total
    )
    grad_kmaps = jnp.einsum(
        "jts,tjf->sf", grad_far, query_feature_maps, preferred_element_type=jnp.float32
    )
    grad_values = jnp.einsum("jts,tjd->sd", weights, grad_numer, preferred_element_type=jnp.float32)
    grad_state = jnp.einsum(
        "tjf,tjd->fd", query_feature_maps, grad_numer, preferred_element_type=jnp.float32
    )
    grad_total = jnp.einsum(
        "tjf,tj->f", query_feature_maps, grad_denom, preferred_element_type=jnp.float32
    )
    return (grad_queries, grad_keys, grad_values, grad_qmaps, grad_kmaps, grad_state, grad_total)


def add_pair(earlier, later_part):
    return (earlier[0] + later_part[0], earlier[1] + later_part[1])


def local(
    tokens,
    lengths,
    norm_attn,
    norm_ffn,
    w_query,
    key_projection,
    value_projection,
    w_output,
    w_gate,
    w_up,
    w_down,
    down_query,
    up_query,
    key_down_matrix,
    key_up_matrix,
    value_down_matrix,
    value_up_matrix,
    down_output,
    up_output,
    feature_query,
    key_feature_weight,
    cotangent,
):
    rows_per_block = tokens.shape[1]
    ext_rows = rows_per_block + WINDOW_KEYS
    heads_per_group = QUERY_HEADS // KEY_VALUE_HEADS
    feature_width = 2 * HEAD_SIZE
    inputs_wide = tokens[0].astype(jnp.float32)
    cot_narrow = cotangent[0]
    cot_wide = cot_narrow.astype(jnp.float32)
    seq_index = lax.axis_index("seq")
    lane_length = lengths[lax.axis_index("fsdp")]
    positions = seq_index * rows_per_block + jnp.arange(rows_per_block)
    cosine_lookup, sine_lookup = rotary(positions)
    gain_attn = norm_attn.astype(jnp.float32)
    gain_ffn = norm_ffn.astype(jnp.float32)
    inverse_attn = lax.rsqrt(jnp.mean(inputs_wide * inputs_wide, axis=-1, keepdims=True) + epsilon)
    normed = (inputs_wide * inverse_attn * gain_attn).astype(jnp.bfloat16)
    pieces = (
        lax.all_gather(w_query, ("seq", "fsdp"), axis=0, tiled=True),
        lax.all_gather(key_projection, ("seq", "fsdp"), axis=0, tiled=True),
        lax.all_gather(value_projection, ("seq", "fsdp"), axis=0, tiled=True),
    )
    sliced = normed
    query_pre, key_before_rotation, value_before_adapter = tuple(
        (jnp.dot(sliced, block_piece, preferred_element_type=jnp.float32) for block_piece in pieces)
    )
    narrow_query = jnp.dot(normed, down_query, preferred_element_type=jnp.float32).astype(
        jnp.bfloat16
    )
    narrow_key = jnp.dot(normed, key_down_matrix, preferred_element_type=jnp.float32).astype(
        jnp.bfloat16
    )
    narrow_value = jnp.dot(normed, value_down_matrix, preferred_element_type=jnp.float32).astype(
        jnp.bfloat16
    )
    query_pre = query_pre + jnp.dot(narrow_query, up_query.T, preferred_element_type=jnp.float32)
    key_before_rotation = key_before_rotation + jnp.dot(
        narrow_key, key_up_matrix.T, preferred_element_type=jnp.float32
    )
    value_before_adapter = value_before_adapter + jnp.dot(
        narrow_value, value_up_matrix.T, preferred_element_type=jnp.float32
    )
    query_rows = apply_rotary(
        query_pre.reshape(rows_per_block, QUERY_HEADS, HEAD_SIZE), cosine_lookup, sine_lookup
    ).astype(jnp.bfloat16)
    device_keys = apply_rotary(
        key_before_rotation.reshape(rows_per_block, KEY_VALUE_HEADS, HEAD_SIZE),
        cosine_lookup,
        sine_lookup,
    ).astype(jnp.bfloat16)
    device_values = value_before_adapter.reshape(rows_per_block, KEY_VALUE_HEADS, HEAD_SIZE).astype(
        jnp.bfloat16
    )
    softmax_query_rows = query_rows.reshape(
        rows_per_block, KEY_VALUE_HEADS, heads_per_group, HEAD_SIZE
    )
    teacher_init = (
        jnp.full((KEY_VALUE_HEADS, heads_per_group, rows_per_block), lowest_precision, jnp.float32),
        jnp.zeros((KEY_VALUE_HEADS, heads_per_group, rows_per_block), jnp.float32),
        jnp.zeros((KEY_VALUE_HEADS, heads_per_group, rows_per_block, HEAD_SIZE), jnp.float32),
        jnp.zeros((WINDOW_KEYS, KEY_VALUE_HEADS, HEAD_SIZE), jnp.bfloat16),
        jnp.zeros((WINDOW_KEYS, KEY_VALUE_HEADS, HEAD_SIZE), jnp.bfloat16),
    )
    portion_keys = lax.all_gather(
        device_keys.reshape(rows_per_block, KEY_VALUE_HEADS * HEAD_SIZE), "seq", axis=0, tiled=True
    )
    portion_values = lax.all_gather(
        device_values.reshape(rows_per_block, KEY_VALUE_HEADS * HEAD_SIZE),
        "seq",
        axis=0,
        tiled=True,
    )
    count_of_shards = portion_keys.shape[0] // rows_per_block
    sharded_keys = portion_keys.reshape(count_of_shards, rows_per_block, KEY_VALUE_HEADS, HEAD_SIZE)
    sharded_values = portion_values.reshape(
        count_of_shards, rows_per_block, KEY_VALUE_HEADS, HEAD_SIZE
    )

    def one_shard(inner, item):
        best, total, accum, rim_keys, rim_values = inner
        shard_number, shard_keys, shard_values = item
        shard_start = shard_number * rows_per_block
        scores = jnp.einsum(
            "tgjd,sgd->gjts", softmax_query_rows, shard_keys, preferred_element_type=jnp.float32
        ) / math.sqrt(HEAD_SIZE)
        allowed = (positions[:, None] >= (shard_start + jnp.arange(rows_per_block))[None, :])[
            None, None
        ]
        masked = jnp.where(allowed, scores, lowest_precision)
        new_best = jnp.maximum(best, jnp.max(masked, axis=-1))
        probs = jnp.where(allowed, jnp.exp(masked - new_best[..., None]), 0.0)
        factor = jnp.exp(best - new_best)
        total = total * factor + jnp.sum(probs, axis=-1)
        accum = accum * factor[..., None] + jnp.einsum(
            "gjts,sgd->gjtd", probs, shard_values.astype(jnp.float32)
        )
        is_before = shard_start // rows_per_block == seq_index - 1
        rim_keys = jnp.where(is_before, shard_keys[rows_per_block - WINDOW_KEYS :], rim_keys)
        rim_values = jnp.where(is_before, shard_values[rows_per_block - WINDOW_KEYS :], rim_values)
        return ((new_best, total, accum, rim_keys, rim_values), None)

    result, unused = lax.scan(
        one_shard, teacher_init, (jnp.arange(count_of_shards), sharded_keys, sharded_values)
    )
    best_all, total_all, accum_all, rim_keys, rim_values = result
    teacher = jnp.transpose(accum_all / total_all[..., None], (2, 0, 1, 3)).reshape(
        rows_per_block, QUERY_HEADS * HEAD_SIZE
    )
    keys_ext = jnp.concatenate([rim_keys, device_keys], axis=0)
    values_ext = jnp.concatenate([rim_values, device_values], axis=0)
    query_features = feature_query.reshape(QUERY_HEADS, HEAD_SIZE, HEAD_SIZE)
    key_features = key_feature_weight.reshape(KEY_VALUE_HEADS, HEAD_SIZE, HEAD_SIZE)
    query_feature_maps = apply_feature_map(query_rows, query_features).astype(jnp.bfloat16)
    key_maps = apply_feature_map(keys_ext, key_features).astype(jnp.bfloat16)
    ext_positions = seq_index * rows_per_block - WINDOW_KEYS + jnp.arange(ext_rows)
    key_valid = ext_positions >= 0
    valid_rows = key_valid[:rows_per_block].astype(jnp.float32)
    used_maps = key_maps[:rows_per_block].astype(jnp.float32) * valid_rows[:, None, None]
    values_head = values_ext[:rows_per_block].astype(jnp.float32)
    local_state = jnp.einsum("sgf,sgd->gfd", used_maps, values_head, precision=precise)
    local_total = jnp.sum(used_maps, axis=0)
    zero_pair = (
        jnp.zeros((KEY_VALUE_HEADS, feature_width, HEAD_SIZE), jnp.float32),
        jnp.zeros((KEY_VALUE_HEADS, feature_width), jnp.float32),
    )
    state_in, total_in = prefix((local_state, local_total), "seq", add_pair, zero_pair, False)
    queries_by_group = jnp.moveaxis(
        query_rows.reshape(rows_per_block, KEY_VALUE_HEADS, heads_per_group, HEAD_SIZE), 1, 0
    )
    query_maps_by_group = jnp.moveaxis(
        query_feature_maps.reshape(rows_per_block, KEY_VALUE_HEADS, heads_per_group, feature_width),
        1,
        0,
    )
    grouped_keys = jnp.moveaxis(keys_ext, 1, 0)
    grouped_values = jnp.moveaxis(values_ext, 1, 0)
    grouped_kmaps = jnp.moveaxis(key_maps, 1, 0)

    def forward_group(operands):
        return attend_group(operands, key_valid)

    numerator, denominator = lax.map(
        forward_group,
        (
            queries_by_group,
            query_maps_by_group,
            grouped_keys,
            grouped_values,
            grouped_kmaps,
            state_in,
            total_in,
        ),
    )
    row_mask = (positions < lane_length).astype(jnp.float32)
    attn_mixed = jnp.moveaxis(numerator / denominator[..., None], 0, 1).reshape(
        rows_per_block, QUERY_HEADS * HEAD_SIZE
    )
    attended = (attn_mixed * row_mask[:, None]).astype(jnp.bfloat16)
    difference = attended.astype(jnp.float32) - teacher * row_mask[:, None]
    local_loss = jnp.sum(difference * difference)
    sliced = attended
    branch = jnp.dot(
        sliced,
        lax.all_gather(w_output, ("seq", "fsdp"), axis=0, tiled=True),
        preferred_element_type=jnp.float32,
    )
    narrow_out = jnp.dot(attended, down_output, preferred_element_type=jnp.float32).astype(
        jnp.bfloat16
    )
    branch = branch + jnp.dot(narrow_out, up_output.T, preferred_element_type=jnp.float32)
    residual = inputs_wide + branch
    inverse_ffn = lax.rsqrt(jnp.mean(residual * residual, axis=-1, keepdims=True) + epsilon)
    normed_ffn = (residual * inverse_ffn * gain_ffn).astype(jnp.bfloat16)
    ffn_weights = (
        lax.all_gather(w_gate, "fsdp", axis=1, tiled=True),
        lax.all_gather(w_up, "fsdp", axis=1, tiled=True),
        lax.all_gather(w_down, "fsdp", axis=1, tiled=True),
    )
    pieces = (
        lax.all_gather(ffn_weights[0], "seq", axis=0, tiled=True),
        lax.all_gather(ffn_weights[1], "seq", axis=0, tiled=True),
    )
    sliced = normed_ffn
    gate_pre = jnp.dot(sliced, pieces[0], preferred_element_type=jnp.float32)
    up_pre = jnp.dot(sliced, pieces[1], preferred_element_type=jnp.float32)
    sigmoid_gate = jax.nn.sigmoid(gate_pre)
    silu_gate = gate_pre * sigmoid_gate
    hidden = (silu_gate * up_pre).astype(jnp.bfloat16)
    ffn_part = jnp.dot(
        hidden,
        lax.all_gather(ffn_weights[2], "seq", axis=0, tiled=True).T,
        preferred_element_type=jnp.float32,
    )
    output = (residual + ffn_part).astype(jnp.bfloat16)
    sliced = cot_narrow
    grad_hidden = jnp.dot(
        sliced,
        lax.all_gather(ffn_weights[2], "seq", axis=0, tiled=True),
        preferred_element_type=jnp.float32,
    )
    grad_gate = (
        grad_hidden * up_pre * sigmoid_gate * (1.0 + gate_pre * (1.0 - sigmoid_gate))
    ).astype(jnp.bfloat16)
    grad_up = (grad_hidden * silu_gate).astype(jnp.bfloat16)
    pieces = lax.all_gather((ffn_weights[0], ffn_weights[1]), "seq", axis=0, tiled=True)
    grad_part = jnp.dot(grad_gate, pieces[0].T, preferred_element_type=jnp.float32) + jnp.dot(
        grad_up, pieces[1].T, preferred_element_type=jnp.float32
    )
    grad_residual = cot_wide + norm_back(residual, inverse_ffn, gain_ffn, grad_part)
    grad_branch = grad_residual.astype(jnp.bfloat16)
    grad_narrow_out = jnp.dot(grad_branch, up_output, preferred_element_type=jnp.float32)
    grad_up_output = jnp.dot(grad_branch.T, narrow_out, preferred_element_type=jnp.float32)
    grad_down_output = jnp.dot(attended.T, grad_narrow_out, preferred_element_type=jnp.float32)
    attended_gradient = (
        jnp.dot(
            grad_branch,
            lax.all_gather(w_output, ("seq", "fsdp"), axis=0, tiled=True).T,
            preferred_element_type=jnp.float32,
        )
        + jnp.dot(grad_narrow_out, down_output.T, preferred_element_type=jnp.float32)
        + 2.0 * difference
    )
    attended_gradient = (
        lax.optimization_barrier(attended_gradient.astype(jnp.bfloat16)).astype(jnp.float32)
        * row_mask[:, None]
    )
    gradient_by_group = jnp.moveaxis(
        attended_gradient.reshape(rows_per_block, KEY_VALUE_HEADS, heads_per_group, HEAD_SIZE), 1, 0
    )

    def backward_group(operands):
        return attend_back(operands, key_valid)

    grad_q, grad_k, grad_v, grad_qm, grad_km, grad_state, grad_total = lax.map(
        backward_group,
        (
            queries_by_group,
            query_maps_by_group,
            grouped_keys,
            grouped_values,
            grouped_kmaps,
            state_in,
            total_in,
            numerator,
            denominator,
            gradient_by_group,
        ),
    )
    later_state, later_total = prefix((grad_state, grad_total), "seq", add_pair, zero_pair, True)
    values_grouped_head = jnp.moveaxis(values_head, 1, 0)
    used_grouped = jnp.moveaxis(used_maps, 1, 0)
    kmaps_head = grad_km[:, :rows_per_block] + valid_rows[None, :, None] * (
        jnp.einsum("gfd,gsd->gsf", later_state, values_grouped_head, precision=precise)
        + later_total[:, None, :]
    )
    grad_km = jnp.concatenate([kmaps_head, grad_km[:, rows_per_block:]], axis=1)
    values_grad_head = grad_v[:, :rows_per_block] + jnp.einsum(
        "gsf,gfd->gsd", used_grouped, later_state, precision=precise
    )
    grad_v = jnp.concatenate([values_grad_head, grad_v[:, rows_per_block:]], axis=1)
    grad_k_feat, key_feature_gradient = feature_back(
        keys_ext, key_features, jnp.moveaxis(grad_km, 0, 1)
    )
    gathered_key_gradient = jnp.moveaxis(grad_k, 0, 1) + grad_k_feat
    gathered_value_gradient = jnp.moveaxis(grad_v, 0, 1)
    grad_q_feat, grad_feature_query = feature_back(
        query_rows,
        query_features,
        jnp.moveaxis(grad_qm, 0, 1).reshape(rows_per_block, QUERY_HEADS, feature_width),
    )
    grad_queries_rot = (
        jnp.moveaxis(grad_q, 0, 1).reshape(rows_per_block, QUERY_HEADS, HEAD_SIZE) + grad_q_feat
    )
    back_keys, back_values = (
        shifted(
            gathered_key_gradient[:WINDOW_KEYS]
            .reshape(WINDOW_KEYS, KEY_VALUE_HEADS * HEAD_SIZE)
            .astype(jnp.bfloat16),
            "seq",
            -1,
        ).astype(jnp.float32),
        shifted(
            as_sent(
                gathered_value_gradient[:WINDOW_KEYS].reshape(
                    WINDOW_KEYS, KEY_VALUE_HEADS * HEAD_SIZE
                )
            ),
            "seq",
            -1,
        ),
    )
    trailing_keys = gathered_key_gradient[WINDOW_KEYS:].reshape(
        rows_per_block, KEY_VALUE_HEADS * HEAD_SIZE
    )
    trailing_values = gathered_value_gradient[WINDOW_KEYS:].reshape(
        rows_per_block, KEY_VALUE_HEADS * HEAD_SIZE
    )
    trailing_keys = jnp.concatenate(
        [
            trailing_keys[: rows_per_block - WINDOW_KEYS],
            trailing_keys[rows_per_block - WINDOW_KEYS :] + back_keys,
        ],
        axis=0,
    )
    trailing_values = jnp.concatenate(
        [
            trailing_values[: rows_per_block - WINDOW_KEYS],
            trailing_values[rows_per_block - WINDOW_KEYS :] + back_values,
        ],
        axis=0,
    )
    grad_query_pre = (
        inverse_rotary(grad_queries_rot, cosine_lookup, sine_lookup)
        .reshape(rows_per_block, QUERY_HEADS * HEAD_SIZE)
        .astype(jnp.bfloat16)
    )
    grad_key_pre = (
        inverse_rotary(
            trailing_keys.reshape(rows_per_block, KEY_VALUE_HEADS, HEAD_SIZE),
            cosine_lookup,
            sine_lookup,
        )
        .reshape(rows_per_block, KEY_VALUE_HEADS * HEAD_SIZE)
        .astype(jnp.bfloat16)
    )
    grad_value_pre = trailing_values.astype(jnp.bfloat16)
    grad_narrow_query = jnp.dot(grad_query_pre, up_query, preferred_element_type=jnp.float32)
    grad_narrow_key = jnp.dot(grad_key_pre, key_up_matrix, preferred_element_type=jnp.float32)
    grad_narrow_value = jnp.dot(grad_value_pre, value_up_matrix, preferred_element_type=jnp.float32)
    grad_up_query = jnp.dot(grad_query_pre.T, narrow_query, preferred_element_type=jnp.float32)
    grad_up_key = jnp.dot(grad_key_pre.T, narrow_key, preferred_element_type=jnp.float32)
    grad_up_value = jnp.dot(grad_value_pre.T, narrow_value, preferred_element_type=jnp.float32)
    grad_down_query = jnp.dot(normed.T, grad_narrow_query, preferred_element_type=jnp.float32)
    grad_down_key = jnp.dot(normed.T, grad_narrow_key, preferred_element_type=jnp.float32)
    grad_down_value = jnp.dot(normed.T, grad_narrow_value, preferred_element_type=jnp.float32)
    pieces = lax.all_gather(
        (w_query, key_projection, value_projection), ("seq", "fsdp"), axis=0, tiled=True
    )
    grad_normed = (
        jnp.dot(grad_query_pre, pieces[0].T, preferred_element_type=jnp.float32)
        + jnp.dot(grad_key_pre, pieces[1].T, preferred_element_type=jnp.float32)
        + jnp.dot(grad_value_pre, pieces[2].T, preferred_element_type=jnp.float32)
    )
    grad_normed = grad_normed + jnp.dot(
        grad_narrow_query, down_query.T, preferred_element_type=jnp.float32
    )
    grad_normed = grad_normed + jnp.dot(
        grad_narrow_key, key_down_matrix.T, preferred_element_type=jnp.float32
    )
    grad_normed = grad_normed + jnp.dot(
        grad_narrow_value, value_down_matrix.T, preferred_element_type=jnp.float32
    )
    grad_tokens = (
        grad_residual + norm_back(inputs_wide, inverse_attn, gain_attn, grad_normed)
    ).astype(jnp.bfloat16)
    device_count = lax.axis_size(("seq", "fsdp"))
    device_number = lax.axis_index(("seq", "fsdp"))
    loss_terms = jnp.where(jnp.arange(device_count) >= device_number, local_loss, 0.0)
    summed = (
        lax.psum_scatter(grad_down_query, ("seq", "fsdp"), scatter_dimension=0, tiled=True),
        lax.psum_scatter(grad_up_query, ("seq", "fsdp"), scatter_dimension=0, tiled=True),
        lax.psum_scatter(grad_down_key, ("seq", "fsdp"), scatter_dimension=0, tiled=True),
        lax.psum_scatter(grad_up_key, ("seq", "fsdp"), scatter_dimension=0, tiled=True),
        lax.psum_scatter(grad_down_value, ("seq", "fsdp"), scatter_dimension=0, tiled=True),
        lax.psum_scatter(grad_up_value, ("seq", "fsdp"), scatter_dimension=0, tiled=True),
        lax.psum_scatter(grad_down_output, ("seq", "fsdp"), scatter_dimension=0, tiled=True),
        lax.psum_scatter(grad_up_output, ("seq", "fsdp"), scatter_dimension=0, tiled=True),
        lax.psum_scatter(
            grad_feature_query.reshape(QUERY_HEADS * HEAD_SIZE, HEAD_SIZE),
            ("seq", "fsdp"),
            scatter_dimension=0,
            tiled=True,
        ),
        lax.psum_scatter(
            key_feature_gradient.reshape(KEY_VALUE_HEADS * HEAD_SIZE, HEAD_SIZE),
            ("seq", "fsdp"),
            scatter_dimension=0,
            tiled=True,
        ),
        lax.psum_scatter(loss_terms, ("seq", "fsdp"), scatter_dimension=0, tiled=True),
    )
    transfer_loss = summed[10] / jnp.sum(lengths).astype(jnp.float32)
    return (
        output[None],
        grad_tokens[None],
        summed[0],
        summed[1],
        summed[2],
        summed[3],
        summed[4],
        summed[5],
        summed[6],
        summed[7],
        summed[8],
        summed[9],
        transfer_loss,
    )

def halves_rotated(first_half, second_half, cosine, sine):
    return (
        first_half * cosine - second_half * sine,
        second_half * cosine + first_half * sine,
    )


def soft_pair(logits):
    plus = jnp.exp(logits - jnp.max(logits, axis=0, keepdims=True))
    minus = jnp.exp(jnp.min(logits, axis=0, keepdims=True) - logits)
    plus = plus * (1.0 / jnp.sum(plus, axis=0, keepdims=True))
    minus = minus * (1.0 / jnp.sum(minus, axis=0, keepdims=True))
    return plus, minus


def mm(a, b):
    return jnp.dot(a, b, preferred_element_type=jnp.float32)


def mm_nt(a, b):
    return lax.dot_general(a, b, (((1,), (1,)), ((), ())), preferred_element_type=jnp.float32)


def mm_tn(a, b):
    return lax.dot_general(a, b, (((0,), (0,)), ((), ())), preferred_element_type=jnp.float32)


def split_wide(x):
    high = x.astype(jnp.bfloat16)
    low = (x - high.astype(jnp.float32)).astype(jnp.bfloat16)
    return high, low


ANYWHERE = pl.BlockSpec(memory_space=pltpu.HBM)


def call(kernel, grid, in_specs, out_specs, out_shape, scratch, flops, moved, scalars=0):
    spec = pltpu.PrefetchScalarGridSpec(
        num_scalar_prefetch=scalars,
        grid=grid,
        in_specs=in_specs,
        out_specs=out_specs,
        scratch_shapes=scratch,
    )
    return pl.pallas_call(
        kernel,
        grid_spec=spec,
        out_shape=out_shape,
        compiler_params=pltpu.CompilerParams(vmem_limit_bytes=VMEM_MIB * 2**20),
        cost_estimate=pl.CostEstimate(
            flops=int(COST * moved), bytes_accessed=1, transcendentals=0
        ),
    )


def spec_whole(*dims):
    return pl.BlockSpec(dims, lambda i, *_: (0,) * len(dims))


def spec_across(height, columns):
    return pl.BlockSpec((height, columns), lambda i, *_: (0, i))


def spec_down(rows, wide):
    return pl.BlockSpec((rows, wide), lambda i, *_: (i, 0))


def spec_block(*dims):
    return pl.BlockSpec((None,) + dims, lambda i, *_: (i, 0, 0))


def spec_placed(spec):
    return pl.BlockSpec(
        spec.block_shape,
        lambda i, place_ref, *_: spec.index_map(lax.bitwise_xor(i, place_ref[0])),
    )


def array(*dims, dtype=jnp.bfloat16):
    return jax.ShapeDtypeStruct(dims, dtype)


def flat(found):
    return [part for parts in found for part in parts]


def grouped(refs, counts):
    found, start = [], 0
    for count in counts:
        found.append(tuple(refs[start : start + count]))
        start += count
    return found, refs[start:]


def fetch(refs, buffer, sems, at, order=lambda step: step):
    steps = len(refs)

    def start(step):
        slot = lax.rem(step, 2)
        wanted = order(step)
        for number, parts in enumerate(refs):

            @pl.when(wanted == number)
            def _():
                height = buffer.shape[1] // len(parts)
                for part, ref in enumerate(parts):
                    pltpu.make_async_copy(
                        ref, buffer.at[slot, part * height : (part + 1) * height], sems.at[slot]
                    ).start()

    @pl.when(at == 0)
    def _():
        start(at)

    @pl.when(at + 1 < steps)
    def _():
        start(at + 1)

    slot = lax.rem(at, 2)
    pltpu.make_async_copy(buffer.at[slot], buffer.at[slot], sems.at[slot]).wait()
    return slot


def start_columns(refs, span, buffer, sem):
    first, end = span
    wide = end - first
    for chunk, ref in enumerate(refs):
        pltpu.make_async_copy(
            ref.at[:, first:end], buffer.at[:, chunk * wide : (chunk + 1) * wide], sem
        ).start()


def chunks_of(ref, order_ref):
    return [ref.at[order_ref[chunk]] for chunk in range(ref.shape[0])]


def wait_whole(buffer, sem):
    pltpu.make_async_copy(buffer, buffer, sem).wait()


def block_shape(blocks):
    return sum(part.shape[0] for part in blocks[0]), blocks[0][0].shape[1]


def fetch_scratch(blocks):
    rows, wide = block_shape(blocks)
    return [pltpu.VMEM((2, rows, wide), jnp.bfloat16), pltpu.SemaphoreType.DMA((2,))]


def project_kernel(counts, place_ref, *refs):
    blocks, refs = grouped(refs, counts)
    (
        w_ref, down_ref, up_ref, map_ref, cos_ref, sin_ref,
        q_ref, kt_ref, vt_ref, k_ref, v_ref, pq_ref, pkt_ref, pk_ref, narrow_ref, wt_ref,
        buffer, sems,
    ) = refs
    group = q_ref.shape[0] // HEAD_SIZE
    half = HEAD_SIZE // 2
    width = (group + 2) * HEAD_SIZE
    slot = fetch(blocks, buffer, sems, pl.program_id(0))

    @pl.when(pl.program_id(0) == 0)
    def _():
        lanes, places, shard, _ = w_ref.shape
        for place in range(places):
            rows = jnp.concatenate([w_ref[lane, place] for lane in range(lanes)], axis=0)
            columns = slice(place * lanes * shard, (place + 1) * lanes * shard)
            wt_ref[:width, columns] = jnp.transpose(rows)
        wt_ref[width:] = down_ref[...]

    full = mm_nt(wt_ref[...], buffer[slot])
    narrow = full[width:].astype(jnp.bfloat16)
    narrow_ref[...] = narrow
    pre = full[:width] + mm(up_ref[...], narrow)
    cosine, sine = cos_ref[...], sin_ref[...]
    for head in range(group + 1):
        base = head * HEAD_SIZE
        low_half, high_half = halves_rotated(
            pre[base : base + half], pre[base + half : base + HEAD_SIZE], cosine, sine
        )
        wide = jnp.concatenate([low_half, high_half], axis=0)
        vector = wide.astype(jnp.bfloat16)
        logits = mm(map_ref[base : base + HEAD_SIZE], vector)
        plus, minus = soft_pair(logits)
        maps = jnp.concatenate([plus, minus], axis=0)
        if head < group:
            q_ref[base : base + HEAD_SIZE] = vector
            pq_ref[2 * base : 2 * base + 2 * HEAD_SIZE] = maps.astype(jnp.bfloat16)
        else:
            kt_ref[...] = vector
            k_ref[...] = jnp.transpose(wide).astype(jnp.bfloat16)
            pkt_ref[...] = maps.astype(jnp.bfloat16)
            pk_ref[...] = jnp.transpose(maps).astype(jnp.bfloat16)
    values = pre[width - HEAD_SIZE : width]
    vt_ref[:HEAD_SIZE] = values.astype(jnp.bfloat16)
    vt_ref[HEAD_SIZE:] = jnp.ones((ONES, values.shape[1]), jnp.bfloat16)
    v_ref[...] = jnp.transpose(values).astype(jnp.bfloat16)


def project(place_row, blocks, weights, down_block, up_block, maps_ahead, cosine, sine):
    places = len(blocks)
    rows, model = block_shape(blocks)
    count = places * rows
    width, spare = up_block.shape
    query_width = width - 2 * HEAD_SIZE
    group = query_width // HEAD_SIZE
    maps = 2 * HEAD_SIZE
    half = HEAD_SIZE // 2
    counts = [len(found) for found in blocks]
    outs = [
        (query_width, False),
        (HEAD_SIZE, False),
        (HEAD_SIZE + ONES, False),
        (HEAD_SIZE, True),
        (HEAD_SIZE, True),
        (group * maps, False),
        (maps, False),
        (maps, True),
        (spare, False),
    ]
    return call(
        functools.partial(project_kernel, counts),
        (places,),
        [ANYWHERE] * sum(counts)
        + [
            spec_whole(*weights.shape),
            spec_whole(spare, model),
            spec_whole(width, spare),
            spec_whole(*maps_ahead.shape),
            spec_placed(spec_across(half, rows)),
            spec_placed(spec_across(half, rows)),
        ],
        [
            spec_placed(spec_down(rows, size) if natural else spec_across(size, rows))
            for size, natural in outs
        ]
        + [spec_whole(width + spare, model)],
        [array(count, size) if natural else array(size, count) for size, natural in outs]
        + [array(width + spare, model)],
        fetch_scratch(blocks),
        0,
        17,
        scalars=1,
    )(place_row, *flat(blocks), weights, down_block, up_block, maps_ahead, cosine, sine)


def side_by_side(ref, size, group, columns):
    return jnp.concatenate(
        [ref[head * size : (head + 1) * size, columns] for head in range(group)], axis=1
    )


def bands():
    shape = (WINDOW_KEYS, SUB)
    query_at = lax.broadcasted_iota(jnp.int32, shape, 1)
    key_at = lax.broadcasted_iota(jnp.int32, shape, 0)
    distance = query_at - key_at
    return (
        distance < 0,
        (distance >= 0) & (distance < WINDOW_KEYS),
        distance >= WINDOW_KEYS,
        distance >= WINDOW_KEYS,
    )


def forward_kernel(
    length_ref, q_ref, pq_ref, k_ref, k_before, pk_ref, pk_before, vt_ref, vt_before,
    att_ref, out_ref, denom_ref, states_ref, weights_ref, state,
):
    step = pl.program_id(0)
    group = q_ref.shape[0] // HEAD_SIZE
    rows = q_ref.shape[1]
    quarter = WINDOW_KEYS
    second, third, third_far, fourth = bands()

    @pl.when(step == 0)
    def _():
        state[...] = jnp.zeros_like(state)

    now = state[...]
    for sub in range(rows // SUB):
        columns = slice(sub * SUB, (sub + 1) * SUB)
        queries = side_by_side(q_ref, HEAD_SIZE, group, columns)
        query_maps = side_by_side(pq_ref, 2 * HEAD_SIZE, group, columns)
        if sub == 0:
            keys = jnp.concatenate([k_before[...], k_ref[:SUB]], axis=0)
            key_maps = jnp.concatenate([pk_before[...], pk_ref[:SUB]], axis=0)
            values = jnp.concatenate([vt_before[...], vt_ref[:, :SUB]], axis=1)
        else:
            around = slice((sub - 1) * SUB, (sub + 1) * SUB)
            keys, key_maps, values = k_ref[around], pk_ref[around], vt_ref[:, around]
        scores = mm(keys[quarter:], queries)
        far = mm(key_maps[: 3 * quarter], query_maps)
        pieces = []
        for head in range(group):
            lanes = slice(head * SUB, (head + 1) * SUB)
            near = jnp.exp(scores[:, lanes] * (1.0 / math.sqrt(HEAD_SIZE)))
            away = far[:, lanes]
            before = jnp.concatenate(
                [
                    away[:quarter],
                    jnp.where(second, near[:quarter], away[quarter : 2 * quarter]),
                ],
                axis=0,
            )
            if sub == 0:
                before = jnp.where(step > 0, before, 0.0)
            pieces.append(
                jnp.concatenate(
                    [
                        before,
                        jnp.where(
                            third,
                            near[quarter : 2 * quarter],
                            jnp.where(third_far, away[2 * quarter :], 0.0),
                        ),
                        jnp.where(fourth, near[2 * quarter :], 0.0),
                    ],
                    axis=0,
                ).astype(jnp.bfloat16)
            )
        weights = jnp.concatenate(pieces, axis=1)
        weights_ref[sub] = weights
        states_ref[sub] = now
        high, low = split_wide(now)
        total = mm(values, weights) + mm(
            jnp.concatenate([high, low], axis=1),
            jnp.concatenate([query_maps, query_maps], axis=0),
        )
        denom = total[HEAD_SIZE : HEAD_SIZE + 1]
        out = total[:HEAD_SIZE] * (1.0 / denom)
        at = step * rows + sub * SUB + lax.broadcasted_iota(jnp.int32, (HEAD_SIZE, SUB), 1)
        inside = at < length_ref[0]
        for head in range(group):
            lanes = slice(head * SUB, (head + 1) * SUB)
            base = head * HEAD_SIZE
            out_ref[base : base + HEAD_SIZE, columns] = out[:, lanes]
            att_ref[base : base + HEAD_SIZE, columns] = jnp.where(
                inside, out[:, lanes], 0.0
            ).astype(jnp.bfloat16)
            denom_ref[head : head + 1, columns] = denom[:, lanes]
        update = mm(values[:, :SUB], key_maps[:SUB])
        if sub == 0:
            update = jnp.where(step > 0, update, 0.0)
        now = now + update
    state[...] = now


def before_down(rows, wide):
    per_step = rows // SUB
    return pl.BlockSpec((SUB, wide), lambda i, *_: (jnp.maximum(per_step * i - 1, 0), 0))


def before_across(rows, height):
    per_step = rows // SUB
    return pl.BlockSpec((height, SUB), lambda i, *_: (0, jnp.maximum(per_step * i - 1, 0)))


def attend(length, q_t, pq_t, keys, key_maps, v_t, rows):
    query_width, count = q_t.shape
    group = query_width // HEAD_SIZE
    places = count // rows
    per_step = rows // SUB
    maps = key_maps.shape[1]
    high = v_t.shape[0]
    wide = jnp.float32
    return call(
        forward_kernel,
        (places,),
        [
            spec_across(query_width, rows),
            spec_across(group * maps, rows),
            spec_down(rows, HEAD_SIZE),
            before_down(rows, HEAD_SIZE),
            spec_down(rows, maps),
            before_down(rows, maps),
            spec_across(high, rows),
            before_across(rows, high),
        ],
        [
            spec_block(query_width, rows),
            spec_across(query_width, rows),
            spec_across(group, rows),
            pl.BlockSpec((per_step, high, maps), lambda i, *_: (i, 0, 0)),
            pl.BlockSpec((per_step, 2 * SUB, group * SUB), lambda i, *_: (i, 0, 0)),
        ],
        [
            array(places, query_width, rows),
            array(query_width, count, dtype=wide),
            array(group, count, dtype=wide),
            array(count // SUB, high, maps, dtype=wide),
            array(count // SUB, 2 * SUB, group * SUB),
        ],
        [pltpu.VMEM((high, maps), wide)],
        0,
        10,
        scalars=1,
    )(length, q_t, pq_t, keys, keys, key_maps, key_maps, v_t, v_t)


def teacher_kernel(first, steps, length_ref, q_ref, k_ref, vt_ref, att_ref, *refs):
    diff_ref, loss_ref = refs[-2:]
    step = pl.program_id(0)
    group = q_ref.shape[0] // HEAD_SIZE
    rows = q_ref.shape[1]
    scale = 1.0 / math.sqrt(HEAD_SIZE)
    at = (first + step) * rows + lax.broadcasted_iota(jnp.int32, (HEAD_SIZE, rows), 1)
    inside = at < length_ref[0]
    shape = (rows, rows)
    ahead = lax.broadcasted_iota(jnp.int32, shape, 0) > lax.broadcasted_iota(jnp.int32, shape, 1)

    for blocks in range(first + 1, first + steps + 1):

        @pl.when(first + step == blocks - 1)
        def _():
            size = blocks * rows
            loss = jnp.zeros((1, rows), jnp.float32)
            for head in range(group):
                base = head * HEAD_SIZE
                query = q_ref[base : base + HEAD_SIZE]
                last = jnp.where(ahead, lowest_precision, mm(k_ref[size - rows : size], query))
                best = jnp.max(last, axis=0, keepdims=True)
                if blocks > 1:
                    early = mm(k_ref[: size - rows], query)
                    best = jnp.maximum(best, jnp.max(early, axis=0, keepdims=True))
                total = mm(
                    vt_ref[:, size - rows : size],
                    jnp.exp((last - best) * scale).astype(jnp.bfloat16),
                )
                if blocks > 1:
                    total = total + mm(
                        vt_ref[:, : size - rows],
                        jnp.exp((early - best) * scale).astype(jnp.bfloat16),
                    )
                taught = total[:HEAD_SIZE] * (1.0 / total[HEAD_SIZE : HEAD_SIZE + 1])
                difference = att_ref[base : base + HEAD_SIZE].astype(jnp.float32) - jnp.where(
                    inside, taught, 0.0
                )
                diff_ref[base : base + HEAD_SIZE] = difference
                loss = loss + jnp.sum(difference * difference, axis=0, keepdims=True)
            loss_ref[...] = jnp.broadcast_to(loss, loss_ref.shape)


def teach(length, q_t, keys, v_t, att, first, end, before=None):
    places, query_width, rows = att.shape
    count = places * rows
    wide = jnp.float32

    def ahead(spec):
        return pl.BlockSpec(spec.block_shape, lambda i, *_: spec.index_map(i + first))

    spec = pltpu.PrefetchScalarGridSpec(
        num_scalar_prefetch=1,
        grid=(end - first,),
        in_specs=[
            ahead(spec_across(query_width, rows)),
            spec_whole(*keys.shape),
            spec_whole(*v_t.shape),
            ahead(spec_block(query_width, rows)),
        ]
        + [ANYWHERE] * (2 if before else 0),
        out_specs=[ahead(spec_across(query_width, rows)), ahead(spec_across(8, rows))],
    )
    return pl.pallas_call(
        functools.partial(teacher_kernel, first, end - first),
        grid_spec=spec,
        out_shape=[array(query_width, count, dtype=wide), array(8, count, dtype=wide)],
        input_output_aliases={5: 0, 6: 1} if before else {},
        compiler_params=pltpu.CompilerParams(vmem_limit_bytes=VMEM_MIB * 2**20),
        cost_estimate=pl.CostEstimate(
            flops=int(COST * 16), bytes_accessed=1, transcendentals=0
        ),
    )(length, q_t, keys, v_t, att, *(before or ()))


def hidden_kernel(counts, order_ref, *refs):
    blocks, refs = grouped(refs, counts)
    *gates, ups, hidden_ref, by_gate_ref, by_up_ref, buffer, sems, both, both_sem = refs

    @pl.when(pl.program_id(0) == 0)
    def _():
        unit = ups.shape[2] // PARTS
        wide = ups.shape[0] * unit
        for part in range(PARTS):
            span = part * unit, (part + 1) * unit
            start_columns(gates, span, both.at[:, part * wide : (part + 1) * wide], both_sem)
            start = (PARTS + part) * wide
            start_columns(chunks_of(ups, order_ref), span, both.at[:, start : start + wide], both_sem)

    slot = fetch(blocks, buffer, sems, pl.program_id(0))

    @pl.when(pl.program_id(0) == 0)
    def _():
        wait_whole(both, both_sem)

    full = mm(buffer[slot], both[...])
    wide = full.shape[1] // 2
    gate, up = full[:, :wide], full[:, wide:]
    sigmoid = 1.0 / (1.0 + jnp.exp(-gate))
    silu = gate * sigmoid
    hidden_ref[...] = (silu * up).astype(jnp.bfloat16)
    by_gate_ref[...] = (up * (sigmoid + silu * (1.0 - sigmoid))).astype(jnp.bfloat16)
    by_up_ref[...] = silu.astype(jnp.bfloat16)


def hidden_units(order, blocks, gates, ups):
    rows, model = block_shape(blocks)
    count = rows * len(blocks)
    share = ups.shape[0] * ups.shape[2]
    counts = [len(found) for found in blocks]
    return call(
        functools.partial(hidden_kernel, counts),
        (len(blocks),),
        [ANYWHERE] * (sum(counts) + 1 + len(gates)),
        [spec_down(rows, share)] * 3,
        [array(count, share)] * 3,
        fetch_scratch(blocks)
        + [pltpu.VMEM((model, 2 * share), jnp.bfloat16), pltpu.SemaphoreType.DMA],
        0,
        25,
        scalars=1,
    )(order, *flat(blocks), *gates, ups)


def ffn_back_kernel(counts, chunks, part, more, order_ref, *refs):
    blocks, refs = grouped(refs, counts)
    *gates, ups, downs, by_gate_ref, by_up_ref = refs[: chunks + 4]
    before_ref = refs[chunks + 4] if more else None
    out_ref, buffer, sems, both, both_sem, down, down_sem = refs[-7:]

    @pl.when(pl.program_id(0) == 0)
    def _():
        wide = both.shape[1] // 2
        unit = downs.shape[2]
        span = part * unit, (part + 1) * unit
        start_columns(chunks_of(downs, order_ref), (0, unit), down, down_sem)
        start_columns(gates, span, both.at[:, :wide], both_sem)
        start_columns(chunks_of(ups, order_ref), span, both.at[:, wide:], both_sem)

    slot = fetch(blocks, buffer, sems, pl.program_id(0))

    @pl.when(pl.program_id(0) == 0)
    def _():
        wait_whole(down, down_sem)

    grad_hidden = mm(buffer[slot], down[...])
    grad_gate = (grad_hidden * by_gate_ref[...].astype(jnp.float32)).astype(jnp.bfloat16)
    grad_up = (grad_hidden * by_up_ref[...].astype(jnp.float32)).astype(jnp.bfloat16)

    @pl.when(pl.program_id(0) == 0)
    def _():
        wait_whole(both, both_sem)

    total = mm_nt(jnp.concatenate([grad_gate, grad_up], axis=1), both[...])
    if more:
        total = total + before_ref[...].astype(jnp.float32)
    out_ref[...] = total.astype(jnp.bfloat16)


def ffn_back(order, blocks, first, each, part, gates, ups, downs, by_gate, by_up, before):
    rows, model = block_shape(blocks)
    share = downs.shape[0] * downs.shape[2]
    counts = [len(found) for found in blocks]
    more = before is not None

    def rows_of(wide, at=0):
        return pl.BlockSpec((rows, wide), lambda i, *_: (first + each * i, at))

    return call(
        functools.partial(ffn_back_kernel, counts, len(gates), part, more),
        (len(blocks),),
        [ANYWHERE] * (sum(counts) + len(gates) + 2)
        + [rows_of(share, part)] * 2
        + [rows_of(model)] * more,
        spec_down(rows, model),
        array(len(blocks) * rows, model),
        fetch_scratch(blocks)
        + [pltpu.VMEM((model, 2 * share), jnp.bfloat16), pltpu.SemaphoreType.DMA]
        + [pltpu.VMEM((model, share), jnp.bfloat16), pltpu.SemaphoreType.DMA],
        0,
        3 * len(blocks),
        scalars=1,
    )(order, *flat(blocks), *gates, ups, downs, by_gate, by_up, *([before] if more else []))


def ffn_out_kernel(place_ref, order_ref, *refs):
    downs, (hidden_ref, out_ref, down, down_sem) = refs[:PARTS], refs[PARTS:]

    @pl.when(pl.program_id(0) == 0)
    def _():
        wide = down.shape[1] // PARTS
        for part, ref in enumerate(downs):
            start_columns(
                chunks_of(ref, order_ref), (0, ref.shape[2]), down.at[:, part * wide : (part + 1) * wide], down_sem
            )
        wait_whole(down, down_sem)

    out_ref[...] = mm_nt(hidden_ref[...], down[...]).astype(jnp.bfloat16)


def ffn_out(place_row, order, hidden, downs, places):
    count, share = hidden.shape
    rows = count // places
    model = downs[0].shape[1]
    return call(
        ffn_out_kernel,
        (places,),
        [ANYWHERE] * PARTS + [spec_down(rows, share)],
        spec_placed(spec_down(rows, model)),
        array(count, model),
        [pltpu.VMEM((model, share), jnp.bfloat16), pltpu.SemaphoreType.DMA],
        0,
        17,
        scalars=2,
    )(place_row, order, *downs, hidden)


def backward_kernel(
    counts, length_ref, place_ref, *refs
):
    blocks, refs = grouped(refs, counts)
    (
    grad_ref, diff_ref, out_ref, denom_ref, q_ref, pq_ref, weights_ref,
    v_ref, v_before, kt_ref, kt_before, pkt_ref, pkt_before, vt_ref, vt_before,
    states_ref, map_ref, back_ref, cos_ref, sin_ref, up_ref, wt_ref,
    pre_ref, gain_ref, fall_ref, give_ref, keep_ref, key_carry, value_carry, map_carry, later,
    buffer, sems,
    ) = refs
    step = pl.num_programs(0) - 1 - pl.program_id(0)
    group = q_ref.shape[0] // HEAD_SIZE
    rows = q_ref.shape[1]
    half = HEAD_SIZE // 2
    quarter = WINDOW_KEYS
    scale = 1.0 / math.sqrt(HEAD_SIZE)
    second, third, third_far, fourth = bands()
    short = jnp.bfloat16
    per_block = grad_ref.shape[2]
    inner = per_block // SUB

    @pl.when(pl.program_id(0) == 0)
    def _():
        gain_ref[...] = jnp.zeros_like(gain_ref)
        key_carry[...] = jnp.zeros_like(key_carry)
        value_carry[...] = jnp.zeros_like(value_carry)
        map_carry[...] = jnp.zeros_like(map_carry)
        later[...] = jnp.zeros_like(later)
        fall_ref[...] = jnp.zeros_like(fall_ref)

    carried_keys, carried_values, carried_maps = key_carry[...], value_carry[...], map_carry[...]
    later_now = later[...]
    query_parts, map_parts, key_parts, value_parts, key_map_parts = [], [], [], [], []
    for sub in reversed(range(rows // SUB)):
        columns = slice(sub * SUB, (sub + 1) * SUB)
        queries = side_by_side(q_ref, HEAD_SIZE, group, columns)
        query_maps = side_by_side(pq_ref, 2 * HEAD_SIZE, group, columns)
        if sub == 0:
            values = jnp.concatenate([v_before[...], v_ref[:SUB]], axis=0)
            keys_t = jnp.concatenate([kt_before[...], kt_ref[:, :SUB]], axis=1)
            key_maps_t = jnp.concatenate([pkt_before[...], pkt_ref[:, :SUB]], axis=1)
            values_before = vt_before[...]
        else:
            around = slice((sub - 1) * SUB, (sub + 1) * SUB)
            values = v_ref[around]
            keys_t, key_maps_t = kt_ref[:, around], pkt_ref[:, around]
            values_before = vt_ref[:, (sub - 1) * SUB : sub * SUB]
        at = step * rows + sub * SUB + lax.broadcasted_iota(jnp.int32, (HEAD_SIZE, SUB), 1)
        inside = at < length_ref[0]
        numers, denoms = [], []
        for head in range(group):
            base = head * HEAD_SIZE
            span = slice(base, base + HEAD_SIZE)
            place_in = slice(sub % inner * SUB, (sub % inner + 1) * SUB)
            incoming = grad_ref[sub // inner, span, place_in].astype(jnp.float32) + 2.0 * diff_ref[span, columns]
            incoming = jnp.where(inside, incoming.astype(short).astype(jnp.float32), 0.0)
            inverse = 1.0 / denom_ref[head : head + 1, columns]
            numers.append((incoming * inverse).astype(short))
            denoms.append(
                -jnp.sum(incoming * out_ref[span, columns], axis=0, keepdims=True) * inverse
            )
        grad_numer = jnp.concatenate(numers, axis=1)
        grad_denom = jnp.concatenate(denoms, axis=1)
        rank = lax.broadcasted_iota(jnp.int32, (ONES, group * SUB), 0)
        denom_high = grad_denom.astype(short).astype(jnp.float32)
        extra = jnp.where(
            rank == 0, denom_high, jnp.where(rank == 1, grad_denom - denom_high, 0.0)
        ).astype(short)
        grad_both = jnp.concatenate([grad_numer, extra], axis=0)
        weights = weights_ref[sub]
        raw = mm(values, grad_numer)
        scores, fars = [], []
        for head in range(group):
            lanes = slice(head * SUB, (head + 1) * SUB)
            grad_weights = raw[:, lanes] + denoms[head]
            if sub == 0:
                kept = jnp.where(step > 0, grad_weights[: 2 * quarter], 0.0)
                grad_weights = jnp.concatenate([kept, grad_weights[2 * quarter :]], axis=0)
            by_score = grad_weights[quarter:] * weights[quarter:, lanes].astype(jnp.float32)
            scores.append(
                jnp.concatenate(
                    [
                        jnp.where(second, by_score[:quarter], 0.0),
                        jnp.where(third, by_score[quarter : 2 * quarter], 0.0),
                        jnp.where(fourth, by_score[2 * quarter :], 0.0),
                    ],
                    axis=0,
                ).astype(short)
            )
            fars.append(
                jnp.concatenate(
                    [
                        grad_weights[:quarter],
                        jnp.where(second, 0.0, grad_weights[quarter : 2 * quarter]),
                        jnp.where(third_far, grad_weights[2 * quarter : 3 * quarter], 0.0),
                    ],
                    axis=0,
                ).astype(short)
            )
        grad_scores = jnp.concatenate(scores, axis=1)
        grad_far = jnp.concatenate(fars, axis=1)
        state_high, state_low = split_wide(jnp.transpose(states_ref[sub]))
        query_parts.append(mm(keys_t[:, quarter:], grad_scores) * scale)
        map_parts.append(
            mm(key_maps_t[:, : 3 * quarter], grad_far)
            + mm(
                jnp.concatenate([state_high, state_low], axis=1),
                jnp.concatenate([grad_both, grad_both], axis=0),
            )
        )
        grad_keys = mm_nt(queries, grad_scores) * scale
        grad_values = mm_nt(grad_numer, weights)
        grad_key_maps = mm_nt(query_maps, grad_far)
        key_parts.append(carried_keys + grad_keys[:, quarter:])
        value_parts.append(carried_values + grad_values[:, SUB:])
        key_map_parts.append(
            jnp.concatenate(
                [
                    carried_maps[:, :quarter] + grad_key_maps[:, 2 * quarter :],
                    carried_maps[:, quarter:],
                ],
                axis=1,
            )
        )
        later_high, later_low = split_wide(jnp.transpose(later_now))
        carried_keys = jnp.concatenate(
            [jnp.zeros((HEAD_SIZE, quarter), jnp.float32), grad_keys[:, :quarter]], axis=1
        )
        carried_values = grad_values[:, :SUB] + mm(
            later_now[:HEAD_SIZE].astype(short), key_maps_t[:, :SUB]
        )
        carried_maps = grad_key_maps[:, : 2 * quarter] + mm(
            jnp.concatenate([later_high, later_low], axis=1),
            jnp.concatenate([values_before, values_before], axis=0),
        )
        later_now = later_now + mm_nt(grad_both, query_maps)
    key_carry[...], value_carry[...], map_carry[...] = carried_keys, carried_values, carried_maps
    later[...] = later_now

    def joined(parts, lanes=slice(None)):
        return jnp.concatenate([part[:, lanes] for part in reversed(parts)], axis=1)

    cosine, sine = cos_ref[...], sin_ref[...]
    for head in range(group + 1):
        base = head * HEAD_SIZE
        span = slice(base, base + HEAD_SIZE)
        lanes = slice(head * SUB, (head + 1) * SUB)
        if head < group:
            vector, direct = q_ref[span], joined(query_parts, lanes)
            grad_maps = joined(map_parts, lanes)
        else:
            vector, direct, grad_maps = kt_ref[...], joined(key_parts), joined(key_map_parts)
        plus, minus = soft_pair(mm(map_ref[span], vector))
        grad_plus, grad_minus = grad_maps[:HEAD_SIZE], grad_maps[HEAD_SIZE:]
        grad_logits = plus * (
            grad_plus - jnp.sum(grad_plus * plus, axis=0, keepdims=True)
        ) - minus * (grad_minus - jnp.sum(grad_minus * minus, axis=0, keepdims=True))
        grad_logits = grad_logits.astype(short)
        gain_ref[span] += mm_nt(vector, grad_logits)
        total = direct + mm(back_ref[span], grad_logits)
        low_half, high_half = halves_rotated(total[:half], total[half:], cosine, -sine)
        pre_ref[base : base + half] = low_half.astype(short)
        pre_ref[base + half : base + HEAD_SIZE] = high_half.astype(short)
    width = (group + 2) * HEAD_SIZE
    pre_ref[width - HEAD_SIZE : width] = joined(value_parts).astype(short)
    pre_ref[width:] = mm_tn(up_ref[...], pre_ref[:width]).astype(short)
    per_step = rows // per_block

    def order(at):
        return (pl.num_programs(0) - 1 - at // per_step) * per_step + lax.rem(at, per_step)

    own_core = lax.rem(place_ref[0], 2)
    for block in range(rows // per_block):
        columns = slice(block * per_block, (block + 1) * per_block)
        here = pre_ref[:, columns]
        grad_normed = mm_tn(here, wt_ref[...]).astype(short)
        slot = fetch(
            blocks,
            buffer,
            sems,
            pl.program_id(0) * (rows // per_block) + block,
            lambda at: lax.bitwise_xor(order(at), place_ref[0]),
        )
        fall_ref[...] += mm(here[width:], buffer[slot])

        @pl.when(own_core == block % 2)
        def _():
            keep_ref[...] = grad_normed

        @pl.when(own_core != block % 2)
        def _():
            give_ref[...] = grad_normed


def heads_back(
    length, place_row, blocks, grad_att, difference, out_t, denom, q_t, pq_t, weights,
    values, k_t, pk_t, v_t, states, maps_ahead, maps_back, cosine, sine, up_block, weights_t,
):
    places, query_width, per_block = grad_att.shape
    count = places * per_block
    rows = 2 * per_block
    steps = count // rows
    group = query_width // HEAD_SIZE
    per_step = rows // SUB
    counts = [len(found) for found in blocks]
    width, spare = up_block.shape
    model = weights_t.shape[1]
    maps = pk_t.shape[0]
    high = v_t.shape[0]
    half = HEAD_SIZE // 2

    def back(spec):
        return pl.BlockSpec(spec.block_shape, lambda i, *_: spec.index_map(steps - 1 - i))

    def by_chip(i, length_ref, place_ref):
        return (lax.bitwise_xor(steps - 1 - i, place_ref[0] // 2), 0, 0)

    def leading(*dims):
        return pl.BlockSpec((per_step,) + dims, lambda i, *_: (i, 0, 0))

    return call(
        functools.partial(backward_kernel, counts),
        (steps,),
        [ANYWHERE] * sum(counts)
        + [
            back(pl.BlockSpec((2, query_width, per_block), lambda i, *_: (i, 0, 0))),
            back(spec_across(query_width, rows)),
            back(spec_across(query_width, rows)),
            back(spec_across(group, rows)),
            back(spec_across(query_width, rows)),
            back(spec_across(group * maps, rows)),
            back(leading(2 * SUB, group * SUB)),
            back(spec_down(rows, HEAD_SIZE)),
            back(before_down(rows, HEAD_SIZE)),
            back(spec_across(HEAD_SIZE, rows)),
            back(before_across(rows, HEAD_SIZE)),
            back(spec_across(maps, rows)),
            back(before_across(rows, maps)),
            back(spec_across(high, rows)),
            back(before_across(rows, high)),
            back(leading(high, maps)),
            spec_whole(*maps_ahead.shape),
            spec_whole(*maps_back.shape),
            back(spec_across(half, rows)),
            back(spec_across(half, rows)),
            spec_whole(width, spare),
            spec_whole(width + spare, model),
        ],
        [
            back(spec_across(width + spare, rows)),
            spec_whole(*maps_back.shape),
            spec_whole(spare, model),
            pl.BlockSpec((None, per_block, model), by_chip),
            pl.BlockSpec((None, per_block, model), by_chip),
        ],
        [
            array(width + spare, count),
            array(*maps_back.shape, dtype=jnp.float32),
            array(spare, model, dtype=jnp.float32),
            array(steps, per_block, model),
            array(steps, per_block, model),
        ],
        [
            pltpu.VMEM((HEAD_SIZE, SUB), jnp.float32),
            pltpu.VMEM((HEAD_SIZE, SUB), jnp.float32),
            pltpu.VMEM((maps, SUB), jnp.float32),
            pltpu.VMEM((high, maps), jnp.float32),
        ]
        + fetch_scratch(blocks),
        0,
        30,
        scalars=2,
    )(
        length, place_row, *flat(blocks), grad_att, difference, out_t, denom, q_t, pq_t, weights,
        values, values, k_t, k_t, pk_t, pk_t, v_t, v_t,
        states, maps_ahead, maps_back, cosine, sine, up_block, weights_t,
    )


def branch_kernel(
    counts, place_ref, *refs
):
    blocks, refs = grouped(refs, counts)
    (
        att_ref, down_ref, up_ref, tokens_ref, gain_ref,
        residual_ref, normed_ref, inverse_ref, narrow_ref, buffer, sems, total, slim,
    ) = refs
    step = pl.program_id(0)
    slot = fetch(blocks, buffer, sems, step)

    @pl.when(step == 0)
    def _():
        total[...] = tokens_ref[...].astype(jnp.float32)
        slim[...] = jnp.zeros_like(slim)

    total[...] += mm_tn(att_ref[...], buffer[slot])
    slim[...] += mm_tn(att_ref[...], down_ref[...])

    @pl.when(step == pl.num_programs(0) - 1)
    def _():
        narrow = slim[...].astype(jnp.bfloat16)
        narrow_ref[...] = narrow
        residual = total[...] + mm_nt(narrow, up_ref[...])
        residual_ref[...] = residual
        inverse = lax.rsqrt(jnp.mean(residual * residual, axis=-1, keepdims=True) + epsilon)
        inverse_ref[...] = jnp.broadcast_to(inverse, inverse_ref.shape)
        normed_ref[...] = (residual * inverse * gain_ref[...]).astype(jnp.bfloat16)


def branch_out(place_row, blocks, att, down_wide, up_wide, tokens, gain):
    places, query_width, rows = att.shape
    model = tokens.shape[1]
    spare = down_wide.shape[1]
    counts = [len(found) for found in blocks]
    wide = jnp.float32
    return call(
        functools.partial(branch_kernel, counts),
        (places,),
        [ANYWHERE] * sum(counts)
        + [
            spec_placed(spec_block(query_width, rows)),
            spec_placed(spec_down(query_width, spare)),
            spec_whole(model, spare),
            spec_whole(rows, model),
            spec_whole(1, model),
        ],
        [
            spec_whole(rows, model),
            spec_whole(rows, model),
            spec_whole(rows, 128),
            spec_whole(rows, spare),
        ],
        [
            array(rows, model, dtype=wide),
            array(rows, model),
            array(rows, 128, dtype=wide),
            array(rows, spare),
        ],
        fetch_scratch(blocks)
        + [pltpu.VMEM((rows, model), wide), pltpu.VMEM((rows, spare), wide)],
        0,
        13,
        scalars=1,
    )(place_row, *flat(blocks), att, down_wide, up_wide, tokens, gain)


def branch_back_kernel(counts, place_ref, *refs):
    blocks, refs = grouped(refs, counts)
    (
        own_ref, from_x, late_x, late_y, from_y, residual_ref, inverse_ref, gain_ref, cot_ref,
        down_ref, up_ref,
        grad_att_ref, grad_ref, branch_ref, slim_ref, buffer, sems,
    ) = refs
    step = pl.program_id(0)
    slot = fetch(blocks, buffer, sems, step)

    @pl.when(step == 0)
    def _():
        wide = jnp.float32
        middle = late_x.shape[0]
        for start, part in enumerate(sums_of(own_ref, from_x, late_x, late_y, from_y)):
            span = slice(start * middle, (start + 1) * middle)
            residual, inverse = residual_ref[span], inverse_ref[span, :1]
            scaled = part * gain_ref[...]
            mean = jnp.mean(scaled * residual, axis=-1, keepdims=True)
            grad = (
                cot_ref[span].astype(wide)
                + inverse * scaled
                - residual * (inverse * inverse * inverse * mean)
            )
            grad_ref[span] = grad
            branch_ref[span] = grad.astype(jnp.bfloat16)
        slim_ref[...] = mm(branch_ref[...], up_ref[...])

    slim = slim_ref[...].astype(jnp.bfloat16)
    grad_att_ref[...] = (
        mm_nt(buffer[slot], branch_ref[...]) + mm_nt(down_ref[...], slim)
    ).astype(jnp.bfloat16)


def branch_back(
    place_row, blocks, sums, residual, inverse, gain, cotangent, down_wide, up_wide
):
    places = len(blocks)
    rows, model = residual.shape
    query_width = model // places
    spare = down_wide.shape[1]
    counts = [len(found) for found in blocks]
    wide = jnp.float32
    return call(
        functools.partial(branch_back_kernel, counts),
        (places,),
        [ANYWHERE] * sum(counts)
        + [spec_whole(*part.shape) for part in sums]
        + [
            spec_whole(rows, model),
            spec_whole(rows, 128),
            spec_whole(1, model),
            spec_whole(rows, model),
            spec_placed(spec_down(query_width, spare)),
            spec_whole(model, spare),
        ],
        [
            spec_placed(spec_block(query_width, rows)),
            spec_whole(rows, model),
            spec_whole(rows, model),
            spec_whole(rows, spare),
        ],
        [
            array(places, query_width, rows),
            array(rows, model, dtype=wide),
            array(rows, model),
            array(rows, spare, dtype=wide),
        ],
        fetch_scratch(blocks),
        0,
        15,
        scalars=1,
    )(
        place_row, *flat(blocks), *sums, residual, inverse, gain, cotangent, down_wide, up_wide
    )


def exchanged(value, bits):
    count = lax.axis_size("seq")
    return lax.ppermute(value, "seq", [(place, place ^ bits) for place in range(count)])


def after(value, *others):
    return pl.pallas_call(
        lambda *refs: None,
        out_shape=jax.ShapeDtypeStruct(value.shape, value.dtype),
        in_specs=[pl.BlockSpec(memory_space=pl.ANY)] * (1 + len(others)),
        out_specs=pl.BlockSpec(memory_space=pl.ANY),
        input_output_aliases={0: 0},
    )(value, *others)


def halves(value):
    middle = value.shape[0] // 2
    return value[:middle], value[middle:]


def regroup_kernel(*refs):
    out_ref = refs[-1]
    for number, ref in enumerate(refs[:-1]):
        out_ref[number] = ref[...]


def regroup(places, *matrices):
    rows, wide = matrices[0].shape
    unit = wide // places
    return call(
        regroup_kernel,
        (places,),
        [spec_across(rows, unit)] * len(matrices),
        pl.BlockSpec((None, len(matrices), rows, unit), lambda i: (i, 0, 0, 0)),
        array(places, len(matrices), rows, unit),
        [],
        0,
        6,
    )(*matrices)


def ungroup_kernel(ref, *refs):
    for number, out_ref in enumerate(refs):
        out_ref[...] = ref[number]


def ungroup(blocks):
    places, count, rows, unit = blocks.shape
    return call(
        ungroup_kernel,
        (places,),
        [pl.BlockSpec((None, count, rows, unit), lambda i: (i, 0, 0, 0))],
        [spec_down(rows, unit)] * count,
        [array(places * rows, unit)] * count,
        [],
        0,
        6,
    )(blocks)


def gather_first(value):
    return exchanged(value, 1), exchanged(value, 2), exchanged(value, 4)


def gather_rest(value, beside, along_x, along_y, *others, last=()):
    upper, lower = halves(along_x)[0], halves(along_y)[1]
    if others:
        upper, lower = after(upper, *others), after(lower, *others)
    first, second = exchanged(upper, 4), exchanged(lower, 2)
    if last:
        first, second = after(first, *last), after(second, *last)
    return [
        (value,),
        (beside,),
        (along_x,),
        (exchanged(along_x, 1),),
        (along_y,),
        (exchanged(along_y, 1),),
        (first, second),
        (exchanged(first, 1), exchanged(second, 1)),
    ]


def plane_gather(value):
    return gather_rest(value, *gather_first(value))


def core_sums_kernel(keep_ref, got_ref, own_ref, to_x, to_y, later_x, later_y):
    wide, short = jnp.float32, jnp.bfloat16
    middle = later_x.shape[0]

    def both(bits, span=slice(None)):
        return keep_ref[bits, span].astype(wide) + got_ref[bits, span].astype(wide)

    upper, lower = slice(0, middle), slice(middle, None)
    own_ref[...] = both(0)
    to_x[upper], to_x[lower] = both(3, upper).astype(short), both(1, upper).astype(short)
    to_y[upper], to_y[lower] = both(3, lower).astype(short), both(2, lower).astype(short)
    later_x[...] = both(1, lower).astype(short)
    later_y[...] = both(2, upper).astype(short)


def core_sums(keep, got):
    _, rows, model = keep.shape
    wide = model // 4
    block = pl.BlockSpec((4, rows, wide), lambda i: (0, 0, i))
    return call(
        core_sums_kernel,
        (4,),
        [block] * 2,
        [spec_across(rows, wide)] * 3 + [spec_across(rows // 2, wide)] * 2,
        [array(rows, model, dtype=jnp.float32)]
        + [array(rows, model)] * 2
        + [array(rows // 2, model)] * 2,
        [],
        0,
        5,
    )(keep, got)


def scatter_first(give, keep):
    own, to_x, to_y, later_x, later_y = core_sums(keep, exchanged(give, 1))
    return own, exchanged(to_x, 2), exchanged(to_y, 4), later_x, later_y


def scatter_rest(own, from_x, from_y, later_x, later_y, *others):
    middle = later_x.shape[0]
    wide, short = jnp.float32, jnp.bfloat16
    if others:
        later_x, later_y = after(later_x, *others), after(later_y, *others)
    late_y = exchanged((later_y.astype(wide) + from_x[:middle].astype(wide)).astype(short), 4)
    late_x = exchanged((later_x.astype(wide) + from_y[:middle].astype(wide)).astype(short), 2)
    return own, from_x, late_x, late_y, from_y


def sums_of(own_ref, from_x, late_x, late_y, from_y):
    wide = jnp.float32
    middle = late_x.shape[0]
    return (
        own_ref[:middle] + from_x[middle:].astype(wide) + late_y[...].astype(wide),
        own_ref[middle:] + late_x[...].astype(wide) + from_y[middle:].astype(wide),
    )


def tokens_back_kernel(
    own_ref, from_x, late_x, late_y, from_y, tokens_ref, inverse_ref, gain_ref, grad_ref, out_ref
):
    middle = late_x.shape[0]
    for start, part in enumerate(sums_of(own_ref, from_x, late_x, late_y, from_y)):
        span = slice(start * middle, (start + 1) * middle)
        values, inverse = tokens_ref[span].astype(jnp.float32), inverse_ref[span, :1]
        scaled = part * gain_ref[...]
        mean = jnp.mean(scaled * values, axis=-1, keepdims=True)
        out_ref[span] = (
            grad_ref[span] + inverse * scaled - values * (inverse * inverse * inverse * mean)
        ).astype(jnp.bfloat16)


def tokens_back(sums, tokens, inverse, gain, grad):
    rows, model = tokens.shape
    return call(
        tokens_back_kernel,
        (1,),
        [spec_whole(*part.shape) for part in (*sums, tokens, inverse, gain, grad)],
        spec_whole(rows, model),
        array(rows, model),
        [],
        0,
        6,
    )(*sums, tokens, inverse, gain, grad)


def ring(value):
    count = lax.axis_size("fsdp")
    found = [value]
    for _ in range(count - 1):
        found.append(ring_step(found[-1]))
    return found


def ring_step(value):
    count = lax.axis_size("fsdp")
    return lax.ppermute(value, "fsdp", [(at, (at + 1) % count) for at in range(count)])


def by_heads(
    tokens,
    lengths,
    norm_attn,
    norm_ffn,
    w_query,
    key_projection,
    value_projection,
    w_output,
    w_gate,
    w_up,
    w_down,
    down_query,
    up_query,
    key_down_matrix,
    key_up_matrix,
    value_down_matrix,
    value_up_matrix,
    down_output,
    up_output,
    feature_query,
    key_feature_weight,
    cotangent,
):
    places = lax.axis_size("seq")
    lanes = lax.axis_size("fsdp")
    rows = tokens.shape[1]
    model = tokens.shape[2]
    count = rows * places
    group = QUERY_HEADS // KEY_VALUE_HEADS
    query_width = group * HEAD_SIZE
    width = query_width + 2 * HEAD_SIZE
    rank = down_query.shape[1]
    spare = 128
    place = lax.axis_index("seq")
    lane = lax.axis_index("fsdp")
    place_row = place.astype(jnp.int32).reshape(1)
    length = lax.dynamic_slice_in_dim(lengths, lane, 1)
    bf16, f32 = jnp.bfloat16, jnp.float32
    inputs_wide = tokens[0].astype(f32)
    gain_attn = norm_attn.astype(f32)
    gain_ffn = norm_ffn.astype(f32).reshape(1, model)

    shard = w_query.shape[0]
    by_place = jnp.concatenate(
        [
            w_query.reshape(shard, places, query_width),
            key_projection.reshape(shard, places, HEAD_SIZE),
            value_projection.reshape(shard, places, HEAD_SIZE),
        ],
        axis=2,
    )
    by_place = lax.all_to_all(jnp.moveaxis(by_place, 1, 0), "seq", 0, 0, tiled=True)
    own_weights = lax.all_gather(by_place, "fsdp", axis=0)

    inverse_attn = lax.rsqrt(jnp.mean(inputs_wide * inputs_wide, axis=-1, keepdims=True) + epsilon)
    normed_all = plane_gather((inputs_wide * inverse_attn * gain_attn).astype(bf16))
    across = normed_all[6]
    down_block = jnp.concatenate(
        [
            down_query.T,
            key_down_matrix.T,
            value_down_matrix.T,
            jnp.zeros((spare - 3 * rank, model), bf16),
        ],
        axis=0,
    )

    output_rows = lax.all_gather(w_output, "fsdp", axis=0)
    swapped = after(regroup(places, w_gate, w_up, w_down), by_place)
    swapped = lax.all_to_all(swapped, "seq", 0, 0, tiled=True)

    def own_rows(matrix, size):
        return lax.dynamic_slice_in_dim(matrix, place * size, size, 0)

    up_own = (
        own_rows(up_query, query_width),
        own_rows(key_up_matrix, HEAD_SIZE),
        own_rows(value_up_matrix, HEAD_SIZE),
    )
    up_block = jnp.concatenate(
        [
            jnp.pad(part, ((0, 0), (at * rank, spare - (at + 1) * rank)))
            for at, part in enumerate(up_own)
        ],
        axis=0,
    )
    maps_back = jnp.concatenate(
        [own_rows(feature_query, query_width), own_rows(key_feature_weight, HEAD_SIZE)], axis=0
    )
    maps_ahead = jnp.swapaxes(
        maps_back.reshape(group + 1, HEAD_SIZE, HEAD_SIZE), 1, 2
    ).reshape((group + 1) * HEAD_SIZE, HEAD_SIZE)
    frequency = rope_base ** (-(jnp.arange(HEAD_SIZE // 2, dtype=f32) * 2.0) / HEAD_SIZE)
    phase = jnp.arange(count, dtype=jnp.int32).astype(f32)[None, :] * frequency[:, None]
    cosine, sine = jnp.cos(phase), jnp.sin(phase)
    down_wide = jnp.pad(down_output, ((0, 0), (0, spare - rank)))
    up_wide = jnp.pad(up_output, ((0, 0), (0, spare - rank)))

    q_t, k_t, v_t, keys, values, pq_t, pk_t, key_maps, narrow_t, own_weights_t = project(
        place_row, normed_all, own_weights, down_block, up_block, maps_ahead, cosine, sine
    )
    output_rows = after(output_rows.reshape(lanes * shard, model), q_t)
    output_first = gather_first(output_rows)
    att, out_t, denom, states, att_weights = attend(
        length, q_t, pq_t, keys, key_maps, v_t, rows
    )
    own_gate, own_up, own_down = ungroup(swapped)
    up_weights = lax.all_gather(own_up, "fsdp", axis=0)
    unit = own_down.shape[1] // PARTS
    down_weights = [
        lax.all_gather(own_down[:, part * unit : (part + 1) * unit], "fsdp", axis=0)
        for part in range(PARTS)
    ]
    gate_weights = ring(own_gate)
    chunk_order = lax.rem(lane - jnp.arange(lanes) + lanes, lanes).astype(jnp.int32)
    output_blocks = gather_rest(output_rows, *output_first, att)
    att_all = lax.all_to_all(att, "seq", 0, 0, tiled=True)
    middle = places // 2 + 1
    taught = teach(
        after(length, *output_first, gate_weights[1]), q_t, keys, v_t, att, 0, middle
    )
    residual, normed_ffn, inverse_ffn, narrow_out = branch_out(
        after(place_row, taught[1]), output_blocks, att_all, down_wide, up_wide, tokens[0], gain_ffn
    )
    ffn_first = gather_first(normed_ffn)
    difference, loss_rows = teach(
        after(length, normed_ffn), q_t, keys, v_t, att, middle, places, taught
    )
    ffn_all = gather_rest(normed_ffn, *ffn_first, loss_rows)
    cot_first = gather_first(after(cotangent[0], *ffn_all[6], gate_weights[2]))
    losses = jnp.sum(loss_rows[0].reshape(places, rows), axis=1)
    hidden, by_gate, by_up = hidden_units(chunk_order, ffn_all, gate_weights, up_weights)
    cot_all = gather_rest(cotangent[0], *cot_first, last=(hidden,))
    early = None
    for part in range(PARTS - 1):
        early = ffn_back(
            chunk_order, cot_all, 0, 1, part, gate_weights, up_weights, down_weights[part], by_gate, by_up, early
        )
    by_chip = (places // 2, rows, model)
    last = (PARTS - 1, gate_weights, up_weights, down_weights[-1], by_gate, by_up, early)
    grad_give = ffn_back(chunk_order, cot_all[1::2], 1, 2, *last)
    grad_keep = ffn_back(chunk_order, cot_all[0::2], 0, 2, *last)
    grad_first = scatter_first(grad_give.reshape(by_chip), grad_keep.reshape(by_chip))
    out_part = ffn_out(after(place_row, grad_first[0]), chunk_order, hidden, down_weights, places)

    grad_sums = scatter_rest(*grad_first, out_part)
    grad_att, grad_residual, grad_branch, grad_narrow_out = branch_back(
        place_row,
        output_blocks, grad_sums, residual, inverse_ffn, gain_ffn, cotangent[0],
        down_wide, up_wide,
    )
    out_sum = lax.psum_scatter(out_part, "seq", scatter_dimension=0, tiled=True)
    output = (residual + out_sum.astype(f32)).astype(bf16)
    grad_att = lax.all_to_all(grad_att, "seq", 0, 0, tiled=True)
    grad_up_output = mm_tn(narrow_out, grad_branch)[:rank]
    grad_down_output = jnp.einsum(
        "sft,tr->rsf", att_all, grad_narrow_out[:, :rank].astype(bf16), preferred_element_type=f32
    ).reshape(rank, model)

    grad_pre_t, grad_maps, grad_down_t, normed_give, normed_keep = heads_back(
        length, place_row, normed_all, grad_att, difference, out_t, denom,
        q_t, pq_t, att_weights, values, k_t, pk_t, v_t, states, maps_ahead, maps_back,
        cosine, sine, up_block, own_weights_t,
    )
    normed_sums = scatter_rest(*scatter_first(normed_give, normed_keep))
    grad_up_block = mm_nt(grad_pre_t[:width], narrow_t)
    grad_down_t = grad_down_t[: 3 * rank]
    grad_tokens = tokens_back(
        normed_sums, tokens[0], jnp.broadcast_to(inverse_attn, (rows, spare)),
        gain_attn.reshape(1, model), grad_residual,
    )

    devices = places * lanes
    ahead = jnp.arange(devices)[None, :] >= (jnp.arange(places) * lanes + lane)[:, None]
    running = jnp.sum(jnp.where(ahead, losses[:, None], 0.0), axis=0)
    loss_row = jnp.pad(running[:, None], ((0, 0), (0, model // devices - 1))).reshape(1, model)
    shared = jnp.concatenate([grad_down_t, grad_down_output, grad_up_output, loss_row], axis=0)
    shared = after(jnp.moveaxis(shared.reshape(-1, devices, model // devices), 1, 0), normed_sums[0])
    shared = jnp.sum(
        lax.all_to_all(shared, ("seq", "fsdp"), 0, 0, tiled=True).reshape(shared.shape), axis=0
    )

    def columns(at):
        return shared[at * rank : (at + 1) * rank].T

    transfer_loss = shared[5 * rank, :1] / jnp.sum(lengths).astype(f32)

    pieces = [
        grad_maps[:query_width].reshape(lanes, -1),
        grad_maps[query_width:].reshape(lanes, -1),
        grad_up_block[:query_width, :rank].reshape(lanes, -1),
        grad_up_block[query_width : query_width + HEAD_SIZE, rank : 2 * rank].reshape(lanes, -1),
        grad_up_block[query_width + HEAD_SIZE :, 2 * rank : 3 * rank].reshape(lanes, -1),
    ]
    packed = after(jnp.concatenate(pieces, axis=1), normed_sums[0])
    packed = jnp.sum(lax.all_to_all(packed, "fsdp", 0, 0, tiled=True).reshape(packed.shape), axis=0)
    ends = [0]
    for piece in pieces:
        ends.append(ends[-1] + piece.shape[1])
    map_query, map_key, up_q, up_k, up_v = (
        packed[ends[at] : ends[at + 1]].reshape(-1, wide)
        for at, wide in enumerate((HEAD_SIZE, HEAD_SIZE, rank, rank, rank))
    )
    return (
        output[None],
        grad_tokens[None],
        columns(0),
        up_q,
        columns(1),
        up_k,
        columns(2),
        up_v,
        columns(3),
        columns(4),
        map_query,
        map_key,
        transfer_loss,
    )


def solution(mesh):
    placed = (
        P("fsdp", "seq", None),
        P(),
        P(),
        P(),
        P(("seq", "fsdp"), None),
        P(("seq", "fsdp"), None),
        P(("seq", "fsdp"), None),
        P(("seq", "fsdp"), None),
        P("seq", "fsdp"),
        P("seq", "fsdp"),
        P("seq", "fsdp"),
        P(),
        P(),
        P(),
        P(),
        P(),
        P(),
        P(),
        P(),
        P(),
        P(),
        P("fsdp", "seq", None),
    )
    sizes = dict(mesh.shape)
    heads_match = sizes["seq"] == KEY_VALUE_HEADS == 8 and (
        QUERY_HEADS // KEY_VALUE_HEADS == sizes["fsdp"]
    )
    return jax.shard_map(
        by_heads if heads_match else local,
        mesh=mesh,
        in_specs=placed,
        out_specs=(
            P("fsdp", "seq", None),
            P("fsdp", "seq", None),
            P(("seq", "fsdp"), None),
            P(("seq", "fsdp"), None),
            P(("seq", "fsdp"), None),
            P(("seq", "fsdp"), None),
            P(("seq", "fsdp"), None),
            P(("seq", "fsdp"), None),
            P(("seq", "fsdp"), None),
            P(("seq", "fsdp"), None),
            P(("seq", "fsdp"), None),
            P(("seq", "fsdp"), None),
            P(("seq", "fsdp")),
        ),
        check_vma=False,
    )
```

```python
import functools
import math

import jax
import jax.numpy as jnp
from jax import lax
from jax.experimental import pallas as pl
from jax.experimental.pallas import tpu as pltpu
from jax.sharding import PartitionSpec as P

QUERY_HEADS = 32
KEY_VALUE_HEADS = 8
HEAD_SIZE = 64
WINDOW_KEYS = 64


epsilon = 1e-05
rope_base = 500000.0
precise = lax.Precision.HIGHEST
lowest_precision = -1e30
ONES = 16
SUB = 128
VMEM_MIB = 56
PARTS = 2
COST = 1.15e9


def prefix(x, axis, join, neutral, backward):
    count = lax.axis_size(axis)
    place = lax.axis_index(axis)
    ahead = count - 1 - place if backward else place
    gathered = jax.tree.map(
        lambda a, kind: lax.all_gather(a.astype(kind), axis), x, (jnp.bfloat16, jnp.bfloat16)
    )
    state = jax.tree.map(lambda a, e: jnp.zeros_like(a) + jnp.asarray(e, a.dtype), x, neutral)

    def one(hop, state):
        source = count - 1 - hop if backward else hop
        return join(
            state,
            jax.tree.map(
                lambda a, own: lax.dynamic_index_in_dim(a, source, 0, False).astype(own.dtype),
                gathered,
                x,
            ),
        )

    return lax.fori_loop(0, ahead, one, state)


def as_sent(x):

    def short(part):
        return part.astype(jnp.bfloat16) if part.dtype == jnp.float32 else part

    return jax.tree.map(short, x)


def shifted(value, axis, steps):
    count = lax.axis_size(axis)
    first, last = (max(0, -steps), min(count, count - steps))
    return lax.ppermute(value, axis, [(source, source + steps) for source in range(first, last)])


def rotary(positions):
    half_dim = HEAD_SIZE // 2
    inverse = rope_base ** (-(jnp.arange(half_dim, dtype=jnp.float32) * 2.0) / HEAD_SIZE)
    phase = positions.astype(jnp.float32)[:, None] * inverse[None, :]
    return (jnp.cos(phase)[:, None, :], jnp.sin(phase)[:, None, :])


def apply_rotary(vectors, cosine_lookup, sine_lookup):
    half_dim = vectors.shape[-1] // 2
    first_half = vectors[..., :half_dim]
    second_half = vectors[..., half_dim:]
    return jnp.concatenate(
        [
            first_half * cosine_lookup - second_half * sine_lookup,
            second_half * cosine_lookup + first_half * sine_lookup,
        ],
        axis=-1,
    )


def inverse_rotary(gradient, cosine_lookup, sine_lookup):
    half_dim = gradient.shape[-1] // 2
    first_half = gradient[..., :half_dim]
    second_half = gradient[..., half_dim:]
    return jnp.concatenate(
        [
            first_half * cosine_lookup + second_half * sine_lookup,
            second_half * cosine_lookup - first_half * sine_lookup,
        ],
        axis=-1,
    )


def apply_feature_map(vectors, weights):
    logits_map = jnp.einsum("thd,hde->the", vectors, weights, preferred_element_type=jnp.float32)
    return jnp.concatenate(
        [jax.nn.softmax(logits_map, axis=-1), jax.nn.softmax(-logits_map, axis=-1)], axis=-1
    )


def feature_back(vectors, weights, gradient):
    logits_map = jnp.einsum("thd,hde->the", vectors, weights, preferred_element_type=jnp.float32)
    plus_soft = jax.nn.softmax(logits_map, axis=-1)
    minus_soft = jax.nn.softmax(-logits_map, axis=-1)
    grad_plus = gradient[..., :HEAD_SIZE]
    grad_minus = gradient[..., HEAD_SIZE:]
    grad_logits = plus_soft * (
        grad_plus - jnp.sum(grad_plus * plus_soft, axis=-1, keepdims=True)
    ) - minus_soft * (grad_minus - jnp.sum(grad_minus * minus_soft, axis=-1, keepdims=True))
    grad_vectors = jnp.einsum(
        "the,hde->thd", grad_logits, weights, preferred_element_type=jnp.float32
    )
    grad_weights = jnp.einsum(
        "thd,the->hde", vectors, grad_logits, preferred_element_type=jnp.float32
    )
    return (grad_vectors, grad_weights)


def norm_back(values, inverse, gain, gradient):
    scaled = gradient * gain
    return inverse * scaled - values * inverse * inverse * inverse * jnp.mean(
        scaled * values, axis=-1, keepdims=True
    )


def coefficients(query_rows, query_feature_maps, keys_ext, key_maps, key_valid):
    row_count = query_rows.shape[0]
    key_count = keys_ext.shape[0]
    offset = (
        jnp.arange(row_count)[:, None] + (key_count - row_count) - jnp.arange(key_count)[None, :]
    )
    window = ((offset >= 0) & (offset < WINDOW_KEYS) & key_valid[None, :])[None]
    linear = ((offset >= WINDOW_KEYS) & key_valid[None, :])[None]
    scores = jnp.einsum(
        "tjd,sd->jts", query_rows, keys_ext, preferred_element_type=jnp.float32
    ) / math.sqrt(HEAD_SIZE)
    exp_scores = jnp.exp(scores)
    near_terms = lax.optimization_barrier(exp_scores.astype(jnp.bfloat16)).astype(jnp.float32)
    far_terms = jnp.einsum(
        "tjf,sf->jts", query_feature_maps, key_maps, preferred_element_type=jnp.float32
    )
    weights = jnp.where(window, near_terms, 0.0) + jnp.where(linear, far_terms, 0.0)
    return (weights, exp_scores, window, linear)


def attend_group(operands, key_valid):
    query_rows, query_feature_maps, keys_ext, values_ext, key_maps, carry_state, carry_total = (
        operands
    )
    weights, exp_scores, window, linear = coefficients(
        query_rows, query_feature_maps, keys_ext, key_maps, key_valid
    )
    maps_wide = query_feature_maps.astype(jnp.float32)
    numerator = jnp.einsum(
        "jts,sd->tjd", weights, values_ext.astype(jnp.float32), precision=precise
    ) + jnp.einsum("tjf,fd->tjd", maps_wide, carry_state, precision=precise)
    denominator = jnp.transpose(jnp.sum(weights, axis=-1)) + jnp.einsum(
        "tjf,f->tj", maps_wide, carry_total, precision=precise
    )
    return (numerator, denominator)


def attend_back(operands, key_valid):
    (
        query_rows,
        query_feature_maps,
        keys_ext,
        values_ext,
        key_maps,
        carry_state,
        carry_total,
        numerator,
        denominator,
        grad_out,
    ) = operands
    weights, exp_scores, window, linear = coefficients(
        query_rows, query_feature_maps, keys_ext, key_maps, key_valid
    )
    grad_numer = grad_out / denominator[..., None]
    grad_denom = -jnp.sum(grad_out * numerator, axis=-1) / (denominator * denominator)
    grad_weights = (
        jnp.einsum("tjd,sd->jts", grad_numer, values_ext, preferred_element_type=jnp.float32)
        + jnp.transpose(grad_denom)[:, :, None]
    )
    grad_scores = jnp.where(window, grad_weights * exp_scores, 0.0) / math.sqrt(HEAD_SIZE)
    grad_far = jnp.where(linear, grad_weights, 0.0)
    grad_queries = jnp.einsum(
        "jts,sd->tjd", grad_scores, keys_ext, preferred_element_type=jnp.float32
    )
    grad_keys = jnp.einsum(
        "jts,tjd->sd", grad_scores, query_rows, preferred_element_type=jnp.float32
    )
    grad_qmaps = (
        jnp.einsum("jts,sf->tjf", grad_far, key_maps, preferred_element_type=jnp.float32)
        + jnp.einsum("tjd,fd->tjf", grad_numer, carry_state, preferred_element_type=jnp.float32)
        + grad_denom[..., None] * carry_total
    )
    grad_kmaps = jnp.einsum(
        "jts,tjf->sf", grad_far, query_feature_maps, preferred_element_type=jnp.float32
    )
    grad_values = jnp.einsum("jts,tjd->sd", weights, grad_numer, preferred_element_type=jnp.float32)
    grad_state = jnp.einsum(
        "tjf,tjd->fd", query_feature_maps, grad_numer, preferred_element_type=jnp.float32
    )
    grad_total = jnp.einsum(
        "tjf,tj->f", query_feature_maps, grad_denom, preferred_element_type=jnp.float32
    )
    return (grad_queries, grad_keys, grad_values, grad_qmaps, grad_kmaps, grad_state, grad_total)


def add_pair(earlier, later_part):
    return (earlier[0] + later_part[0], earlier[1] + later_part[1])


def local(
    tokens,
    lengths,
    norm_attn,
    norm_ffn,
    w_query,
    key_projection,
    value_projection,
    w_output,
    w_gate,
    w_up,
    w_down,
    down_query,
    up_query,
    key_down_matrix,
    key_up_matrix,
    value_down_matrix,
    value_up_matrix,
    down_output,
    up_output,
    feature_query,
    key_feature_weight,
    cotangent,
):
    rows_per_block = tokens.shape[1]
    ext_rows = rows_per_block + WINDOW_KEYS
    heads_per_group = QUERY_HEADS // KEY_VALUE_HEADS
    feature_width = 2 * HEAD_SIZE
    inputs_wide = tokens[0].astype(jnp.float32)
    cot_narrow = cotangent[0]
    cot_wide = cot_narrow.astype(jnp.float32)
    seq_index = lax.axis_index("seq")
    lane_length = lengths[lax.axis_index("fsdp")]
    positions = seq_index * rows_per_block + jnp.arange(rows_per_block)
    cosine_lookup, sine_lookup = rotary(positions)
    gain_attn = norm_attn.astype(jnp.float32)
    gain_ffn = norm_ffn.astype(jnp.float32)
    inverse_attn = lax.rsqrt(jnp.mean(inputs_wide * inputs_wide, axis=-1, keepdims=True) + epsilon)
    normed = (inputs_wide * inverse_attn * gain_attn).astype(jnp.bfloat16)
    pieces = (
        lax.all_gather(w_query, ("seq", "fsdp"), axis=0, tiled=True),
        lax.all_gather(key_projection, ("seq", "fsdp"), axis=0, tiled=True),
        lax.all_gather(value_projection, ("seq", "fsdp"), axis=0, tiled=True),
    )
    sliced = normed
    query_pre, key_before_rotation, value_before_adapter = tuple(
        (jnp.dot(sliced, block_piece, preferred_element_type=jnp.float32) for block_piece in pieces)
    )
    narrow_query = jnp.dot(normed, down_query, preferred_element_type=jnp.float32).astype(
        jnp.bfloat16
    )
    narrow_key = jnp.dot(normed, key_down_matrix, preferred_element_type=jnp.float32).astype(
        jnp.bfloat16
    )
    narrow_value = jnp.dot(normed, value_down_matrix, preferred_element_type=jnp.float32).astype(
        jnp.bfloat16
    )
    query_pre = query_pre + jnp.dot(narrow_query, up_query.T, preferred_element_type=jnp.float32)
    key_before_rotation = key_before_rotation + jnp.dot(
        narrow_key, key_up_matrix.T, preferred_element_type=jnp.float32
    )
    value_before_adapter = value_before_adapter + jnp.dot(
        narrow_value, value_up_matrix.T, preferred_element_type=jnp.float32
    )
    query_rows = apply_rotary(
        query_pre.reshape(rows_per_block, QUERY_HEADS, HEAD_SIZE), cosine_lookup, sine_lookup
    ).astype(jnp.bfloat16)
    device_keys = apply_rotary(
        key_before_rotation.reshape(rows_per_block, KEY_VALUE_HEADS, HEAD_SIZE),
        cosine_lookup,
        sine_lookup,
    ).astype(jnp.bfloat16)
    device_values = value_before_adapter.reshape(rows_per_block, KEY_VALUE_HEADS, HEAD_SIZE).astype(
        jnp.bfloat16
    )
    softmax_query_rows = query_rows.reshape(
        rows_per_block, KEY_VALUE_HEADS, heads_per_group, HEAD_SIZE
    )
    teacher_init = (
        jnp.full((KEY_VALUE_HEADS, heads_per_group, rows_per_block), lowest_precision, jnp.float32),
        jnp.zeros((KEY_VALUE_HEADS, heads_per_group, rows_per_block), jnp.float32),
        jnp.zeros((KEY_VALUE_HEADS, heads_per_group, rows_per_block, HEAD_SIZE), jnp.float32),
        jnp.zeros((WINDOW_KEYS, KEY_VALUE_HEADS, HEAD_SIZE), jnp.bfloat16),
        jnp.zeros((WINDOW_KEYS, KEY_VALUE_HEADS, HEAD_SIZE), jnp.bfloat16),
    )
    portion_keys = lax.all_gather(
        device_keys.reshape(rows_per_block, KEY_VALUE_HEADS * HEAD_SIZE), "seq", axis=0, tiled=True
    )
    portion_values = lax.all_gather(
        device_values.reshape(rows_per_block, KEY_VALUE_HEADS * HEAD_SIZE),
        "seq",
        axis=0,
        tiled=True,
    )
    count_of_shards = portion_keys.shape[0] // rows_per_block
    sharded_keys = portion_keys.reshape(count_of_shards, rows_per_block, KEY_VALUE_HEADS, HEAD_SIZE)
    sharded_values = portion_values.reshape(
        count_of_shards, rows_per_block, KEY_VALUE_HEADS, HEAD_SIZE
    )

    def one_shard(inner, item):
        best, total, accum, rim_keys, rim_values = inner
        shard_number, shard_keys, shard_values = item
        shard_start = shard_number * rows_per_block
        scores = jnp.einsum(
            "tgjd,sgd->gjts", softmax_query_rows, shard_keys, preferred_element_type=jnp.float32
        ) / math.sqrt(HEAD_SIZE)
        allowed = (positions[:, None] >= (shard_start + jnp.arange(rows_per_block))[None, :])[
            None, None
        ]
        masked = jnp.where(allowed, scores, lowest_precision)
        new_best = jnp.maximum(best, jnp.max(masked, axis=-1))
        probs = jnp.where(allowed, jnp.exp(masked - new_best[..., None]), 0.0)
        factor = jnp.exp(best - new_best)
        total = total * factor + jnp.sum(probs, axis=-1)
        accum = accum * factor[..., None] + jnp.einsum(
            "gjts,sgd->gjtd", probs, shard_values.astype(jnp.float32)
        )
        is_before = shard_start // rows_per_block == seq_index - 1
        rim_keys = jnp.where(is_before, shard_keys[rows_per_block - WINDOW_KEYS :], rim_keys)
        rim_values = jnp.where(is_before, shard_values[rows_per_block - WINDOW_KEYS :], rim_values)
        return ((new_best, total, accum, rim_keys, rim_values), None)

    result, unused = lax.scan(
        one_shard, teacher_init, (jnp.arange(count_of_shards), sharded_keys, sharded_values)
    )
    best_all, total_all, accum_all, rim_keys, rim_values = result
    teacher = jnp.transpose(accum_all / total_all[..., None], (2, 0, 1, 3)).reshape(
        rows_per_block, QUERY_HEADS * HEAD_SIZE
    )
    keys_ext = jnp.concatenate([rim_keys, device_keys], axis=0)
    values_ext = jnp.concatenate([rim_values, device_values], axis=0)
    query_features = feature_query.reshape(QUERY_HEADS, HEAD_SIZE, HEAD_SIZE)
    key_features = key_feature_weight.reshape(KEY_VALUE_HEADS, HEAD_SIZE, HEAD_SIZE)
    query_feature_maps = apply_feature_map(query_rows, query_features).astype(jnp.bfloat16)
    key_maps = apply_feature_map(keys_ext, key_features).astype(jnp.bfloat16)
    ext_positions = seq_index * rows_per_block - WINDOW_KEYS + jnp.arange(ext_rows)
    key_valid = ext_positions >= 0
    valid_rows = key_valid[:rows_per_block].astype(jnp.float32)
    used_maps = key_maps[:rows_per_block].astype(jnp.float32) * valid_rows[:, None, None]
    values_head = values_ext[:rows_per_block].astype(jnp.float32)
    local_state = jnp.einsum("sgf,sgd->gfd", used_maps, values_head, precision=precise)
    local_total = jnp.sum(used_maps, axis=0)
    zero_pair = (
        jnp.zeros((KEY_VALUE_HEADS, feature_width, HEAD_SIZE), jnp.float32),
        jnp.zeros((KEY_VALUE_HEADS, feature_width), jnp.float32),
    )
    state_in, total_in = prefix((local_state, local_total), "seq", add_pair, zero_pair, False)
    queries_by_group = jnp.moveaxis(
        query_rows.reshape(rows_per_block, KEY_VALUE_HEADS, heads_per_group, HEAD_SIZE), 1, 0
    )
    query_maps_by_group = jnp.moveaxis(
        query_feature_maps.reshape(rows_per_block, KEY_VALUE_HEADS, heads_per_group, feature_width),
        1,
        0,
    )
    grouped_keys = jnp.moveaxis(keys_ext, 1, 0)
    grouped_values = jnp.moveaxis(values_ext, 1, 0)
    grouped_kmaps = jnp.moveaxis(key_maps, 1, 0)

    def forward_group(operands):
        return attend_group(operands, key_valid)

    numerator, denominator = lax.map(
        forward_group,
        (
            queries_by_group,
            query_maps_by_group,
            grouped_keys,
            grouped_values,
            grouped_kmaps,
            state_in,
            total_in,
        ),
    )
    row_mask = (positions < lane_length).astype(jnp.float32)
    attn_mixed = jnp.moveaxis(numerator / denominator[..., None], 0, 1).reshape(
        rows_per_block, QUERY_HEADS * HEAD_SIZE
    )
    attended = (attn_mixed * row_mask[:, None]).astype(jnp.bfloat16)
    difference = attended.astype(jnp.float32) - teacher * row_mask[:, None]
    local_loss = jnp.sum(difference * difference)
    sliced = attended
    branch = jnp.dot(
        sliced,
        lax.all_gather(w_output, ("seq", "fsdp"), axis=0, tiled=True),
        preferred_element_type=jnp.float32,
    )
    narrow_out = jnp.dot(attended, down_output, preferred_element_type=jnp.float32).astype(
        jnp.bfloat16
    )
    branch = branch + jnp.dot(narrow_out, up_output.T, preferred_element_type=jnp.float32)
    residual = inputs_wide + branch
    inverse_ffn = lax.rsqrt(jnp.mean(residual * residual, axis=-1, keepdims=True) + epsilon)
    normed_ffn = (residual * inverse_ffn * gain_ffn).astype(jnp.bfloat16)
    ffn_weights = (
        lax.all_gather(w_gate, "fsdp", axis=1, tiled=True),
        lax.all_gather(w_up, "fsdp", axis=1, tiled=True),
        lax.all_gather(w_down, "fsdp", axis=1, tiled=True),
    )
    pieces = (
        lax.all_gather(ffn_weights[0], "seq", axis=0, tiled=True),
        lax.all_gather(ffn_weights[1], "seq", axis=0, tiled=True),
    )
    sliced = normed_ffn
    gate_pre = jnp.dot(sliced, pieces[0], preferred_element_type=jnp.float32)
    up_pre = jnp.dot(sliced, pieces[1], preferred_element_type=jnp.float32)
    sigmoid_gate = jax.nn.sigmoid(gate_pre)
    silu_gate = gate_pre * sigmoid_gate
    hidden = (silu_gate * up_pre).astype(jnp.bfloat16)
    ffn_part = jnp.dot(
        hidden,
        lax.all_gather(ffn_weights[2], "seq", axis=0, tiled=True).T,
        preferred_element_type=jnp.float32,
    )
    output = (residual + ffn_part).astype(jnp.bfloat16)
    sliced = cot_narrow
    grad_hidden = jnp.dot(
        sliced,
        lax.all_gather(ffn_weights[2], "seq", axis=0, tiled=True),
        preferred_element_type=jnp.float32,
    )
    grad_gate = (
        grad_hidden * up_pre * sigmoid_gate * (1.0 + gate_pre * (1.0 - sigmoid_gate))
    ).astype(jnp.bfloat16)
    grad_up = (grad_hidden * silu_gate).astype(jnp.bfloat16)
    pieces = lax.all_gather((ffn_weights[0], ffn_weights[1]), "seq", axis=0, tiled=True)
    grad_part = jnp.dot(grad_gate, pieces[0].T, preferred_element_type=jnp.float32) + jnp.dot(
        grad_up, pieces[1].T, preferred_element_type=jnp.float32
    )
    grad_residual = cot_wide + norm_back(residual, inverse_ffn, gain_ffn, grad_part)
    grad_branch = grad_residual.astype(jnp.bfloat16)
    grad_narrow_out = jnp.dot(grad_branch, up_output, preferred_element_type=jnp.float32)
    grad_up_output = jnp.dot(grad_branch.T, narrow_out, preferred_element_type=jnp.float32)
    grad_down_output = jnp.dot(attended.T, grad_narrow_out, preferred_element_type=jnp.float32)
    attended_gradient = (
        jnp.dot(
            grad_branch,
            lax.all_gather(w_output, ("seq", "fsdp"), axis=0, tiled=True).T,
            preferred_element_type=jnp.float32,
        )
        + jnp.dot(grad_narrow_out, down_output.T, preferred_element_type=jnp.float32)
        + 2.0 * difference
    )
    attended_gradient = (
        lax.optimization_barrier(attended_gradient.astype(jnp.bfloat16)).astype(jnp.float32)
        * row_mask[:, None]
    )
    gradient_by_group = jnp.moveaxis(
        attended_gradient.reshape(rows_per_block, KEY_VALUE_HEADS, heads_per_group, HEAD_SIZE), 1, 0
    )

    def backward_group(operands):
        return attend_back(operands, key_valid)

    grad_q, grad_k, grad_v, grad_qm, grad_km, grad_state, grad_total = lax.map(
        backward_group,
        (
            queries_by_group,
            query_maps_by_group,
            grouped_keys,
            grouped_values,
            grouped_kmaps,
            state_in,
            total_in,
            numerator,
            denominator,
            gradient_by_group,
        ),
    )
    later_state, later_total = prefix((grad_state, grad_total), "seq", add_pair, zero_pair, True)
    values_grouped_head = jnp.moveaxis(values_head, 1, 0)
    used_grouped = jnp.moveaxis(used_maps, 1, 0)
    kmaps_head = grad_km[:, :rows_per_block] + valid_rows[None, :, None] * (
        jnp.einsum("gfd,gsd->gsf", later_state, values_grouped_head, precision=precise)
        + later_total[:, None, :]
    )
    grad_km = jnp.concatenate([kmaps_head, grad_km[:, rows_per_block:]], axis=1)
    values_grad_head = grad_v[:, :rows_per_block] + jnp.einsum(
        "gsf,gfd->gsd", used_grouped, later_state, precision=precise
    )
    grad_v = jnp.concatenate([values_grad_head, grad_v[:, rows_per_block:]], axis=1)
    grad_k_feat, key_feature_gradient = feature_back(
        keys_ext, key_features, jnp.moveaxis(grad_km, 0, 1)
    )
    gathered_key_gradient = jnp.moveaxis(grad_k, 0, 1) + grad_k_feat
    gathered_value_gradient = jnp.moveaxis(grad_v, 0, 1)
    grad_q_feat, grad_feature_query = feature_back(
        query_rows,
        query_features,
        jnp.moveaxis(grad_qm, 0, 1).reshape(rows_per_block, QUERY_HEADS, feature_width),
    )
    grad_queries_rot = (
        jnp.moveaxis(grad_q, 0, 1).reshape(rows_per_block, QUERY_HEADS, HEAD_SIZE) + grad_q_feat
    )
    back_keys, back_values = (
        shifted(
            gathered_key_gradient[:WINDOW_KEYS]
            .reshape(WINDOW_KEYS, KEY_VALUE_HEADS * HEAD_SIZE)
            .astype(jnp.bfloat16),
            "seq",
            -1,
        ).astype(jnp.float32),
        shifted(
            as_sent(
                gathered_value_gradient[:WINDOW_KEYS].reshape(
                    WINDOW_KEYS, KEY_VALUE_HEADS * HEAD_SIZE
                )
            ),
            "seq",
            -1,
        ),
    )
    trailing_keys = gathered_key_gradient[WINDOW_KEYS:].reshape(
        rows_per_block, KEY_VALUE_HEADS * HEAD_SIZE
    )
    trailing_values = gathered_value_gradient[WINDOW_KEYS:].reshape(
        rows_per_block, KEY_VALUE_HEADS * HEAD_SIZE
    )
    trailing_keys = jnp.concatenate(
        [
            trailing_keys[: rows_per_block - WINDOW_KEYS],
            trailing_keys[rows_per_block - WINDOW_KEYS :] + back_keys,
        ],
        axis=0,
    )
    trailing_values = jnp.concatenate(
        [
            trailing_values[: rows_per_block - WINDOW_KEYS],
            trailing_values[rows_per_block - WINDOW_KEYS :] + back_values,
        ],
        axis=0,
    )
    grad_query_pre = (
        inverse_rotary(grad_queries_rot, cosine_lookup, sine_lookup)
        .reshape(rows_per_block, QUERY_HEADS * HEAD_SIZE)
        .astype(jnp.bfloat16)
    )
    grad_key_pre = (
        inverse_rotary(
            trailing_keys.reshape(rows_per_block, KEY_VALUE_HEADS, HEAD_SIZE),
            cosine_lookup,
            sine_lookup,
        )
        .reshape(rows_per_block, KEY_VALUE_HEADS * HEAD_SIZE)
        .astype(jnp.bfloat16)
    )
    grad_value_pre = trailing_values.astype(jnp.bfloat16)
    grad_narrow_query = jnp.dot(grad_query_pre, up_query, preferred_element_type=jnp.float32)
    grad_narrow_key = jnp.dot(grad_key_pre, key_up_matrix, preferred_element_type=jnp.float32)
    grad_narrow_value = jnp.dot(grad_value_pre, value_up_matrix, preferred_element_type=jnp.float32)
    grad_up_query = jnp.dot(grad_query_pre.T, narrow_query, preferred_element_type=jnp.float32)
    grad_up_key = jnp.dot(grad_key_pre.T, narrow_key, preferred_element_type=jnp.float32)
    grad_up_value = jnp.dot(grad_value_pre.T, narrow_value, preferred_element_type=jnp.float32)
    grad_down_query = jnp.dot(normed.T, grad_narrow_query, preferred_element_type=jnp.float32)
    grad_down_key = jnp.dot(normed.T, grad_narrow_key, preferred_element_type=jnp.float32)
    grad_down_value = jnp.dot(normed.T, grad_narrow_value, preferred_element_type=jnp.float32)
    pieces = lax.all_gather(
        (w_query, key_projection, value_projection), ("seq", "fsdp"), axis=0, tiled=True
    )
    grad_normed = (
        jnp.dot(grad_query_pre, pieces[0].T, preferred_element_type=jnp.float32)
        + jnp.dot(grad_key_pre, pieces[1].T, preferred_element_type=jnp.float32)
        + jnp.dot(grad_value_pre, pieces[2].T, preferred_element_type=jnp.float32)
    )
    grad_normed = grad_normed + jnp.dot(
        grad_narrow_query, down_query.T, preferred_element_type=jnp.float32
    )
    grad_normed = grad_normed + jnp.dot(
        grad_narrow_key, key_down_matrix.T, preferred_element_type=jnp.float32
    )
    grad_normed = grad_normed + jnp.dot(
        grad_narrow_value, value_down_matrix.T, preferred_element_type=jnp.float32
    )
    grad_tokens = (
        grad_residual + norm_back(inputs_wide, inverse_attn, gain_attn, grad_normed)
    ).astype(jnp.bfloat16)
    device_count = lax.axis_size(("seq", "fsdp"))
    device_number = lax.axis_index(("seq", "fsdp"))
    loss_terms = jnp.where(jnp.arange(device_count) >= device_number, local_loss, 0.0)
    summed = (
        lax.psum_scatter(grad_down_query, ("seq", "fsdp"), scatter_dimension=0, tiled=True),
        lax.psum_scatter(grad_up_query, ("seq", "fsdp"), scatter_dimension=0, tiled=True),
        lax.psum_scatter(grad_down_key, ("seq", "fsdp"), scatter_dimension=0, tiled=True),
        lax.psum_scatter(grad_up_key, ("seq", "fsdp"), scatter_dimension=0, tiled=True),
        lax.psum_scatter(grad_down_value, ("seq", "fsdp"), scatter_dimension=0, tiled=True),
        lax.psum_scatter(grad_up_value, ("seq", "fsdp"), scatter_dimension=0, tiled=True),
        lax.psum_scatter(grad_down_output, ("seq", "fsdp"), scatter_dimension=0, tiled=True),
        lax.psum_scatter(grad_up_output, ("seq", "fsdp"), scatter_dimension=0, tiled=True),
        lax.psum_scatter(
            grad_feature_query.reshape(QUERY_HEADS * HEAD_SIZE, HEAD_SIZE),
            ("seq", "fsdp"),
            scatter_dimension=0,
            tiled=True,
        ),
        lax.psum_scatter(
            key_feature_gradient.reshape(KEY_VALUE_HEADS * HEAD_SIZE, HEAD_SIZE),
            ("seq", "fsdp"),
            scatter_dimension=0,
            tiled=True,
        ),
        lax.psum_scatter(loss_terms, ("seq", "fsdp"), scatter_dimension=0, tiled=True),
    )
    transfer_loss = summed[10] / jnp.sum(lengths).astype(jnp.float32)
    return (
        output[None],
        grad_tokens[None],
        summed[0],
        summed[1],
        summed[2],
        summed[3],
        summed[4],
        summed[5],
        summed[6],
        summed[7],
        summed[8],
        summed[9],
        transfer_loss,
    )

def halves_rotated(first_half, second_half, cosine, sine):
    return (
        first_half * cosine - second_half * sine,
        second_half * cosine + first_half * sine,
    )


def soft_pair(logits):
    plus = jnp.exp(logits - jnp.max(logits, axis=0, keepdims=True))
    minus = jnp.exp(jnp.min(logits, axis=0, keepdims=True) - logits)
    plus = plus * (1.0 / jnp.sum(plus, axis=0, keepdims=True))
    minus = minus * (1.0 / jnp.sum(minus, axis=0, keepdims=True))
    return plus, minus


def mm(a, b):
    return jnp.dot(a, b, preferred_element_type=jnp.float32)


def mm_nt(a, b):
    return lax.dot_general(a, b, (((1,), (1,)), ((), ())), preferred_element_type=jnp.float32)


def mm_tn(a, b):
    return lax.dot_general(a, b, (((0,), (0,)), ((), ())), preferred_element_type=jnp.float32)


def split_wide(x):
    high = x.astype(jnp.bfloat16)
    low = (x - high.astype(jnp.float32)).astype(jnp.bfloat16)
    return high, low


ANYWHERE = pl.BlockSpec(memory_space=pltpu.HBM)


def call(kernel, grid, in_specs, out_specs, out_shape, scratch, flops, moved, scalars=0):
    spec = pltpu.PrefetchScalarGridSpec(
        num_scalar_prefetch=scalars,
        grid=grid,
        in_specs=in_specs,
        out_specs=out_specs,
        scratch_shapes=scratch,
    )
    return pl.pallas_call(
        kernel,
        grid_spec=spec,
        out_shape=out_shape,
        compiler_params=pltpu.CompilerParams(vmem_limit_bytes=VMEM_MIB * 2**20),
        cost_estimate=pl.CostEstimate(
            flops=int(COST * moved), bytes_accessed=1, transcendentals=0
        ),
    )


def spec_whole(*dims):
    return pl.BlockSpec(dims, lambda i, *_: (0,) * len(dims))


def spec_across(height, columns):
    return pl.BlockSpec((height, columns), lambda i, *_: (0, i))


def spec_down(rows, wide):
    return pl.BlockSpec((rows, wide), lambda i, *_: (i, 0))


def spec_block(*dims):
    return pl.BlockSpec((None,) + dims, lambda i, *_: (i, 0, 0))


def spec_placed(spec):
    return pl.BlockSpec(
        spec.block_shape,
        lambda i, place_ref, *_: spec.index_map(lax.bitwise_xor(i, place_ref[0])),
    )


def array(*dims, dtype=jnp.bfloat16):
    return jax.ShapeDtypeStruct(dims, dtype)


def flat(found):
    return [part for parts in found for part in parts]


def grouped(refs, counts):
    found, start = [], 0
    for count in counts:
        found.append(tuple(refs[start : start + count]))
        start += count
    return found, refs[start:]


def fetch(refs, buffer, sems, at, order=lambda step: step):
    steps = len(refs)

    def start(step):
        slot = lax.rem(step, 2)
        wanted = order(step)
        for number, parts in enumerate(refs):

            @pl.when(wanted == number)
            def _():
                height = buffer.shape[1] // len(parts)
                for part, ref in enumerate(parts):
                    pltpu.make_async_copy(
                        ref, buffer.at[slot, part * height : (part + 1) * height], sems.at[slot]
                    ).start()

    @pl.when(at == 0)
    def _():
        start(at)

    @pl.when(at + 1 < steps)
    def _():
        start(at + 1)

    slot = lax.rem(at, 2)
    pltpu.make_async_copy(buffer.at[slot], buffer.at[slot], sems.at[slot]).wait()
    return slot


def start_columns(refs, span, buffer, sem):
    first, end = span
    wide = end - first
    for chunk, ref in enumerate(refs):
        pltpu.make_async_copy(
            ref.at[:, first:end], buffer.at[:, chunk * wide : (chunk + 1) * wide], sem
        ).start()


def chunks_of(ref, order_ref):
    return [ref.at[order_ref[chunk]] for chunk in range(ref.shape[0])]


def wait_whole(buffer, sem):
    pltpu.make_async_copy(buffer, buffer, sem).wait()


def block_shape(blocks):
    return sum(part.shape[0] for part in blocks[0]), blocks[0][0].shape[1]


def fetch_scratch(blocks):
    rows, wide = block_shape(blocks)
    return [pltpu.VMEM((2, rows, wide), jnp.bfloat16), pltpu.SemaphoreType.DMA((2,))]


def project_kernel(counts, place_ref, *refs):
    blocks, refs = grouped(refs, counts)
    (
        w_ref, down_ref, up_ref, map_ref, cos_ref, sin_ref,
        q_ref, kt_ref, vt_ref, k_ref, v_ref, pq_ref, pkt_ref, pk_ref, narrow_ref, wt_ref,
        buffer, sems,
    ) = refs
    group = q_ref.shape[0] // HEAD_SIZE
    half = HEAD_SIZE // 2
    width = (group + 2) * HEAD_SIZE
    slot = fetch(blocks, buffer, sems, pl.program_id(0))

    @pl.when(pl.program_id(0) == 0)
    def _():
        lanes, places, shard, _ = w_ref.shape
        for place in range(places):
            rows = jnp.concatenate([w_ref[lane, place] for lane in range(lanes)], axis=0)
            columns = slice(place * lanes * shard, (place + 1) * lanes * shard)
            wt_ref[:width, columns] = jnp.transpose(rows)
        wt_ref[width:] = down_ref[...]

    full = mm_nt(wt_ref[...], buffer[slot])
    narrow = full[width:].astype(jnp.bfloat16)
    narrow_ref[...] = narrow
    pre = full[:width] + mm(up_ref[...], narrow)
    cosine, sine = cos_ref[...], sin_ref[...]
    for head in range(group + 1):
        base = head * HEAD_SIZE
        low_half, high_half = halves_rotated(
            pre[base : base + half], pre[base + half : base + HEAD_SIZE], cosine, sine
        )
        wide = jnp.concatenate([low_half, high_half], axis=0)
        vector = wide.astype(jnp.bfloat16)
        logits = mm(map_ref[base : base + HEAD_SIZE], vector)
        plus, minus = soft_pair(logits)
        maps = jnp.concatenate([plus, minus], axis=0)
        if head < group:
            q_ref[base : base + HEAD_SIZE] = vector
            pq_ref[2 * base : 2 * base + 2 * HEAD_SIZE] = maps.astype(jnp.bfloat16)
        else:
            kt_ref[...] = vector
            k_ref[...] = jnp.transpose(wide).astype(jnp.bfloat16)
            pkt_ref[...] = maps.astype(jnp.bfloat16)
            pk_ref[...] = jnp.transpose(maps).astype(jnp.bfloat16)
    values = pre[width - HEAD_SIZE : width]
    vt_ref[:HEAD_SIZE] = values.astype(jnp.bfloat16)
    vt_ref[HEAD_SIZE:] = jnp.ones((ONES, values.shape[1]), jnp.bfloat16)
    v_ref[...] = jnp.transpose(values).astype(jnp.bfloat16)


def project(place_row, blocks, weights, down_block, up_block, maps_ahead, cosine, sine):
    places = len(blocks)
    rows, model = block_shape(blocks)
    count = places * rows
    width, spare = up_block.shape
    query_width = width - 2 * HEAD_SIZE
    group = query_width // HEAD_SIZE
    maps = 2 * HEAD_SIZE
    half = HEAD_SIZE // 2
    counts = [len(found) for found in blocks]
    outs = [
        (query_width, False),
        (HEAD_SIZE, False),
        (HEAD_SIZE + ONES, False),
        (HEAD_SIZE, True),
        (HEAD_SIZE, True),
        (group * maps, False),
        (maps, False),
        (maps, True),
        (spare, False),
    ]
    return call(
        functools.partial(project_kernel, counts),
        (places,),
        [ANYWHERE] * sum(counts)
        + [
            spec_whole(*weights.shape),
            spec_whole(spare, model),
            spec_whole(width, spare),
            spec_whole(*maps_ahead.shape),
            spec_placed(spec_across(half, rows)),
            spec_placed(spec_across(half, rows)),
        ],
        [
            spec_placed(spec_down(rows, size) if natural else spec_across(size, rows))
            for size, natural in outs
        ]
        + [spec_whole(width + spare, model)],
        [array(count, size) if natural else array(size, count) for size, natural in outs]
        + [array(width + spare, model)],
        fetch_scratch(blocks),
        0,
        17,
        scalars=1,
    )(place_row, *flat(blocks), weights, down_block, up_block, maps_ahead, cosine, sine)


def side_by_side(ref, size, group, columns):
    return jnp.concatenate(
        [ref[head * size : (head + 1) * size, columns] for head in range(group)], axis=1
    )


def bands():
    shape = (WINDOW_KEYS, SUB)
    query_at = lax.broadcasted_iota(jnp.int32, shape, 1)
    key_at = lax.broadcasted_iota(jnp.int32, shape, 0)
    distance = query_at - key_at
    return (
        distance < 0,
        (distance >= 0) & (distance < WINDOW_KEYS),
        distance >= WINDOW_KEYS,
        distance >= WINDOW_KEYS,
    )


def forward_kernel(
    length_ref, q_ref, pq_ref, k_ref, k_before, pk_ref, pk_before, vt_ref, vt_before,
    att_ref, out_ref, denom_ref, states_ref, weights_ref, state,
):
    step = pl.program_id(0)
    group = q_ref.shape[0] // HEAD_SIZE
    rows = q_ref.shape[1]
    quarter = WINDOW_KEYS
    second, third, third_far, fourth = bands()

    @pl.when(step == 0)
    def _():
        state[...] = jnp.zeros_like(state)

    now = state[...]
    for sub in range(rows // SUB):
        columns = slice(sub * SUB, (sub + 1) * SUB)
        queries = side_by_side(q_ref, HEAD_SIZE, group, columns)
        query_maps = side_by_side(pq_ref, 2 * HEAD_SIZE, group, columns)
        if sub == 0:
            keys = jnp.concatenate([k_before[...], k_ref[:SUB]], axis=0)
            key_maps = jnp.concatenate([pk_before[...], pk_ref[:SUB]], axis=0)
            values = jnp.concatenate([vt_before[...], vt_ref[:, :SUB]], axis=1)
        else:
            around = slice((sub - 1) * SUB, (sub + 1) * SUB)
            keys, key_maps, values = k_ref[around], pk_ref[around], vt_ref[:, around]
        scores = mm(keys[quarter:], queries)
        far = mm(key_maps[: 3 * quarter], query_maps)
        pieces = []
        for head in range(group):
            lanes = slice(head * SUB, (head + 1) * SUB)
            near = jnp.exp(scores[:, lanes] * (1.0 / math.sqrt(HEAD_SIZE)))
            away = far[:, lanes]
            before = jnp.concatenate(
                [
                    away[:quarter],
                    jnp.where(second, near[:quarter], away[quarter : 2 * quarter]),
                ],
                axis=0,
            )
            if sub == 0:
                before = jnp.where(step > 0, before, 0.0)
            pieces.append(
                jnp.concatenate(
                    [
                        before,
                        jnp.where(
                            third,
                            near[quarter : 2 * quarter],
                            jnp.where(third_far, away[2 * quarter :], 0.0),
                        ),
                        jnp.where(fourth, near[2 * quarter :], 0.0),
                    ],
                    axis=0,
                ).astype(jnp.bfloat16)
            )
        weights = jnp.concatenate(pieces, axis=1)
        weights_ref[sub] = weights
        states_ref[sub] = now
        high, low = split_wide(now)
        total = mm(values, weights) + mm(
            jnp.concatenate([high, low], axis=1),
            jnp.concatenate([query_maps, query_maps], axis=0),
        )
        denom = total[HEAD_SIZE : HEAD_SIZE + 1]
        out = total[:HEAD_SIZE] * (1.0 / denom)
        at = step * rows + sub * SUB + lax.broadcasted_iota(jnp.int32, (HEAD_SIZE, SUB), 1)
        inside = at < length_ref[0]
        for head in range(group):
            lanes = slice(head * SUB, (head + 1) * SUB)
            base = head * HEAD_SIZE
            out_ref[base : base + HEAD_SIZE, columns] = out[:, lanes]
            att_ref[base : base + HEAD_SIZE, columns] = jnp.where(
                inside, out[:, lanes], 0.0
            ).astype(jnp.bfloat16)
            denom_ref[head : head + 1, columns] = denom[:, lanes]
        update = mm(values[:, :SUB], key_maps[:SUB])
        if sub == 0:
            update = jnp.where(step > 0, update, 0.0)
        now = now + update
    state[...] = now


def before_down(rows, wide):
    per_step = rows // SUB
    return pl.BlockSpec((SUB, wide), lambda i, *_: (jnp.maximum(per_step * i - 1, 0), 0))


def before_across(rows, height):
    per_step = rows // SUB
    return pl.BlockSpec((height, SUB), lambda i, *_: (0, jnp.maximum(per_step * i - 1, 0)))


def attend(length, q_t, pq_t, keys, key_maps, v_t, rows):
    query_width, count = q_t.shape
    group = query_width // HEAD_SIZE
    places = count // rows
    per_step = rows // SUB
    maps = key_maps.shape[1]
    high = v_t.shape[0]
    wide = jnp.float32
    return call(
        forward_kernel,
        (places,),
        [
            spec_across(query_width, rows),
            spec_across(group * maps, rows),
            spec_down(rows, HEAD_SIZE),
            before_down(rows, HEAD_SIZE),
            spec_down(rows, maps),
            before_down(rows, maps),
            spec_across(high, rows),
            before_across(rows, high),
        ],
        [
            spec_block(query_width, rows),
            spec_across(query_width, rows),
            spec_across(group, rows),
            pl.BlockSpec((per_step, high, maps), lambda i, *_: (i, 0, 0)),
            pl.BlockSpec((per_step, 2 * SUB, group * SUB), lambda i, *_: (i, 0, 0)),
        ],
        [
            array(places, query_width, rows),
            array(query_width, count, dtype=wide),
            array(group, count, dtype=wide),
            array(count // SUB, high, maps, dtype=wide),
            array(count // SUB, 2 * SUB, group * SUB),
        ],
        [pltpu.VMEM((high, maps), wide)],
        0,
        10,
        scalars=1,
    )(length, q_t, pq_t, keys, keys, key_maps, key_maps, v_t, v_t)


def teacher_kernel(first, steps, length_ref, q_ref, k_ref, vt_ref, att_ref, *refs):
    diff_ref, loss_ref = refs[-2:]
    step = pl.program_id(0)
    group = q_ref.shape[0] // HEAD_SIZE
    rows = q_ref.shape[1]
    scale = 1.0 / math.sqrt(HEAD_SIZE)
    at = (first + step) * rows + lax.broadcasted_iota(jnp.int32, (HEAD_SIZE, rows), 1)
    inside = at < length_ref[0]
    shape = (rows, rows)
    ahead = lax.broadcasted_iota(jnp.int32, shape, 0) > lax.broadcasted_iota(jnp.int32, shape, 1)

    for blocks in range(first + 1, first + steps + 1):

        @pl.when(first + step == blocks - 1)
        def _():
            size = blocks * rows
            loss = jnp.zeros((1, rows), jnp.float32)
            for head in range(group):
                base = head * HEAD_SIZE
                query = q_ref[base : base + HEAD_SIZE]
                last = jnp.where(ahead, lowest_precision, mm(k_ref[size - rows : size], query))
                best = jnp.max(last, axis=0, keepdims=True)
                if blocks > 1:
                    early = mm(k_ref[: size - rows], query)
                    best = jnp.maximum(best, jnp.max(early, axis=0, keepdims=True))
                total = mm(
                    vt_ref[:, size - rows : size],
                    jnp.exp((last - best) * scale).astype(jnp.bfloat16),
                )
                if blocks > 1:
                    total = total + mm(
                        vt_ref[:, : size - rows],
                        jnp.exp((early - best) * scale).astype(jnp.bfloat16),
                    )
                taught = total[:HEAD_SIZE] * (1.0 / total[HEAD_SIZE : HEAD_SIZE + 1])
                difference = att_ref[base : base + HEAD_SIZE].astype(jnp.float32) - jnp.where(
                    inside, taught, 0.0
                )
                diff_ref[base : base + HEAD_SIZE] = difference
                loss = loss + jnp.sum(difference * difference, axis=0, keepdims=True)
            loss_ref[...] = jnp.broadcast_to(loss, loss_ref.shape)


def teach(length, q_t, keys, v_t, att, first, end, before=None):
    places, query_width, rows = att.shape
    count = places * rows
    wide = jnp.float32

    def ahead(spec):
        return pl.BlockSpec(spec.block_shape, lambda i, *_: spec.index_map(i + first))

    spec = pltpu.PrefetchScalarGridSpec(
        num_scalar_prefetch=1,
        grid=(end - first,),
        in_specs=[
            ahead(spec_across(query_width, rows)),
            spec_whole(*keys.shape),
            spec_whole(*v_t.shape),
            ahead(spec_block(query_width, rows)),
        ]
        + [ANYWHERE] * (2 if before else 0),
        out_specs=[ahead(spec_across(query_width, rows)), ahead(spec_across(8, rows))],
    )
    return pl.pallas_call(
        functools.partial(teacher_kernel, first, end - first),
        grid_spec=spec,
        out_shape=[array(query_width, count, dtype=wide), array(8, count, dtype=wide)],
        input_output_aliases={5: 0, 6: 1} if before else {},
        compiler_params=pltpu.CompilerParams(vmem_limit_bytes=VMEM_MIB * 2**20),
        cost_estimate=pl.CostEstimate(
            flops=int(COST * 16), bytes_accessed=1, transcendentals=0
        ),
    )(length, q_t, keys, v_t, att, *(before or ()))


def hidden_kernel(counts, order_ref, *refs):
    blocks, refs = grouped(refs, counts)
    *gates, ups, hidden_ref, by_gate_ref, by_up_ref, buffer, sems, both, both_sem = refs

    @pl.when(pl.program_id(0) == 0)
    def _():
        unit = ups.shape[2] // PARTS
        wide = ups.shape[0] * unit
        for part in range(PARTS):
            span = part * unit, (part + 1) * unit
            start_columns(gates, span, both.at[:, part * wide : (part + 1) * wide], both_sem)
            start = (PARTS + part) * wide
            start_columns(chunks_of(ups, order_ref), span, both.at[:, start : start + wide], both_sem)

    slot = fetch(blocks, buffer, sems, pl.program_id(0))

    @pl.when(pl.program_id(0) == 0)
    def _():
        wait_whole(both, both_sem)

    full = mm(buffer[slot], both[...])
    wide = full.shape[1] // 2
    gate, up = full[:, :wide], full[:, wide:]
    sigmoid = 1.0 / (1.0 + jnp.exp(-gate))
    silu = gate * sigmoid
    hidden_ref[...] = (silu * up).astype(jnp.bfloat16)
    by_gate_ref[...] = (up * (sigmoid + silu * (1.0 - sigmoid))).astype(jnp.bfloat16)
    by_up_ref[...] = silu.astype(jnp.bfloat16)


def hidden_units(order, blocks, gates, ups):
    rows, model = block_shape(blocks)
    count = rows * len(blocks)
    share = ups.shape[0] * ups.shape[2]
    counts = [len(found) for found in blocks]
    return call(
        functools.partial(hidden_kernel, counts),
        (len(blocks),),
        [ANYWHERE] * (sum(counts) + 1 + len(gates)),
        [spec_down(rows, share)] * 3,
        [array(count, share)] * 3,
        fetch_scratch(blocks)
        + [pltpu.VMEM((model, 2 * share), jnp.bfloat16), pltpu.SemaphoreType.DMA],
        0,
        25,
        scalars=1,
    )(order, *flat(blocks), *gates, ups)


def ffn_back_kernel(counts, chunks, part, more, order_ref, *refs):
    blocks, refs = grouped(refs, counts)
    *gates, ups, downs, by_gate_ref, by_up_ref = refs[: chunks + 4]
    before_ref = refs[chunks + 4] if more else None
    out_ref, buffer, sems, both, both_sem, down, down_sem = refs[-7:]

    @pl.when(pl.program_id(0) == 0)
    def _():
        wide = both.shape[1] // 2
        unit = downs.shape[2]
        span = part * unit, (part + 1) * unit
        start_columns(chunks_of(downs, order_ref), (0, unit), down, down_sem)
        start_columns(gates, span, both.at[:, :wide], both_sem)
        start_columns(chunks_of(ups, order_ref), span, both.at[:, wide:], both_sem)

    slot = fetch(blocks, buffer, sems, pl.program_id(0))

    @pl.when(pl.program_id(0) == 0)
    def _():
        wait_whole(down, down_sem)

    grad_hidden = mm(buffer[slot], down[...])
    grad_gate = (grad_hidden * by_gate_ref[...].astype(jnp.float32)).astype(jnp.bfloat16)
    grad_up = (grad_hidden * by_up_ref[...].astype(jnp.float32)).astype(jnp.bfloat16)

    @pl.when(pl.program_id(0) == 0)
    def _():
        wait_whole(both, both_sem)

    total = mm_nt(jnp.concatenate([grad_gate, grad_up], axis=1), both[...])
    if more:
        total = total + before_ref[...].astype(jnp.float32)
    out_ref[...] = total.astype(jnp.bfloat16)


def ffn_back(order, blocks, first, each, part, gates, ups, downs, by_gate, by_up, before):
    rows, model = block_shape(blocks)
    share = downs.shape[0] * downs.shape[2]
    counts = [len(found) for found in blocks]
    more = before is not None

    def rows_of(wide, at=0):
        return pl.BlockSpec((rows, wide), lambda i, *_: (first + each * i, at))

    return call(
        functools.partial(ffn_back_kernel, counts, len(gates), part, more),
        (len(blocks),),
        [ANYWHERE] * (sum(counts) + len(gates) + 2)
        + [rows_of(share, part)] * 2
        + [rows_of(model)] * more,
        spec_down(rows, model),
        array(len(blocks) * rows, model),
        fetch_scratch(blocks)
        + [pltpu.VMEM((model, 2 * share), jnp.bfloat16), pltpu.SemaphoreType.DMA]
        + [pltpu.VMEM((model, share), jnp.bfloat16), pltpu.SemaphoreType.DMA],
        0,
        3 * len(blocks),
        scalars=1,
    )(order, *flat(blocks), *gates, ups, downs, by_gate, by_up, *([before] if more else []))


def ffn_out_kernel(place_ref, order_ref, *refs):
    downs, (hidden_ref, out_ref, down, down_sem) = refs[:PARTS], refs[PARTS:]

    @pl.when(pl.program_id(0) == 0)
    def _():
        wide = down.shape[1] // PARTS
        for part, ref in enumerate(downs):
            start_columns(
                chunks_of(ref, order_ref), (0, ref.shape[2]), down.at[:, part * wide : (part + 1) * wide], down_sem
            )
        wait_whole(down, down_sem)

    out_ref[...] = mm_nt(hidden_ref[...], down[...]).astype(jnp.bfloat16)


def ffn_out(place_row, order, hidden, downs, places):
    count, share = hidden.shape
    rows = count // places
    model = downs[0].shape[1]
    return call(
        ffn_out_kernel,
        (places,),
        [ANYWHERE] * PARTS + [spec_down(rows, share)],
        spec_placed(spec_down(rows, model)),
        array(count, model),
        [pltpu.VMEM((model, share), jnp.bfloat16), pltpu.SemaphoreType.DMA],
        0,
        17,
        scalars=2,
    )(place_row, order, *downs, hidden)


def backward_kernel(
    counts, length_ref, place_ref, *refs
):
    blocks, refs = grouped(refs, counts)
    (
    grad_ref, diff_ref, out_ref, denom_ref, q_ref, pq_ref, weights_ref,
    v_ref, v_before, kt_ref, kt_before, pkt_ref, pkt_before, vt_ref, vt_before,
    states_ref, map_ref, back_ref, cos_ref, sin_ref, up_ref, wt_ref,
    pre_ref, gain_ref, fall_ref, give_ref, keep_ref, key_carry, value_carry, map_carry, later,
    buffer, sems,
    ) = refs
    step = pl.num_programs(0) - 1 - pl.program_id(0)
    group = q_ref.shape[0] // HEAD_SIZE
    rows = q_ref.shape[1]
    half = HEAD_SIZE // 2
    quarter = WINDOW_KEYS
    scale = 1.0 / math.sqrt(HEAD_SIZE)
    second, third, third_far, fourth = bands()
    short = jnp.bfloat16
    per_block = grad_ref.shape[2]
    inner = per_block // SUB

    @pl.when(pl.program_id(0) == 0)
    def _():
        gain_ref[...] = jnp.zeros_like(gain_ref)
        key_carry[...] = jnp.zeros_like(key_carry)
        value_carry[...] = jnp.zeros_like(value_carry)
        map_carry[...] = jnp.zeros_like(map_carry)
        later[...] = jnp.zeros_like(later)
        fall_ref[...] = jnp.zeros_like(fall_ref)

    carried_keys, carried_values, carried_maps = key_carry[...], value_carry[...], map_carry[...]
    later_now = later[...]
    query_parts, map_parts, key_parts, value_parts, key_map_parts = [], [], [], [], []
    for sub in reversed(range(rows // SUB)):
        columns = slice(sub * SUB, (sub + 1) * SUB)
        queries = side_by_side(q_ref, HEAD_SIZE, group, columns)
        query_maps = side_by_side(pq_ref, 2 * HEAD_SIZE, group, columns)
        if sub == 0:
            values = jnp.concatenate([v_before[...], v_ref[:SUB]], axis=0)
            keys_t = jnp.concatenate([kt_before[...], kt_ref[:, :SUB]], axis=1)
            key_maps_t = jnp.concatenate([pkt_before[...], pkt_ref[:, :SUB]], axis=1)
            values_before = vt_before[...]
        else:
            around = slice((sub - 1) * SUB, (sub + 1) * SUB)
            values = v_ref[around]
            keys_t, key_maps_t = kt_ref[:, around], pkt_ref[:, around]
            values_before = vt_ref[:, (sub - 1) * SUB : sub * SUB]
        at = step * rows + sub * SUB + lax.broadcasted_iota(jnp.int32, (HEAD_SIZE, SUB), 1)
        inside = at < length_ref[0]
        numers, denoms = [], []
        for head in range(group):
            base = head * HEAD_SIZE
            span = slice(base, base + HEAD_SIZE)
            place_in = slice(sub % inner * SUB, (sub % inner + 1) * SUB)
            incoming = grad_ref[sub // inner, span, place_in].astype(jnp.float32) + 2.0 * diff_ref[span, columns]
            incoming = jnp.where(inside, incoming.astype(short).astype(jnp.float32), 0.0)
            inverse = 1.0 / denom_ref[head : head + 1, columns]
            numers.append((incoming * inverse).astype(short))
            denoms.append(
                -jnp.sum(incoming * out_ref[span, columns], axis=0, keepdims=True) * inverse
            )
        grad_numer = jnp.concatenate(numers, axis=1)
        grad_denom = jnp.concatenate(denoms, axis=1)
        rank = lax.broadcasted_iota(jnp.int32, (ONES, group * SUB), 0)
        denom_high = grad_denom.astype(short).astype(jnp.float32)
        extra = jnp.where(
            rank == 0, denom_high, jnp.where(rank == 1, grad_denom - denom_high, 0.0)
        ).astype(short)
        grad_both = jnp.concatenate([grad_numer, extra], axis=0)
        weights = weights_ref[sub]
        raw = mm(values, grad_numer)
        scores, fars = [], []
        for head in range(group):
            lanes = slice(head * SUB, (head + 1) * SUB)
            grad_weights = raw[:, lanes] + denoms[head]
            if sub == 0:
                kept = jnp.where(step > 0, grad_weights[: 2 * quarter], 0.0)
                grad_weights = jnp.concatenate([kept, grad_weights[2 * quarter :]], axis=0)
            by_score = grad_weights[quarter:] * weights[quarter:, lanes].astype(jnp.float32)
            scores.append(
                jnp.concatenate(
                    [
                        jnp.where(second, by_score[:quarter], 0.0),
                        jnp.where(third, by_score[quarter : 2 * quarter], 0.0),
                        jnp.where(fourth, by_score[2 * quarter :], 0.0),
                    ],
                    axis=0,
                ).astype(short)
            )
            fars.append(
                jnp.concatenate(
                    [
                        grad_weights[:quarter],
                        jnp.where(second, 0.0, grad_weights[quarter : 2 * quarter]),
                        jnp.where(third_far, grad_weights[2 * quarter : 3 * quarter], 0.0),
                    ],
                    axis=0,
                ).astype(short)
            )
        grad_scores = jnp.concatenate(scores, axis=1)
        grad_far = jnp.concatenate(fars, axis=1)
        state_high, state_low = split_wide(jnp.transpose(states_ref[sub]))
        query_parts.append(mm(keys_t[:, quarter:], grad_scores) * scale)
        map_parts.append(
            mm(key_maps_t[:, : 3 * quarter], grad_far)
            + mm(
                jnp.concatenate([state_high, state_low], axis=1),
                jnp.concatenate([grad_both, grad_both], axis=0),
            )
        )
        grad_keys = mm_nt(queries, grad_scores) * scale
        grad_values = mm_nt(grad_numer, weights)
        grad_key_maps = mm_nt(query_maps, grad_far)
        key_parts.append(carried_keys + grad_keys[:, quarter:])
        value_parts.append(carried_values + grad_values[:, SUB:])
        key_map_parts.append(
            jnp.concatenate(
                [
                    carried_maps[:, :quarter] + grad_key_maps[:, 2 * quarter :],
                    carried_maps[:, quarter:],
                ],
                axis=1,
            )
        )
        later_high, later_low = split_wide(jnp.transpose(later_now))
        carried_keys = jnp.concatenate(
            [jnp.zeros((HEAD_SIZE, quarter), jnp.float32), grad_keys[:, :quarter]], axis=1
        )
        carried_values = grad_values[:, :SUB] + mm(
            later_now[:HEAD_SIZE].astype(short), key_maps_t[:, :SUB]
        )
        carried_maps = grad_key_maps[:, : 2 * quarter] + mm(
            jnp.concatenate([later_high, later_low], axis=1),
            jnp.concatenate([values_before, values_before], axis=0),
        )
        later_now = later_now + mm_nt(grad_both, query_maps)
    key_carry[...], value_carry[...], map_carry[...] = carried_keys, carried_values, carried_maps
    later[...] = later_now

    def joined(parts, lanes=slice(None)):
        return jnp.concatenate([part[:, lanes] for part in reversed(parts)], axis=1)

    cosine, sine = cos_ref[...], sin_ref[...]
    for head in range(group + 1):
        base = head * HEAD_SIZE
        span = slice(base, base + HEAD_SIZE)
        lanes = slice(head * SUB, (head + 1) * SUB)
        if head < group:
            vector, direct = q_ref[span], joined(query_parts, lanes)
            grad_maps = joined(map_parts, lanes)
        else:
            vector, direct, grad_maps = kt_ref[...], joined(key_parts), joined(key_map_parts)
        plus, minus = soft_pair(mm(map_ref[span], vector))
        grad_plus, grad_minus = grad_maps[:HEAD_SIZE], grad_maps[HEAD_SIZE:]
        grad_logits = plus * (
            grad_plus - jnp.sum(grad_plus * plus, axis=0, keepdims=True)
        ) - minus * (grad_minus - jnp.sum(grad_minus * minus, axis=0, keepdims=True))
        grad_logits = grad_logits.astype(short)
        gain_ref[span] += mm_nt(vector, grad_logits)
        total = direct + mm(back_ref[span], grad_logits)
        low_half, high_half = halves_rotated(total[:half], total[half:], cosine, -sine)
        pre_ref[base : base + half] = low_half.astype(short)
        pre_ref[base + half : base + HEAD_SIZE] = high_half.astype(short)
    width = (group + 2) * HEAD_SIZE
    pre_ref[width - HEAD_SIZE : width] = joined(value_parts).astype(short)
    pre_ref[width:] = mm_tn(up_ref[...], pre_ref[:width]).astype(short)
    per_step = rows // per_block

    def order(at):
        return (pl.num_programs(0) - 1 - at // per_step) * per_step + lax.rem(at, per_step)

    own_core = lax.rem(place_ref[0], 2)
    for block in range(rows // per_block):
        columns = slice(block * per_block, (block + 1) * per_block)
        here = pre_ref[:, columns]
        grad_normed = mm_tn(here, wt_ref[...]).astype(short)
        slot = fetch(
            blocks,
            buffer,
            sems,
            pl.program_id(0) * (rows // per_block) + block,
            lambda at: lax.bitwise_xor(order(at), place_ref[0]),
        )
        fall_ref[...] += mm(here[width:], buffer[slot])

        @pl.when(own_core == block % 2)
        def _():
            keep_ref[...] = grad_normed

        @pl.when(own_core != block % 2)
        def _():
            give_ref[...] = grad_normed


def heads_back(
    length, place_row, blocks, grad_att, difference, out_t, denom, q_t, pq_t, weights,
    values, k_t, pk_t, v_t, states, maps_ahead, maps_back, cosine, sine, up_block, weights_t,
):
    places, query_width, per_block = grad_att.shape
    count = places * per_block
    rows = 2 * per_block
    steps = count // rows
    group = query_width // HEAD_SIZE
    per_step = rows // SUB
    counts = [len(found) for found in blocks]
    width, spare = up_block.shape
    model = weights_t.shape[1]
    maps = pk_t.shape[0]
    high = v_t.shape[0]
    half = HEAD_SIZE // 2

    def back(spec):
        return pl.BlockSpec(spec.block_shape, lambda i, *_: spec.index_map(steps - 1 - i))

    def by_chip(i, length_ref, place_ref):
        return (lax.bitwise_xor(steps - 1 - i, place_ref[0] // 2), 0, 0)

    def leading(*dims):
        return pl.BlockSpec((per_step,) + dims, lambda i, *_: (i, 0, 0))

    return call(
        functools.partial(backward_kernel, counts),
        (steps,),
        [ANYWHERE] * sum(counts)
        + [
            back(pl.BlockSpec((2, query_width, per_block), lambda i, *_: (i, 0, 0))),
            back(spec_across(query_width, rows)),
            back(spec_across(query_width, rows)),
            back(spec_across(group, rows)),
            back(spec_across(query_width, rows)),
            back(spec_across(group * maps, rows)),
            back(leading(2 * SUB, group * SUB)),
            back(spec_down(rows, HEAD_SIZE)),
            back(before_down(rows, HEAD_SIZE)),
            back(spec_across(HEAD_SIZE, rows)),
            back(before_across(rows, HEAD_SIZE)),
            back(spec_across(maps, rows)),
            back(before_across(rows, maps)),
            back(spec_across(high, rows)),
            back(before_across(rows, high)),
            back(leading(high, maps)),
            spec_whole(*maps_ahead.shape),
            spec_whole(*maps_back.shape),
            back(spec_across(half, rows)),
            back(spec_across(half, rows)),
            spec_whole(width, spare),
            spec_whole(width + spare, model),
        ],
        [
            back(spec_across(width + spare, rows)),
            spec_whole(*maps_back.shape),
            spec_whole(spare, model),
            pl.BlockSpec((None, per_block, model), by_chip),
            pl.BlockSpec((None, per_block, model), by_chip),
        ],
        [
            array(width + spare, count),
            array(*maps_back.shape, dtype=jnp.float32),
            array(spare, model, dtype=jnp.float32),
            array(steps, per_block, model),
            array(steps, per_block, model),
        ],
        [
            pltpu.VMEM((HEAD_SIZE, SUB), jnp.float32),
            pltpu.VMEM((HEAD_SIZE, SUB), jnp.float32),
            pltpu.VMEM((maps, SUB), jnp.float32),
            pltpu.VMEM((high, maps), jnp.float32),
        ]
        + fetch_scratch(blocks),
        0,
        30,
        scalars=2,
    )(
        length, place_row, *flat(blocks), grad_att, difference, out_t, denom, q_t, pq_t, weights,
        values, values, k_t, k_t, pk_t, pk_t, v_t, v_t,
        states, maps_ahead, maps_back, cosine, sine, up_block, weights_t,
    )


def start_all(blocks, buffer, sems):
    for number, parts in enumerate(blocks):
        height = buffer.shape[1] // len(parts)
        for part, ref in enumerate(parts):
            pltpu.make_async_copy(
                ref, buffer.at[number, part * height : (part + 1) * height], sems.at[number]
            ).start()


def all_scratch(blocks):
    rows, wide = block_shape(blocks)
    return [
        pltpu.VMEM((len(blocks), rows, wide), jnp.bfloat16),
        pltpu.SemaphoreType.DMA((len(blocks),)),
    ]


def placed_rows(ref, place, rows):
    return ref[pl.ds(pl.multiple_of(place * rows, rows), rows)]


def branch_kernel(counts, place_ref, *refs):
    blocks, refs = grouped(refs, counts)
    (
        att_ref, down_ref, up_ref, tokens_ref, gain_ref,
        residual_ref, normed_ref, inverse_ref, narrow_ref, buffer, sems,
    ) = refs
    start_all(blocks, buffer, sems)
    width = att_ref.shape[1]
    total, slim = tokens_ref[...].astype(jnp.float32), None
    for number in range(len(blocks)):
        place = lax.bitwise_xor(place_ref[0], number)
        att = att_ref[place]
        part = mm_tn(att, placed_rows(down_ref, place, width))
        slim = part if slim is None else slim + part
        wait_whole(buffer.at[number], sems.at[number])
        total = total + mm_tn(att, buffer[number])
    narrow = slim.astype(jnp.bfloat16)
    narrow_ref[...] = narrow
    residual = total + mm_nt(narrow, up_ref[...])
    residual_ref[...] = residual
    inverse = lax.rsqrt(jnp.mean(residual * residual, axis=-1, keepdims=True) + epsilon)
    inverse_ref[...] = jnp.broadcast_to(inverse, inverse_ref.shape)
    normed_ref[...] = (residual * inverse * gain_ref[...]).astype(jnp.bfloat16)


def branch_out(place_row, blocks, att, down_wide, up_wide, tokens, gain):
    places, query_width, rows = att.shape
    model = tokens.shape[1]
    spare = down_wide.shape[1]
    counts = [len(found) for found in blocks]
    wide = jnp.float32
    return call(
        functools.partial(branch_kernel, counts),
        (1,),
        [ANYWHERE] * sum(counts)
        + [spec_whole(*part.shape) for part in (att, down_wide, up_wide, tokens, gain)],
        [
            spec_whole(rows, model),
            spec_whole(rows, model),
            spec_whole(rows, 128),
            spec_whole(rows, spare),
        ],
        [
            array(rows, model, dtype=wide),
            array(rows, model),
            array(rows, 128, dtype=wide),
            array(rows, spare),
        ],
        all_scratch(blocks),
        0,
        13,
        scalars=1,
    )(place_row, *flat(blocks), att, down_wide, up_wide, tokens, gain)


def branch_back_kernel(counts, place_ref, *refs):
    blocks, refs = grouped(refs, counts)
    (
        own_ref, from_x, late_x, late_y, from_y, residual_ref, inverse_ref, gain_ref, cot_ref,
        down_ref, up_ref,
        grad_att_ref, grad_ref, branch_ref, slim_ref, buffer, sems,
    ) = refs
    start_all(blocks, buffer, sems)
    wide = jnp.float32
    middle = late_x.shape[0]
    for start, part in enumerate(sums_of(own_ref, from_x, late_x, late_y, from_y)):
        span = slice(start * middle, (start + 1) * middle)
        residual, inverse = residual_ref[span], inverse_ref[span, :1]
        scaled = part * gain_ref[...]
        mean = jnp.mean(scaled * residual, axis=-1, keepdims=True)
        grad = (
            cot_ref[span].astype(wide)
            + inverse * scaled
            - residual * (inverse * inverse * inverse * mean)
        )
        grad_ref[span] = grad
        branch_ref[span] = grad.astype(jnp.bfloat16)
    branch = branch_ref[...]
    slim = mm(branch, up_ref[...])
    slim_ref[...] = slim
    slim = slim.astype(jnp.bfloat16)
    width = grad_att_ref.shape[1]
    for number in range(len(blocks)):
        place = lax.bitwise_xor(place_ref[0], number)
        part = mm_nt(placed_rows(down_ref, place, width), slim)
        wait_whole(buffer.at[number], sems.at[number])
        grad_att_ref[place] = (mm_nt(buffer[number], branch) + part).astype(jnp.bfloat16)


def branch_back(
    place_row, blocks, sums, residual, inverse, gain, cotangent, down_wide, up_wide
):
    places = len(blocks)
    rows, model = residual.shape
    query_width = model // places
    spare = down_wide.shape[1]
    counts = [len(found) for found in blocks]
    wide = jnp.float32
    given = (*sums, residual, inverse, gain, cotangent, down_wide, up_wide)
    return call(
        functools.partial(branch_back_kernel, counts),
        (1,),
        [ANYWHERE] * sum(counts) + [spec_whole(*part.shape) for part in given],
        [
            spec_whole(places, query_width, rows),
            spec_whole(rows, model),
            spec_whole(rows, model),
            spec_whole(rows, spare),
        ],
        [
            array(places, query_width, rows),
            array(rows, model, dtype=wide),
            array(rows, model),
            array(rows, spare, dtype=wide),
        ],
        all_scratch(blocks),
        0,
        15,
        scalars=1,
    )(place_row, *flat(blocks), *given)


def exchanged(value, bits):
    count = lax.axis_size("seq")
    return lax.ppermute(value, "seq", [(place, place ^ bits) for place in range(count)])


def after(value, *others):
    return pl.pallas_call(
        lambda *refs: None,
        out_shape=jax.ShapeDtypeStruct(value.shape, value.dtype),
        in_specs=[pl.BlockSpec(memory_space=pl.ANY)] * (1 + len(others)),
        out_specs=pl.BlockSpec(memory_space=pl.ANY),
        input_output_aliases={0: 0},
    )(value, *others)


def halves(value):
    middle = value.shape[0] // 2
    return value[:middle], value[middle:]


def regroup_kernel(*refs):
    out_ref = refs[-1]
    for number, ref in enumerate(refs[:-1]):
        out_ref[number] = ref[...]


def regroup(places, *matrices):
    rows, wide = matrices[0].shape
    unit = wide // places
    return call(
        regroup_kernel,
        (places,),
        [spec_across(rows, unit)] * len(matrices),
        pl.BlockSpec((None, len(matrices), rows, unit), lambda i: (i, 0, 0, 0)),
        array(places, len(matrices), rows, unit),
        [],
        0,
        6,
    )(*matrices)


def ungroup_kernel(ref, *refs):
    for number, out_ref in enumerate(refs):
        out_ref[...] = ref[number]


def ungroup(blocks):
    places, count, rows, unit = blocks.shape
    return call(
        ungroup_kernel,
        (places,),
        [pl.BlockSpec((None, count, rows, unit), lambda i: (i, 0, 0, 0))],
        [spec_down(rows, unit)] * count,
        [array(places * rows, unit)] * count,
        [],
        0,
        6,
    )(blocks)


def gather_first(value):
    return exchanged(value, 1), exchanged(value, 2), exchanged(value, 4)


def gather_rest(value, beside, along_x, along_y, *others, last=()):
    upper, lower = halves(along_x)[0], halves(along_y)[1]
    if others:
        upper, lower = after(upper, *others), after(lower, *others)
    first, second = exchanged(upper, 4), exchanged(lower, 2)
    if last:
        first, second = after(first, *last), after(second, *last)
    return [
        (value,),
        (beside,),
        (along_x,),
        (exchanged(along_x, 1),),
        (along_y,),
        (exchanged(along_y, 1),),
        (first, second),
        (exchanged(first, 1), exchanged(second, 1)),
    ]


def plane_gather(value):
    return gather_rest(value, *gather_first(value))


def core_sums_kernel(keep_ref, got_ref, own_ref, to_x, to_y, later_x, later_y):
    wide, short = jnp.float32, jnp.bfloat16
    middle = later_x.shape[0]

    def both(bits, span=slice(None)):
        return keep_ref[bits, span].astype(wide) + got_ref[bits, span].astype(wide)

    upper, lower = slice(0, middle), slice(middle, None)
    own_ref[...] = both(0)
    to_x[upper], to_x[lower] = both(3, upper).astype(short), both(1, upper).astype(short)
    to_y[upper], to_y[lower] = both(3, lower).astype(short), both(2, lower).astype(short)
    later_x[...] = both(1, lower).astype(short)
    later_y[...] = both(2, upper).astype(short)


def core_sums(keep, got):
    _, rows, model = keep.shape
    wide = model // 2
    block = pl.BlockSpec((4, rows, wide), lambda i: (0, 0, i))
    return call(
        core_sums_kernel,
        (2,),
        [block] * 2,
        [spec_across(rows, wide)] * 3 + [spec_across(rows // 2, wide)] * 2,
        [array(rows, model, dtype=jnp.float32)]
        + [array(rows, model)] * 2
        + [array(rows // 2, model)] * 2,
        [],
        0,
        5,
    )(keep, got)


def scatter_first(give, keep):
    own, to_x, to_y, later_x, later_y = core_sums(keep, exchanged(give, 1))
    return own, exchanged(to_x, 2), exchanged(to_y, 4), later_x, later_y


def scatter_rest(own, from_x, from_y, later_x, later_y, *others):
    middle = later_x.shape[0]
    wide, short = jnp.float32, jnp.bfloat16
    if others:
        later_x, later_y = after(later_x, *others), after(later_y, *others)
    late_y = exchanged((later_y.astype(wide) + from_x[:middle].astype(wide)).astype(short), 4)
    late_x = exchanged((later_x.astype(wide) + from_y[:middle].astype(wide)).astype(short), 2)
    return own, from_x, late_x, late_y, from_y


def sums_of(own_ref, from_x, late_x, late_y, from_y):
    wide = jnp.float32
    middle = late_x.shape[0]
    return (
        own_ref[:middle] + from_x[middle:].astype(wide) + late_y[...].astype(wide),
        own_ref[middle:] + late_x[...].astype(wide) + from_y[middle:].astype(wide),
    )


def tokens_back_kernel(
    own_ref, from_x, late_x, late_y, from_y, tokens_ref, inverse_ref, gain_ref, grad_ref, out_ref
):
    middle = late_x.shape[0]
    for start, part in enumerate(sums_of(own_ref, from_x, late_x, late_y, from_y)):
        span = slice(start * middle, (start + 1) * middle)
        values, inverse = tokens_ref[span].astype(jnp.float32), inverse_ref[span, :1]
        scaled = part * gain_ref[...]
        mean = jnp.mean(scaled * values, axis=-1, keepdims=True)
        out_ref[span] = (
            grad_ref[span] + inverse * scaled - values * (inverse * inverse * inverse * mean)
        ).astype(jnp.bfloat16)


def tokens_back(sums, tokens, inverse, gain, grad):
    rows, model = tokens.shape
    return call(
        tokens_back_kernel,
        (1,),
        [spec_whole(*part.shape) for part in (*sums, tokens, inverse, gain, grad)],
        spec_whole(rows, model),
        array(rows, model),
        [],
        0,
        6,
    )(*sums, tokens, inverse, gain, grad)


def ring(value):
    count = lax.axis_size("fsdp")
    found = [value]
    for _ in range(count - 1):
        found.append(ring_step(found[-1]))
    return found


def ring_step(value):
    count = lax.axis_size("fsdp")
    return lax.ppermute(value, "fsdp", [(at, (at + 1) % count) for at in range(count)])


def by_heads(
    tokens,
    lengths,
    norm_attn,
    norm_ffn,
    w_query,
    key_projection,
    value_projection,
    w_output,
    w_gate,
    w_up,
    w_down,
    down_query,
    up_query,
    key_down_matrix,
    key_up_matrix,
    value_down_matrix,
    value_up_matrix,
    down_output,
    up_output,
    feature_query,
    key_feature_weight,
    cotangent,
):
    places = lax.axis_size("seq")
    lanes = lax.axis_size("fsdp")
    rows = tokens.shape[1]
    model = tokens.shape[2]
    count = rows * places
    group = QUERY_HEADS // KEY_VALUE_HEADS
    query_width = group * HEAD_SIZE
    width = query_width + 2 * HEAD_SIZE
    rank = down_query.shape[1]
    spare = 128
    place = lax.axis_index("seq")
    lane = lax.axis_index("fsdp")
    place_row = place.astype(jnp.int32).reshape(1)
    length = lax.dynamic_slice_in_dim(lengths, lane, 1)
    bf16, f32 = jnp.bfloat16, jnp.float32
    inputs_wide = tokens[0].astype(f32)
    gain_attn = norm_attn.astype(f32)
    gain_ffn = norm_ffn.astype(f32).reshape(1, model)

    shard = w_query.shape[0]
    by_place = jnp.concatenate(
        [
            w_query.reshape(shard, places, query_width),
            key_projection.reshape(shard, places, HEAD_SIZE),
            value_projection.reshape(shard, places, HEAD_SIZE),
        ],
        axis=2,
    )
    by_place = lax.all_to_all(jnp.moveaxis(by_place, 1, 0), "seq", 0, 0, tiled=True)
    own_weights = lax.all_gather(by_place, "fsdp", axis=0)

    inverse_attn = lax.rsqrt(jnp.mean(inputs_wide * inputs_wide, axis=-1, keepdims=True) + epsilon)
    normed_all = plane_gather((inputs_wide * inverse_attn * gain_attn).astype(bf16))
    across = normed_all[6]
    down_block = jnp.concatenate(
        [
            down_query.T,
            key_down_matrix.T,
            value_down_matrix.T,
            jnp.zeros((spare - 3 * rank, model), bf16),
        ],
        axis=0,
    )

    output_rows = lax.all_gather(w_output, "fsdp", axis=0)
    swapped = after(regroup(places, w_gate, w_up, w_down), by_place)
    swapped = lax.all_to_all(swapped, "seq", 0, 0, tiled=True)

    def own_rows(matrix, size):
        return lax.dynamic_slice_in_dim(matrix, place * size, size, 0)

    up_own = (
        own_rows(up_query, query_width),
        own_rows(key_up_matrix, HEAD_SIZE),
        own_rows(value_up_matrix, HEAD_SIZE),
    )
    up_block = jnp.concatenate(
        [
            jnp.pad(part, ((0, 0), (at * rank, spare - (at + 1) * rank)))
            for at, part in enumerate(up_own)
        ],
        axis=0,
    )
    maps_back = jnp.concatenate(
        [own_rows(feature_query, query_width), own_rows(key_feature_weight, HEAD_SIZE)], axis=0
    )
    maps_ahead = jnp.swapaxes(
        maps_back.reshape(group + 1, HEAD_SIZE, HEAD_SIZE), 1, 2
    ).reshape((group + 1) * HEAD_SIZE, HEAD_SIZE)
    frequency = rope_base ** (-(jnp.arange(HEAD_SIZE // 2, dtype=f32) * 2.0) / HEAD_SIZE)
    phase = jnp.arange(count, dtype=jnp.int32).astype(f32)[None, :] * frequency[:, None]
    cosine, sine = jnp.cos(phase), jnp.sin(phase)
    down_wide = jnp.pad(down_output, ((0, 0), (0, spare - rank)))
    up_wide = jnp.pad(up_output, ((0, 0), (0, spare - rank)))

    q_t, k_t, v_t, keys, values, pq_t, pk_t, key_maps, narrow_t, own_weights_t = project(
        place_row, normed_all, own_weights, down_block, up_block, maps_ahead, cosine, sine
    )
    output_rows = after(output_rows.reshape(lanes * shard, model), q_t)
    output_first = gather_first(output_rows)
    att, out_t, denom, states, att_weights = attend(
        length, q_t, pq_t, keys, key_maps, v_t, rows
    )
    own_gate, own_up, own_down = ungroup(swapped)
    up_weights = lax.all_gather(own_up, "fsdp", axis=0)
    unit = own_down.shape[1] // PARTS
    down_weights = [
        lax.all_gather(own_down[:, part * unit : (part + 1) * unit], "fsdp", axis=0)
        for part in range(PARTS)
    ]
    gate_weights = ring(own_gate)
    chunk_order = lax.rem(lane - jnp.arange(lanes) + lanes, lanes).astype(jnp.int32)
    output_blocks = gather_rest(output_rows, *output_first, att)
    att_all = lax.all_to_all(att, "seq", 0, 0, tiled=True)
    middle = places // 2 + 1
    taught = teach(
        after(length, *output_first, gate_weights[1]), q_t, keys, v_t, att, 0, middle
    )
    residual, normed_ffn, inverse_ffn, narrow_out = branch_out(
        after(place_row, taught[1]), output_blocks, att_all, down_wide, up_wide, tokens[0], gain_ffn
    )
    ffn_first = gather_first(normed_ffn)
    difference, loss_rows = teach(
        after(length, normed_ffn), q_t, keys, v_t, att, middle, places, taught
    )
    ffn_all = gather_rest(normed_ffn, *ffn_first, loss_rows)
    cot_first = gather_first(after(cotangent[0], *ffn_all[6], gate_weights[2]))
    losses = jnp.sum(loss_rows[0].reshape(places, rows), axis=1)
    hidden, by_gate, by_up = hidden_units(chunk_order, ffn_all, gate_weights, up_weights)
    cot_all = gather_rest(cotangent[0], *cot_first, last=(hidden,))
    early = None
    for part in range(PARTS - 1):
        early = ffn_back(
            chunk_order, cot_all, 0, 1, part, gate_weights, up_weights, down_weights[part], by_gate, by_up, early
        )
    by_chip = (places // 2, rows, model)
    last = (PARTS - 1, gate_weights, up_weights, down_weights[-1], by_gate, by_up, early)
    grad_give = ffn_back(chunk_order, cot_all[1::2], 1, 2, *last)
    grad_keep = ffn_back(chunk_order, cot_all[0::2], 0, 2, *last)
    grad_first = scatter_first(grad_give.reshape(by_chip), grad_keep.reshape(by_chip))
    out_part = ffn_out(after(place_row, grad_first[0]), chunk_order, hidden, down_weights, places)

    grad_sums = scatter_rest(*grad_first, out_part)
    grad_att, grad_residual, grad_branch, grad_narrow_out = branch_back(
        place_row,
        output_blocks, grad_sums, residual, inverse_ffn, gain_ffn, cotangent[0],
        down_wide, up_wide,
    )
    out_sum = lax.psum_scatter(out_part, "seq", scatter_dimension=0, tiled=True)
    output = (residual + out_sum.astype(f32)).astype(bf16)
    grad_att = lax.all_to_all(grad_att, "seq", 0, 0, tiled=True)
    grad_up_output = mm_tn(narrow_out, grad_branch)[:rank]
    grad_down_output = jnp.einsum(
        "sft,tr->rsf", att_all, grad_narrow_out[:, :rank].astype(bf16), preferred_element_type=f32
    ).reshape(rank, model)

    grad_pre_t, grad_maps, grad_down_t, normed_give, normed_keep = heads_back(
        length, place_row, normed_all, grad_att, difference, out_t, denom,
        q_t, pq_t, att_weights, values, k_t, pk_t, v_t, states, maps_ahead, maps_back,
        cosine, sine, up_block, own_weights_t,
    )
    normed_sums = scatter_rest(*scatter_first(normed_give, normed_keep))
    grad_up_block = mm_nt(grad_pre_t[:width], narrow_t)
    grad_down_t = grad_down_t[: 3 * rank]
    grad_tokens = tokens_back(
        normed_sums, tokens[0], jnp.broadcast_to(inverse_attn, (rows, spare)),
        gain_attn.reshape(1, model), grad_residual,
    )

    devices = places * lanes
    ahead = jnp.arange(devices)[None, :] >= (jnp.arange(places) * lanes + lane)[:, None]
    running = jnp.sum(jnp.where(ahead, losses[:, None], 0.0), axis=0)
    loss_row = jnp.pad(running[:, None], ((0, 0), (0, model // devices - 1))).reshape(1, model)
    shared = jnp.concatenate([grad_down_t, grad_down_output, grad_up_output, loss_row], axis=0)
    shared = after(jnp.moveaxis(shared.reshape(-1, devices, model // devices), 1, 0), normed_sums[0])
    shared = jnp.sum(
        lax.all_to_all(shared, ("seq", "fsdp"), 0, 0, tiled=True).reshape(shared.shape), axis=0
    )

    def columns(at):
        return shared[at * rank : (at + 1) * rank].T

    transfer_loss = shared[5 * rank, :1] / jnp.sum(lengths).astype(f32)

    pieces = [
        grad_maps[:query_width].reshape(lanes, -1),
        grad_maps[query_width:].reshape(lanes, -1),
        grad_up_block[:query_width, :rank].reshape(lanes, -1),
        grad_up_block[query_width : query_width + HEAD_SIZE, rank : 2 * rank].reshape(lanes, -1),
        grad_up_block[query_width + HEAD_SIZE :, 2 * rank : 3 * rank].reshape(lanes, -1),
    ]
    packed = after(jnp.concatenate(pieces, axis=1), normed_sums[0])
    packed = jnp.sum(lax.all_to_all(packed, "fsdp", 0, 0, tiled=True).reshape(packed.shape), axis=0)
    ends = [0]
    for piece in pieces:
        ends.append(ends[-1] + piece.shape[1])
    map_query, map_key, up_q, up_k, up_v = (
        packed[ends[at] : ends[at + 1]].reshape(-1, wide)
        for at, wide in enumerate((HEAD_SIZE, HEAD_SIZE, rank, rank, rank))
    )
    return (
        output[None],
        grad_tokens[None],
        columns(0),
        up_q,
        columns(1),
        up_k,
        columns(2),
        up_v,
        columns(3),
        columns(4),
        map_query,
        map_key,
        transfer_loss,
    )


def solution(mesh):
    placed = (
        P("fsdp", "seq", None),
        P(),
        P(),
        P(),
        P(("seq", "fsdp"), None),
        P(("seq", "fsdp"), None),
        P(("seq", "fsdp"), None),
        P(("seq", "fsdp"), None),
        P("seq", "fsdp"),
        P("seq", "fsdp"),
        P("seq", "fsdp"),
        P(),
        P(),
        P(),
        P(),
        P(),
        P(),
        P(),
        P(),
        P(),
        P(),
        P("fsdp", "seq", None),
    )
    sizes = dict(mesh.shape)
    heads_match = sizes["seq"] == KEY_VALUE_HEADS == 8 and (
        QUERY_HEADS // KEY_VALUE_HEADS == sizes["fsdp"]
    )
    return jax.shard_map(
        by_heads if heads_match else local,
        mesh=mesh,
        in_specs=placed,
        out_specs=(
            P("fsdp", "seq", None),
            P("fsdp", "seq", None),
            P(("seq", "fsdp"), None),
            P(("seq", "fsdp"), None),
            P(("seq", "fsdp"), None),
            P(("seq", "fsdp"), None),
            P(("seq", "fsdp"), None),
            P(("seq", "fsdp"), None),
            P(("seq", "fsdp"), None),
            P(("seq", "fsdp"), None),
            P(("seq", "fsdp"), None),
            P(("seq", "fsdp"), None),
            P(("seq", "fsdp")),
        ),
        check_vma=False,
    )
```

```python
import functools
import math

import jax
import jax.numpy as jnp
from jax import lax
from jax.experimental import pallas as pl
from jax.experimental.pallas import tpu as pltpu
from jax.sharding import PartitionSpec as P

QUERY_HEADS = 32
KEY_VALUE_HEADS = 8
HEAD_SIZE = 64
WINDOW_KEYS = 64


epsilon = 1e-05
rope_base = 500000.0
precise = lax.Precision.HIGHEST
lowest_precision = -1e30
ONES = 16
SUB = 128
VMEM_MIB = 56
PARTS = 2
PAIR = 2
COST = 1.15e9


def prefix(x, axis, join, neutral, backward):
    count = lax.axis_size(axis)
    place = lax.axis_index(axis)
    ahead = count - 1 - place if backward else place
    gathered = jax.tree.map(
        lambda a, kind: lax.all_gather(a.astype(kind), axis), x, (jnp.bfloat16, jnp.bfloat16)
    )
    state = jax.tree.map(lambda a, e: jnp.zeros_like(a) + jnp.asarray(e, a.dtype), x, neutral)

    def one(hop, state):
        source = count - 1 - hop if backward else hop
        return join(
            state,
            jax.tree.map(
                lambda a, own: lax.dynamic_index_in_dim(a, source, 0, False).astype(own.dtype),
                gathered,
                x,
            ),
        )

    return lax.fori_loop(0, ahead, one, state)


def as_sent(x):

    def short(part):
        return part.astype(jnp.bfloat16) if part.dtype == jnp.float32 else part

    return jax.tree.map(short, x)


def shifted(value, axis, steps):
    count = lax.axis_size(axis)
    first, last = (max(0, -steps), min(count, count - steps))
    return lax.ppermute(value, axis, [(source, source + steps) for source in range(first, last)])


def rotary(positions):
    half_dim = HEAD_SIZE // 2
    inverse = rope_base ** (-(jnp.arange(half_dim, dtype=jnp.float32) * 2.0) / HEAD_SIZE)
    phase = positions.astype(jnp.float32)[:, None] * inverse[None, :]
    return (jnp.cos(phase)[:, None, :], jnp.sin(phase)[:, None, :])


def apply_rotary(vectors, cosine_lookup, sine_lookup):
    half_dim = vectors.shape[-1] // 2
    first_half = vectors[..., :half_dim]
    second_half = vectors[..., half_dim:]
    return jnp.concatenate(
        [
            first_half * cosine_lookup - second_half * sine_lookup,
            second_half * cosine_lookup + first_half * sine_lookup,
        ],
        axis=-1,
    )


def inverse_rotary(gradient, cosine_lookup, sine_lookup):
    half_dim = gradient.shape[-1] // 2
    first_half = gradient[..., :half_dim]
    second_half = gradient[..., half_dim:]
    return jnp.concatenate(
        [
            first_half * cosine_lookup + second_half * sine_lookup,
            second_half * cosine_lookup - first_half * sine_lookup,
        ],
        axis=-1,
    )


def apply_feature_map(vectors, weights):
    logits_map = jnp.einsum("thd,hde->the", vectors, weights, preferred_element_type=jnp.float32)
    return jnp.concatenate(
        [jax.nn.softmax(logits_map, axis=-1), jax.nn.softmax(-logits_map, axis=-1)], axis=-1
    )


def feature_back(vectors, weights, gradient):
    logits_map = jnp.einsum("thd,hde->the", vectors, weights, preferred_element_type=jnp.float32)
    plus_soft = jax.nn.softmax(logits_map, axis=-1)
    minus_soft = jax.nn.softmax(-logits_map, axis=-1)
    grad_plus = gradient[..., :HEAD_SIZE]
    grad_minus = gradient[..., HEAD_SIZE:]
    grad_logits = plus_soft * (
        grad_plus - jnp.sum(grad_plus * plus_soft, axis=-1, keepdims=True)
    ) - minus_soft * (grad_minus - jnp.sum(grad_minus * minus_soft, axis=-1, keepdims=True))
    grad_vectors = jnp.einsum(
        "the,hde->thd", grad_logits, weights, preferred_element_type=jnp.float32
    )
    grad_weights = jnp.einsum(
        "thd,the->hde", vectors, grad_logits, preferred_element_type=jnp.float32
    )
    return (grad_vectors, grad_weights)


def norm_back(values, inverse, gain, gradient):
    scaled = gradient * gain
    return inverse * scaled - values * inverse * inverse * inverse * jnp.mean(
        scaled * values, axis=-1, keepdims=True
    )


def coefficients(query_rows, query_feature_maps, keys_ext, key_maps, key_valid):
    row_count = query_rows.shape[0]
    key_count = keys_ext.shape[0]
    offset = (
        jnp.arange(row_count)[:, None] + (key_count - row_count) - jnp.arange(key_count)[None, :]
    )
    window = ((offset >= 0) & (offset < WINDOW_KEYS) & key_valid[None, :])[None]
    linear = ((offset >= WINDOW_KEYS) & key_valid[None, :])[None]
    scores = jnp.einsum(
        "tjd,sd->jts", query_rows, keys_ext, preferred_element_type=jnp.float32
    ) / math.sqrt(HEAD_SIZE)
    exp_scores = jnp.exp(scores)
    near_terms = lax.optimization_barrier(exp_scores.astype(jnp.bfloat16)).astype(jnp.float32)
    far_terms = jnp.einsum(
        "tjf,sf->jts", query_feature_maps, key_maps, preferred_element_type=jnp.float32
    )
    weights = jnp.where(window, near_terms, 0.0) + jnp.where(linear, far_terms, 0.0)
    return (weights, exp_scores, window, linear)


def attend_group(operands, key_valid):
    query_rows, query_feature_maps, keys_ext, values_ext, key_maps, carry_state, carry_total = (
        operands
    )
    weights, exp_scores, window, linear = coefficients(
        query_rows, query_feature_maps, keys_ext, key_maps, key_valid
    )
    maps_wide = query_feature_maps.astype(jnp.float32)
    numerator = jnp.einsum(
        "jts,sd->tjd", weights, values_ext.astype(jnp.float32), precision=precise
    ) + jnp.einsum("tjf,fd->tjd", maps_wide, carry_state, precision=precise)
    denominator = jnp.transpose(jnp.sum(weights, axis=-1)) + jnp.einsum(
        "tjf,f->tj", maps_wide, carry_total, precision=precise
    )
    return (numerator, denominator)


def attend_back(operands, key_valid):
    (
        query_rows,
        query_feature_maps,
        keys_ext,
        values_ext,
        key_maps,
        carry_state,
        carry_total,
        numerator,
        denominator,
        grad_out,
    ) = operands
    weights, exp_scores, window, linear = coefficients(
        query_rows, query_feature_maps, keys_ext, key_maps, key_valid
    )
    grad_numer = grad_out / denominator[..., None]
    grad_denom = -jnp.sum(grad_out * numerator, axis=-1) / (denominator * denominator)
    grad_weights = (
        jnp.einsum("tjd,sd->jts", grad_numer, values_ext, preferred_element_type=jnp.float32)
        + jnp.transpose(grad_denom)[:, :, None]
    )
    grad_scores = jnp.where(window, grad_weights * exp_scores, 0.0) / math.sqrt(HEAD_SIZE)
    grad_far = jnp.where(linear, grad_weights, 0.0)
    grad_queries = jnp.einsum(
        "jts,sd->tjd", grad_scores, keys_ext, preferred_element_type=jnp.float32
    )
    grad_keys = jnp.einsum(
        "jts,tjd->sd", grad_scores, query_rows, preferred_element_type=jnp.float32
    )
    grad_qmaps = (
        jnp.einsum("jts,sf->tjf", grad_far, key_maps, preferred_element_type=jnp.float32)
        + jnp.einsum("tjd,fd->tjf", grad_numer, carry_state, preferred_element_type=jnp.float32)
        + grad_denom[..., None] * carry_total
    )
    grad_kmaps = jnp.einsum(
        "jts,tjf->sf", grad_far, query_feature_maps, preferred_element_type=jnp.float32
    )
    grad_values = jnp.einsum("jts,tjd->sd", weights, grad_numer, preferred_element_type=jnp.float32)
    grad_state = jnp.einsum(
        "tjf,tjd->fd", query_feature_maps, grad_numer, preferred_element_type=jnp.float32
    )
    grad_total = jnp.einsum(
        "tjf,tj->f", query_feature_maps, grad_denom, preferred_element_type=jnp.float32
    )
    return (grad_queries, grad_keys, grad_values, grad_qmaps, grad_kmaps, grad_state, grad_total)


def add_pair(earlier, later_part):
    return (earlier[0] + later_part[0], earlier[1] + later_part[1])


def local(
    tokens,
    lengths,
    norm_attn,
    norm_ffn,
    w_query,
    key_projection,
    value_projection,
    w_output,
    w_gate,
    w_up,
    w_down,
    down_query,
    up_query,
    key_down_matrix,
    key_up_matrix,
    value_down_matrix,
    value_up_matrix,
    down_output,
    up_output,
    feature_query,
    key_feature_weight,
    cotangent,
):
    rows_per_block = tokens.shape[1]
    ext_rows = rows_per_block + WINDOW_KEYS
    heads_per_group = QUERY_HEADS // KEY_VALUE_HEADS
    feature_width = 2 * HEAD_SIZE
    inputs_wide = tokens[0].astype(jnp.float32)
    cot_narrow = cotangent[0]
    cot_wide = cot_narrow.astype(jnp.float32)
    seq_index = lax.axis_index("seq")
    lane_length = lengths[lax.axis_index("fsdp")]
    positions = seq_index * rows_per_block + jnp.arange(rows_per_block)
    cosine_lookup, sine_lookup = rotary(positions)
    gain_attn = norm_attn.astype(jnp.float32)
    gain_ffn = norm_ffn.astype(jnp.float32)
    inverse_attn = lax.rsqrt(jnp.mean(inputs_wide * inputs_wide, axis=-1, keepdims=True) + epsilon)
    normed = (inputs_wide * inverse_attn * gain_attn).astype(jnp.bfloat16)
    pieces = (
        lax.all_gather(w_query, ("seq", "fsdp"), axis=0, tiled=True),
        lax.all_gather(key_projection, ("seq", "fsdp"), axis=0, tiled=True),
        lax.all_gather(value_projection, ("seq", "fsdp"), axis=0, tiled=True),
    )
    sliced = normed
    query_pre, key_before_rotation, value_before_adapter = tuple(
        (jnp.dot(sliced, block_piece, preferred_element_type=jnp.float32) for block_piece in pieces)
    )
    narrow_query = jnp.dot(normed, down_query, preferred_element_type=jnp.float32).astype(
        jnp.bfloat16
    )
    narrow_key = jnp.dot(normed, key_down_matrix, preferred_element_type=jnp.float32).astype(
        jnp.bfloat16
    )
    narrow_value = jnp.dot(normed, value_down_matrix, preferred_element_type=jnp.float32).astype(
        jnp.bfloat16
    )
    query_pre = query_pre + jnp.dot(narrow_query, up_query.T, preferred_element_type=jnp.float32)
    key_before_rotation = key_before_rotation + jnp.dot(
        narrow_key, key_up_matrix.T, preferred_element_type=jnp.float32
    )
    value_before_adapter = value_before_adapter + jnp.dot(
        narrow_value, value_up_matrix.T, preferred_element_type=jnp.float32
    )
    query_rows = apply_rotary(
        query_pre.reshape(rows_per_block, QUERY_HEADS, HEAD_SIZE), cosine_lookup, sine_lookup
    ).astype(jnp.bfloat16)
    device_keys = apply_rotary(
        key_before_rotation.reshape(rows_per_block, KEY_VALUE_HEADS, HEAD_SIZE),
        cosine_lookup,
        sine_lookup,
    ).astype(jnp.bfloat16)
    device_values = value_before_adapter.reshape(rows_per_block, KEY_VALUE_HEADS, HEAD_SIZE).astype(
        jnp.bfloat16
    )
    softmax_query_rows = query_rows.reshape(
        rows_per_block, KEY_VALUE_HEADS, heads_per_group, HEAD_SIZE
    )
    teacher_init = (
        jnp.full((KEY_VALUE_HEADS, heads_per_group, rows_per_block), lowest_precision, jnp.float32),
        jnp.zeros((KEY_VALUE_HEADS, heads_per_group, rows_per_block), jnp.float32),
        jnp.zeros((KEY_VALUE_HEADS, heads_per_group, rows_per_block, HEAD_SIZE), jnp.float32),
        jnp.zeros((WINDOW_KEYS, KEY_VALUE_HEADS, HEAD_SIZE), jnp.bfloat16),
        jnp.zeros((WINDOW_KEYS, KEY_VALUE_HEADS, HEAD_SIZE), jnp.bfloat16),
    )
    portion_keys = lax.all_gather(
        device_keys.reshape(rows_per_block, KEY_VALUE_HEADS * HEAD_SIZE), "seq", axis=0, tiled=True
    )
    portion_values = lax.all_gather(
        device_values.reshape(rows_per_block, KEY_VALUE_HEADS * HEAD_SIZE),
        "seq",
        axis=0,
        tiled=True,
    )
    count_of_shards = portion_keys.shape[0] // rows_per_block
    sharded_keys = portion_keys.reshape(count_of_shards, rows_per_block, KEY_VALUE_HEADS, HEAD_SIZE)
    sharded_values = portion_values.reshape(
        count_of_shards, rows_per_block, KEY_VALUE_HEADS, HEAD_SIZE
    )

    def one_shard(inner, item):
        best, total, accum, rim_keys, rim_values = inner
        shard_number, shard_keys, shard_values = item
        shard_start = shard_number * rows_per_block
        scores = jnp.einsum(
            "tgjd,sgd->gjts", softmax_query_rows, shard_keys, preferred_element_type=jnp.float32
        ) / math.sqrt(HEAD_SIZE)
        allowed = (positions[:, None] >= (shard_start + jnp.arange(rows_per_block))[None, :])[
            None, None
        ]
        masked = jnp.where(allowed, scores, lowest_precision)
        new_best = jnp.maximum(best, jnp.max(masked, axis=-1))
        probs = jnp.where(allowed, jnp.exp(masked - new_best[..., None]), 0.0)
        factor = jnp.exp(best - new_best)
        total = total * factor + jnp.sum(probs, axis=-1)
        accum = accum * factor[..., None] + jnp.einsum(
            "gjts,sgd->gjtd", probs, shard_values.astype(jnp.float32)
        )
        is_before = shard_start // rows_per_block == seq_index - 1
        rim_keys = jnp.where(is_before, shard_keys[rows_per_block - WINDOW_KEYS :], rim_keys)
        rim_values = jnp.where(is_before, shard_values[rows_per_block - WINDOW_KEYS :], rim_values)
        return ((new_best, total, accum, rim_keys, rim_values), None)

    result, unused = lax.scan(
        one_shard, teacher_init, (jnp.arange(count_of_shards), sharded_keys, sharded_values)
    )
    best_all, total_all, accum_all, rim_keys, rim_values = result
    teacher = jnp.transpose(accum_all / total_all[..., None], (2, 0, 1, 3)).reshape(
        rows_per_block, QUERY_HEADS * HEAD_SIZE
    )
    keys_ext = jnp.concatenate([rim_keys, device_keys], axis=0)
    values_ext = jnp.concatenate([rim_values, device_values], axis=0)
    query_features = feature_query.reshape(QUERY_HEADS, HEAD_SIZE, HEAD_SIZE)
    key_features = key_feature_weight.reshape(KEY_VALUE_HEADS, HEAD_SIZE, HEAD_SIZE)
    query_feature_maps = apply_feature_map(query_rows, query_features).astype(jnp.bfloat16)
    key_maps = apply_feature_map(keys_ext, key_features).astype(jnp.bfloat16)
    ext_positions = seq_index * rows_per_block - WINDOW_KEYS + jnp.arange(ext_rows)
    key_valid = ext_positions >= 0
    valid_rows = key_valid[:rows_per_block].astype(jnp.float32)
    used_maps = key_maps[:rows_per_block].astype(jnp.float32) * valid_rows[:, None, None]
    values_head = values_ext[:rows_per_block].astype(jnp.float32)
    local_state = jnp.einsum("sgf,sgd->gfd", used_maps, values_head, precision=precise)
    local_total = jnp.sum(used_maps, axis=0)
    zero_pair = (
        jnp.zeros((KEY_VALUE_HEADS, feature_width, HEAD_SIZE), jnp.float32),
        jnp.zeros((KEY_VALUE_HEADS, feature_width), jnp.float32),
    )
    state_in, total_in = prefix((local_state, local_total), "seq", add_pair, zero_pair, False)
    queries_by_group = jnp.moveaxis(
        query_rows.reshape(rows_per_block, KEY_VALUE_HEADS, heads_per_group, HEAD_SIZE), 1, 0
    )
    query_maps_by_group = jnp.moveaxis(
        query_feature_maps.reshape(rows_per_block, KEY_VALUE_HEADS, heads_per_group, feature_width),
        1,
        0,
    )
    grouped_keys = jnp.moveaxis(keys_ext, 1, 0)
    grouped_values = jnp.moveaxis(values_ext, 1, 0)
    grouped_kmaps = jnp.moveaxis(key_maps, 1, 0)

    def forward_group(operands):
        return attend_group(operands, key_valid)

    numerator, denominator = lax.map(
        forward_group,
        (
            queries_by_group,
            query_maps_by_group,
            grouped_keys,
            grouped_values,
            grouped_kmaps,
            state_in,
            total_in,
        ),
    )
    row_mask = (positions < lane_length).astype(jnp.float32)
    attn_mixed = jnp.moveaxis(numerator / denominator[..., None], 0, 1).reshape(
        rows_per_block, QUERY_HEADS * HEAD_SIZE
    )
    attended = (attn_mixed * row_mask[:, None]).astype(jnp.bfloat16)
    difference = attended.astype(jnp.float32) - teacher * row_mask[:, None]
    local_loss = jnp.sum(difference * difference)
    sliced = attended
    branch = jnp.dot(
        sliced,
        lax.all_gather(w_output, ("seq", "fsdp"), axis=0, tiled=True),
        preferred_element_type=jnp.float32,
    )
    narrow_out = jnp.dot(attended, down_output, preferred_element_type=jnp.float32).astype(
        jnp.bfloat16
    )
    branch = branch + jnp.dot(narrow_out, up_output.T, preferred_element_type=jnp.float32)
    residual = inputs_wide + branch
    inverse_ffn = lax.rsqrt(jnp.mean(residual * residual, axis=-1, keepdims=True) + epsilon)
    normed_ffn = (residual * inverse_ffn * gain_ffn).astype(jnp.bfloat16)
    ffn_weights = (
        lax.all_gather(w_gate, "fsdp", axis=1, tiled=True),
        lax.all_gather(w_up, "fsdp", axis=1, tiled=True),
        lax.all_gather(w_down, "fsdp", axis=1, tiled=True),
    )
    pieces = (
        lax.all_gather(ffn_weights[0], "seq", axis=0, tiled=True),
        lax.all_gather(ffn_weights[1], "seq", axis=0, tiled=True),
    )
    sliced = normed_ffn
    gate_pre = jnp.dot(sliced, pieces[0], preferred_element_type=jnp.float32)
    up_pre = jnp.dot(sliced, pieces[1], preferred_element_type=jnp.float32)
    sigmoid_gate = jax.nn.sigmoid(gate_pre)
    silu_gate = gate_pre * sigmoid_gate
    hidden = (silu_gate * up_pre).astype(jnp.bfloat16)
    ffn_part = jnp.dot(
        hidden,
        lax.all_gather(ffn_weights[2], "seq", axis=0, tiled=True).T,
        preferred_element_type=jnp.float32,
    )
    output = (residual + ffn_part).astype(jnp.bfloat16)
    sliced = cot_narrow
    grad_hidden = jnp.dot(
        sliced,
        lax.all_gather(ffn_weights[2], "seq", axis=0, tiled=True),
        preferred_element_type=jnp.float32,
    )
    grad_gate = (
        grad_hidden * up_pre * sigmoid_gate * (1.0 + gate_pre * (1.0 - sigmoid_gate))
    ).astype(jnp.bfloat16)
    grad_up = (grad_hidden * silu_gate).astype(jnp.bfloat16)
    pieces = lax.all_gather((ffn_weights[0], ffn_weights[1]), "seq", axis=0, tiled=True)
    grad_part = jnp.dot(grad_gate, pieces[0].T, preferred_element_type=jnp.float32) + jnp.dot(
        grad_up, pieces[1].T, preferred_element_type=jnp.float32
    )
    grad_residual = cot_wide + norm_back(residual, inverse_ffn, gain_ffn, grad_part)
    grad_branch = grad_residual.astype(jnp.bfloat16)
    grad_narrow_out = jnp.dot(grad_branch, up_output, preferred_element_type=jnp.float32)
    grad_up_output = jnp.dot(grad_branch.T, narrow_out, preferred_element_type=jnp.float32)
    grad_down_output = jnp.dot(attended.T, grad_narrow_out, preferred_element_type=jnp.float32)
    attended_gradient = (
        jnp.dot(
            grad_branch,
            lax.all_gather(w_output, ("seq", "fsdp"), axis=0, tiled=True).T,
            preferred_element_type=jnp.float32,
        )
        + jnp.dot(grad_narrow_out, down_output.T, preferred_element_type=jnp.float32)
        + 2.0 * difference
    )
    attended_gradient = (
        lax.optimization_barrier(attended_gradient.astype(jnp.bfloat16)).astype(jnp.float32)
        * row_mask[:, None]
    )
    gradient_by_group = jnp.moveaxis(
        attended_gradient.reshape(rows_per_block, KEY_VALUE_HEADS, heads_per_group, HEAD_SIZE), 1, 0
    )

    def backward_group(operands):
        return attend_back(operands, key_valid)

    grad_q, grad_k, grad_v, grad_qm, grad_km, grad_state, grad_total = lax.map(
        backward_group,
        (
            queries_by_group,
            query_maps_by_group,
            grouped_keys,
            grouped_values,
            grouped_kmaps,
            state_in,
            total_in,
            numerator,
            denominator,
            gradient_by_group,
        ),
    )
    later_state, later_total = prefix((grad_state, grad_total), "seq", add_pair, zero_pair, True)
    values_grouped_head = jnp.moveaxis(values_head, 1, 0)
    used_grouped = jnp.moveaxis(used_maps, 1, 0)
    kmaps_head = grad_km[:, :rows_per_block] + valid_rows[None, :, None] * (
        jnp.einsum("gfd,gsd->gsf", later_state, values_grouped_head, precision=precise)
        + later_total[:, None, :]
    )
    grad_km = jnp.concatenate([kmaps_head, grad_km[:, rows_per_block:]], axis=1)
    values_grad_head = grad_v[:, :rows_per_block] + jnp.einsum(
        "gsf,gfd->gsd", used_grouped, later_state, precision=precise
    )
    grad_v = jnp.concatenate([values_grad_head, grad_v[:, rows_per_block:]], axis=1)
    grad_k_feat, key_feature_gradient = feature_back(
        keys_ext, key_features, jnp.moveaxis(grad_km, 0, 1)
    )
    gathered_key_gradient = jnp.moveaxis(grad_k, 0, 1) + grad_k_feat
    gathered_value_gradient = jnp.moveaxis(grad_v, 0, 1)
    grad_q_feat, grad_feature_query = feature_back(
        query_rows,
        query_features,
        jnp.moveaxis(grad_qm, 0, 1).reshape(rows_per_block, QUERY_HEADS, feature_width),
    )
    grad_queries_rot = (
        jnp.moveaxis(grad_q, 0, 1).reshape(rows_per_block, QUERY_HEADS, HEAD_SIZE) + grad_q_feat
    )
    back_keys, back_values = (
        shifted(
            gathered_key_gradient[:WINDOW_KEYS]
            .reshape(WINDOW_KEYS, KEY_VALUE_HEADS * HEAD_SIZE)
            .astype(jnp.bfloat16),
            "seq",
            -1,
        ).astype(jnp.float32),
        shifted(
            as_sent(
                gathered_value_gradient[:WINDOW_KEYS].reshape(
                    WINDOW_KEYS, KEY_VALUE_HEADS * HEAD_SIZE
                )
            ),
            "seq",
            -1,
        ),
    )
    trailing_keys = gathered_key_gradient[WINDOW_KEYS:].reshape(
        rows_per_block, KEY_VALUE_HEADS * HEAD_SIZE
    )
    trailing_values = gathered_value_gradient[WINDOW_KEYS:].reshape(
        rows_per_block, KEY_VALUE_HEADS * HEAD_SIZE
    )
    trailing_keys = jnp.concatenate(
        [
            trailing_keys[: rows_per_block - WINDOW_KEYS],
            trailing_keys[rows_per_block - WINDOW_KEYS :] + back_keys,
        ],
        axis=0,
    )
    trailing_values = jnp.concatenate(
        [
            trailing_values[: rows_per_block - WINDOW_KEYS],
            trailing_values[rows_per_block - WINDOW_KEYS :] + back_values,
        ],
        axis=0,
    )
    grad_query_pre = (
        inverse_rotary(grad_queries_rot, cosine_lookup, sine_lookup)
        .reshape(rows_per_block, QUERY_HEADS * HEAD_SIZE)
        .astype(jnp.bfloat16)
    )
    grad_key_pre = (
        inverse_rotary(
            trailing_keys.reshape(rows_per_block, KEY_VALUE_HEADS, HEAD_SIZE),
            cosine_lookup,
            sine_lookup,
        )
        .reshape(rows_per_block, KEY_VALUE_HEADS * HEAD_SIZE)
        .astype(jnp.bfloat16)
    )
    grad_value_pre = trailing_values.astype(jnp.bfloat16)
    grad_narrow_query = jnp.dot(grad_query_pre, up_query, preferred_element_type=jnp.float32)
    grad_narrow_key = jnp.dot(grad_key_pre, key_up_matrix, preferred_element_type=jnp.float32)
    grad_narrow_value = jnp.dot(grad_value_pre, value_up_matrix, preferred_element_type=jnp.float32)
    grad_up_query = jnp.dot(grad_query_pre.T, narrow_query, preferred_element_type=jnp.float32)
    grad_up_key = jnp.dot(grad_key_pre.T, narrow_key, preferred_element_type=jnp.float32)
    grad_up_value = jnp.dot(grad_value_pre.T, narrow_value, preferred_element_type=jnp.float32)
    grad_down_query = jnp.dot(normed.T, grad_narrow_query, preferred_element_type=jnp.float32)
    grad_down_key = jnp.dot(normed.T, grad_narrow_key, preferred_element_type=jnp.float32)
    grad_down_value = jnp.dot(normed.T, grad_narrow_value, preferred_element_type=jnp.float32)
    pieces = lax.all_gather(
        (w_query, key_projection, value_projection), ("seq", "fsdp"), axis=0, tiled=True
    )
    grad_normed = (
        jnp.dot(grad_query_pre, pieces[0].T, preferred_element_type=jnp.float32)
        + jnp.dot(grad_key_pre, pieces[1].T, preferred_element_type=jnp.float32)
        + jnp.dot(grad_value_pre, pieces[2].T, preferred_element_type=jnp.float32)
    )
    grad_normed = grad_normed + jnp.dot(
        grad_narrow_query, down_query.T, preferred_element_type=jnp.float32
    )
    grad_normed = grad_normed + jnp.dot(
        grad_narrow_key, key_down_matrix.T, preferred_element_type=jnp.float32
    )
    grad_normed = grad_normed + jnp.dot(
        grad_narrow_value, value_down_matrix.T, preferred_element_type=jnp.float32
    )
    grad_tokens = (
        grad_residual + norm_back(inputs_wide, inverse_attn, gain_attn, grad_normed)
    ).astype(jnp.bfloat16)
    device_count = lax.axis_size(("seq", "fsdp"))
    device_number = lax.axis_index(("seq", "fsdp"))
    loss_terms = jnp.where(jnp.arange(device_count) >= device_number, local_loss, 0.0)
    summed = (
        lax.psum_scatter(grad_down_query, ("seq", "fsdp"), scatter_dimension=0, tiled=True),
        lax.psum_scatter(grad_up_query, ("seq", "fsdp"), scatter_dimension=0, tiled=True),
        lax.psum_scatter(grad_down_key, ("seq", "fsdp"), scatter_dimension=0, tiled=True),
        lax.psum_scatter(grad_up_key, ("seq", "fsdp"), scatter_dimension=0, tiled=True),
        lax.psum_scatter(grad_down_value, ("seq", "fsdp"), scatter_dimension=0, tiled=True),
        lax.psum_scatter(grad_up_value, ("seq", "fsdp"), scatter_dimension=0, tiled=True),
        lax.psum_scatter(grad_down_output, ("seq", "fsdp"), scatter_dimension=0, tiled=True),
        lax.psum_scatter(grad_up_output, ("seq", "fsdp"), scatter_dimension=0, tiled=True),
        lax.psum_scatter(
            grad_feature_query.reshape(QUERY_HEADS * HEAD_SIZE, HEAD_SIZE),
            ("seq", "fsdp"),
            scatter_dimension=0,
            tiled=True,
        ),
        lax.psum_scatter(
            key_feature_gradient.reshape(KEY_VALUE_HEADS * HEAD_SIZE, HEAD_SIZE),
            ("seq", "fsdp"),
            scatter_dimension=0,
            tiled=True,
        ),
        lax.psum_scatter(loss_terms, ("seq", "fsdp"), scatter_dimension=0, tiled=True),
    )
    transfer_loss = summed[10] / jnp.sum(lengths).astype(jnp.float32)
    return (
        output[None],
        grad_tokens[None],
        summed[0],
        summed[1],
        summed[2],
        summed[3],
        summed[4],
        summed[5],
        summed[6],
        summed[7],
        summed[8],
        summed[9],
        transfer_loss,
    )

def halves_rotated(first_half, second_half, cosine, sine):
    return (
        first_half * cosine - second_half * sine,
        second_half * cosine + first_half * sine,
    )


def soft_pair(logits):
    plus = jnp.exp(logits - jnp.max(logits, axis=0, keepdims=True))
    minus = jnp.exp(jnp.min(logits, axis=0, keepdims=True) - logits)
    plus = plus * (1.0 / jnp.sum(plus, axis=0, keepdims=True))
    minus = minus * (1.0 / jnp.sum(minus, axis=0, keepdims=True))
    return plus, minus


def mm(a, b):
    return jnp.dot(a, b, preferred_element_type=jnp.float32)


def mm_nt(a, b):
    return lax.dot_general(a, b, (((1,), (1,)), ((), ())), preferred_element_type=jnp.float32)


def mm_tn(a, b):
    return lax.dot_general(a, b, (((0,), (0,)), ((), ())), preferred_element_type=jnp.float32)


def split_wide(x):
    high = x.astype(jnp.bfloat16)
    low = (x - high.astype(jnp.float32)).astype(jnp.bfloat16)
    return high, low


ANYWHERE = pl.BlockSpec(memory_space=pltpu.HBM)


def call(kernel, grid, in_specs, out_specs, out_shape, scratch, flops, moved, scalars=0):
    spec = pltpu.PrefetchScalarGridSpec(
        num_scalar_prefetch=scalars,
        grid=grid,
        in_specs=in_specs,
        out_specs=out_specs,
        scratch_shapes=scratch,
    )
    return pl.pallas_call(
        kernel,
        grid_spec=spec,
        out_shape=out_shape,
        compiler_params=pltpu.CompilerParams(vmem_limit_bytes=VMEM_MIB * 2**20),
        cost_estimate=pl.CostEstimate(
            flops=int(COST * moved), bytes_accessed=1, transcendentals=0
        ),
    )


def spec_whole(*dims):
    return pl.BlockSpec(dims, lambda i, *_: (0,) * len(dims))


def spec_across(height, columns):
    return pl.BlockSpec((height, columns), lambda i, *_: (0, i))


def spec_down(rows, wide):
    return pl.BlockSpec((rows, wide), lambda i, *_: (i, 0))


def spec_block(*dims):
    return pl.BlockSpec((None,) + dims, lambda i, *_: (i, 0, 0))


def spec_placed(spec):
    return pl.BlockSpec(
        spec.block_shape,
        lambda i, place_ref, *_: spec.index_map(lax.bitwise_xor(i, place_ref[0])),
    )


def array(*dims, dtype=jnp.bfloat16):
    return jax.ShapeDtypeStruct(dims, dtype)


def flat(found):
    return [part for parts in found for part in parts]


def grouped(refs, counts):
    found, start = [], 0
    for count in counts:
        found.append(tuple(refs[start : start + count]))
        start += count
    return found, refs[start:]


def fetch(refs, buffer, sems, at, order=lambda step: step):
    steps = len(refs)

    def start(step):
        slot = lax.rem(step, 2)
        wanted = order(step)
        for number, parts in enumerate(refs):

            @pl.when(wanted == number)
            def _():
                height = buffer.shape[1] // len(parts)
                for part, ref in enumerate(parts):
                    pltpu.make_async_copy(
                        ref, buffer.at[slot, part * height : (part + 1) * height], sems.at[slot]
                    ).start()

    @pl.when(at == 0)
    def _():
        start(at)

    @pl.when(at + 1 < steps)
    def _():
        start(at + 1)

    slot = lax.rem(at, 2)
    pltpu.make_async_copy(buffer.at[slot], buffer.at[slot], sems.at[slot]).wait()
    return slot


def start_columns(refs, span, buffer, sem):
    first, end = span
    wide = end - first
    for chunk, ref in enumerate(refs):
        pltpu.make_async_copy(
            ref.at[:, first:end], buffer.at[:, chunk * wide : (chunk + 1) * wide], sem
        ).start()


def chunks_of(ref, order_ref):
    return [ref.at[order_ref[chunk]] for chunk in range(ref.shape[0])]


def wait_whole(buffer, sem):
    pltpu.make_async_copy(buffer, buffer, sem).wait()


def block_shape(blocks):
    return sum(part.shape[0] for part in blocks[0]), blocks[0][0].shape[1]


def fetch_scratch(blocks):
    rows, wide = block_shape(blocks)
    return [pltpu.VMEM((2, rows, wide), jnp.bfloat16), pltpu.SemaphoreType.DMA((2,))]


def project_kernel(counts, place_ref, *refs):
    blocks, refs = grouped(refs, counts)
    (
        w_ref, down_ref, up_ref, map_ref, cos_ref, sin_ref,
        q_ref, kt_ref, vt_ref, k_ref, v_ref, pq_ref, pkt_ref, pk_ref, narrow_ref, wt_ref,
        buffer, sems,
    ) = refs
    group = q_ref.shape[0] // HEAD_SIZE
    half = HEAD_SIZE // 2
    width = (group + 2) * HEAD_SIZE
    slot = fetch(blocks, buffer, sems, pl.program_id(0))

    @pl.when(pl.program_id(0) == 0)
    def _():
        lanes, places, shard, _ = w_ref.shape
        for place in range(places):
            rows = jnp.concatenate([w_ref[lane, place] for lane in range(lanes)], axis=0)
            columns = slice(place * lanes * shard, (place + 1) * lanes * shard)
            wt_ref[:width, columns] = jnp.transpose(rows)
        wt_ref[width:] = down_ref[...]

    full = mm_nt(wt_ref[...], buffer[slot])
    narrow = full[width:].astype(jnp.bfloat16)
    narrow_ref[...] = narrow
    pre = full[:width] + mm(up_ref[...], narrow)
    cosine, sine = cos_ref[...], sin_ref[...]
    for head in range(group + 1):
        base = head * HEAD_SIZE
        low_half, high_half = halves_rotated(
            pre[base : base + half], pre[base + half : base + HEAD_SIZE], cosine, sine
        )
        wide = jnp.concatenate([low_half, high_half], axis=0)
        vector = wide.astype(jnp.bfloat16)
        logits = mm(map_ref[base : base + HEAD_SIZE], vector)
        plus, minus = soft_pair(logits)
        maps = jnp.concatenate([plus, minus], axis=0)
        if head < group:
            q_ref[base : base + HEAD_SIZE] = vector
            pq_ref[2 * base : 2 * base + 2 * HEAD_SIZE] = maps.astype(jnp.bfloat16)
        else:
            kt_ref[...] = vector
            k_ref[...] = jnp.transpose(wide).astype(jnp.bfloat16)
            pkt_ref[...] = maps.astype(jnp.bfloat16)
            pk_ref[...] = jnp.transpose(maps).astype(jnp.bfloat16)
    values = pre[width - HEAD_SIZE : width]
    vt_ref[:HEAD_SIZE] = values.astype(jnp.bfloat16)
    vt_ref[HEAD_SIZE:] = jnp.ones((ONES, values.shape[1]), jnp.bfloat16)
    v_ref[...] = jnp.transpose(values).astype(jnp.bfloat16)


def project(place_row, blocks, weights, down_block, up_block, maps_ahead, cosine, sine):
    places = len(blocks)
    rows, model = block_shape(blocks)
    count = places * rows
    width, spare = up_block.shape
    query_width = width - 2 * HEAD_SIZE
    group = query_width // HEAD_SIZE
    maps = 2 * HEAD_SIZE
    half = HEAD_SIZE // 2
    counts = [len(found) for found in blocks]
    outs = [
        (query_width, False),
        (HEAD_SIZE, False),
        (HEAD_SIZE + ONES, False),
        (HEAD_SIZE, True),
        (HEAD_SIZE, True),
        (group * maps, False),
        (maps, False),
        (maps, True),
        (spare, False),
    ]
    return call(
        functools.partial(project_kernel, counts),
        (places,),
        [ANYWHERE] * sum(counts)
        + [
            spec_whole(*weights.shape),
            spec_whole(spare, model),
            spec_whole(width, spare),
            spec_whole(*maps_ahead.shape),
            spec_placed(spec_across(half, rows)),
            spec_placed(spec_across(half, rows)),
        ],
        [
            spec_placed(spec_down(rows, size) if natural else spec_across(size, rows))
            for size, natural in outs
        ]
        + [spec_whole(width + spare, model)],
        [array(count, size) if natural else array(size, count) for size, natural in outs]
        + [array(width + spare, model)],
        fetch_scratch(blocks),
        0,
        17,
        scalars=1,
    )(place_row, *flat(blocks), weights, down_block, up_block, maps_ahead, cosine, sine)


def side_by_side(ref, size, group, columns):
    return jnp.concatenate(
        [ref[head * size : (head + 1) * size, columns] for head in range(group)], axis=1
    )


def bands():
    shape = (WINDOW_KEYS, SUB)
    query_at = lax.broadcasted_iota(jnp.int32, shape, 1)
    key_at = lax.broadcasted_iota(jnp.int32, shape, 0)
    distance = query_at - key_at
    return (
        distance < 0,
        (distance >= 0) & (distance < WINDOW_KEYS),
        distance >= WINDOW_KEYS,
        distance >= WINDOW_KEYS,
    )


def forward_kernel(
    length_ref, q_ref, pq_ref, k_ref, k_before, pk_ref, pk_before, vt_ref, vt_before,
    att_ref, out_ref, denom_ref, states_ref, weights_ref, state,
):
    step = pl.program_id(0)
    group = q_ref.shape[0] // HEAD_SIZE
    rows = q_ref.shape[1]
    quarter = WINDOW_KEYS
    second, third, third_far, fourth = bands()

    @pl.when(step == 0)
    def _():
        state[...] = jnp.zeros_like(state)

    now = state[...]
    for sub in range(rows // SUB):
        columns = slice(sub * SUB, (sub + 1) * SUB)
        queries = side_by_side(q_ref, HEAD_SIZE, group, columns)
        query_maps = side_by_side(pq_ref, 2 * HEAD_SIZE, group, columns)
        if sub == 0:
            keys = jnp.concatenate([k_before[...], k_ref[:SUB]], axis=0)
            key_maps = jnp.concatenate([pk_before[...], pk_ref[:SUB]], axis=0)
            values = jnp.concatenate([vt_before[...], vt_ref[:, :SUB]], axis=1)
        else:
            around = slice((sub - 1) * SUB, (sub + 1) * SUB)
            keys, key_maps, values = k_ref[around], pk_ref[around], vt_ref[:, around]
        scores = mm(keys[quarter:], queries)
        far = mm(key_maps[: 3 * quarter], query_maps)
        pieces = []
        for head in range(group):
            lanes = slice(head * SUB, (head + 1) * SUB)
            near = jnp.exp(scores[:, lanes] * (1.0 / math.sqrt(HEAD_SIZE)))
            away = far[:, lanes]
            before = jnp.concatenate(
                [
                    away[:quarter],
                    jnp.where(second, near[:quarter], away[quarter : 2 * quarter]),
                ],
                axis=0,
            )
            if sub == 0:
                before = jnp.where(step > 0, before, 0.0)
            pieces.append(
                jnp.concatenate(
                    [
                        before,
                        jnp.where(
                            third,
                            near[quarter : 2 * quarter],
                            jnp.where(third_far, away[2 * quarter :], 0.0),
                        ),
                        jnp.where(fourth, near[2 * quarter :], 0.0),
                    ],
                    axis=0,
                ).astype(jnp.bfloat16)
            )
        weights = jnp.concatenate(pieces, axis=1)
        weights_ref[sub] = weights
        states_ref[sub] = now
        high, low = split_wide(now)
        total = mm(values, weights) + mm(
            jnp.concatenate([high, low], axis=1),
            jnp.concatenate([query_maps, query_maps], axis=0),
        )
        denom = total[HEAD_SIZE : HEAD_SIZE + 1]
        out = total[:HEAD_SIZE] * (1.0 / denom)
        at = step * rows + sub * SUB + lax.broadcasted_iota(jnp.int32, (HEAD_SIZE, SUB), 1)
        inside = at < length_ref[0]
        for head in range(group):
            lanes = slice(head * SUB, (head + 1) * SUB)
            base = head * HEAD_SIZE
            out_ref[base : base + HEAD_SIZE, columns] = out[:, lanes]
            att_ref[base : base + HEAD_SIZE, columns] = jnp.where(
                inside, out[:, lanes], 0.0
            ).astype(jnp.bfloat16)
            denom_ref[head : head + 1, columns] = denom[:, lanes]
        update = mm(values[:, :SUB], key_maps[:SUB])
        if sub == 0:
            update = jnp.where(step > 0, update, 0.0)
        now = now + update
    state[...] = now


def before_down(rows, wide):
    per_step = rows // SUB
    return pl.BlockSpec((SUB, wide), lambda i, *_: (jnp.maximum(per_step * i - 1, 0), 0))


def before_across(rows, height):
    per_step = rows // SUB
    return pl.BlockSpec((height, SUB), lambda i, *_: (0, jnp.maximum(per_step * i - 1, 0)))


def attend(length, q_t, pq_t, keys, key_maps, v_t, rows):
    query_width, count = q_t.shape
    group = query_width // HEAD_SIZE
    places = count // rows
    per_step = rows // SUB
    maps = key_maps.shape[1]
    high = v_t.shape[0]
    wide = jnp.float32
    return call(
        forward_kernel,
        (places,),
        [
            spec_across(query_width, rows),
            spec_across(group * maps, rows),
            spec_down(rows, HEAD_SIZE),
            before_down(rows, HEAD_SIZE),
            spec_down(rows, maps),
            before_down(rows, maps),
            spec_across(high, rows),
            before_across(rows, high),
        ],
        [
            spec_block(query_width, rows),
            spec_across(query_width, rows),
            spec_across(group, rows),
            pl.BlockSpec((per_step, high, maps), lambda i, *_: (i, 0, 0)),
            pl.BlockSpec((per_step, 2 * SUB, group * SUB), lambda i, *_: (i, 0, 0)),
        ],
        [
            array(places, query_width, rows),
            array(query_width, count, dtype=wide),
            array(group, count, dtype=wide),
            array(count // SUB, high, maps, dtype=wide),
            array(count // SUB, 2 * SUB, group * SUB),
        ],
        [pltpu.VMEM((high, maps), wide)],
        0,
        10,
        scalars=1,
    )(length, q_t, pq_t, keys, keys, key_maps, key_maps, v_t, v_t)


def teacher_kernel(first, steps, length_ref, q_ref, k_ref, vt_ref, att_ref, *refs):
    diff_ref, loss_ref = refs[-2:]
    step = pl.program_id(0)
    group = q_ref.shape[0] // HEAD_SIZE
    rows = q_ref.shape[1]
    scale = 1.0 / math.sqrt(HEAD_SIZE)
    at = (first + step) * rows + lax.broadcasted_iota(jnp.int32, (HEAD_SIZE, rows), 1)
    inside = at < length_ref[0]
    shape = (rows, rows)
    ahead = lax.broadcasted_iota(jnp.int32, shape, 0) > lax.broadcasted_iota(jnp.int32, shape, 1)

    for blocks in range(first + 1, first + steps + 1):

        @pl.when(first + step == blocks - 1)
        def _():
            size = blocks * rows
            loss = jnp.zeros((1, rows), jnp.float32)
            for head in range(group):
                base = head * HEAD_SIZE
                query = q_ref[base : base + HEAD_SIZE]
                last = jnp.where(ahead, lowest_precision, mm(k_ref[size - rows : size], query))
                best = jnp.max(last, axis=0, keepdims=True)
                if blocks > 1:
                    early = mm(k_ref[: size - rows], query)
                    best = jnp.maximum(best, jnp.max(early, axis=0, keepdims=True))
                total = mm(
                    vt_ref[:, size - rows : size],
                    jnp.exp((last - best) * scale).astype(jnp.bfloat16),
                )
                if blocks > 1:
                    total = total + mm(
                        vt_ref[:, : size - rows],
                        jnp.exp((early - best) * scale).astype(jnp.bfloat16),
                    )
                taught = total[:HEAD_SIZE] * (1.0 / total[HEAD_SIZE : HEAD_SIZE + 1])
                difference = att_ref[base : base + HEAD_SIZE].astype(jnp.float32) - jnp.where(
                    inside, taught, 0.0
                )
                diff_ref[base : base + HEAD_SIZE] = difference
                loss = loss + jnp.sum(difference * difference, axis=0, keepdims=True)
            loss_ref[...] = jnp.broadcast_to(loss, loss_ref.shape)


def teach(length, q_t, keys, v_t, att, first, end, before=None):
    places, query_width, rows = att.shape
    count = places * rows
    wide = jnp.float32

    def ahead(spec):
        return pl.BlockSpec(spec.block_shape, lambda i, *_: spec.index_map(i + first))

    spec = pltpu.PrefetchScalarGridSpec(
        num_scalar_prefetch=1,
        grid=(end - first,),
        in_specs=[
            ahead(spec_across(query_width, rows)),
            spec_whole(*keys.shape),
            spec_whole(*v_t.shape),
            ahead(spec_block(query_width, rows)),
        ]
        + [ANYWHERE] * (2 if before else 0),
        out_specs=[ahead(spec_across(query_width, rows)), ahead(spec_across(8, rows))],
    )
    return pl.pallas_call(
        functools.partial(teacher_kernel, first, end - first),
        grid_spec=spec,
        out_shape=[array(query_width, count, dtype=wide), array(8, count, dtype=wide)],
        input_output_aliases={5: 0, 6: 1} if before else {},
        compiler_params=pltpu.CompilerParams(vmem_limit_bytes=VMEM_MIB * 2**20),
        cost_estimate=pl.CostEstimate(
            flops=int(COST * 16), bytes_accessed=1, transcendentals=0
        ),
    )(length, q_t, keys, v_t, att, *(before or ()))


def hidden_kernel(counts, order_ref, *refs):
    blocks, refs = grouped(refs, counts)
    *gates, ups, hidden_ref, by_gate_ref, by_up_ref, buffer, sems, both, both_sem = refs

    @pl.when(pl.program_id(0) == 0)
    def _():
        unit = ups.shape[2] // PARTS
        wide = ups.shape[0] * unit
        for part in range(PARTS):
            span = part * unit, (part + 1) * unit
            start_columns(gates, span, both.at[:, part * wide : (part + 1) * wide], both_sem)
            start = (PARTS + part) * wide
            start_columns(chunks_of(ups, order_ref), span, both.at[:, start : start + wide], both_sem)

    slot = fetch(blocks, buffer, sems, pl.program_id(0))

    @pl.when(pl.program_id(0) == 0)
    def _():
        wait_whole(both, both_sem)

    full = mm(buffer[slot], both[...])
    wide = full.shape[1] // 2
    gate, up = full[:, :wide], full[:, wide:]
    sigmoid = 1.0 / (1.0 + jnp.exp(-gate))
    silu = gate * sigmoid
    hidden_ref[...] = (silu * up).astype(jnp.bfloat16)
    by_gate_ref[...] = (up * (sigmoid + silu * (1.0 - sigmoid))).astype(jnp.bfloat16)
    by_up_ref[...] = silu.astype(jnp.bfloat16)


def hidden_units(order, blocks, gates, ups):
    rows, model = block_shape(blocks)
    count = rows * len(blocks)
    share = ups.shape[0] * ups.shape[2]
    counts = [len(found) for found in blocks]
    return call(
        functools.partial(hidden_kernel, counts),
        (len(blocks),),
        [ANYWHERE] * (sum(counts) + 1 + len(gates)),
        [spec_down(rows, share)] * 3,
        [array(count, share)] * 3,
        fetch_scratch(blocks)
        + [pltpu.VMEM((model, 2 * share), jnp.bfloat16), pltpu.SemaphoreType.DMA],
        0,
        25,
        scalars=1,
    )(order, *flat(blocks), *gates, ups)


def ffn_back_kernel(counts, chunks, part, more, order_ref, *refs):
    blocks, refs = grouped(refs, counts)
    *gates, ups, downs, by_gate_ref, by_up_ref = refs[: chunks + 4]
    before_ref = refs[chunks + 4] if more else None
    out_ref, buffer, sems, both, both_sem, down, down_sem = refs[-7:]

    @pl.when(pl.program_id(0) == 0)
    def _():
        wide = both.shape[1] // 2
        unit = downs.shape[2]
        span = part * unit, (part + 1) * unit
        start_columns(chunks_of(downs, order_ref), (0, unit), down, down_sem)
        start_columns(gates, span, both.at[:, :wide], both_sem)
        start_columns(chunks_of(ups, order_ref), span, both.at[:, wide:], both_sem)

    slot = fetch(blocks, buffer, sems, pl.program_id(0))

    @pl.when(pl.program_id(0) == 0)
    def _():
        wait_whole(down, down_sem)

    grad_hidden = mm(buffer[slot], down[...])
    grad_gate = (grad_hidden * by_gate_ref[...].astype(jnp.float32)).astype(jnp.bfloat16)
    grad_up = (grad_hidden * by_up_ref[...].astype(jnp.float32)).astype(jnp.bfloat16)

    @pl.when(pl.program_id(0) == 0)
    def _():
        wait_whole(both, both_sem)

    total = mm_nt(jnp.concatenate([grad_gate, grad_up], axis=1), both[...])
    if more:
        total = total + before_ref[...].astype(jnp.float32)
    out_ref[...] = total.astype(jnp.bfloat16)


def ffn_back(order, blocks, first, each, part, gates, ups, downs, by_gate, by_up, before):
    rows, model = block_shape(blocks)
    share = downs.shape[0] * downs.shape[2]
    counts = [len(found) for found in blocks]
    more = before is not None

    def rows_of(wide, at=0):
        return pl.BlockSpec((rows, wide), lambda i, *_: (first + each * i, at))

    return call(
        functools.partial(ffn_back_kernel, counts, len(gates), part, more),
        (len(blocks),),
        [ANYWHERE] * (sum(counts) + len(gates) + 2)
        + [rows_of(share, part)] * 2
        + [rows_of(model)] * more,
        spec_down(rows, model),
        array(len(blocks) * rows, model),
        fetch_scratch(blocks)
        + [pltpu.VMEM((model, 2 * share), jnp.bfloat16), pltpu.SemaphoreType.DMA]
        + [pltpu.VMEM((model, share), jnp.bfloat16), pltpu.SemaphoreType.DMA],
        0,
        3 * len(blocks),
        scalars=1,
    )(order, *flat(blocks), *gates, ups, downs, by_gate, by_up, *([before] if more else []))


def ffn_out_kernel(place_ref, order_ref, *refs):
    downs, (hidden_ref, out_ref, down, down_sem) = refs[:PARTS], refs[PARTS:]

    @pl.when(pl.program_id(0) == 0)
    def _():
        wide = down.shape[1] // PARTS
        for part, ref in enumerate(downs):
            start_columns(
                chunks_of(ref, order_ref), (0, ref.shape[2]), down.at[:, part * wide : (part + 1) * wide], down_sem
            )
        wait_whole(down, down_sem)

    out_ref[...] = mm_nt(hidden_ref[...], down[...]).astype(jnp.bfloat16)


def ffn_out(place_row, order, hidden, downs, places):
    count, share = hidden.shape
    rows = count // places
    model = downs[0].shape[1]
    return call(
        ffn_out_kernel,
        (places,),
        [ANYWHERE] * PARTS + [spec_down(rows, share)],
        spec_placed(spec_down(rows, model)),
        array(count, model),
        [pltpu.VMEM((model, share), jnp.bfloat16), pltpu.SemaphoreType.DMA],
        0,
        17,
        scalars=2,
    )(place_row, order, *downs, hidden)


def backward_kernel(
    counts, length_ref, place_ref, *refs
):
    blocks, refs = grouped(refs, counts)
    (
    grad_ref, diff_ref, out_ref, denom_ref, q_ref, pq_ref, weights_ref,
    v_ref, v_before, kt_ref, kt_before, pkt_ref, pkt_before, vt_ref, vt_before,
    states_ref, map_ref, back_ref, cos_ref, sin_ref, up_ref, wt_ref,
    pre_ref, gain_ref, fall_ref, give_ref, keep_ref, key_carry, value_carry, map_carry, later,
    buffer, sems,
    ) = refs
    step = pl.num_programs(0) - 1 - pl.program_id(0)
    group = q_ref.shape[0] // HEAD_SIZE
    rows = q_ref.shape[1]
    half = HEAD_SIZE // 2
    quarter = WINDOW_KEYS
    scale = 1.0 / math.sqrt(HEAD_SIZE)
    second, third, third_far, fourth = bands()
    short = jnp.bfloat16
    per_block = grad_ref.shape[2]
    inner = per_block // SUB

    @pl.when(pl.program_id(0) == 0)
    def _():
        gain_ref[...] = jnp.zeros_like(gain_ref)
        key_carry[...] = jnp.zeros_like(key_carry)
        value_carry[...] = jnp.zeros_like(value_carry)
        map_carry[...] = jnp.zeros_like(map_carry)
        later[...] = jnp.zeros_like(later)
        fall_ref[...] = jnp.zeros_like(fall_ref)

    carried_keys, carried_values, carried_maps = key_carry[...], value_carry[...], map_carry[...]
    later_now = later[...]
    query_parts, map_parts, key_parts, value_parts, key_map_parts = [], [], [], [], []
    for sub in reversed(range(rows // SUB)):
        columns = slice(sub * SUB, (sub + 1) * SUB)
        queries = side_by_side(q_ref, HEAD_SIZE, group, columns)
        query_maps = side_by_side(pq_ref, 2 * HEAD_SIZE, group, columns)
        if sub == 0:
            values = jnp.concatenate([v_before[...], v_ref[:SUB]], axis=0)
            keys_t = jnp.concatenate([kt_before[...], kt_ref[:, :SUB]], axis=1)
            key_maps_t = jnp.concatenate([pkt_before[...], pkt_ref[:, :SUB]], axis=1)
            values_before = vt_before[...]
        else:
            around = slice((sub - 1) * SUB, (sub + 1) * SUB)
            values = v_ref[around]
            keys_t, key_maps_t = kt_ref[:, around], pkt_ref[:, around]
            values_before = vt_ref[:, (sub - 1) * SUB : sub * SUB]
        at = step * rows + sub * SUB + lax.broadcasted_iota(jnp.int32, (HEAD_SIZE, SUB), 1)
        inside = at < length_ref[0]
        numers, denoms = [], []
        for head in range(group):
            base = head * HEAD_SIZE
            span = slice(base, base + HEAD_SIZE)
            place_in = slice(sub % inner * SUB, (sub % inner + 1) * SUB)
            incoming = grad_ref[sub // inner, span, place_in].astype(jnp.float32) + 2.0 * diff_ref[span, columns]
            incoming = jnp.where(inside, incoming.astype(short).astype(jnp.float32), 0.0)
            inverse = 1.0 / denom_ref[head : head + 1, columns]
            numers.append((incoming * inverse).astype(short))
            denoms.append(
                -jnp.sum(incoming * out_ref[span, columns], axis=0, keepdims=True) * inverse
            )
        grad_numer = jnp.concatenate(numers, axis=1)
        grad_denom = jnp.concatenate(denoms, axis=1)
        rank = lax.broadcasted_iota(jnp.int32, (ONES, group * SUB), 0)
        denom_high = grad_denom.astype(short).astype(jnp.float32)
        extra = jnp.where(
            rank == 0, denom_high, jnp.where(rank == 1, grad_denom - denom_high, 0.0)
        ).astype(short)
        grad_both = jnp.concatenate([grad_numer, extra], axis=0)
        weights = weights_ref[sub]
        raw = mm(values, grad_numer)
        scores, fars = [], []
        for head in range(group):
            lanes = slice(head * SUB, (head + 1) * SUB)
            grad_weights = raw[:, lanes] + denoms[head]
            if sub == 0:
                kept = jnp.where(step > 0, grad_weights[: 2 * quarter], 0.0)
                grad_weights = jnp.concatenate([kept, grad_weights[2 * quarter :]], axis=0)
            by_score = grad_weights[quarter:] * weights[quarter:, lanes].astype(jnp.float32)
            scores.append(
                jnp.concatenate(
                    [
                        jnp.where(second, by_score[:quarter], 0.0),
                        jnp.where(third, by_score[quarter : 2 * quarter], 0.0),
                        jnp.where(fourth, by_score[2 * quarter :], 0.0),
                    ],
                    axis=0,
                ).astype(short)
            )
            fars.append(
                jnp.concatenate(
                    [
                        grad_weights[:quarter],
                        jnp.where(second, 0.0, grad_weights[quarter : 2 * quarter]),
                        jnp.where(third_far, grad_weights[2 * quarter : 3 * quarter], 0.0),
                    ],
                    axis=0,
                ).astype(short)
            )
        grad_scores = jnp.concatenate(scores, axis=1)
        grad_far = jnp.concatenate(fars, axis=1)
        state_high, state_low = split_wide(jnp.transpose(states_ref[sub]))
        query_parts.append(mm(keys_t[:, quarter:], grad_scores) * scale)
        map_parts.append(
            mm(key_maps_t[:, : 3 * quarter], grad_far)
            + mm(
                jnp.concatenate([state_high, state_low], axis=1),
                jnp.concatenate([grad_both, grad_both], axis=0),
            )
        )
        grad_keys = mm_nt(queries, grad_scores) * scale
        grad_values = mm_nt(grad_numer, weights)
        grad_key_maps = mm_nt(query_maps, grad_far)
        key_parts.append(carried_keys + grad_keys[:, quarter:])
        value_parts.append(carried_values + grad_values[:, SUB:])
        key_map_parts.append(
            jnp.concatenate(
                [
                    carried_maps[:, :quarter] + grad_key_maps[:, 2 * quarter :],
                    carried_maps[:, quarter:],
                ],
                axis=1,
            )
        )
        later_high, later_low = split_wide(jnp.transpose(later_now))
        carried_keys = jnp.concatenate(
            [jnp.zeros((HEAD_SIZE, quarter), jnp.float32), grad_keys[:, :quarter]], axis=1
        )
        carried_values = grad_values[:, :SUB] + mm(
            later_now[:HEAD_SIZE].astype(short), key_maps_t[:, :SUB]
        )
        carried_maps = grad_key_maps[:, : 2 * quarter] + mm(
            jnp.concatenate([later_high, later_low], axis=1),
            jnp.concatenate([values_before, values_before], axis=0),
        )
        later_now = later_now + mm_nt(grad_both, query_maps)
    key_carry[...], value_carry[...], map_carry[...] = carried_keys, carried_values, carried_maps
    later[...] = later_now

    def joined(parts, lanes=slice(None)):
        return jnp.concatenate([part[:, lanes] for part in reversed(parts)], axis=1)

    cosine, sine = cos_ref[...], sin_ref[...]
    for head in range(group + 1):
        base = head * HEAD_SIZE
        span = slice(base, base + HEAD_SIZE)
        lanes = slice(head * SUB, (head + 1) * SUB)
        if head < group:
            vector, direct = q_ref[span], joined(query_parts, lanes)
            grad_maps = joined(map_parts, lanes)
        else:
            vector, direct, grad_maps = kt_ref[...], joined(key_parts), joined(key_map_parts)
        plus, minus = soft_pair(mm(map_ref[span], vector))
        grad_plus, grad_minus = grad_maps[:HEAD_SIZE], grad_maps[HEAD_SIZE:]
        grad_logits = plus * (
            grad_plus - jnp.sum(grad_plus * plus, axis=0, keepdims=True)
        ) - minus * (grad_minus - jnp.sum(grad_minus * minus, axis=0, keepdims=True))
        grad_logits = grad_logits.astype(short)
        gain_ref[span] += mm_nt(vector, grad_logits)
        total = direct + mm(back_ref[span], grad_logits)
        low_half, high_half = halves_rotated(total[:half], total[half:], cosine, -sine)
        pre_ref[base : base + half] = low_half.astype(short)
        pre_ref[base + half : base + HEAD_SIZE] = high_half.astype(short)
    width = (group + 2) * HEAD_SIZE
    pre_ref[width - HEAD_SIZE : width] = joined(value_parts).astype(short)
    pre_ref[width:] = mm_tn(up_ref[...], pre_ref[:width]).astype(short)
    per_step = rows // per_block

    def order(at):
        return (pl.num_programs(0) - 1 - at // per_step) * per_step + lax.rem(at, per_step)

    own_core = lax.rem(place_ref[0], 2)
    for block in range(rows // per_block):
        columns = slice(block * per_block, (block + 1) * per_block)
        here = pre_ref[:, columns]
        grad_normed = mm_tn(here, wt_ref[...]).astype(short)
        slot = fetch(
            blocks,
            buffer,
            sems,
            pl.program_id(0) * (rows // per_block) + block,
            lambda at: lax.bitwise_xor(order(at), place_ref[0]),
        )
        fall_ref[...] += mm(here[width:], buffer[slot])

        @pl.when(own_core == block % 2)
        def _():
            keep_ref[...] = grad_normed

        @pl.when(own_core != block % 2)
        def _():
            give_ref[...] = grad_normed


def heads_back(
    length, place_row, blocks, grad_att, difference, out_t, denom, q_t, pq_t, weights,
    values, k_t, pk_t, v_t, states, maps_ahead, maps_back, cosine, sine, up_block, weights_t,
):
    places, query_width, per_block = grad_att.shape
    count = places * per_block
    rows = 2 * per_block
    steps = count // rows
    group = query_width // HEAD_SIZE
    per_step = rows // SUB
    counts = [len(found) for found in blocks]
    width, spare = up_block.shape
    model = weights_t.shape[1]
    maps = pk_t.shape[0]
    high = v_t.shape[0]
    half = HEAD_SIZE // 2

    def back(spec):
        return pl.BlockSpec(spec.block_shape, lambda i, *_: spec.index_map(steps - 1 - i))

    def by_chip(i, length_ref, place_ref):
        return (lax.bitwise_xor(steps - 1 - i, place_ref[0] // 2), 0, 0)

    def leading(*dims):
        return pl.BlockSpec((per_step,) + dims, lambda i, *_: (i, 0, 0))

    return call(
        functools.partial(backward_kernel, counts),
        (steps,),
        [ANYWHERE] * sum(counts)
        + [
            back(pl.BlockSpec((2, query_width, per_block), lambda i, *_: (i, 0, 0))),
            back(spec_across(query_width, rows)),
            back(spec_across(query_width, rows)),
            back(spec_across(group, rows)),
            back(spec_across(query_width, rows)),
            back(spec_across(group * maps, rows)),
            back(leading(2 * SUB, group * SUB)),
            back(spec_down(rows, HEAD_SIZE)),
            back(before_down(rows, HEAD_SIZE)),
            back(spec_across(HEAD_SIZE, rows)),
            back(before_across(rows, HEAD_SIZE)),
            back(spec_across(maps, rows)),
            back(before_across(rows, maps)),
            back(spec_across(high, rows)),
            back(before_across(rows, high)),
            back(leading(high, maps)),
            spec_whole(*maps_ahead.shape),
            spec_whole(*maps_back.shape),
            back(spec_across(half, rows)),
            back(spec_across(half, rows)),
            spec_whole(width, spare),
            spec_whole(width + spare, model),
        ],
        [
            back(spec_across(width + spare, rows)),
            spec_whole(*maps_back.shape),
            spec_whole(spare, model),
            pl.BlockSpec((None, per_block, model), by_chip),
            pl.BlockSpec((None, per_block, model), by_chip),
        ],
        [
            array(width + spare, count),
            array(*maps_back.shape, dtype=jnp.float32),
            array(spare, model, dtype=jnp.float32),
            array(steps, per_block, model),
            array(steps, per_block, model),
        ],
        [
            pltpu.VMEM((HEAD_SIZE, SUB), jnp.float32),
            pltpu.VMEM((HEAD_SIZE, SUB), jnp.float32),
            pltpu.VMEM((maps, SUB), jnp.float32),
            pltpu.VMEM((high, maps), jnp.float32),
        ]
        + fetch_scratch(blocks),
        0,
        30,
        scalars=2,
    )(
        length, place_row, *flat(blocks), grad_att, difference, out_t, denom, q_t, pq_t, weights,
        values, values, k_t, k_t, pk_t, pk_t, v_t, v_t,
        states, maps_ahead, maps_back, cosine, sine, up_block, weights_t,
    )


def start_all(blocks, buffer, sems):
    for number, parts in enumerate(blocks):
        height = buffer.shape[1] // len(parts)
        for part, ref in enumerate(parts):
            pltpu.make_async_copy(
                ref, buffer.at[number, part * height : (part + 1) * height], sems.at[number]
            ).start()


def all_scratch(blocks):
    rows, wide = block_shape(blocks)
    return [
        pltpu.VMEM((len(blocks), rows, wide), jnp.bfloat16),
        pltpu.SemaphoreType.DMA((len(blocks),)),
    ]


def placed_rows(ref, place, rows):
    return ref[pl.ds(pl.multiple_of(place * rows, rows), rows)]


def branch_kernel(counts, place_ref, *refs):
    blocks, refs = grouped(refs, counts)
    (
        att_ref, down_ref, up_ref, tokens_ref, gain_ref,
        residual_ref, normed_ref, inverse_ref, narrow_ref, buffer, sems,
    ) = refs
    start_all(blocks, buffer, sems)
    width = att_ref.shape[1]
    total, slim = tokens_ref[...].astype(jnp.float32), None
    for number in range(len(blocks)):
        place = lax.bitwise_xor(place_ref[0], number)
        att = att_ref[place]
        part = mm_tn(att, placed_rows(down_ref, place, width))
        slim = part if slim is None else slim + part
        wait_whole(buffer.at[number], sems.at[number])
        total = total + mm_tn(att, buffer[number])
    narrow = slim.astype(jnp.bfloat16)
    narrow_ref[...] = narrow
    residual = total + mm_nt(narrow, up_ref[...])
    residual_ref[...] = residual
    inverse = lax.rsqrt(jnp.mean(residual * residual, axis=-1, keepdims=True) + epsilon)
    inverse_ref[...] = jnp.broadcast_to(inverse, inverse_ref.shape)
    normed_ref[...] = (residual * inverse * gain_ref[...]).astype(jnp.bfloat16)


def branch_out(place_row, blocks, att, down_wide, up_wide, tokens, gain):
    places, query_width, rows = att.shape
    model = tokens.shape[1]
    spare = down_wide.shape[1]
    counts = [len(found) for found in blocks]
    wide = jnp.float32
    return call(
        functools.partial(branch_kernel, counts),
        (1,),
        [ANYWHERE] * sum(counts)
        + [spec_whole(*part.shape) for part in (att, down_wide, up_wide, tokens, gain)],
        [
            spec_whole(rows, model),
            spec_whole(rows, model),
            spec_whole(rows, 128),
            spec_whole(rows, spare),
        ],
        [
            array(rows, model, dtype=wide),
            array(rows, model),
            array(rows, 128, dtype=wide),
            array(rows, spare),
        ],
        all_scratch(blocks),
        0,
        13,
        scalars=1,
    )(place_row, *flat(blocks), att, down_wide, up_wide, tokens, gain)


def branch_back_kernel(counts, place_ref, *refs):
    blocks, refs = grouped(refs, counts)
    (
        own_ref, from_x, late_x, late_y, from_y, residual_ref, inverse_ref, gain_ref, cot_ref,
        down_ref, up_ref,
        grad_att_ref, grad_ref, branch_ref, slim_ref, buffer, sems,
    ) = refs
    start_all(blocks, buffer, sems)
    wide = jnp.float32
    middle = late_x.shape[0]
    for start, part in enumerate(sums_of(own_ref, from_x, late_x, late_y, from_y)):
        span = slice(start * middle, (start + 1) * middle)
        residual, inverse = residual_ref[span], inverse_ref[span, :1]
        scaled = part * gain_ref[...]
        mean = jnp.mean(scaled * residual, axis=-1, keepdims=True)
        grad = (
            cot_ref[span].astype(wide)
            + inverse * scaled
            - residual * (inverse * inverse * inverse * mean)
        )
        grad_ref[span] = grad
        branch_ref[span] = grad.astype(jnp.bfloat16)
    branch = branch_ref[...]
    slim = mm(branch, up_ref[...])
    slim_ref[...] = slim
    slim = slim.astype(jnp.bfloat16)
    width = grad_att_ref.shape[1]
    for number in range(len(blocks)):
        place = lax.bitwise_xor(place_ref[0], number)
        part = mm_nt(placed_rows(down_ref, place, width), slim)
        wait_whole(buffer.at[number], sems.at[number])
        grad_att_ref[place] = (mm_nt(buffer[number], branch) + part).astype(jnp.bfloat16)


def branch_back(
    place_row, blocks, sums, residual, inverse, gain, cotangent, down_wide, up_wide
):
    places = len(blocks)
    rows, model = residual.shape
    query_width = model // places
    spare = down_wide.shape[1]
    counts = [len(found) for found in blocks]
    wide = jnp.float32
    given = (*sums, residual, inverse, gain, cotangent, down_wide, up_wide)
    return call(
        functools.partial(branch_back_kernel, counts),
        (1,),
        [ANYWHERE] * sum(counts) + [spec_whole(*part.shape) for part in given],
        [
            spec_whole(places, query_width, rows),
            spec_whole(rows, model),
            spec_whole(rows, model),
            spec_whole(rows, spare),
        ],
        [
            array(places, query_width, rows),
            array(rows, model, dtype=wide),
            array(rows, model),
            array(rows, spare, dtype=wide),
        ],
        all_scratch(blocks),
        0,
        15,
        scalars=1,
    )(place_row, *flat(blocks), *given)


def exchanged(value, bits):
    count = lax.axis_size("seq")
    return lax.ppermute(value, "seq", [(place, place ^ bits) for place in range(count)])


def after(value, *others):
    return pl.pallas_call(
        lambda *refs: None,
        out_shape=jax.ShapeDtypeStruct(value.shape, value.dtype),
        in_specs=[pl.BlockSpec(memory_space=pl.ANY)] * (1 + len(others)),
        out_specs=pl.BlockSpec(memory_space=pl.ANY),
        input_output_aliases={0: 0},
    )(value, *others)


def halves(value):
    middle = value.shape[0] // 2
    return value[:middle], value[middle:]


def regroup_kernel(*refs):
    out_ref = refs[-1]
    unit = out_ref.shape[3]
    for number, ref in enumerate(refs[:-1]):
        for place in range(out_ref.shape[0]):
            out_ref[place, number] = ref[:, place * unit : (place + 1) * unit]


def regroup(places, *matrices):
    rows, wide = matrices[0].shape
    unit = wide // places
    return call(
        regroup_kernel,
        (places // PAIR,),
        [spec_across(rows, PAIR * unit)] * len(matrices),
        pl.BlockSpec((PAIR, len(matrices), rows, unit), lambda i: (i, 0, 0, 0)),
        array(places, len(matrices), rows, unit),
        [],
        0,
        6,
    )(*matrices)


def ungroup_kernel(ref, *refs):
    rows = ref.shape[2]
    for number, out_ref in enumerate(refs):
        for place in range(ref.shape[0]):
            out_ref[place * rows : (place + 1) * rows] = ref[place, number]


def ungroup(blocks):
    places, count, rows, unit = blocks.shape
    return call(
        ungroup_kernel,
        (places // PAIR,),
        [pl.BlockSpec((PAIR, count, rows, unit), lambda i: (i, 0, 0, 0))],
        [spec_down(PAIR * rows, unit)] * count,
        [array(places * rows, unit)] * count,
        [],
        0,
        6,
    )(blocks)


def gather_first(value):
    return exchanged(value, 1), exchanged(value, 2), exchanged(value, 4)


def gather_rest(value, beside, along_x, along_y, *others, last=()):
    upper, lower = halves(along_x)[0], halves(along_y)[1]
    if others:
        upper, lower = after(upper, *others), after(lower, *others)
    first, second = exchanged(upper, 4), exchanged(lower, 2)
    if last:
        first, second = after(first, *last), after(second, *last)
    return [
        (value,),
        (beside,),
        (along_x,),
        (exchanged(along_x, 1),),
        (along_y,),
        (exchanged(along_y, 1),),
        (first, second),
        (exchanged(first, 1), exchanged(second, 1)),
    ]


def plane_gather(value):
    return gather_rest(value, *gather_first(value))


def core_sums_kernel(keep_ref, got_ref, own_ref, to_x, to_y, later_x, later_y):
    wide, short = jnp.float32, jnp.bfloat16
    middle = later_x.shape[0]

    def both(bits, span=slice(None)):
        return keep_ref[bits, span].astype(wide) + got_ref[bits, span].astype(wide)

    upper, lower = slice(0, middle), slice(middle, None)
    own_ref[...] = both(0)
    to_x[upper], to_x[lower] = both(3, upper).astype(short), both(1, upper).astype(short)
    to_y[upper], to_y[lower] = both(3, lower).astype(short), both(2, lower).astype(short)
    later_x[...] = both(1, lower).astype(short)
    later_y[...] = both(2, upper).astype(short)


def core_sums(keep, got):
    _, rows, model = keep.shape
    wide = model // 2
    block = pl.BlockSpec((4, rows, wide), lambda i: (0, 0, i))
    return call(
        core_sums_kernel,
        (2,),
        [block] * 2,
        [spec_across(rows, wide)] * 3 + [spec_across(rows // 2, wide)] * 2,
        [array(rows, model, dtype=jnp.float32)]
        + [array(rows, model)] * 2
        + [array(rows // 2, model)] * 2,
        [],
        0,
        5,
    )(keep, got)


def scatter_first(give, keep):
    own, to_x, to_y, later_x, later_y = core_sums(keep, exchanged(give, 1))
    return own, exchanged(to_x, 2), exchanged(to_y, 4), later_x, later_y


def scatter_rest(own, from_x, from_y, later_x, later_y, *others):
    middle = later_x.shape[0]
    wide, short = jnp.float32, jnp.bfloat16
    if others:
        later_x, later_y = after(later_x, *others), after(later_y, *others)
    late_y = exchanged((later_y.astype(wide) + from_x[:middle].astype(wide)).astype(short), 4)
    late_x = exchanged((later_x.astype(wide) + from_y[:middle].astype(wide)).astype(short), 2)
    return own, from_x, late_x, late_y, from_y


def sums_of(own_ref, from_x, late_x, late_y, from_y):
    wide = jnp.float32
    middle = late_x.shape[0]
    return (
        own_ref[:middle] + from_x[middle:].astype(wide) + late_y[...].astype(wide),
        own_ref[middle:] + late_x[...].astype(wide) + from_y[middle:].astype(wide),
    )


def tokens_back_kernel(
    own_ref, from_x, late_x, late_y, from_y, tokens_ref, inverse_ref, gain_ref, grad_ref, out_ref
):
    middle = late_x.shape[0]
    for start, part in enumerate(sums_of(own_ref, from_x, late_x, late_y, from_y)):
        span = slice(start * middle, (start + 1) * middle)
        values, inverse = tokens_ref[span].astype(jnp.float32), inverse_ref[span, :1]
        scaled = part * gain_ref[...]
        mean = jnp.mean(scaled * values, axis=-1, keepdims=True)
        out_ref[span] = (
            grad_ref[span] + inverse * scaled - values * (inverse * inverse * inverse * mean)
        ).astype(jnp.bfloat16)


def tokens_back(sums, tokens, inverse, gain, grad):
    rows, model = tokens.shape
    return call(
        tokens_back_kernel,
        (1,),
        [spec_whole(*part.shape) for part in (*sums, tokens, inverse, gain, grad)],
        spec_whole(rows, model),
        array(rows, model),
        [],
        0,
        6,
    )(*sums, tokens, inverse, gain, grad)


def ring(value):
    count = lax.axis_size("fsdp")
    found = [value]
    for _ in range(count - 1):
        found.append(ring_step(found[-1]))
    return found


def ring_step(value):
    count = lax.axis_size("fsdp")
    return lax.ppermute(value, "fsdp", [(at, (at + 1) % count) for at in range(count)])


def by_heads(
    tokens,
    lengths,
    norm_attn,
    norm_ffn,
    w_query,
    key_projection,
    value_projection,
    w_output,
    w_gate,
    w_up,
    w_down,
    down_query,
    up_query,
    key_down_matrix,
    key_up_matrix,
    value_down_matrix,
    value_up_matrix,
    down_output,
    up_output,
    feature_query,
    key_feature_weight,
    cotangent,
):
    places = lax.axis_size("seq")
    lanes = lax.axis_size("fsdp")
    rows = tokens.shape[1]
    model = tokens.shape[2]
    count = rows * places
    group = QUERY_HEADS // KEY_VALUE_HEADS
    query_width = group * HEAD_SIZE
    width = query_width + 2 * HEAD_SIZE
    rank = down_query.shape[1]
    spare = 128
    place = lax.axis_index("seq")
    lane = lax.axis_index("fsdp")
    place_row = place.astype(jnp.int32).reshape(1)
    length = lax.dynamic_slice_in_dim(lengths, lane, 1)
    bf16, f32 = jnp.bfloat16, jnp.float32
    inputs_wide = tokens[0].astype(f32)
    gain_attn = norm_attn.astype(f32)
    gain_ffn = norm_ffn.astype(f32).reshape(1, model)

    shard = w_query.shape[0]
    by_place = jnp.concatenate(
        [
            w_query.reshape(shard, places, query_width),
            key_projection.reshape(shard, places, HEAD_SIZE),
            value_projection.reshape(shard, places, HEAD_SIZE),
        ],
        axis=2,
    )
    by_place = lax.all_to_all(jnp.moveaxis(by_place, 1, 0), "seq", 0, 0, tiled=True)
    own_weights = lax.all_gather(by_place, "fsdp", axis=0)

    inverse_attn = lax.rsqrt(jnp.mean(inputs_wide * inputs_wide, axis=-1, keepdims=True) + epsilon)
    normed_all = plane_gather((inputs_wide * inverse_attn * gain_attn).astype(bf16))
    across = normed_all[6]
    down_block = jnp.concatenate(
        [
            down_query.T,
            key_down_matrix.T,
            value_down_matrix.T,
            jnp.zeros((spare - 3 * rank, model), bf16),
        ],
        axis=0,
    )

    output_rows = lax.all_gather(w_output, "fsdp", axis=0)
    swapped = after(regroup(places, w_gate, w_up, w_down), by_place)
    swapped = lax.all_to_all(swapped, "seq", 0, 0, tiled=True)

    def own_rows(matrix, size):
        return lax.dynamic_slice_in_dim(matrix, place * size, size, 0)

    up_own = (
        own_rows(up_query, query_width),
        own_rows(key_up_matrix, HEAD_SIZE),
        own_rows(value_up_matrix, HEAD_SIZE),
    )
    up_block = jnp.concatenate(
        [
            jnp.pad(part, ((0, 0), (at * rank, spare - (at + 1) * rank)))
            for at, part in enumerate(up_own)
        ],
        axis=0,
    )
    maps_back = jnp.concatenate(
        [own_rows(feature_query, query_width), own_rows(key_feature_weight, HEAD_SIZE)], axis=0
    )
    maps_ahead = jnp.swapaxes(
        maps_back.reshape(group + 1, HEAD_SIZE, HEAD_SIZE), 1, 2
    ).reshape((group + 1) * HEAD_SIZE, HEAD_SIZE)
    frequency = rope_base ** (-(jnp.arange(HEAD_SIZE // 2, dtype=f32) * 2.0) / HEAD_SIZE)
    phase = jnp.arange(count, dtype=jnp.int32).astype(f32)[None, :] * frequency[:, None]
    cosine, sine = jnp.cos(phase), jnp.sin(phase)
    down_wide = jnp.pad(down_output, ((0, 0), (0, spare - rank)))
    up_wide = jnp.pad(up_output, ((0, 0), (0, spare - rank)))

    q_t, k_t, v_t, keys, values, pq_t, pk_t, key_maps, narrow_t, own_weights_t = project(
        place_row, normed_all, own_weights, down_block, up_block, maps_ahead, cosine, sine
    )
    output_rows = after(output_rows.reshape(lanes * shard, model), q_t)
    output_first = gather_first(output_rows)
    att, out_t, denom, states, att_weights = attend(
        length, q_t, pq_t, keys, key_maps, v_t, rows
    )
    own_gate, own_up, own_down = ungroup(swapped)
    up_weights = lax.all_gather(own_up, "fsdp", axis=0)
    unit = own_down.shape[1] // PARTS
    down_weights = [
        lax.all_gather(own_down[:, part * unit : (part + 1) * unit], "fsdp", axis=0)
        for part in range(PARTS)
    ]
    gate_weights = ring(own_gate)
    chunk_order = lax.rem(lane - jnp.arange(lanes) + lanes, lanes).astype(jnp.int32)
    output_blocks = gather_rest(output_rows, *output_first, att)
    att_all = lax.all_to_all(att, "seq", 0, 0, tiled=True)
    middle = places // 2 + 1
    taught = teach(
        after(length, *output_first, gate_weights[1]), q_t, keys, v_t, att, 0, middle
    )
    residual, normed_ffn, inverse_ffn, narrow_out = branch_out(
        after(place_row, taught[1]), output_blocks, att_all, down_wide, up_wide, tokens[0], gain_ffn
    )
    ffn_first = gather_first(normed_ffn)
    difference, loss_rows = teach(
        after(length, normed_ffn), q_t, keys, v_t, att, middle, places, taught
    )
    ffn_all = gather_rest(normed_ffn, *ffn_first, loss_rows)
    cot_first = gather_first(after(cotangent[0], *ffn_all[6], gate_weights[2]))
    losses = jnp.sum(loss_rows[0].reshape(places, rows), axis=1)
    hidden, by_gate, by_up = hidden_units(chunk_order, ffn_all, gate_weights, up_weights)
    cot_all = gather_rest(cotangent[0], *cot_first, last=(hidden,))
    early = None
    for part in range(PARTS - 1):
        early = ffn_back(
            chunk_order, cot_all, 0, 1, part, gate_weights, up_weights, down_weights[part], by_gate, by_up, early
        )
    by_chip = (places // 2, rows, model)
    last = (PARTS - 1, gate_weights, up_weights, down_weights[-1], by_gate, by_up, early)
    grad_give = ffn_back(chunk_order, cot_all[1::2], 1, 2, *last)
    grad_keep = ffn_back(chunk_order, cot_all[0::2], 0, 2, *last)
    grad_first = scatter_first(grad_give.reshape(by_chip), grad_keep.reshape(by_chip))
    out_part = ffn_out(after(place_row, grad_first[0]), chunk_order, hidden, down_weights, places)

    grad_sums = scatter_rest(*grad_first, out_part)
    grad_att, grad_residual, grad_branch, grad_narrow_out = branch_back(
        place_row,
        output_blocks, grad_sums, residual, inverse_ffn, gain_ffn, cotangent[0],
        down_wide, up_wide,
    )
    out_sum = lax.psum_scatter(out_part, "seq", scatter_dimension=0, tiled=True)
    output = (residual + out_sum.astype(f32)).astype(bf16)
    grad_att = lax.all_to_all(grad_att, "seq", 0, 0, tiled=True)
    grad_up_output = mm_tn(narrow_out, grad_branch)[:rank]
    grad_down_output = jnp.einsum(
        "sft,tr->rsf", att_all, grad_narrow_out[:, :rank].astype(bf16), preferred_element_type=f32
    ).reshape(rank, model)

    grad_pre_t, grad_maps, grad_down_t, normed_give, normed_keep = heads_back(
        length, place_row, normed_all, grad_att, difference, out_t, denom,
        q_t, pq_t, att_weights, values, k_t, pk_t, v_t, states, maps_ahead, maps_back,
        cosine, sine, up_block, own_weights_t,
    )
    normed_sums = scatter_rest(*scatter_first(normed_give, normed_keep))
    grad_up_block = mm_nt(grad_pre_t[:width], narrow_t)
    grad_down_t = grad_down_t[: 3 * rank]
    grad_tokens = tokens_back(
        normed_sums, tokens[0], jnp.broadcast_to(inverse_attn, (rows, spare)),
        gain_attn.reshape(1, model), grad_residual,
    )

    devices = places * lanes
    ahead = jnp.arange(devices)[None, :] >= (jnp.arange(places) * lanes + lane)[:, None]
    running = jnp.sum(jnp.where(ahead, losses[:, None], 0.0), axis=0)
    loss_row = jnp.pad(running[:, None], ((0, 0), (0, model // devices - 1))).reshape(1, model)
    shared = jnp.concatenate([grad_down_t, grad_down_output, grad_up_output, loss_row], axis=0)
    shared = after(jnp.moveaxis(shared.reshape(-1, devices, model // devices), 1, 0), normed_sums[0])
    shared = jnp.sum(
        lax.all_to_all(shared, ("seq", "fsdp"), 0, 0, tiled=True).reshape(shared.shape), axis=0
    )

    def columns(at):
        return shared[at * rank : (at + 1) * rank].T

    transfer_loss = shared[5 * rank, :1] / jnp.sum(lengths).astype(f32)

    pieces = [
        grad_maps[:query_width].reshape(lanes, -1),
        grad_maps[query_width:].reshape(lanes, -1),
        grad_up_block[:query_width, :rank].reshape(lanes, -1),
        grad_up_block[query_width : query_width + HEAD_SIZE, rank : 2 * rank].reshape(lanes, -1),
        grad_up_block[query_width + HEAD_SIZE :, 2 * rank : 3 * rank].reshape(lanes, -1),
    ]
    packed = after(jnp.concatenate(pieces, axis=1), normed_sums[0])
    packed = jnp.sum(lax.all_to_all(packed, "fsdp", 0, 0, tiled=True).reshape(packed.shape), axis=0)
    ends = [0]
    for piece in pieces:
        ends.append(ends[-1] + piece.shape[1])
    map_query, map_key, up_q, up_k, up_v = (
        packed[ends[at] : ends[at + 1]].reshape(-1, wide)
        for at, wide in enumerate((HEAD_SIZE, HEAD_SIZE, rank, rank, rank))
    )
    return (
        output[None],
        grad_tokens[None],
        columns(0),
        up_q,
        columns(1),
        up_k,
        columns(2),
        up_v,
        columns(3),
        columns(4),
        map_query,
        map_key,
        transfer_loss,
    )


def solution(mesh):
    placed = (
        P("fsdp", "seq", None),
        P(),
        P(),
        P(),
        P(("seq", "fsdp"), None),
        P(("seq", "fsdp"), None),
        P(("seq", "fsdp"), None),
        P(("seq", "fsdp"), None),
        P("seq", "fsdp"),
        P("seq", "fsdp"),
        P("seq", "fsdp"),
        P(),
        P(),
        P(),
        P(),
        P(),
        P(),
        P(),
        P(),
        P(),
        P(),
        P("fsdp", "seq", None),
    )
    sizes = dict(mesh.shape)
    heads_match = sizes["seq"] == KEY_VALUE_HEADS == 8 and (
        QUERY_HEADS // KEY_VALUE_HEADS == sizes["fsdp"]
    )
    return jax.shard_map(
        by_heads if heads_match else local,
        mesh=mesh,
        in_specs=placed,
        out_specs=(
            P("fsdp", "seq", None),
            P("fsdp", "seq", None),
            P(("seq", "fsdp"), None),
            P(("seq", "fsdp"), None),
            P(("seq", "fsdp"), None),
            P(("seq", "fsdp"), None),
            P(("seq", "fsdp"), None),
            P(("seq", "fsdp"), None),
            P(("seq", "fsdp"), None),
            P(("seq", "fsdp"), None),
            P(("seq", "fsdp"), None),
            P(("seq", "fsdp"), None),
            P(("seq", "fsdp")),
        ),
        check_vma=False,
    )
```
